32 devices in a mesh: dp: 8 (over z, x), tensor: 4 (over y, core).
Axes of the slice: x: 2, y: 2, z: 4, core: 2. Of those that a mesh axis runs over, the one named last changes fastest.
Arguments:
- tokens: bfloat16 [16384, 1536], P(('dp', 'tensor')), may hold values from -6 to 6
- cotangent: bfloat16 [16384, 1536], P(('dp', 'tensor')), may hold values from -6 to 6
- lengths: int32 [16], P('dp'), may hold values from 1 to 1024, 12288 in all
- qkv_weight: float32 [1536, 3072], P('dp', 'tensor')
- out_weight: float32 [1536, 1536], P('tensor', 'dp'), may hold values from -6 to 6
- gate_up_weight: float32 [2, 1536, 4096], P(None, 'dp', 'tensor'), may hold values from -1 to 1
- down_weight: float32 [4096, 1536], P('tensor', 'dp')
- norm_gains: float32 [2, 1536], P(None, ('dp', 'tensor')), may hold values from 0 to 4
- qkv_first: float32 [1536, 3072], P('dp', 'tensor')
- out_first: float32 [1536, 1536], P('tensor', 'dp')
- gate_up_first: float32 [2, 1536, 4096], P(None, 'dp', 'tensor')
- down_first: float32 [4096, 1536], P('tensor', 'dp')
- gains_first: float32 [2, 1536], P(None, ('dp', 'tensor'))
- qkv_second: float32 [1536, 3072], P('dp', 'tensor'), as said below
- out_second: float32 [1536, 1536], P('tensor', 'dp'), as said below
- gate_up_second: float32 [2, 1536, 4096], P(None, 'dp', 'tensor'), as said below
- down_second: float32 [4096, 1536], P('tensor', 'dp'), as said below
- gains_second: float32 [2, 1536], P(None, ('dp', 'tensor')), as said below
Outputs:
- layer_out: bfloat16 [16384, 1536], P(('dp', 'tensor'))
- grad_tokens: float32 [16384, 1536], P(('dp', 'tensor'))
- new_qkv: float32 [1536, 3072], P('dp', 'tensor')
- new_out: float32 [1536, 1536], P('tensor', 'dp')
- new_gate_up: float32 [2, 1536, 4096], P(None, 'dp', 'tensor')
- new_down: float32 [4096, 1536], P('tensor', 'dp')
- new_gains: float32 [2, 1536], P(None, ('dp', 'tensor'))
- next_qkv_first: float32 [1536, 3072], P('dp', 'tensor')
- next_out_first: float32 [1536, 1536], P('tensor', 'dp')
- next_gate_up_first: float32 [2, 1536, 4096], P(None, 'dp', 'tensor')
- next_down_first: float32 [4096, 1536], P('tensor', 'dp')
- next_gains_first: float32 [2, 1536], P(None, ('dp', 'tensor'))
- next_qkv_second: float32 [1536, 3072], P('dp', 'tensor')
- next_out_second: float32 [1536, 1536], P('tensor', 'dp')
- next_gate_up_second: float32 [2, 1536, 4096], P(None, 'dp', 'tensor')
- next_down_second: float32 [4096, 1536], P('tensor', 'dp')
- next_gains_second: float32 [2, 1536], P(None, ('dp', 'tensor'))
- weight_norms: float32 [7], replicated
- update_norms: float32 [5], replicated
- gain_update_norms: float32 [2], replicated
The draws below stay inside these ranges and needn't reach their ends.
Inputs may be any that keep to these rules, and one draw needn't show every extreme that they name: Sequence lengths sum to 12288. `qkv_second`: Positive. `out_second`: Positive. `gate_up_second`: Positive. `down_second`: Positive. `gains_second`: Positive.
All inputs are finite; a program needn't handle non-finite values. No bound on the sum of `lengths` on one device may be relied on, other than what follows from the above.
Results may differ from the reference program's by a relative error of at most 0.023.
Values may be sent and summed in bfloat16 or wider, within the bound.
A program may use at most 256 MiB of HBM per device.

```python
import math
import jax
import jax.numpy as jnp
import numpy as np
from jax import lax

D = 1536
HEADS = 16
KV_HEADS = 8
HEAD = 96
FF = 4096
SEQ_LEN = 1024
STEP = 10
GROUP = 2
QKV = 3072
SEQS = 16
TOKENS = 16384


def rising(array_shape, sharded, steepness):
    factor = jnp.ones(array_shape, jnp.float32)
    for dim_index in sharded:
        fraction = lax.broadcasted_iota(jnp.float32, array_shape, dim_index) / array_shape[dim_index]
        factor = factor * (1.0 + steepness * fraction) / (1.0 + 0.5 * steepness)
    return factor


def scaled_normal(subkey, array_shape, sharded, spread, steepness):
    normal_part = jax.random.truncated_normal(subkey, -4.0, 4.0, array_shape, jnp.float32)
    return normal_part * spread * jnp.sqrt(rising(array_shape, sharded, steepness))


def positive_square(subkey, array_shape, spread):
    return jax.random.uniform(subkey, array_shape, jnp.float32, 1.0, 4.0) * spread


def attended_square():
    return min(1.0, 2.7 * (math.log(SEQ_LEN) + 0.6) / SEQ_LEN)


def size_qkv():
    return 1.5 * TOKENS ** 0.5


def size_out():
    return 1.1 * (attended_square() * TOKENS) ** 0.5


def size_gate_up():
    return 0.6 * (D / FF) ** 0.5 * TOKENS ** 0.5


def size_down():
    return 0.6 * TOKENS ** 0.5


def size_gains():
    return jnp.array([1.5 * (QKV / D) ** 0.5, 0.8], jnp.float32)[:, None] * TOKENS ** 0.5


def draw_qkv_weight(key, part):
    key = jax.random.fold_in(key, 1)
    steepness = 2.0
    return scaled_normal(key, (D, QKV), (0, 1), D ** (-0.5), steepness)


def draw_out_weight(key, part):
    key = jax.random.fold_in(key, 2)
    steepness = 2.0
    return scaled_normal(key, (HEADS * HEAD, D), (0, 1), (HEADS * HEAD) ** (-0.5) * (SEQ_LEN / 16.0) ** 0.5, steepness)


def draw_gate_up_weight(key, part):
    key = jax.random.fold_in(key, 3)
    steepness = 2.0
    return scaled_normal(key, (2, D, FF), (1, 2), D ** (-0.5), steepness)


def draw_down_weight(key, part):
    key = jax.random.fold_in(key, 4)
    steepness = 2.0
    return scaled_normal(key, (FF, D), (0, 1), FF ** (-0.5), steepness)


def draw_norm_gains(key, part):
    key = jax.random.fold_in(key, 5)
    steepness = 2.0
    base_gain = 1.0 + 0.1 * jax.random.truncated_normal(key, -4.0, 4.0, (2, D), jnp.float32)
    return base_gain * jnp.sqrt(rising((2, D), (1,), steepness))


def draw_qkv_first(key, part):
    key = jax.random.fold_in(key, 6)
    steepness = 2.0
    return scaled_normal(key, (D, QKV), (0, 1), 0.1 / 0.9 * size_qkv(), steepness)


def draw_out_first(key, part):
    key = jax.random.fold_in(key, 7)
    steepness = 2.0
    return scaled_normal(key, (HEADS * HEAD, D), (0, 1), 0.1 / 0.9 * size_out(), steepness)


def draw_gate_up_first(key, part):
    key = jax.random.fold_in(key, 8)
    steepness = 2.0
    return scaled_normal(key, (2, D, FF), (1, 2), 0.1 / 0.9 * size_gate_up(), steepness)


def draw_down_first(key, part):
    key = jax.random.fold_in(key, 9)
    steepness = 2.0
    return scaled_normal(key, (FF, D), (0, 1), 0.1 / 0.9 * size_down(), steepness)


def draw_gains_first(key, part):
    key = jax.random.fold_in(key, 10)
    steepness = 2.0
    return scaled_normal(key, (2, D), (1,), 1.0, steepness) * (0.1 / 0.9 * size_gains())


def draw_qkv_second(key, part):
    key = jax.random.fold_in(key, 11)
    return positive_square(key, (D, QKV), 0.001 / 0.999 * size_qkv() ** 2)


def draw_out_second(key, part):
    key = jax.random.fold_in(key, 12)
    return positive_square(key, (HEADS * HEAD, D), 0.001 / 0.999 * size_out() ** 2)


def draw_gate_up_second(key, part):
    key = jax.random.fold_in(key, 13)
    return positive_square(key, (2, D, FF), 0.001 / 0.999 * size_gate_up() ** 2)


def draw_down_second(key, part):
    key = jax.random.fold_in(key, 14)
    return positive_square(key, (FF, D), 0.001 / 0.999 * size_down() ** 2)


def draw_gains_second(key, part):
    key = jax.random.fold_in(key, 15)
    return positive_square(key, (2, D), 1.0) * (0.001 / 0.999 * size_gains() ** 2)


def level_of(own_key, dims, cuts, least, high):
    loudness = 1.0
    for axis_at, parts in cuts:
        draws = jax.random.uniform(jax.random.fold_in(jax.random.fold_in(own_key, 6), axis_at), (parts,), jnp.float32, least / len(cuts), high / len(cuts))
        loudness = loudness * jnp.repeat(jnp.exp(draws), dims[axis_at] // parts).reshape((-1,) + (1,) * (len(dims) - 1 - axis_at))
    return loudness


def split_up(amount, total, reach, lean):
    weights = [(1 << 20) // math.isqrt(grade ** lean) + 1 for grade in range(2, amount + 1)]
    spare, given = total - reach - (amount - 1), [1] * (amount - 1)
    while spare > 0:
        free = [i for i in range(amount - 1) if given[i] < reach]
        mass, left = sum([weights[i] for i in free]), spare
        for i in free:
            addition = min(reach - given[i], max(1, left * weights[i] // mass), spare)
            given[i] = given[i] + addition
            spare = spare - addition
    return np.array([reach] + given)


def uneven(rng, number_of, total, limit, skew):
    if number_of == 2:
        one = jax.random.randint(rng, (), max(1, total - limit), min(limit, total - 1) + 1)
        return jnp.stack([one, total - one])
    tallies = jnp.asarray(split_up(number_of, total, limit, skew), jnp.int32)
    pairs = (number_of - 1) // 2
    source_of, receiver = tallies[1:1 + 2 * pairs:2], tallies[2:2 + 2 * pairs:2]
    slack = jnp.minimum(source_of - 1, limit - receiver)
    moved = jax.random.randint(jax.random.fold_in(rng, 1), (pairs,), 0, 1 << 20) % (slack + 1)
    tallies = tallies.at[1:1 + 2 * pairs:2].set(source_of - moved).at[2:2 + 2 * pairs:2].set(receiver + moved)
    return tallies[jax.random.permutation(jax.random.fold_in(rng, 2), number_of)]


def noise(own_key, shape, width, limit, pieces=(), held_as=jnp.bfloat16):
    level = level_of(own_key, shape, pieces, -0.22, 0.18) if pieces else 1.0
    values = jax.random.normal(own_key, shape, jnp.float32) * width * level
    return jnp.minimum(jnp.maximum(values, -limit), limit).astype(held_as)


def setup_inputs(seed: int = 0) -> dict:
    splits = jax.random.split(jax.random.key(seed), 19)
    tokens = noise(splits[0], (TOKENS, D), 1.0, 6.0, ((0, 32),))
    cotangent = noise(splits[1], (TOKENS, D), 1.0, 6.0, ((0, 32),))
    lengths = uneven(splits[2], SEQS, SEQS * SEQ_LEN * 3 // 4, SEQ_LEN, 1).astype(jnp.int32)
    qkv_weight = draw_qkv_weight(jax.random.fold_in(splits[18], 71), 0)
    out_weight = draw_out_weight(jax.random.fold_in(splits[18], 71), 0)
    gate_up_weight = draw_gate_up_weight(jax.random.fold_in(splits[18], 71), 0)
    down_weight = draw_down_weight(jax.random.fold_in(splits[18], 71), 0)
    norm_gains = draw_norm_gains(jax.random.fold_in(splits[18], 71), 0)
    qkv_first = draw_qkv_first(jax.random.fold_in(splits[18], 71), 0)
    out_first = draw_out_first(jax.random.fold_in(splits[18], 71), 0)
    gate_up_first = draw_gate_up_first(jax.random.fold_in(splits[18], 71), 0)
    down_first = draw_down_first(jax.random.fold_in(splits[18], 71), 0)
    gains_first = draw_gains_first(jax.random.fold_in(splits[18], 71), 0)
    qkv_second = draw_qkv_second(jax.random.fold_in(splits[18], 71), 0)
    out_second = draw_out_second(jax.random.fold_in(splits[18], 71), 0)
    gate_up_second = draw_gate_up_second(jax.random.fold_in(splits[18], 71), 0)
    down_second = draw_down_second(jax.random.fold_in(splits[18], 71), 0)
    gains_second = draw_gains_second(jax.random.fold_in(splits[18], 71), 0)
    return dict(tokens=tokens, cotangent=cotangent, lengths=lengths, qkv_weight=qkv_weight, out_weight=out_weight, gate_up_weight=gate_up_weight, down_weight=down_weight, norm_gains=norm_gains, qkv_first=qkv_first, out_first=out_first, gate_up_first=gate_up_first, down_first=down_first, gains_first=gains_first, qkv_second=qkv_second, out_second=out_second, gate_up_second=gate_up_second, down_second=down_second, gains_second=gains_second)


NORM_EPSILON = 1e-05
ROPE_THETA = 100000.0
BETA_ONE = 0.9
BETA_TWO = 0.999
ADAM_EPSILON = 1e-06
WEIGHT_DECAY = 0.01
LEARN_RATE = 0.3
NEGATIVE = -1e+30
PRECISE = lax.Precision.HIGHEST

@jax.custom_vjp
def low(v):
    return lax.optimization_barrier(v.astype(jnp.bfloat16)).astype(jnp.float32)

@jax.custom_vjp
def low_back(v):
    return v

def low_keep(v):
    return (low(v), None)

def low_pass(kept, grad):
    return (grad,)

def back_keep(v):
    return (v, None)

def back_low(kept, grad):
    return (low(grad),)
low.defvjp(low_keep, low_pass)
low_back.defvjp(back_keep, back_low)

def product(left, right):
    return jnp.dot(left, right, precision=PRECISE)

def rms_norm(values, gain_row):
    return values * lax.rsqrt(lax.optimization_barrier(jnp.mean(values * values, axis=-1, keepdims=True)) + NORM_EPSILON) * gain_row

def rotary_tables(length):
    half_width = HEAD // 2
    frequency = ROPE_THETA ** (-(jnp.arange(half_width, dtype=jnp.float32) * (2.0 / HEAD)))
    angles = jnp.arange(length, dtype=jnp.float32)[:, None] * frequency[None, :]
    return (jnp.cos(angles), jnp.sin(angles))

def rotate(values, cosine, sine_part):
    half_width = values.shape[-1] // 2
    first_half = values[..., :half_width]
    second_half = values[..., half_width:]
    return jnp.concatenate([first_half * cosine - second_half * sine_part, second_half * cosine + first_half * sine_part], axis=-1)

def layer_sequence(inputs, length, working):
    qkv_weight, out_weight, gate_weight, up_weight, down_weight, attention_gain, feedforward_gain = working
    seq_len = inputs.shape[0]
    normed = low(rms_norm(inputs, attention_gain))
    projected = low_back(product(normed, qkv_weight)).reshape(seq_len, KV_HEADS, GROUP + 2, HEAD)
    cosine, sine_part = rotary_tables(seq_len)
    queries = low(rotate(projected[:, :, :GROUP], cosine[:, None, None, :], sine_part[:, None, None, :]))
    key_rows = low(rotate(projected[:, :, GROUP], cosine[:, None, :], sine_part[:, None, :]))
    value_rows = low(projected[:, :, GROUP + 1])
    scores = low_back(jnp.einsum('qkgd,lkd->kgql', queries, key_rows, precision=PRECISE) * HEAD ** (-0.5))
    position = jnp.arange(seq_len)
    allowed = (position[None, :] <= position[:, None]) & (position[None, :] < length)
    scores = jnp.where(allowed, scores, NEGATIVE)
    weights = low(jax.nn.softmax(scores, axis=-1))
    attended = jnp.einsum('kgql,lkd->qkgd', weights, value_rows, precision=PRECISE)
    attended = low(low_back(attended.reshape(seq_len, HEADS * HEAD)))
    residual = inputs + low_back(product(attended, out_weight))
    normed_two = low(rms_norm(residual, feedforward_gain))
    gate_proj = low_back(product(normed_two, gate_weight))
    up_proj = low_back(product(normed_two, up_weight))
    hidden = low(jax.nn.silu(gate_proj) * up_proj)
    return residual + product(hidden, down_weight)

def reference(tokens, cotangent, lengths, qkv_weight, out_weight, gate_up_weight, down_weight, norm_gains, qkv_first, out_first, gate_up_first, down_first, gains_first, qkv_second, out_second, gate_up_second, down_second, gains_second):
    masters = (qkv_weight, out_weight, gate_up_weight[0], gate_up_weight[1], down_weight, norm_gains[0], norm_gains[1])
    firsts = (qkv_first, out_first, gate_up_first[0], gate_up_first[1], down_first, gains_first[0], gains_first[1])
    seconds = (qkv_second, out_second, gate_up_second[0], gate_up_second[1], down_second, gains_second[0], gains_second[1])
    inputs = tokens.astype(jnp.float32).reshape(SEQS, SEQ_LEN, D)

    def forward(stacked, params):
        working = tuple((low(weight) for weight in params))

        def one_sequence(member):
            return jax.checkpoint(layer_sequence)(member[0], member[1], working)
        return lax.map(one_sequence, (stacked, lengths))
    outputs, pullback = jax.vjp(forward, inputs, masters)
    grad_inputs, gradients = pullback(cotangent.astype(jnp.float32).reshape(SEQS, SEQ_LEN, D))
    correct_one = 1.0 - BETA_ONE ** STEP
    correct_two = 1.0 - BETA_TWO ** STEP
    new_firsts = []
    new_seconds = []
    updates = []
    for weight, moment, square, gradient in zip(masters, firsts, seconds, gradients):
        moment = BETA_ONE * moment + (1.0 - BETA_ONE) * gradient
        square = BETA_TWO * square + (1.0 - BETA_TWO) * gradient * gradient
        new_firsts.append(moment)
        new_seconds.append(square)
        updates.append(moment / correct_one / (jnp.sqrt(square / correct_two) + ADAM_EPSILON) + WEIGHT_DECAY * weight)
    weight_norms = jnp.stack([jnp.sqrt(jnp.sum(weight * weight)) for weight in masters])
    all_update_norms = jnp.stack([jnp.sqrt(jnp.sum(update * update)) for update in updates])
    new_weights = [masters[index_value] - LEARN_RATE * (weight_norms[index_value] / all_update_norms[index_value]) * updates[index_value] for index_value in range(7)]
    return (outputs.reshape(TOKENS, D).astype(jnp.bfloat16), grad_inputs.reshape(TOKENS, D), new_weights[0], new_weights[1], jnp.stack([new_weights[2], new_weights[3]]), new_weights[4], jnp.stack([new_weights[5], new_weights[6]]), new_firsts[0], new_firsts[1], jnp.stack([new_firsts[2], new_firsts[3]]), new_firsts[4], jnp.stack([new_firsts[5], new_firsts[6]]), new_seconds[0], new_seconds[1], jnp.stack([new_seconds[2], new_seconds[3]]), new_seconds[4], jnp.stack([new_seconds[5], new_seconds[6]]), weight_norms, all_update_norms[:5], all_update_norms[5:])
```

```python
import functools

import jax
import jax.numpy as jnp
import numpy as np
from jax import lax
from jax.experimental import pallas as pl
from jax.experimental.pallas import tpu as pltpu
from jax.sharding import PartitionSpec as P

HEAD = 96
PAD = 128
SEQ_LEN = 1024
SEQS_DEV = 2
STEP = 10
GROUP = 2

NORM_EPSILON = 1e-05
ROPE_THETA = 100000.0
BETA_ONE = 0.9
BETA_TWO = 0.999
ADAM_EPSILON = 1e-06
WEIGHT_DECAY = 0.01
LEARN_RATE = 0.3
NEGATIVE = -1e30
LOG2E = 1.4426950408889634
SCALE = HEAD ** (-0.5)
Q_ROWS = 256
G_COLS = 4 * HEAD
G_PAD = 4 * PAD
VMEM_LIMIT = 56 << 20

F32 = jnp.float32
BF16 = jnp.bfloat16
VM = pl.BlockSpec(memory_space=pltpu.VMEM)
SM = pl.BlockSpec(memory_space=pltpu.SMEM)


def dot_nn(a, b):
    return lax.dot_general(a, b, (((1,), (0,)), ((), ())), preferred_element_type=F32)


def dot_nt(a, b):
    return lax.dot_general(a, b, (((1,), (1,)), ((), ())), preferred_element_type=F32)


def dot_tn(a, b):
    return lax.dot_general(a, b, (((0,), (0,)), ((), ())), preferred_element_type=F32)


def params():
    return pltpu.CompilerParams(vmem_limit_bytes=VMEM_LIMIT)


def cost(flops, moved):
    return pl.CostEstimate(flops=int(flops), bytes_accessed=int(moved), transcendentals=0)


def spread_matrix():
    source = lax.broadcasted_iota(jnp.int32, (G_COLS, G_PAD), 0)
    target = lax.broadcasted_iota(jnp.int32, (G_COLS, G_PAD), 1)
    return ((target // PAD) * HEAD + target % PAD == source) & (target % PAD < HEAD)


def assemble_kernel(n_z, blk, info, spread, *refs):
    n_blocks = 2 * n_z
    blocks, out, rows = refs[:n_blocks], refs[n_blocks], refs[n_blocks + 1]
    z, x = info[0], info[1]
    for j in range(2):
        for k in range(n_z):
            source = (lax.rem(z + n_z - k, n_z)) * 2 + (x ^ j)
            rows[pl.ds(pl.multiple_of(source * blk, 16), blk), :] = blocks[j * n_z + k][...]
    groups = out.shape[1] // G_PAD
    for g in range(groups):
        out[:, g * G_PAD : (g + 1) * G_PAD] = dot_nn(
            rows[:, g * G_COLS : (g + 1) * G_COLS], spread[...]
        ).astype(BF16)


def assemble(blocks, info, spread, n_z):
    blk, cols = blocks[0].shape
    depth = blk * len(blocks)
    wide = cols // G_COLS * G_PAD
    return pl.pallas_call(
        functools.partial(assemble_kernel, n_z, blk),
        out_shape=jax.ShapeDtypeStruct((depth, wide), BF16),
        in_specs=[SM, VM] + [VM] * len(blocks),
        out_specs=VM,
        scratch_shapes=[pltpu.VMEM((depth, cols), BF16)],
        compiler_params=params(),
        cost_estimate=cost(2 * depth * cols * G_PAD, 4 * depth * cols),
        name="assemble_weights",
    )(info, spread, *blocks)


def swap_halves(values):
    lane = lax.broadcasted_iota(jnp.int32, values.shape, 1)
    return jnp.where(
        lane < HEAD // 2,
        pltpu.roll(values, PAD - HEAD // 2, 1),
        pltpu.roll(values, HEAD // 2, 1),
    )


def store_relative(refs, rows_each, start, local, value):
    index = start // rows_each
    offset = start % rows_each
    for r, ref in enumerate(refs):

        @pl.when((local ^ r) == index)
        def _():
            ref[offset : offset + value.shape[0], :] = value


def attn_fwd_kernel(nb, rows_each, kv, info, *refs):
    xs = refs[:nb]
    gain, w_qkv, w_out, cos_t, sin_t = refs[nb : nb + 5]
    normed, qkvp, att, lse = refs[nb + 5 : nb + 9]
    parts = refs[nb + 9 : nb + 9 + nb]
    length, local = info[0], info[1]
    seq_len = nb * rows_each
    chunk = 32
    for r in range(nb):
        base = (local ^ r) * rows_each

        def norm_rows(i, carry):
            v = xs[r][pl.ds(pl.multiple_of(i * chunk, chunk), chunk), :].astype(F32)
            inv = lax.rsqrt(jnp.mean(v * v, axis=-1, keepdims=True) + NORM_EPSILON)
            normed[pl.ds(pl.multiple_of(base + i * chunk, chunk), chunk), :] = (
                v * inv * gain[...]
            ).astype(BF16)
            return carry

        lax.fori_loop(0, rows_each // chunk, norm_rows, 0)

    for i in range(seq_len // Q_ROWS):
        rows = slice(i * Q_ROWS, (i + 1) * Q_ROWS)
        for j in range(kv):
            proj = dot_nn(normed[rows, :], w_qkv[:, j * G_PAD : (j + 1) * G_PAD])
            for h in range(4):
                part = proj[:, h * PAD : (h + 1) * PAD]
                if h < 3:
                    part = part * cos_t[rows, :] + swap_halves(part) * sin_t[rows, :]
                qkvp[rows, (4 * j + h) * PAD : (4 * j + h + 1) * PAD] = part.astype(BF16)

    lse[...] = jnp.zeros_like(lse)

    def one_head(h, carry):
        group = h // GROUP
        q_col = pl.ds(pl.multiple_of((4 * group + h % GROUP) * PAD, PAD), PAD)
        k_col = pl.ds(pl.multiple_of((4 * group + 2) * PAD, PAD), PAD)
        v_col = pl.ds(pl.multiple_of((4 * group + 3) * PAD, PAD), PAD)
        a_col = pl.ds(pl.multiple_of(h * PAD, PAD), PAD)
        for i in range(seq_len // Q_ROWS):
            n = (i + 1) * Q_ROWS
            rows = slice(i * Q_ROWS, n)
            s = dot_nt(qkvp[rows, q_col], qkvp[0:n, k_col])
            row_ids = lax.broadcasted_iota(jnp.int32, (Q_ROWS, 1), 0) + i * Q_ROWS + 1
            limit = jnp.minimum(row_ids, length)
            col_ids = lax.broadcasted_iota(jnp.int32, (Q_ROWS, n), 1)
            s = jnp.where(col_ids < limit, s, NEGATIVE)
            top = jnp.max(s, axis=-1, keepdims=True)
            e = jnp.exp2((s - top) * (SCALE * LOG2E))
            total = jnp.sum(e, axis=-1, keepdims=True)
            p = (e * (1.0 / total)).astype(BF16)
            att[rows, a_col] = dot_nn(p, qkvp[0:n, v_col]).astype(BF16)
            lane = lax.broadcasted_iota(jnp.int32, (Q_ROWS, PAD), 1)
            log_total = top * (SCALE * LOG2E) + jnp.log2(total)
            lse[rows, :] = jnp.where(lane == h, log_total, lse[rows, :])
        return carry

    lax.fori_loop(0, kv * GROUP, one_head, 0)

    for i in range(seq_len // Q_ROWS):
        rows = slice(i * Q_ROWS, (i + 1) * Q_ROWS)
        part = dot_nt(att[rows, :], w_out[...]).astype(BF16)
        store_relative(parts, rows_each, i * Q_ROWS, local, part)


def attn_fwd(xs, info, gain, w_qkv, w_out, cos_t, sin_t):
    nb = len(xs)
    rows_each, width = xs[0].shape
    seq_len = nb * rows_each
    kv = w_qkv.shape[1] // G_PAD
    heads = kv * GROUP
    flops = 2 * seq_len * width * (kv * G_PAD + heads * PAD) + heads * seq_len * seq_len * 4 * 256
    return pl.pallas_call(
        functools.partial(attn_fwd_kernel, nb, rows_each, kv),
        out_shape=[
            jax.ShapeDtypeStruct((seq_len, width), BF16),
            jax.ShapeDtypeStruct((seq_len, kv * G_PAD), BF16),
            jax.ShapeDtypeStruct((seq_len, heads * PAD), BF16),
            jax.ShapeDtypeStruct((seq_len, PAD), F32),
        ]
        + [jax.ShapeDtypeStruct((rows_each, width), BF16)] * nb,
        in_specs=[SM] + [VM] * (nb + 5),
        out_specs=[VM] * (4 + nb),
        compiler_params=params(),
        cost_estimate=cost(flops, 20 << 20),
        name="attention_forward",
    )(info, *xs, gain, w_qkv, w_out, cos_t, sin_t)


def attn_bwd_kernel(nb, rows_each, kv, info, *refs):
    ags = refs[:nb]
    w_qkv, w_out, qkvp, lse, cos_t, sin_t = refs[nb : nb + 6]
    dproj = refs[nb + 6]
    parts = refs[nb + 7 : nb + 7 + nb]
    datt, dk_acc, dv_acc = refs[nb + 7 + nb :]
    length, local = info[0], info[1]
    seq_len = nb * rows_each
    heads = kv * GROUP
    for r in range(nb):
        base = (local ^ r) * rows_each
        for i in range(rows_each // Q_ROWS):
            datt[pl.ds(pl.multiple_of(base + i * Q_ROWS, Q_ROWS), Q_ROWS), :] = dot_nn(
                ags[r][i * Q_ROWS : (i + 1) * Q_ROWS, :], w_out[...]
            ).astype(BF16)

    def unrotate(grad, rows):
        return grad * cos_t[rows, :] - swap_halves(grad) * sin_t[rows, :]

    def one_head(h, carry):
        group = h // GROUP
        member = h % GROUP
        q_col = pl.ds(pl.multiple_of((4 * group + member) * PAD, PAD), PAD)
        k_col = pl.ds(pl.multiple_of((4 * group + 2) * PAD, PAD), PAD)
        v_col = pl.ds(pl.multiple_of((4 * group + 3) * PAD, PAD), PAD)
        a_col = pl.ds(pl.multiple_of(h * PAD, PAD), PAD)

        @pl.when(member == 0)
        def _():
            dk_acc[...] = jnp.zeros_like(dk_acc)
            dv_acc[...] = jnp.zeros_like(dv_acc)

        for i in range(seq_len // Q_ROWS):
            n = (i + 1) * Q_ROWS
            rows = slice(i * Q_ROWS, n)
            q = qkvp[rows, q_col]
            keys = qkvp[0:n, k_col]
            do = datt[rows, a_col]
            lane = lax.broadcasted_iota(jnp.int32, (Q_ROWS, PAD), 1)
            row_lse = jnp.sum(jnp.where(lane == h, lse[rows, :], 0.0), axis=-1, keepdims=True)
            s = dot_nt(q, keys)
            row_ids = lax.broadcasted_iota(jnp.int32, (Q_ROWS, 1), 0) + i * Q_ROWS + 1
            limit = jnp.minimum(row_ids, length)
            col_ids = lax.broadcasted_iota(jnp.int32, (Q_ROWS, n), 1)
            s = jnp.where(col_ids < limit, s, NEGATIVE)
            p = jnp.exp2(s * (SCALE * LOG2E) - row_lse)
            dp = dot_nt(do, qkvp[0:n, v_col])
            inner = jnp.sum(p * dp, axis=-1, keepdims=True)
            ds = (p * (dp - inner)).astype(BF16)
            dv_acc[0:n, :] += dot_tn(p.astype(BF16), do)
            dk_acc[0:n, :] += dot_tn(ds, q)
            dq = dot_nn(ds, keys) * SCALE
            dproj[rows, q_col] = unrotate(dq, rows).astype(BF16)

        @pl.when(member == GROUP - 1)
        def _():
            for i in range(seq_len // Q_ROWS):
                rows = slice(i * Q_ROWS, (i + 1) * Q_ROWS)
                dproj[rows, k_col] = unrotate(dk_acc[rows, :] * SCALE, rows).astype(BF16)
                dproj[rows, v_col] = dv_acc[rows, :].astype(BF16)

        return carry

    lax.fori_loop(0, heads, one_head, 0)

    for i in range(seq_len // Q_ROWS):
        rows = slice(i * Q_ROWS, (i + 1) * Q_ROWS)
        part = dot_nt(dproj[rows, :], w_qkv[...]).astype(BF16)
        store_relative(parts, rows_each, i * Q_ROWS, local, part)


def attn_bwd(ags, info, w_qkv, w_out, qkvp, lse, cos_t, sin_t):
    nb = len(ags)
    rows_each, width = ags[0].shape
    seq_len = nb * rows_each
    kv = w_qkv.shape[1] // G_PAD
    heads = kv * GROUP
    flops = 2 * seq_len * width * (kv * G_PAD + heads * PAD) + heads * seq_len * seq_len * 10 * 256
    return pl.pallas_call(
        functools.partial(attn_bwd_kernel, nb, rows_each, kv),
        out_shape=[jax.ShapeDtypeStruct((seq_len, kv * G_PAD), BF16)]
        + [jax.ShapeDtypeStruct((rows_each, width), BF16)] * nb,
        in_specs=[SM] + [VM] * (nb + 6),
        out_specs=[VM] * (1 + nb),
        scratch_shapes=[
            pltpu.VMEM((seq_len, heads * PAD), BF16),
            pltpu.VMEM((seq_len, PAD), F32),
            pltpu.VMEM((seq_len, PAD), F32),
        ],
        compiler_params=params(),
        cost_estimate=cost(flops, 20 << 20),
        name="attention_backward",
    )(info, *ags, w_qkv, w_out, qkvp, lse, cos_t, sin_t)


def weight_grad_kernel(n_z, blk, n_pairs, row_counts, info, spread, *refs):
    lefts, rights = refs[:n_pairs], refs[n_pairs : 2 * n_pairs]
    same, other = refs[2 * n_pairs :]
    z, x = info[0], info[1]
    width = lefts[0].shape[1]
    for c in range(width // G_COLS):
        cols = slice(c * G_COLS, (c + 1) * G_COLS)
        total = None
        for p in range(n_pairs):
            if row_counts is None:
                right = rights[p][...]
            else:
                start = pl.multiple_of(info[2 + p], 16)
                right = rights[p][pl.ds(start, lefts[p].shape[0]), :]
            term = dot_tn(lefts[p][:, cols], right)
            total = term if total is None else total + term
        compact = dot_nt(total.astype(BF16), spread[...]).astype(BF16)
        for b in range(G_COLS // blk):
            owner = c * (G_COLS // blk) + b
            shift = lax.rem(owner // 2 + n_z - z, n_z)
            value = compact[b * blk : (b + 1) * blk, :]

            @pl.when(x == owner % 2)
            def _():
                same[shift, :, :] = value

            @pl.when(x != owner % 2)
            def _():
                other[shift, :, :] = value


def weight_grad(lefts, rights, info, spread, n_z, blk, right_cols, offsets):
    n_pairs = len(lefts)
    rows, width = lefts[0].shape
    out = jax.ShapeDtypeStruct((n_z, blk, G_COLS), BF16)
    right_specs = [
        pl.BlockSpec((right.shape[0], G_PAD), functools.partial(lambda c, i: (0, c), right_cols))
        for right in rights
    ]
    full = lambda a: pl.BlockSpec(a.shape, lambda i: (0,) * a.ndim)
    return pl.pallas_call(
        functools.partial(weight_grad_kernel, n_z, blk, n_pairs, offsets),
        grid=(1,),
        out_shape=[out, out],
        in_specs=[SM, full(spread)] + [full(left) for left in lefts] + right_specs,
        out_specs=[pl.BlockSpec(out.shape, lambda i: (0, 0, 0))] * 2,
        compiler_params=params(),
        cost_estimate=cost(2 * n_pairs * rows * width * G_PAD, 12 << 20),
        name="attention_weight_gradient",
    )(info, spread, *lefts, *rights)


def ffn_kernel(nb, rows_each, *refs):
    ns, ups = refs[:nb], refs[nb : 2 * nb]
    w = refs[2 * nb]
    hidden, d_gate, d_up = refs[2 * nb + 1 : 2 * nb + 4]
    outs = refs[2 * nb + 4 : 3 * nb + 4]
    grads = refs[3 * nb + 4 : 4 * nb + 4]
    for r in range(nb):

        def rows_step(i, carry):
            rows = pl.ds(pl.multiple_of(i * Q_ROWS, Q_ROWS), Q_ROWS)
            kept = pl.ds(pl.multiple_of(r * rows_each + i * Q_ROWS, Q_ROWS), Q_ROWS)
            n = ns[r][rows, :]
            gate = dot_nn(n, w[0])
            up = dot_nn(n, w[1])
            sig = 1.0 / (1.0 + jnp.exp(-gate))
            silu = gate * sig
            hid = (silu * up).astype(BF16)
            hidden[kept, :] = hid
            dh = dot_nn(ups[r][rows, :], w[2])
            dg = (dh * up * sig * (1.0 + gate * (1.0 - sig))).astype(BF16)
            du = (dh * silu).astype(BF16)
            d_gate[kept, :] = dg
            d_up[kept, :] = du
            grads[r][rows, :] = (dot_nt(dg, w[0]) + dot_nt(du, w[1])).astype(BF16)
            outs[r][rows, :] = dot_nt(hid, w[2]).astype(BF16)
            return carry

        lax.fori_loop(0, rows_each // Q_ROWS, rows_step, 0)


def ffn(ns, ups, w):
    nb = len(ns)
    rows_each, width = ns[0].shape
    units = w.shape[2]
    kept = jax.ShapeDtypeStruct((nb * rows_each, units), BF16)
    part = jax.ShapeDtypeStruct((rows_each, width), BF16)
    return pl.pallas_call(
        functools.partial(ffn_kernel, nb, rows_each),
        out_shape=[kept] * 3 + [part] * (2 * nb),
        in_specs=[VM] * (2 * nb + 1),
        out_specs=[VM] * (3 + 2 * nb),
        compiler_params=params(),
        cost_estimate=cost(12 * nb * rows_each * width * units, 28 << 20),
        name="feed_forward",
    )(*ns, *ups, w)


def ffn_grad_kernel(n_blocks, n_halves, rows_each, *refs):
    ns, ups = refs[:n_blocks], refs[n_blocks : 2 * n_blocks]
    kept = refs[2 * n_blocks : 2 * n_blocks + 3 * n_halves]
    out = refs[-1]
    width = ns[0].shape[1]
    per_half = n_blocks // n_halves
    tile = G_COLS
    for which in range(3):
        lefts = ups if which == 2 else ns

        def col_step(c, carry):
            cols = pl.ds(pl.multiple_of(c * tile, tile), tile)
            total = None
            for b in range(n_blocks):
                half, r = b // per_half, b % per_half
                right = kept[3 * half + (0 if which == 2 else 1 + which)]
                term = dot_tn(
                    lefts[b][:, cols], right[r * rows_each : (r + 1) * rows_each, :]
                )
                total = term if total is None else total + term
            out[which, cols, :] = total.astype(BF16)
            return carry

        lax.fori_loop(0, width // tile, col_step, 0)


def ffn_grad(ns, ups, kept):
    n_blocks = len(ns)
    rows_each, width = ns[0].shape
    units = kept[0].shape[1]
    return pl.pallas_call(
        functools.partial(ffn_grad_kernel, n_blocks, len(kept) // 3, rows_each),
        out_shape=jax.ShapeDtypeStruct((3, width, units), BF16),
        in_specs=[VM] * (2 * n_blocks + len(kept)),
        out_specs=VM,
        compiler_params=params(),
        cost_estimate=cost(6 * n_blocks * rows_each * width * units, 34 << 20),
        name="feed_forward_weight_gradient",
    )(*ns, *ups, *kept)


def permute_xor(value, axis, bit):
    size = lax.axis_size(axis)
    return lax.ppermute(value, axis, [(i, i ^ bit) for i in range(size)])


def shift_z(value, k, n_z):
    return lax.ppermute(
        value, "dp", [(z * 2 + x, ((z + k) % n_z) * 2 + x) for z in range(n_z) for x in range(2)]
    )


def bits_down(size):
    bits = []
    bit = size // 2
    while bit:
        bits.append(bit)
        bit //= 2
    return bits


def gather_relative(block):
    size = lax.axis_size("tensor")
    have = {0: block}
    for bit in bits_down(size):
        for r in list(have):
            have[r ^ bit] = permute_xor(have[r], "tensor", bit)
    return [have[r] for r in range(size)]


def scatter_relative(parts):
    size = lax.axis_size("tensor")
    have = dict(enumerate(parts))
    for bit in reversed(bits_down(size)):
        for r in [r for r in have if r & bit]:
            received = permute_xor(have.pop(r), "tensor", bit)
            summed = have[r ^ bit].astype(F32) + received.astype(F32)
            have[r ^ bit] = summed if bit == size // 2 else summed.astype(BF16)
    return have[0].astype(F32)


def gather_dp(block, n_z):
    same = [block] + [shift_z(block, k, n_z) for k in range(1, n_z)]
    return same + [permute_xor(b, "dp", 1) for b in same]


def scatter_dp(same, other, n_z):
    received = permute_xor(other, "dp", 1)
    held = same.astype(F32) + received.astype(F32)
    total = held[0]
    narrow = held.astype(BF16)
    for k in range(1, n_z):
        total = total + shift_z(narrow[k], k, n_z).astype(F32)
    return total


def sum_everywhere(value):
    for axis in ("tensor", "dp"):
        for bit in reversed(bits_down(lax.axis_size(axis))):
            value = value + permute_xor(value, axis, bit)
    return value


def rms_norm(values, gain_row):
    return (
        values
        * lax.rsqrt(jnp.mean(values * values, axis=-1, keepdims=True) + NORM_EPSILON)
        * gain_row
    )


def rotary_tables():
    half = HEAD // 2
    frequency = ROPE_THETA ** (-(jnp.arange(half, dtype=F32) * (2.0 / HEAD)))
    angles = jnp.arange(SEQ_LEN, dtype=F32)[:, None] * frequency[None, :]
    cosine, sine = jnp.cos(angles), jnp.sin(angles)
    empty = jnp.zeros((SEQ_LEN, PAD - HEAD), F32)
    return (
        jnp.concatenate([cosine, cosine, empty], axis=1),
        jnp.concatenate([-sine, sine, empty], axis=1),
    )


def shards(
    tokens,
    cotangent,
    lengths,
    qkv_weight,
    out_weight,
    gate_up_weight,
    down_weight,
    norm_gains,
    qkv_first,
    out_first,
    gate_up_first,
    down_first,
    gains_first,
    qkv_second,
    out_second,
    gate_up_second,
    down_second,
    gains_second,
):
    rows_each, width = tokens.shape
    n_t = lax.axis_size("tensor")
    n_dp = lax.axis_size("dp")
    n_z = n_dp // 2
    nb = n_t // 2
    t = lax.axis_index("tensor")
    d = lax.axis_index("dp")
    local = lax.rem(t, nb)
    mine = t // nb
    place = jnp.stack([d // 2, lax.rem(d, 2)]).astype(jnp.int32)
    info = [
        jnp.stack([lengths[mine], local]).astype(jnp.int32),
        jnp.stack([lengths[1 - mine], local]).astype(jnp.int32),
    ]
    spread = spread_matrix().astype(BF16)
    blk = qkv_weight.shape[0]
    kv = qkv_weight.shape[1] // G_COLS

    gain_cols = norm_gains.shape[1]
    gain_start = (d * n_t + t) * gain_cols
    gain_rows = lax.dynamic_update_slice(
        jnp.zeros((2, width), F32),
        norm_gains.astype(BF16).astype(F32),
        (0, gain_start),
    )
    gain_work = sum_everywhere(gain_rows)
    attention_gain, feedforward_gain = gain_work[0:1], gain_work[1:2]

    qkv_half = qkv_weight.astype(BF16)
    out_half = out_weight.astype(BF16).T
    w_qkv = assemble(gather_dp(qkv_half, n_z), place, spread, n_z)
    w_out_cols = out_half.shape[1]
    out_fill = -w_out_cols % G_COLS
    out_blocks = gather_dp(out_half, n_z)
    if out_fill:
        out_blocks = [jnp.pad(b, ((0, 0), (0, out_fill))) for b in out_blocks]
    w_out = assemble(out_blocks, place, spread, n_z)[:, : kv * GROUP * PAD]
    ffn_half = jnp.concatenate(
        [gate_up_weight.astype(BF16), down_weight.astype(BF16).T[None]], axis=0
    )
    w_ffn = lax.all_gather(ffn_half, "dp", axis=1, tiled=True)

    inputs = tokens.astype(F32)
    x_blocks = gather_relative(tokens)
    cos_t, sin_t = rotary_tables()
    fwd = [
        attn_fwd(
            x_blocks[s * nb : (s + 1) * nb], info[s], attention_gain, w_qkv, w_out, cos_t, sin_t
        )
        for s in range(2)
    ]
    residual = inputs + scatter_relative(list(fwd[0][4:]) + list(fwd[1][4:]))

    n_blocks = gather_relative(rms_norm(residual, feedforward_gain).astype(BF16))
    c_blocks = gather_relative(cotangent)
    far = ffn(n_blocks[nb:], c_blocks[nb:], w_ffn)
    near = ffn(n_blocks[:nb], c_blocks[:nb], w_ffn)
    normed_two_grad = scatter_relative(list(near[3 + nb :]) + list(far[3 + nb :]))
    out_sum = scatter_relative(list(near[3 : 3 + nb]) + list(far[3 : 3 + nb]))
    layer_out = (residual + out_sum).astype(BF16)
    ffn_grads = ffn_grad(n_blocks, c_blocks, list(near[:3]) + list(far[:3]))
    ffn_sum = lax.psum_scatter(ffn_grads, "dp", scatter_dimension=1, tiled=True).astype(F32)

    _, norm_pull = jax.vjp(rms_norm, residual, feedforward_gain)
    residual_part, ffn_gain_grad = norm_pull(normed_two_grad)
    residual_grad = cotangent.astype(F32) + residual_part
    a_blocks = gather_relative(residual_grad.astype(BF16))
    bwd = [
        attn_bwd(
            a_blocks[s * nb : (s + 1) * nb],
            info[s],
            w_qkv,
            w_out,
            fwd[s][1],
            fwd[s][3],
            cos_t,
            sin_t,
        )
        for s in range(2)
    ]
    starts = [(local ^ r) * rows_each for r in range(nb)] * 2
    out_info = jnp.concatenate([place, jnp.stack(starts).astype(jnp.int32)])
    att = [fwd[0][2]] * nb + [fwd[1][2]] * nb
    att_fill = -att[0].shape[1] % G_PAD
    if att_fill:
        att = [jnp.pad(a, ((0, 0), (0, att_fill))) for a in att]
    out_pair = weight_grad(a_blocks, att, out_info, spread, n_z, blk, 0, True)
    out_grad_sum = scatter_dp(*out_pair, n_z)[:, :w_out_cols].T
    qkv_grad_sum = jnp.concatenate(
        [
            scatter_dp(
                *weight_grad(
                    [fwd[0][0], fwd[1][0]],
                    [bwd[0][0], bwd[1][0]],
                    place,
                    spread,
                    n_z,
                    blk,
                    j,
                    None,
                ),
                n_z,
            )
            for j in range(kv)
        ],
        axis=1,
    )
    normed_grad = scatter_relative(list(bwd[0][1:]) + list(bwd[1][1:]))
    _, first_pull = jax.vjp(rms_norm, inputs, attention_gain)
    input_part, attention_gain_grad = first_pull(normed_grad)
    grad_tokens = residual_grad + input_part
    gain_all = sum_everywhere(jnp.concatenate([attention_gain_grad, ffn_gain_grad], axis=0))
    gain_sums = lax.dynamic_slice(gain_all, (0, gain_start), (2, gain_cols))

    masters = (
        qkv_weight,
        out_weight,
        gate_up_weight[0],
        gate_up_weight[1],
        down_weight,
        norm_gains[0],
        norm_gains[1],
    )
    firsts = (
        qkv_first,
        out_first,
        gate_up_first[0],
        gate_up_first[1],
        down_first,
        gains_first[0],
        gains_first[1],
    )
    seconds = (
        qkv_second,
        out_second,
        gate_up_second[0],
        gate_up_second[1],
        down_second,
        gains_second[0],
        gains_second[1],
    )
    gradients = (
        qkv_grad_sum,
        out_grad_sum,
        ffn_sum[0],
        ffn_sum[1],
        ffn_sum[2].T,
        gain_sums[0],
        gain_sums[1],
    )
    correct_one = 1.0 - BETA_ONE**STEP
    correct_two = 1.0 - BETA_TWO**STEP
    new_firsts = []
    new_seconds = []
    updates = []
    for master, moment, square, gradient in zip(masters, firsts, seconds, gradients):
        moment = BETA_ONE * moment + (1.0 - BETA_ONE) * gradient
        square = BETA_TWO * square + (1.0 - BETA_TWO) * gradient * gradient
        new_firsts.append(moment)
        new_seconds.append(square)
        updates.append(
            moment / correct_one / (jnp.sqrt(square / correct_two) + ADAM_EPSILON)
            + WEIGHT_DECAY * master
        )
    squares = jnp.stack(
        [jnp.sum(master * master) for master in masters]
        + [jnp.sum(update * update) for update in updates]
    )
    norms = jnp.sqrt(sum_everywhere(squares[None])[0])
    weight_norms, all_update_norms = norms[:7], norms[7:]
    new_weights = [
        masters[number]
        - LEARN_RATE * (weight_norms[number] / all_update_norms[number]) * updates[number]
        for number in range(7)
    ]
    return (
        layer_out,
        grad_tokens,
        new_weights[0],
        new_weights[1],
        jnp.stack([new_weights[2], new_weights[3]]),
        new_weights[4],
        jnp.stack([new_weights[5], new_weights[6]]),
        new_firsts[0],
        new_firsts[1],
        jnp.stack([new_firsts[2], new_firsts[3]]),
        new_firsts[4],
        jnp.stack([new_firsts[5], new_firsts[6]]),
        new_seconds[0],
        new_seconds[1],
        jnp.stack([new_seconds[2], new_seconds[3]]),
        new_seconds[4],
        jnp.stack([new_seconds[5], new_seconds[6]]),
        weight_norms,
        all_update_norms[:5],
        all_update_norms[5:],
    )


def solution(mesh):
    rows = P(("dp", "tensor"), None)
    gains = P(None, ("dp", "tensor"))
    weights = (P("dp", "tensor"), P("tensor", "dp"), P(None, "dp", "tensor"), P("tensor", "dp"), gains)
    in_specs = (rows, rows, P("dp")) + weights * 3
    out_specs = (rows, rows) + weights * 3 + (P(), P(), P())
    return jax.shard_map(shards, mesh=mesh, in_specs=in_specs, out_specs=out_specs, check_vma=False)
```

```python
import functools

import jax
import jax.numpy as jnp
import numpy as np
from jax import lax
from jax.experimental import pallas as pl
from jax.experimental.pallas import tpu as pltpu
from jax.sharding import PartitionSpec as P

HEAD = 96
PAD = 128
SEQ_LEN = 1024
SEQS_DEV = 2
STEP = 10
GROUP = 2

NORM_EPSILON = 1e-05
ROPE_THETA = 100000.0
BETA_ONE = 0.9
BETA_TWO = 0.999
ADAM_EPSILON = 1e-06
WEIGHT_DECAY = 0.01
LEARN_RATE = 0.3
NEGATIVE = -1e30
LOG2E = 1.4426950408889634
SCALE = HEAD ** (-0.5)
Q_ROWS = 256
G_COLS = 4 * HEAD
G_PAD = 4 * PAD
VMEM_LIMIT = 56 << 20

F32 = jnp.float32
BF16 = jnp.bfloat16
VM = pl.BlockSpec(memory_space=pltpu.VMEM)
SM = pl.BlockSpec(memory_space=pltpu.SMEM)
ANY = pl.BlockSpec(memory_space=pl.ANY)
MESH = pl.DeviceIdType.MESH


def dot_nn(a, b):
    return lax.dot_general(a, b, (((1,), (0,)), ((), ())), preferred_element_type=F32)


def dot_nt(a, b):
    return lax.dot_general(a, b, (((1,), (1,)), ((), ())), preferred_element_type=F32)


def dot_tn(a, b):
    return lax.dot_general(a, b, (((0,), (0,)), ((), ())), preferred_element_type=F32)


def cost(flops, moved):
    return pl.CostEstimate(flops=int(flops), bytes_accessed=int(moved), transcendentals=0)


def permuted(axis, bit):
    return {axis: lax.axis_index(axis) ^ bit}


def carrying_kernel(body, counts, sends, meets, *refs):
    n_in, n_deps, n_out, n_scratch = counts
    n_sends = len(sends)
    refs = list(refs)

    def take(n):
        taken = refs[:n]
        del refs[:n]
        return taken

    inputs, sources, _, outputs, targets = (
        take(n_in),
        take(n_sends),
        take(n_deps),
        take(n_out),
        take(n_sends),
    )
    scratch = take(n_scratch)
    copies = []
    if sends:
        send_sem, recv_sem = refs
        barrier = pltpu.get_barrier_semaphore()
        peers = sorted(set(sends) | set(meets))
        for peer in peers:
            pl.semaphore_signal(barrier, inc=1, device_id=permuted(*peer), device_id_type=MESH)
        pl.semaphore_wait(barrier, len(peers))
        for i, peer in enumerate(sends):
            copy = pltpu.make_async_remote_copy(
                src_ref=sources[i],
                dst_ref=targets[i],
                send_sem=send_sem.at[i],
                recv_sem=recv_sem.at[i],
                device_id=permuted(*peer),
                device_id_type=MESH,
            )
            copy.start()
            copies.append(copy)
    body(*inputs, *outputs, *scratch)
    for copy in copies:
        copy.wait()


def call(body, name, inputs, outs, flops, scratch=(), sends=(), deps=(), meets=(), collective_id=None, specs=None):
    n_sends = len(sends)
    specs = [VM] * len(inputs) if specs is None else specs
    arrays = [array for array, _ in sends]
    dma = pltpu.SemaphoreType.DMA
    moved = sum(a.size * a.dtype.itemsize for a in list(inputs) + list(outs))
    extra = dict(collective_id=collective_id, has_side_effects=True) if sends else {}
    return pl.pallas_call(
        functools.partial(
            carrying_kernel,
            body,
            (len(inputs), len(deps), len(outs), len(scratch)),
            [peer for _, peer in sends],
            meets,
        ),
        out_shape=list(outs) + [jax.ShapeDtypeStruct(a.shape, a.dtype) for a in arrays],
        in_specs=specs + [ANY] * (n_sends + len(deps)),
        out_specs=[VM] * len(outs) + [ANY] * n_sends,
        scratch_shapes=list(scratch) + ([dma((n_sends,)), dma((n_sends,))] if sends else []),
        compiler_params=pltpu.CompilerParams(vmem_limit_bytes=VMEM_LIMIT, **extra),
        cost_estimate=cost(flops, moved),
        name=name,
    )(*inputs, *arrays, *deps)


def spread_matrix():
    source = lax.broadcasted_iota(jnp.int32, (G_COLS, G_PAD), 0)
    target = lax.broadcasted_iota(jnp.int32, (G_COLS, G_PAD), 1)
    return ((target // PAD) * HEAD + target % PAD == source) & (target % PAD < HEAD)


def pad_kernel(spread, wq, wo, wq_pad, wo_pad):
    for source, target in ((wq, wq_pad), (wo, wo_pad)):
        for g in range(target.shape[1] // G_PAD):
            target[:, g * G_PAD : (g + 1) * G_PAD] = dot_nn(
                source[:, g * G_COLS : (g + 1) * G_COLS], spread[...]
            ).astype(BF16)


def pad_weights(wq, wo, spread):
    depth = wq.shape[0]
    outs = [jax.ShapeDtypeStruct((depth, w.shape[1] // G_COLS * G_PAD), BF16) for w in (wq, wo)]
    return call(pad_kernel, "pad_weights", [spread, wq, wo], outs, 6 * depth * G_COLS * G_PAD)


def swap_halves(values):
    lane = lax.broadcasted_iota(jnp.int32, values.shape, 1)
    return jnp.where(
        lane < HEAD // 2,
        pltpu.roll(values, PAD - HEAD // 2, 1),
        pltpu.roll(values, HEAD // 2, 1),
    )


def store_relative(refs, rows_each, start, local, value):
    index = start // rows_each
    offset = start % rows_each
    for r, ref in enumerate(refs):

        @pl.when((local ^ r) == index)
        def _():
            ref[offset : offset + value.shape[0], :] = value


def attn_fwd_kernel(nb, rows_each, kv, info, *refs):
    xs = refs[:nb]
    gain, w_qkv, w_out, cos_t, sin_t = refs[nb : nb + 5]
    normed, qkvp, att, lse = refs[nb + 5 : nb + 9]
    parts = refs[nb + 9 : nb + 9 + nb]
    length, local = info[0], lax.rem(lax.axis_index("tensor"), nb)
    seq_len = nb * rows_each
    chunk = 32
    for r in range(nb):
        base = (local ^ r) * rows_each

        def norm_rows(i, carry):
            v = xs[r][pl.ds(pl.multiple_of(i * chunk, chunk), chunk), :].astype(F32)
            inv = lax.rsqrt(jnp.mean(v * v, axis=-1, keepdims=True) + NORM_EPSILON)
            normed[pl.ds(pl.multiple_of(base + i * chunk, chunk), chunk), :] = (
                v * inv * gain[...]
            ).astype(BF16)
            return carry

        lax.fori_loop(0, rows_each // chunk, norm_rows, 0)

    for i in range(seq_len // Q_ROWS):
        rows = slice(i * Q_ROWS, (i + 1) * Q_ROWS)
        for j in range(kv):
            proj = dot_nn(normed[rows, :], w_qkv[:, j * G_PAD : (j + 1) * G_PAD])
            for h in range(4):
                part = proj[:, h * PAD : (h + 1) * PAD]
                if h < 3:
                    part = part * cos_t[rows, :] + swap_halves(part) * sin_t[rows, :]
                qkvp[rows, (4 * j + h) * PAD : (4 * j + h + 1) * PAD] = part.astype(BF16)

    lse[...] = jnp.zeros_like(lse)

    def one_head(h, carry):
        group = h // GROUP
        q_col = pl.ds(pl.multiple_of((4 * group + h % GROUP) * PAD, PAD), PAD)
        k_col = pl.ds(pl.multiple_of((4 * group + 2) * PAD, PAD), PAD)
        v_col = pl.ds(pl.multiple_of((4 * group + 3) * PAD, PAD), PAD)
        a_col = pl.ds(pl.multiple_of(h * PAD, PAD), PAD)
        for i in range(seq_len // Q_ROWS):
            n = (i + 1) * Q_ROWS
            rows = slice(i * Q_ROWS, n)
            s = dot_nt(qkvp[rows, q_col], qkvp[0:n, k_col])
            row_ids = lax.broadcasted_iota(jnp.int32, (Q_ROWS, 1), 0) + i * Q_ROWS + 1
            limit = jnp.minimum(row_ids, length)
            col_ids = lax.broadcasted_iota(jnp.int32, (Q_ROWS, n), 1)
            s = jnp.where(col_ids < limit, s, NEGATIVE)
            top = jnp.max(s, axis=-1, keepdims=True)
            e = jnp.exp2((s - top) * (SCALE * LOG2E))
            total = jnp.sum(e, axis=-1, keepdims=True)
            p = (e * (1.0 / total)).astype(BF16)
            att[rows, a_col] = dot_nn(p, qkvp[0:n, v_col]).astype(BF16)
            lane = lax.broadcasted_iota(jnp.int32, (Q_ROWS, PAD), 1)
            log_total = top * (SCALE * LOG2E) + jnp.log2(total)
            lse[rows, :] = jnp.where(lane == h, log_total, lse[rows, :])
        return carry

    lax.fori_loop(0, kv * GROUP, one_head, 0)

    for i in range(seq_len // Q_ROWS):
        rows = slice(i * Q_ROWS, (i + 1) * Q_ROWS)
        part = dot_nt(att[rows, :], w_out[...]).astype(BF16)
        store_relative(parts, rows_each, i * Q_ROWS, local, part)


def attn_fwd(xs, info, gain, w_qkv, w_out, cos_t, sin_t, **more):
    nb = len(xs)
    rows_each, width = xs[0].shape
    seq_len = nb * rows_each
    kv = w_qkv.shape[1] // G_PAD
    heads = kv * GROUP
    outs = [
        jax.ShapeDtypeStruct((seq_len, width), BF16),
        jax.ShapeDtypeStruct((seq_len, kv * G_PAD), BF16),
        jax.ShapeDtypeStruct((seq_len, heads * PAD), BF16),
        jax.ShapeDtypeStruct((seq_len, PAD), F32),
    ] + [jax.ShapeDtypeStruct((rows_each, width), BF16)] * nb
    return call(
        functools.partial(attn_fwd_kernel, nb, rows_each, kv),
        "attention_forward",
        [info, *xs, gain, w_qkv, w_out, cos_t, sin_t],
        outs,
        2 * seq_len * width * (kv * G_PAD + heads * PAD) + heads * seq_len * seq_len * 4 * 256,
        specs=[SM] + [VM] * (nb + 5),
        **more,
    )


def attn_bwd_kernel(nb, rows_each, kv, info, *refs):
    ags = refs[:nb]
    w_qkv, w_out, qkvp, lse, cos_t, sin_t = refs[nb : nb + 6]
    dproj = refs[nb + 6]
    parts = refs[nb + 7 : nb + 7 + nb]
    datt, dk_acc, dv_acc = refs[nb + 7 + nb :]
    length, local = info[0], lax.rem(lax.axis_index("tensor"), nb)
    seq_len = nb * rows_each
    heads = kv * GROUP
    for r in range(nb):
        base = (local ^ r) * rows_each
        for i in range(rows_each // Q_ROWS):
            datt[pl.ds(pl.multiple_of(base + i * Q_ROWS, Q_ROWS), Q_ROWS), :] = dot_nn(
                ags[r][i * Q_ROWS : (i + 1) * Q_ROWS, :], w_out[...]
            ).astype(BF16)

    def unrotate(grad, rows):
        return grad * cos_t[rows, :] - swap_halves(grad) * sin_t[rows, :]

    def one_head(h, carry):
        group = h // GROUP
        member = h % GROUP
        q_col = pl.ds(pl.multiple_of((4 * group + member) * PAD, PAD), PAD)
        k_col = pl.ds(pl.multiple_of((4 * group + 2) * PAD, PAD), PAD)
        v_col = pl.ds(pl.multiple_of((4 * group + 3) * PAD, PAD), PAD)
        a_col = pl.ds(pl.multiple_of(h * PAD, PAD), PAD)

        @pl.when(member == 0)
        def _():
            dk_acc[...] = jnp.zeros_like(dk_acc)
            dv_acc[...] = jnp.zeros_like(dv_acc)

        for i in range(seq_len // Q_ROWS):
            n = (i + 1) * Q_ROWS
            rows = slice(i * Q_ROWS, n)
            q = qkvp[rows, q_col]
            keys = qkvp[0:n, k_col]
            do = datt[rows, a_col]
            lane = lax.broadcasted_iota(jnp.int32, (Q_ROWS, PAD), 1)
            row_lse = jnp.sum(jnp.where(lane == h, lse[rows, :], 0.0), axis=-1, keepdims=True)
            s = dot_nt(q, keys)
            row_ids = lax.broadcasted_iota(jnp.int32, (Q_ROWS, 1), 0) + i * Q_ROWS + 1
            limit = jnp.minimum(row_ids, length)
            col_ids = lax.broadcasted_iota(jnp.int32, (Q_ROWS, n), 1)
            s = jnp.where(col_ids < limit, s, NEGATIVE)
            p = jnp.exp2(s * (SCALE * LOG2E) - row_lse)
            dp = dot_nt(do, qkvp[0:n, v_col])
            inner = jnp.sum(p * dp, axis=-1, keepdims=True)
            ds = (p * (dp - inner)).astype(BF16)
            dv_acc[0:n, :] += dot_tn(p.astype(BF16), do)
            dk_acc[0:n, :] += dot_tn(ds, q)
            dq = dot_nn(ds, keys) * SCALE
            dproj[rows, q_col] = unrotate(dq, rows).astype(BF16)

        @pl.when(member == GROUP - 1)
        def _():
            for i in range(seq_len // Q_ROWS):
                rows = slice(i * Q_ROWS, (i + 1) * Q_ROWS)
                dproj[rows, k_col] = unrotate(dk_acc[rows, :] * SCALE, rows).astype(BF16)
                dproj[rows, v_col] = dv_acc[rows, :].astype(BF16)

        return carry

    lax.fori_loop(0, heads, one_head, 0)

    for i in range(seq_len // Q_ROWS):
        rows = slice(i * Q_ROWS, (i + 1) * Q_ROWS)
        part = dot_nt(dproj[rows, :], w_qkv[...]).astype(BF16)
        store_relative(parts, rows_each, i * Q_ROWS, local, part)


def attn_bwd(ags, info, w_qkv, w_out, qkvp, lse, cos_t, sin_t, **more):
    nb = len(ags)
    rows_each, width = ags[0].shape
    seq_len = nb * rows_each
    kv = w_qkv.shape[1] // G_PAD
    heads = kv * GROUP
    outs = [jax.ShapeDtypeStruct((seq_len, kv * G_PAD), BF16)] + [
        jax.ShapeDtypeStruct((rows_each, width), BF16)
    ] * nb
    return call(
        functools.partial(attn_bwd_kernel, nb, rows_each, kv),
        "attention_backward",
        [info, *ags, w_qkv, w_out, qkvp, lse, cos_t, sin_t],
        outs,
        2 * seq_len * width * (kv * G_PAD + heads * PAD) + heads * seq_len * seq_len * 10 * 256,
        scratch=[
            pltpu.VMEM((seq_len, heads * PAD), BF16),
            pltpu.VMEM((seq_len, PAD), F32),
            pltpu.VMEM((seq_len, PAD), F32),
        ],
        specs=[SM] + [VM] * (nb + 6),
        **more,
    )


def weight_grad_kernel(n_z, blk, nb, kv, spread, *refs):
    ags, refs = refs[: 2 * nb], refs[2 * nb :]
    atts, normeds, dprojs, refs = refs[:2], refs[2:4], refs[4:6], refs[6:]
    sames, others, arrived, send_sem, recv_sem = refs[0], refs[1], refs[2], refs[3], refs[4]
    d, t = lax.axis_index("dp"), lax.axis_index("tensor")
    z, x = d // 2, lax.rem(d, 2)
    local = lax.rem(t, nb)
    rows_each, width = ags[0].shape
    copies = []
    for which in range(kv + 1):

        def chunk(c, carry):
            cols = pl.ds(pl.multiple_of(c * G_COLS, G_COLS), G_COLS)
            if which == 0:
                wide = atts[0].shape[1]
                total = jnp.zeros((G_COLS, wide), F32)
                for r in range(2 * nb):
                    start = pl.multiple_of((local ^ (r % nb)) * rows_each, rows_each)
                    total += dot_tn(ags[r][:, cols], atts[r // nb][pl.ds(start, rows_each), :])
                compact = dot_nt(total.astype(BF16), spread[:, :wide])
            else:
                part = slice((which - 1) * G_PAD, which * G_PAD)
                total = dot_tn(normeds[0][:, cols], dprojs[0][:, part])
                total += dot_tn(normeds[1][:, cols], dprojs[1][:, part])
                compact = dot_nt(total.astype(BF16), spread[...])
            compact = compact.astype(BF16)
            for b in range(G_COLS // blk):
                owner = c * (G_COLS // blk) + b
                shift = lax.rem(owner // 2 + n_z - z, n_z)
                value = compact[b * blk : (b + 1) * blk, :]

                @pl.when(x == lax.rem(owner, 2))
                def _():
                    sames[which, shift, :, :] = value

                @pl.when(x != lax.rem(owner, 2))
                def _():
                    others[which, shift, :, :] = value

            return carry

        lax.fori_loop(0, width // G_COLS, chunk, 0)
        copy = pltpu.make_async_remote_copy(
            src_ref=others.at[which],
            dst_ref=arrived.at[which],
            send_sem=send_sem.at[which],
            recv_sem=recv_sem.at[which],
            device_id=permuted("dp", 1),
            device_id_type=MESH,
        )
        copy.start()
        copies.append(copy)
    for copy in copies:
        copy.wait()


def weight_grad(ags, atts, normeds, dprojs, spread, n_z, blk, **more):
    nb = len(ags) // 2
    rows, width = ags[0].shape
    kv = dprojs[0].shape[1] // G_PAD
    out = jax.ShapeDtypeStruct((kv + 1, n_z, blk, G_COLS), BF16)
    return call(
        functools.partial(weight_grad_kernel, n_z, blk, nb, kv),
        "attention_weight_gradients",
        [spread, *ags, *atts, *normeds, *dprojs],
        [out, out, out],
        4 * nb * rows * width * G_PAD * (kv + 1),
        scratch=[pltpu.SemaphoreType.DMA((kv + 1,)), pltpu.SemaphoreType.DMA((kv + 1,))],
        **more,
    )


def z_sum_kernel(n_z, same, other, out, narrow, arrived, send_sem, recv_sem):
    d = lax.axis_index("dp")
    z, x = d // 2, lax.rem(d, 2)
    barrier = pltpu.get_barrier_semaphore()
    peers = [{"dp": lax.rem(z + k, n_z) * 2 + x} for k in range(1, n_z)]
    for peer in peers:
        pl.semaphore_signal(barrier, inc=1, device_id=peer, device_id_type=MESH)
    pl.semaphore_wait(barrier, n_z - 1)
    copies = []
    n_which = same.shape[0]
    for which in range(n_which):
        for k in range(1, n_z):
            held = same[which, k, :, :].astype(F32) + other[which, k, :, :].astype(F32)
            narrow[which, k, :, :] = held.astype(BF16)
            copy = pltpu.make_async_remote_copy(
                src_ref=narrow.at[which, k],
                dst_ref=arrived.at[which, k],
                send_sem=send_sem.at[which, k],
                recv_sem=recv_sem.at[which, k],
                device_id=peers[k - 1],
                device_id_type=MESH,
            )
            copy.start()
            copies.append(copy)
    for which in range(n_which):
        total = same[which, 0, :, :].astype(F32) + other[which, 0, :, :].astype(F32)
        for k in range(1, n_z):
            copies[which * (n_z - 1) + k - 1].wait()
            total = total + arrived[which, k, :, :].astype(F32)
        out[which, :, :] = total


def z_sum(same, other, n_z, collective_id, deps=()):
    n_which, _, blk, cols = same.shape
    dma = pltpu.SemaphoreType.DMA
    return pl.pallas_call(
        lambda a, b, *rest: z_sum_kernel(n_z, a, b, *rest[len(deps) :]),
        out_shape=jax.ShapeDtypeStruct((n_which, blk, cols), F32),
        in_specs=[VM, VM] + [ANY] * len(deps),
        out_specs=VM,
        scratch_shapes=[
            pltpu.VMEM(same.shape, BF16),
            pltpu.VMEM(same.shape, BF16),
            dma((n_which, n_z)),
            dma((n_which, n_z)),
        ],
        compiler_params=pltpu.CompilerParams(
            collective_id=collective_id, has_side_effects=True, vmem_limit_bytes=24 << 20
        ),
        cost_estimate=cost(0, 40 << 20),
        name="sum_attention_gradients",
    )(same, other, *deps)


def ffn_kernel(nb, rows_each, *refs):
    ns, ups = refs[:nb], refs[nb : 2 * nb]
    w = refs[2 * nb]
    hidden, d_gate, d_up = refs[2 * nb + 1 : 2 * nb + 4]
    outs = refs[2 * nb + 4 : 3 * nb + 4]
    grads = refs[3 * nb + 4 : 4 * nb + 4]
    for r in range(nb):

        def rows_step(i, carry):
            rows = pl.ds(pl.multiple_of(i * Q_ROWS, Q_ROWS), Q_ROWS)
            kept = pl.ds(pl.multiple_of(r * rows_each + i * Q_ROWS, Q_ROWS), Q_ROWS)
            n = ns[r][rows, :]
            gate = dot_nn(n, w[0])
            up = dot_nn(n, w[1])
            sig = 1.0 / (1.0 + jnp.exp(-gate))
            silu = gate * sig
            hid = (silu * up).astype(BF16)
            hidden[kept, :] = hid
            dh = dot_nn(ups[r][rows, :], w[2])
            dg = (dh * up * sig * (1.0 + gate * (1.0 - sig))).astype(BF16)
            du = (dh * silu).astype(BF16)
            d_gate[kept, :] = dg
            d_up[kept, :] = du
            grads[r][rows, :] = (dot_nt(dg, w[0]) + dot_nt(du, w[1])).astype(BF16)
            outs[r][rows, :] = dot_nt(hid, w[2]).astype(BF16)
            return carry

        lax.fori_loop(0, rows_each // Q_ROWS, rows_step, 0)


def ffn(ns, ups, w, **more):
    nb = len(ns)
    rows_each, width = ns[0].shape
    units = w.shape[2]
    kept = jax.ShapeDtypeStruct((nb * rows_each, units), BF16)
    part = jax.ShapeDtypeStruct((rows_each, width), BF16)
    return call(
        functools.partial(ffn_kernel, nb, rows_each),
        "feed_forward",
        [*ns, *ups, w],
        [kept] * 3 + [part] * (2 * nb),
        12 * nb * rows_each * width * units,
        **more,
    )


def ffn_grad_kernel(n_blocks, n_halves, rows_each, *refs):
    ns, ups = refs[:n_blocks], refs[n_blocks : 2 * n_blocks]
    kept = refs[2 * n_blocks : 2 * n_blocks + 3 * n_halves]
    out = refs[-1]
    width = ns[0].shape[1]
    per_half = n_blocks // n_halves
    tile = G_COLS
    for which in range(3):
        lefts = ups if which == 2 else ns

        def col_step(c, carry):
            cols = pl.ds(pl.multiple_of(c * tile, tile), tile)
            total = None
            for b in range(n_blocks):
                half, r = b // per_half, b % per_half
                right = kept[3 * half + (0 if which == 2 else 1 + which)]
                term = dot_tn(
                    lefts[b][:, cols], right[r * rows_each : (r + 1) * rows_each, :]
                )
                total = term if total is None else total + term
            out[which, cols, :] = total.astype(BF16)
            return carry

        lax.fori_loop(0, width // tile, col_step, 0)


def ffn_grad(ns, ups, kept, **more):
    n_blocks = len(ns)
    rows_each, width = ns[0].shape
    units = kept[0].shape[1]
    return call(
        functools.partial(ffn_grad_kernel, n_blocks, len(kept) // 3, rows_each),
        "feed_forward_weight_gradient",
        [*ns, *ups, *kept],
        [jax.ShapeDtypeStruct((3, width, units), BF16)],
        6 * n_blocks * rows_each * width * units,
        **more,
    )


def prologue_kernel(n_z, n_t, blk, *refs):
    tokens, qkv, outw, gains = refs[:4]
    xs, wq, wo, gain_sum = refs[4:8]
    held, got, own_sem, tok_send, tok_recv, z_send, z_recv, x_send, x_recv, g_send, g_recv = refs[8:]
    d, t = lax.axis_index("dp"), lax.axis_index("tensor")
    z, x = d // 2, lax.rem(d, 2)
    bits = bits_down(n_t)

    def at_z(k):
        return {"dp": lax.rem(z + k, n_z) * 2 + x}

    other_x = {"dp": z * 2 + (1 - x)}

    def at_t(bit):
        return {"tensor": t ^ bit}

    barrier = pltpu.get_barrier_semaphore()
    peers = [at_z(k) for k in range(1, n_z)] + [other_x] + [at_t(bit) for bit in bits]
    for peer in peers:
        pl.semaphore_signal(barrier, inc=1, device_id=peer, device_id_type=MESH)
    pl.semaphore_wait(barrier, len(peers))

    def send(src, dst, send_sem, recv_sem, peer):
        copy = pltpu.make_async_remote_copy(
            src_ref=src,
            dst_ref=dst,
            send_sem=send_sem,
            recv_sem=recv_sem,
            device_id=peer,
            device_id_type=MESH,
        )
        copy.start()
        return copy

    def owned(k):
        return pl.ds(pl.multiple_of((lax.rem(z + n_z - k, n_z) * 2 + x) * blk, 16), blk)

    pending = []
    held[0, :, :] = gains[...]
    stages = [at_t(bit) for bit in bits] + [other_x]
    gain_copy = send(held.at[0], got.at[0], g_send.at[0], g_recv.at[0], stages[0])
    token_copies = {}
    for bit in bits:
        token_copies[bit] = send(
            tokens, xs.at[bit - 1], tok_send.at[bit], tok_recv.at[bit], at_t(bit)
        )
    locals_ = [
        pltpu.make_async_copy(qkv, wq.at[owned(0)], own_sem.at[0]),
        pltpu.make_async_copy(outw, wo.at[owned(0)], own_sem.at[1]),
    ]
    for copy in locals_:
        copy.start()
    z_copies, x_copies = {}, {}
    for k in range(1, n_z):
        z_copies[0, k] = send(qkv, wq.at[owned(0)], z_send.at[0, k], z_recv.at[0, k], at_z(k))
    x_copies[0, 0] = send(qkv, wq.at[owned(0)], x_send.at[0, 0], x_recv.at[0, 0], other_x)
    for stage in range(len(stages)):
        gain_copy.wait()
        held[stage + 1, :, :] = held[stage, :, :] + got[stage, :, :]
        if stage + 1 < len(stages):
            gain_copy = send(
                held.at[stage + 1],
                got.at[stage + 1],
                g_send.at[stage + 1],
                g_recv.at[stage + 1],
                stages[stage + 1],
            )
    last = len(stages)
    gain_z = [
        send(held.at[last], got.at[last + k - 1], g_send.at[last + k - 1], g_recv.at[last + k - 1], at_z(k))
        for k in range(1, n_z)
    ]
    for k in range(1, n_z):
        z_copies[1, k] = send(outw, wo.at[owned(0)], z_send.at[1, k], z_recv.at[1, k], at_z(k))
    for which, whole in ((0, wq), (1, wo)):
        if which == 1:
            x_copies[1, 0] = send(outw, wo.at[owned(0)], x_send.at[1, 0], x_recv.at[1, 0], other_x)
        for k in range(1, n_z):
            z_copies[which, k].wait_recv()
            x_copies[which, k] = send(
                whole.at[owned(k)],
                whole.at[owned(k)],
                x_send.at[which, k],
                x_recv.at[which, k],
                other_x,
            )
    arrived = [0]
    for bit in bits:
        for r in list(arrived):
            if r:
                token_copies[r ^ bit] = send(
                    xs.at[r - 1], xs.at[(r ^ bit) - 1], tok_send.at[r ^ bit], tok_recv.at[r ^ bit], at_t(bit)
                )
        for r in list(arrived):
            token_copies[r ^ bit].wait_recv()
            arrived.append(r ^ bit)
    total = held[last, :, :]
    for k in range(1, n_z):
        gain_z[k - 1].wait()
        total = total + got[last + k - 1, :, :]
    gain_sum[...] = total
    for copy in token_copies.values():
        copy.wait_send()
    for copy in z_copies.values():
        copy.wait_send()
    for copy in x_copies.values():
        copy.wait()
    for copy in locals_:
        copy.wait()


def prologue(tokens, qkv, outw, gains, n_z, n_t, n_dp):
    blk = qkv.shape[0]
    n_gain = len(bits_down(n_t)) + 1 + n_z - 1
    dma = pltpu.SemaphoreType.DMA
    return pl.pallas_call(
        functools.partial(prologue_kernel, n_z, n_t, blk),
        out_shape=[
            jax.ShapeDtypeStruct((n_t - 1,) + tokens.shape, BF16),
            jax.ShapeDtypeStruct((blk * n_dp, qkv.shape[1]), BF16),
            jax.ShapeDtypeStruct((blk * n_dp, outw.shape[1]), BF16),
            jax.ShapeDtypeStruct(gains.shape, F32),
        ],
        in_specs=[ANY, ANY, ANY, VM],
        out_specs=[ANY, ANY, ANY, VM],
        scratch_shapes=[
            pltpu.VMEM((n_gain + 1,) + gains.shape, F32),
            pltpu.VMEM((n_gain,) + gains.shape, F32),
            dma((2,)),
            dma((n_t,)),
            dma((n_t,)),
            dma((2, n_z)),
            dma((2, n_z)),
            dma((2, n_z)),
            dma((2, n_z)),
            dma((n_gain,)),
            dma((n_gain,)),
        ],
        compiler_params=pltpu.CompilerParams(
            collective_id=0, has_side_effects=True, vmem_limit_bytes=4 << 20
        ),
        cost_estimate=cost(0, 60 << 20),
        name="gather_tokens_and_weights",
    )(tokens, qkv, outw, gains)


def sum_kernel(n_dp, n_t, value, out, first, second, send_sem, recv_sem):
    d, t = lax.axis_index("dp"), lax.axis_index("tensor")
    peers = [{"tensor": lax.rem(t + k, n_t)} for k in range(1, n_t)]
    peers += [{"dp": lax.rem(d + k, n_dp)} for k in range(1, n_dp)]
    barrier = pltpu.get_barrier_semaphore()
    for peer in peers:
        pl.semaphore_signal(barrier, inc=1, device_id=peer, device_id_type=MESH)
    pl.semaphore_wait(barrier, len(peers))

    def exchange(buffer, me, targets, base):
        copies = []
        for k, peer in enumerate(targets):
            copy = pltpu.make_async_remote_copy(
                src_ref=buffer.at[me],
                dst_ref=buffer.at[me],
                send_sem=send_sem.at[base + k],
                recv_sem=recv_sem.at[base + k],
                device_id=peer,
                device_id_type=MESH,
            )
            copy.start()
            copies.append(copy)
        for copy in copies:
            copy.wait()
        total = buffer[0, :, :]
        for i in range(1, len(targets) + 1):
            total = total + buffer[i, :, :]
        return total

    first[t, :, :] = value[...]
    second[d, :, :] = exchange(first, t, peers[: n_t - 1], 0)
    out[...] = exchange(second, d, peers[n_t - 1 :], n_t - 1)


def sum_all(value, n_dp, n_t, collective_id, name):
    dma = pltpu.SemaphoreType.DMA
    return pl.pallas_call(
        functools.partial(sum_kernel, n_dp, n_t),
        out_shape=jax.ShapeDtypeStruct(value.shape, F32),
        in_specs=[VM],
        out_specs=VM,
        scratch_shapes=[
            pltpu.VMEM((n_t,) + value.shape, F32),
            pltpu.VMEM((n_dp,) + value.shape, F32),
            dma((n_t + n_dp,)),
            dma((n_t + n_dp,)),
        ],
        compiler_params=pltpu.CompilerParams(
            collective_id=collective_id, has_side_effects=True, vmem_limit_bytes=8 << 20
        ),
        cost_estimate=cost(0, 8 << 20),
        name=name,
    )(value)


def permute_xor(value, axis, bit):
    size = lax.axis_size(axis)
    return lax.ppermute(value, axis, [(i, i ^ bit) for i in range(size)])


def bits_down(size):
    bits = []
    bit = size // 2
    while bit:
        bits.append(bit)
        bit //= 2
    return bits


def after(value, *earlier):
    return lax.optimization_barrier((value,) + earlier)[0]


def gather_group(block):
    have = {0: block}
    for bit in bits_down(lax.axis_size("tensor") // 2):
        for r in list(have):
            have[r ^ bit] = permute_xor(have[r], "tensor", bit)
    return [have[r] for r in range(len(have))]


def reduce_group(parts):
    have = dict(enumerate(parts))
    for bit in reversed(bits_down(len(parts))):
        for r in [r for r in have if r & bit]:
            received = permute_xor(have.pop(r).astype(BF16), "tensor", bit)
            have[r ^ bit] = have[r ^ bit].astype(F32) + received.astype(F32)
    return have[0].astype(F32)


def rms_norm(values, gain_row):
    return (
        values
        * lax.rsqrt(jnp.mean(values * values, axis=-1, keepdims=True) + NORM_EPSILON)
        * gain_row
    )


def rotary_tables():
    half = HEAD // 2
    frequency = ROPE_THETA ** (-(jnp.arange(half, dtype=F32) * (2.0 / HEAD)))
    angles = jnp.arange(SEQ_LEN, dtype=F32)[:, None] * frequency[None, :]
    cosine, sine = jnp.cos(angles), jnp.sin(angles)
    empty = jnp.zeros((SEQ_LEN, PAD - HEAD), F32)
    return (
        jnp.concatenate([cosine, cosine, empty], axis=1),
        jnp.concatenate([-sine, sine, empty], axis=1),
    )


def shards(
    tokens,
    cotangent,
    lengths,
    qkv_weight,
    out_weight,
    gate_up_weight,
    down_weight,
    norm_gains,
    qkv_first,
    out_first,
    gate_up_first,
    down_first,
    gains_first,
    qkv_second,
    out_second,
    gate_up_second,
    down_second,
    gains_second,
):
    rows_each, width = tokens.shape
    n_t = lax.axis_size("tensor")
    n_dp = lax.axis_size("dp")
    n_z = n_dp // 2
    nb = n_t // 2
    t = lax.axis_index("tensor")
    d = lax.axis_index("dp")
    mine = t // nb
    info = [lengths[mine][None], lengths[1 - mine][None]]
    spread = spread_matrix().astype(BF16)
    blk = qkv_weight.shape[0]
    kv = qkv_weight.shape[1] // G_COLS

    over = ("tensor", nb)

    gain_cols = norm_gains.shape[1]
    gain_start = (d * n_t + t) * gain_cols
    gain_rows = lax.dynamic_update_slice(
        jnp.zeros((2, width), F32),
        norm_gains.astype(BF16).astype(F32),
        (0, gain_start),
    )
    out_half = out_weight.astype(BF16).T
    x_rest, wq, wo, gain_work = prologue(
        tokens, qkv_weight.astype(BF16), out_half, gain_rows, n_z, n_t, n_dp
    )
    attention_gain, feedforward_gain = gain_work[0:1], gain_work[1:2]
    w_out_cols = out_half.shape[1]
    if w_out_cols % G_COLS:
        wo = jnp.pad(wo, ((0, 0), (0, -w_out_cols % G_COLS)))
    w_qkv, w_out = pad_weights(wq, wo, spread)
    w_out = w_out[:, : kv * GROUP * PAD]
    ffn_half = jnp.concatenate(
        [gate_up_weight.astype(BF16), down_weight.astype(BF16).T[None]], axis=0
    )
    w_ffn = lax.all_gather(ffn_half, "dp", axis=1, tiled=True)

    inputs = tokens.astype(F32)
    x_blocks = [tokens] + [x_rest[r] for r in range(n_t - 1)]
    cos_t, sin_t = rotary_tables()
    *far_fwd, c_far = attn_fwd(
        x_blocks[nb:],
        info[1],
        attention_gain,
        w_qkv,
        w_out,
        cos_t,
        sin_t,
        sends=[(cotangent, over)],
        collective_id=3,
    )
    far_sum = reduce_group(far_fwd[4:]).astype(BF16)
    *near_fwd, far_sum = attn_fwd(
        x_blocks[:nb],
        info[0],
        attention_gain,
        w_qkv,
        w_out,
        cos_t,
        sin_t,
        sends=[(far_sum, over)],
        collective_id=4,
    )
    residual = inputs + (reduce_group(near_fwd[4:]) + far_sum.astype(F32))

    normed_two = rms_norm(residual, feedforward_gain).astype(BF16)
    n_near = gather_group(normed_two)
    c_near = gather_group(cotangent)
    c_far = gather_group(c_far)
    *near, n_far = ffn(n_near, c_near, w_ffn, sends=[(normed_two, over)], collective_id=5)
    n_far = gather_group(n_far)
    far = ffn(n_far, c_far, w_ffn)
    far_grad = reduce_group(far[3 + nb :]).astype(BF16)
    ffn_grads, far_grad = ffn_grad(
        n_near + n_far,
        c_near + c_far,
        list(near[:3]) + list(far[:3]),
        sends=[(far_grad, over)],
        collective_id=6,
    )
    normed_two_grad = reduce_group(near[3 + nb :]) + far_grad.astype(F32)
    ffn_sum = lax.psum_scatter(ffn_grads, "dp", scatter_dimension=1, tiled=True).astype(F32)

    _, norm_pull = jax.vjp(rms_norm, residual, feedforward_gain)
    residual_part, ffn_gain_grad = norm_pull(normed_two_grad)
    residual_grad = cotangent.astype(F32) + residual_part
    attention_grad = residual_grad.astype(BF16)
    a_near = gather_group(attention_grad)
    *near_bwd, a_far = attn_bwd(
        a_near,
        info[0],
        w_qkv,
        w_out,
        near_fwd[1],
        near_fwd[3],
        cos_t,
        sin_t,
        sends=[(attention_grad, over)],
        collective_id=7,
    )
    a_far = gather_group(a_far)
    far_out = reduce_group(far[3 : 3 + nb]).astype(BF16)
    *far_bwd, far_out = attn_bwd(
        a_far,
        info[1],
        w_qkv,
        w_out,
        far_fwd[1],
        far_fwd[3],
        cos_t,
        sin_t,
        sends=[(far_out, over)],
        collective_id=8,
    )
    layer_out = (residual + (reduce_group(near[3 : 3 + nb]) + far_out.astype(F32))).astype(BF16)
    far_sum = reduce_group(far_bwd[1:]).astype(BF16)
    same, _, other, far_sum = weight_grad(
        a_near + a_far,
        [near_fwd[2], far_fwd[2]],
        [near_fwd[0], far_fwd[0]],
        [near_bwd[0], far_bwd[0]],
        spread,
        n_z,
        blk,
        sends=[(far_sum, over)],
        meets=[("dp", 1)],
        collective_id=9,
    )
    normed_grad = reduce_group(near_bwd[1:]) + far_sum.astype(F32)
    attention_sum = z_sum(same, other, n_z, 10)
    out_grad_sum = attention_sum[0, :, :w_out_cols].T
    qkv_grad_sum = jnp.concatenate([attention_sum[1 + j] for j in range(kv)], axis=1)
    _, first_pull = jax.vjp(rms_norm, inputs, attention_gain)
    input_part, attention_gain_grad = first_pull(normed_grad)
    grad_tokens = residual_grad + input_part
    gain_grads = jnp.concatenate([attention_gain_grad, ffn_gain_grad], axis=0)
    gain_all = sum_all(
        gain_grads.reshape(-1, PAD), n_dp, n_t, 1, "sum_gain_gradients"
    ).reshape(2, width)
    gain_sums = lax.dynamic_slice(gain_all, (0, gain_start), (2, gain_cols))

    masters = (
        qkv_weight,
        out_weight,
        gate_up_weight[0],
        gate_up_weight[1],
        down_weight,
        norm_gains[0],
        norm_gains[1],
    )
    firsts = (
        qkv_first,
        out_first,
        gate_up_first[0],
        gate_up_first[1],
        down_first,
        gains_first[0],
        gains_first[1],
    )
    seconds = (
        qkv_second,
        out_second,
        gate_up_second[0],
        gate_up_second[1],
        down_second,
        gains_second[0],
        gains_second[1],
    )
    gradients = (
        qkv_grad_sum,
        out_grad_sum,
        ffn_sum[0],
        ffn_sum[1],
        ffn_sum[2].T,
        gain_sums[0],
        gain_sums[1],
    )
    correct_one = 1.0 - BETA_ONE**STEP
    correct_two = 1.0 - BETA_TWO**STEP
    new_firsts = []
    new_seconds = []
    updates = []
    for master, moment, square, gradient in zip(masters, firsts, seconds, gradients):
        moment = BETA_ONE * moment + (1.0 - BETA_ONE) * gradient
        square = BETA_TWO * square + (1.0 - BETA_TWO) * gradient * gradient
        new_firsts.append(moment)
        new_seconds.append(square)
        updates.append(
            moment / correct_one / (jnp.sqrt(square / correct_two) + ADAM_EPSILON)
            + WEIGHT_DECAY * master
        )
    squares = jnp.stack(
        [jnp.sum(master * master) for master in masters]
        + [jnp.sum(update * update) for update in updates]
    )
    squares = jnp.pad(squares[None], ((0, 7), (0, PAD - 14)))
    norms = jnp.sqrt(sum_all(squares, n_dp, n_t, 2, "sum_squares")[0, :14])
    weight_norms, all_update_norms = norms[:7], norms[7:]
    new_weights = [
        masters[number]
        - LEARN_RATE * (weight_norms[number] / all_update_norms[number]) * updates[number]
        for number in range(7)
    ]
    return (
        layer_out,
        grad_tokens,
        new_weights[0],
        new_weights[1],
        jnp.stack([new_weights[2], new_weights[3]]),
        new_weights[4],
        jnp.stack([new_weights[5], new_weights[6]]),
        new_firsts[0],
        new_firsts[1],
        jnp.stack([new_firsts[2], new_firsts[3]]),
        new_firsts[4],
        jnp.stack([new_firsts[5], new_firsts[6]]),
        new_seconds[0],
        new_seconds[1],
        jnp.stack([new_seconds[2], new_seconds[3]]),
        new_seconds[4],
        jnp.stack([new_seconds[5], new_seconds[6]]),
        weight_norms,
        all_update_norms[:5],
        all_update_norms[5:],
    )


def solution(mesh):
    rows = P(("dp", "tensor"), None)
    gains = P(None, ("dp", "tensor"))
    weights = (P("dp", "tensor"), P("tensor", "dp"), P(None, "dp", "tensor"), P("tensor", "dp"), gains)
    in_specs = (rows, rows, P("dp")) + weights * 3
    out_specs = (rows, rows) + weights * 3 + (P(), P(), P())
    return jax.shard_map(shards, mesh=mesh, in_specs=in_specs, out_specs=out_specs, check_vma=False)
```

```python
import functools

import jax
import jax.numpy as jnp
import numpy as np
from jax import lax
from jax.experimental import pallas as pl
from jax.experimental.pallas import tpu as pltpu
from jax.sharding import PartitionSpec as P

HEAD = 96
PAD = 128
SEQ_LEN = 1024
SEQS_DEV = 2
STEP = 10
GROUP = 2

NORM_EPSILON = 1e-05
ROPE_THETA = 100000.0
BETA_ONE = 0.9
BETA_TWO = 0.999
ADAM_EPSILON = 1e-06
WEIGHT_DECAY = 0.01
LEARN_RATE = 0.3
NEGATIVE = -1e30
LOG2E = 1.4426950408889634
SCALE = HEAD ** (-0.5)
Q_ROWS = 256
G_COLS = 4 * HEAD
G_PAD = 4 * PAD
VMEM_LIMIT = 56 << 20

F32 = jnp.float32
BF16 = jnp.bfloat16
VM = pl.BlockSpec(memory_space=pltpu.VMEM)
SM = pl.BlockSpec(memory_space=pltpu.SMEM)
ANY = pl.BlockSpec(memory_space=pl.ANY)
MESH = pl.DeviceIdType.MESH


def dot_nn(a, b):
    return lax.dot_general(a, b, (((1,), (0,)), ((), ())), preferred_element_type=F32)


def dot_nt(a, b):
    return lax.dot_general(a, b, (((1,), (1,)), ((), ())), preferred_element_type=F32)


def dot_tn(a, b):
    return lax.dot_general(a, b, (((0,), (0,)), ((), ())), preferred_element_type=F32)


def cost(flops, moved):
    return pl.CostEstimate(flops=int(flops), bytes_accessed=int(moved), transcendentals=0)


def spread_matrix():
    source = lax.broadcasted_iota(jnp.int32, (G_COLS, G_PAD), 0)
    target = lax.broadcasted_iota(jnp.int32, (G_COLS, G_PAD), 1)
    return ((target // PAD) * HEAD + target % PAD == source) & (target % PAD < HEAD)


def pad_kernel(spread, wq, wo, wq_pad, wo_pad):
    for source, target in ((wq, wq_pad), (wo, wo_pad)):
        for g in range(target.shape[1] // G_PAD):
            target[:, g * G_PAD : (g + 1) * G_PAD] = dot_nn(
                source[:, g * G_COLS : (g + 1) * G_COLS], spread[...]
            ).astype(BF16)


def pad_weights(wq, wo, spread):
    depth = wq.shape[0]
    return pl.pallas_call(
        pad_kernel,
        out_shape=[
            jax.ShapeDtypeStruct((depth, w.shape[1] // G_COLS * G_PAD), BF16) for w in (wq, wo)
        ],
        in_specs=[VM] * 3,
        out_specs=[VM] * 2,
        compiler_params=pltpu.CompilerParams(vmem_limit_bytes=VMEM_LIMIT),
        cost_estimate=cost(6 * depth * G_COLS * G_PAD, 8 << 20),
        name="pad_weights",
    )(spread, wq, wo)


def swap_halves(values):
    lane = lax.broadcasted_iota(jnp.int32, values.shape, 1)
    return jnp.where(
        lane < HEAD // 2,
        pltpu.roll(values, PAD - HEAD // 2, 1),
        pltpu.roll(values, HEAD // 2, 1),
    )


def permuted(axis, bit):
    return {axis: lax.axis_index(axis) ^ bit}


class Remote:
    def __init__(self, copy):
        self.copy = copy
        self.landed = False

    def wait_recv(self):
        if not self.landed:
            self.copy.wait_recv()
        self.landed = True


class Frame:
    def __init__(self, names, refs):
        self.refs = dict(zip(names, refs))
        self.loading, self.remotes, self.storing = {}, [], []
        self.next_local = 0

    def __getitem__(self, name):
        return self.refs[name]

    def meet(self, peers):
        barrier = pltpu.get_barrier_semaphore()
        for peer in peers:
            pl.semaphore_signal(barrier, inc=1, device_id=peer, device_id_type=MESH)
        pl.semaphore_wait(barrier, len(peers))

    def local(self, source, target):
        copy = pltpu.make_async_copy(source, target, self.refs["local_sem"].at[self.next_local])
        self.next_local += 1
        copy.start()
        return copy

    def load(self, *names):
        for name in names:
            self.loading[name] = self.local(self.refs["any_" + name], self.refs[name])

    def ready(self, *names):
        for name in names:
            if name in self.loading:
                self.loading.pop(name).wait()

    def store(self, source, target):
        self.storing.append(self.local(source, target))

    def flush(self, name):
        self.store(self.refs[name], self.refs["any_" + name])

    def remote(self, source, target, peer):
        n = len(self.remotes)
        copy = pltpu.make_async_remote_copy(
            src_ref=source,
            dst_ref=target,
            send_sem=self.refs["send_sem"].at[n],
            recv_sem=self.refs["recv_sem"].at[n],
            device_id=peer,
            device_id_type=MESH,
        )
        copy.start()
        self.remotes.append(Remote(copy))
        return self.remotes[-1]

    def finish(self):
        for remote in self.remotes:
            remote.copy.wait_send()
            remote.wait_recv()
        for copy in self.storing:
            copy.wait()


def frame_call(body, name, inputs, outputs, scratch, flops, collective_id, n_sems=40):
    names, specs, arrays = [], [], []
    spec_of = {"vmem": VM, "smem": SM, "any": ANY, "load": ANY, "flush": ANY}
    for key, (array, kind) in inputs.items():
        names.append("any_" + key if kind == "load" else key)
        specs.append(spec_of[kind])
        arrays.append(array)
    out_specs, out_shapes = [], []
    for key, (shape, kind) in outputs.items():
        names.append("any_" + key if kind == "flush" else key)
        out_specs.append(spec_of[kind])
        out_shapes.append(shape)
    shapes = []
    for table, kind_of in ((inputs, "load"), (outputs, "flush")):
        for key, (array, kind) in table.items():
            if kind == kind_of:
                names.append(key)
                shapes.append(pltpu.VMEM(array.shape, array.dtype))
    for key, shape in scratch.items():
        names.append(key)
        shapes.append(shape)
    for key in ("local_sem", "send_sem", "recv_sem"):
        names.append(key)
        shapes.append(pltpu.SemaphoreType.DMA((n_sems,)))

    def kernel(*refs):
        frame = Frame(names, refs)
        body(frame)
        frame.finish()

    moved = sum(a.size * a.dtype.itemsize for a in arrays)
    results = pl.pallas_call(
        kernel,
        out_shape=out_shapes,
        in_specs=specs,
        out_specs=out_specs,
        scratch_shapes=shapes,
        compiler_params=pltpu.CompilerParams(
            vmem_limit_bytes=VMEM_LIMIT, collective_id=collective_id, has_side_effects=True
        ),
        cost_estimate=cost(flops, moved),
        name=name,
    )(*arrays)
    return dict(zip(outputs, results))


def half_peers(nb):
    return [(r, permuted("tensor", r)) for r in range(1, nb)]


def rows_of(c):
    return pl.ds(c * Q_ROWS, Q_ROWS)


def bits_down(size):
    bits = []
    bit = size // 2
    while bit:
        bits.append(bit)
        bit //= 2
    return bits


def prologue_kernel(n_z, n_t, blk, *refs):
    tokens, cotangent, qkv, outw, gains = refs[:5]
    xs, c_far, wq, wo, gain_sum = refs[5:10]
    held, got, own_sem, tok_send, tok_recv, z_send, z_recv, x_send, x_recv, g_send, g_recv = refs[10:]
    d, t = lax.axis_index("dp"), lax.axis_index("tensor")
    z, x = d // 2, lax.rem(d, 2)
    bits = bits_down(n_t)

    def at_z(k):
        return {"dp": lax.rem(z + k, n_z) * 2 + x}

    other_x = {"dp": z * 2 + (1 - x)}

    def at_t(bit):
        return {"tensor": t ^ bit}

    barrier = pltpu.get_barrier_semaphore()
    peers = [at_z(k) for k in range(1, n_z)] + [other_x] + [at_t(bit) for bit in bits]
    for peer in peers:
        pl.semaphore_signal(barrier, inc=1, device_id=peer, device_id_type=MESH)
    pl.semaphore_wait(barrier, len(peers))

    def send(src, dst, send_sem, recv_sem, peer):
        copy = pltpu.make_async_remote_copy(
            src_ref=src,
            dst_ref=dst,
            send_sem=send_sem,
            recv_sem=recv_sem,
            device_id=peer,
            device_id_type=MESH,
        )
        copy.start()
        return copy

    def owned(k):
        return pl.ds(pl.multiple_of((lax.rem(z + n_z - k, n_z) * 2 + x) * blk, 16), blk)

    pending = []
    held[0, :, :] = gains[...]
    stages = [at_t(bit) for bit in bits] + [other_x]
    gain_copy = send(held.at[0], got.at[0], g_send.at[0], g_recv.at[0], stages[0])
    token_copies = {}
    for bit in bits:
        token_copies[bit] = send(
            tokens, xs.at[bit], tok_send.at[bit], tok_recv.at[bit], at_t(bit)
        )
    locals_ = [
        pltpu.make_async_copy(qkv, wq.at[owned(0)], own_sem.at[0]),
        pltpu.make_async_copy(outw, wo.at[owned(0)], own_sem.at[1]),
        pltpu.make_async_copy(tokens, xs.at[0], own_sem.at[2]),
    ]
    for copy in locals_:
        copy.start()
    z_copies, x_copies = {}, {}
    for k in range(1, n_z):
        z_copies[0, k] = send(qkv, wq.at[owned(0)], z_send.at[0, k], z_recv.at[0, k], at_z(k))
    x_copies[0, 0] = send(qkv, wq.at[owned(0)], x_send.at[0, 0], x_recv.at[0, 0], other_x)
    for stage in range(len(stages)):
        gain_copy.wait()
        held[stage + 1, :, :] = held[stage, :, :] + got[stage, :, :]
        if stage + 1 < len(stages):
            gain_copy = send(
                held.at[stage + 1],
                got.at[stage + 1],
                g_send.at[stage + 1],
                g_recv.at[stage + 1],
                stages[stage + 1],
            )
    last = len(stages)
    gain_z = [
        send(held.at[last], got.at[last + k - 1], g_send.at[last + k - 1], g_recv.at[last + k - 1], at_z(k))
        for k in range(1, n_z)
    ]
    for k in range(1, n_z):
        z_copies[1, k] = send(outw, wo.at[owned(0)], z_send.at[1, k], z_recv.at[1, k], at_z(k))
    for which, whole in ((0, wq), (1, wo)):
        if which == 1:
            x_copies[1, 0] = send(outw, wo.at[owned(0)], x_send.at[1, 0], x_recv.at[1, 0], other_x)
        for k in range(1, n_z):
            z_copies[which, k].wait_recv()
            x_copies[which, k] = send(
                whole.at[owned(k)],
                whole.at[owned(k)],
                x_send.at[which, k],
                x_recv.at[which, k],
                other_x,
            )
    arrived = [0]
    for bit in bits:
        for r in list(arrived):
            if r:
                token_copies[r ^ bit] = send(
                    xs.at[r], xs.at[r ^ bit], tok_send.at[r ^ bit], tok_recv.at[r ^ bit], at_t(bit)
                )
        for r in list(arrived):
            token_copies[r ^ bit].wait_recv()
            arrived.append(r ^ bit)
    c_copy = send(cotangent, c_far, tok_send.at[0], tok_recv.at[0], at_t(n_t // 2))
    total = held[last, :, :]
    for k in range(1, n_z):
        gain_z[k - 1].wait()
        total = total + got[last + k - 1, :, :]
    gain_sum[...] = total
    for copy in token_copies.values():
        copy.wait_send()
    for copy in z_copies.values():
        copy.wait_send()
    for copy in x_copies.values():
        copy.wait()
    for copy in locals_:
        copy.wait()
    c_copy.wait()


def prologue(tokens, cotangent, qkv, outw, gains, n_z, n_t, n_dp):
    blk = qkv.shape[0]
    n_gain = len(bits_down(n_t)) + 1 + n_z - 1
    dma = pltpu.SemaphoreType.DMA
    return pl.pallas_call(
        functools.partial(prologue_kernel, n_z, n_t, blk),
        out_shape=[
            jax.ShapeDtypeStruct((n_t,) + tokens.shape, BF16),
            jax.ShapeDtypeStruct(cotangent.shape, BF16),
            jax.ShapeDtypeStruct((blk * n_dp, qkv.shape[1]), BF16),
            jax.ShapeDtypeStruct((blk * n_dp, outw.shape[1]), BF16),
            jax.ShapeDtypeStruct(gains.shape, F32),
        ],
        in_specs=[ANY, ANY, ANY, ANY, VM],
        out_specs=[ANY, ANY, ANY, ANY, VM],
        scratch_shapes=[
            pltpu.VMEM((n_gain + 1,) + gains.shape, F32),
            pltpu.VMEM((n_gain,) + gains.shape, F32),
            dma((3,)),
            dma((n_t,)),
            dma((n_t,)),
            dma((2, n_z)),
            dma((2, n_z)),
            dma((2, n_z)),
            dma((2, n_z)),
            dma((n_gain,)),
            dma((n_gain,)),
        ],
        compiler_params=pltpu.CompilerParams(
            collective_id=0, has_side_effects=True, vmem_limit_bytes=4 << 20
        ),
        cost_estimate=cost(0, 60 << 20),
        name="gather_tokens_and_weights",
    )(tokens, cotangent, qkv, outw, gains)


def attention_rows(k, tag, i, length, kv):
    qkvp, att, lse = k[tag + "qkvp"], k[tag + "att"], k[tag + "lse"]
    n = (i + 1) * Q_ROWS
    rows = slice(i * Q_ROWS, n)
    lane = lax.broadcasted_iota(jnp.int32, (Q_ROWS, PAD), 1)

    def one_head(h, log_totals):
        group = h // GROUP
        q_col = pl.ds(pl.multiple_of((4 * group + h % GROUP) * PAD, PAD), PAD)
        k_col = pl.ds(pl.multiple_of((4 * group + 2) * PAD, PAD), PAD)
        v_col = pl.ds(pl.multiple_of((4 * group + 3) * PAD, PAD), PAD)
        a_col = pl.ds(pl.multiple_of(h * PAD, PAD), PAD)
        s = dot_nt(qkvp[rows, q_col], qkvp[0:n, k_col])
        row_ids = lax.broadcasted_iota(jnp.int32, (Q_ROWS, 1), 0) + i * Q_ROWS + 1
        limit = jnp.minimum(row_ids, length)
        col_ids = lax.broadcasted_iota(jnp.int32, (Q_ROWS, n), 1)
        s = jnp.where(col_ids < limit, s, NEGATIVE)
        top = jnp.max(s, axis=-1, keepdims=True)
        e = jnp.exp2((s - top) * (SCALE * LOG2E))
        total = jnp.sum(e, axis=-1, keepdims=True)
        p = (e * (1.0 / total)).astype(BF16)
        att[rows, a_col] = dot_nn(p, qkvp[0:n, v_col]).astype(BF16)
        log_total = top * (SCALE * LOG2E) + jnp.log2(total)
        return jnp.where(lane == h, log_total, log_totals)

    lse[rows, :] = lax.fori_loop(0, kv * GROUP, one_head, jnp.zeros((Q_ROWS, PAD), F32))


def attention_forward_body(nb, rows_each, kv, k):
    local = lax.rem(lax.axis_index("tensor"), nb)
    seq_len = nb * rows_each
    per_block = rows_each // Q_ROWS
    over = permuted("tensor", nb)
    far_load = k.local(k["xs"].at[pl.ds(nb, nb)], k["far_x"])
    k.load("w_qkv", "cos_t", "sin_t", "w_out")
    near_load = k.local(k["xs"].at[pl.ds(0, nb)], k["near_x"])
    k.meet([over] + [peer for _, peer in half_peers(nb)])
    landing = []
    waiting = []
    chunk = 32
    for tag, length in (("far_", k["lengths"][1]), ("near_", k["lengths"][0])):
        x_ref, normed, qkvp = k[tag + "x"], k[tag + "normed"], k[tag + "qkvp"]
        parts, got = k[tag + "parts"], k[tag + "got"]
        (far_load if tag == "far_" else near_load).wait()
        for r in range(nb):
            base = (local ^ r) * rows_each

            def norm_rows(i, carry):
                v = x_ref[r, pl.ds(pl.multiple_of(i * chunk, chunk), chunk), :].astype(F32)
                inv = lax.rsqrt(jnp.mean(v * v, axis=-1, keepdims=True) + NORM_EPSILON)
                normed[pl.ds(pl.multiple_of(base + i * chunk, chunk), chunk), :] = (
                    v * inv * k["gain_one"][...]
                ).astype(BF16)
                return carry

            lax.fori_loop(0, rows_each // chunk, norm_rows, 0)
        k.flush(tag + "normed")
        k.ready("w_qkv", "cos_t", "sin_t")
        for i in range(seq_len // Q_ROWS):
            rows = slice(i * Q_ROWS, (i + 1) * Q_ROWS)
            for j in range(kv):
                proj = dot_nn(normed[rows, :], k["w_qkv"][:, j * G_PAD : (j + 1) * G_PAD])
                for h in range(4):
                    part = proj[:, h * PAD : (h + 1) * PAD]
                    if h < 3:
                        part = part * k["cos_t"][rows, :] + swap_halves(part) * k["sin_t"][rows, :]
                    qkvp[rows, (4 * j + h) * PAD : (4 * j + h + 1) * PAD] = part.astype(BF16)
        k.flush(tag + "qkvp")
        k.ready("w_out")
        for c in range(per_block):
            rows = slice(c * Q_ROWS, (c + 1) * Q_ROWS)
            for b in range(nb):
                i = b * per_block + c
                attention_rows(k, tag, i, length, kv)
                part = dot_nt(k[tag + "att"][i * Q_ROWS : (i + 1) * Q_ROWS, :], k["w_out"][...])
                parts[local ^ b, rows, :] = part.astype(BF16)
                if waiting:
                    waiting.pop()()
            copies = [
                k.remote(parts.at[r, rows_of(c)], got.at[r - 1, rows_of(c)], peer)
                for r, peer in half_peers(nb)
            ]

            def complete(rows=rows, c=c, copies=copies, parts=parts, got=got, tag=tag):
                total = parts[0, rows, :].astype(F32)
                for r, copy in enumerate(copies):
                    copy.wait_recv()
                    total = total + got[r, rows, :].astype(F32)
                if tag == "far_":
                    parts[0, rows, :] = total.astype(BF16)
                    landing.append(
                        k.remote(parts.at[0, rows_of(c)], k["landed"].at[rows_of(c)], over)
                    )
                else:
                    k["residual"][rows, :] = k["near_x"][0, rows, :].astype(F32) + total

            waiting.append(complete)
        k.flush(tag + "att")
        k.flush(tag + "lse")
    waiting.pop()()
    for c in range(per_block):
        landing[c].wait_recv()

        def residual_rows(i, carry):
            rows = pl.ds(pl.multiple_of(c * Q_ROWS + i * chunk, chunk), chunk)
            v = k["residual"][rows, :] + k["landed"][rows, :].astype(F32)
            k["residual"][rows, :] = v
            inv = lax.rsqrt(jnp.mean(v * v, axis=-1, keepdims=True) + NORM_EPSILON)
            k["normed_two"][rows, :] = (v * inv * k["gain_two"][...]).astype(BF16)
            return carry

        lax.fori_loop(0, Q_ROWS // chunk, residual_rows, 0)
    k.flush("residual")
    k.flush("normed_two")


def attention_forward(xs, lengths, gains, w_qkv, w_out, cos_t, sin_t, collective_id):
    n_t, rows_each, width = xs.shape
    nb = n_t // 2
    seq_len = nb * rows_each
    kv = w_qkv.shape[1] // G_PAD
    heads = kv * GROUP
    sds = jax.ShapeDtypeStruct
    outputs = {}
    for tag in ("far_", "near_"):
        outputs[tag + "normed"] = (sds((seq_len, width), BF16), "flush")
        outputs[tag + "qkvp"] = (sds((seq_len, kv * G_PAD), BF16), "flush")
        outputs[tag + "att"] = (sds((seq_len, heads * PAD), BF16), "flush")
        outputs[tag + "lse"] = (sds((seq_len, PAD), F32), "flush")
    outputs["residual"] = (sds((rows_each, width), F32), "flush")
    outputs["normed_two"] = (sds((rows_each, width), BF16), "flush")
    block = pltpu.VMEM((nb, rows_each, width), BF16)
    others = pltpu.VMEM((nb - 1, rows_each, width), BF16)
    return frame_call(
        functools.partial(attention_forward_body, nb, rows_each, kv),
        "attention_forward",
        {
            "lengths": (lengths, "smem"),
            "gain_one": (gains[0:1], "vmem"),
            "gain_two": (gains[1:2], "vmem"),
            "xs": (xs, "any"),
            "w_qkv": (w_qkv, "load"),
            "w_out": (w_out, "load"),
            "cos_t": (cos_t, "load"),
            "sin_t": (sin_t, "load"),
        },
        outputs,
        {
            "near_x": block,
            "far_x": block,
            "far_parts": block,
            "near_parts": block,
            "far_got": others,
            "near_got": others,
            "landed": pltpu.VMEM((rows_each, width), BF16),
        },
        4 * seq_len * width * (kv * G_PAD + heads * PAD) + heads * seq_len * seq_len * 8 * 256,
        collective_id,
    )


def feed_forward_body(nb, rows_each, k):
    over = permuted("tensor", nb)
    peers = half_peers(nb)
    per_block = rows_each // Q_ROWS
    w = k["w"]
    width = w.shape[1]
    near_n, near_c, far_n, far_c = k["near_n"], k["near_c"], k["far_n"], k["far_c"]
    own_n = k.local(k["own_n"], near_n.at[0])
    own_c = k.local(k["own_c"], near_c.at[0])
    k.load("w")
    own_far_c = k.local(k["own_far_c"], far_c.at[0])
    k.meet([over] + [peer for _, peer in peers])
    far_first = [
        k.remote(k["own_n"].at[rows_of(c)], far_n.at[0, rows_of(c)], over) for c in range(per_block)
    ]
    n_copies = [k.remote(k["own_n"], near_n.at[r], peer) for r, peer in peers]
    c_copies = [k.remote(k["own_c"], near_c.at[r], peer) for r, peer in peers]
    far_c_copies = [k.remote(k["own_far_c"], far_c.at[r], peer) for r, peer in peers]
    own_n.wait()
    own_c.wait()
    k.ready("w")

    def rows_step(side, r, c):
        rows = slice(c * Q_ROWS, (c + 1) * Q_ROWS)
        start = (0 if side == "near_" else nb * rows_each) + r * rows_each + c * Q_ROWS
        kept = slice(start, start + Q_ROWS)
        n = k[side + "n"][r, rows, :]
        gate = dot_nn(n, w[0])
        up = dot_nn(n, w[1])
        sig = 1.0 / (1.0 + jnp.exp(-gate))
        silu = gate * sig
        hid = (silu * up).astype(BF16)
        k["hidden"][kept, :] = hid
        dh = dot_nn(k[side + "c"][r, rows, :], w[2])
        dg = (dh * up * sig * (1.0 + gate * (1.0 - sig))).astype(BF16)
        du = (dh * silu).astype(BF16)
        k["d_gate"][kept, :] = dg
        k["d_up"][kept, :] = du
        k[side + "grad"][r, rows, :] = (dot_nt(dg, w[0]) + dot_nt(du, w[1])).astype(BF16)
        k[side + "out"][r, rows, :] = dot_nt(hid, w[2]).astype(BF16)

    for r in range(nb):
        if r:
            n_copies[r - 1].wait_recv()
            c_copies[r - 1].wait_recv()
        for c in range(per_block):
            rows_step("near_", r, c)
        for name in ("grad", "out"):
            part = k["near_" + name].at[r]
            if r:
                k.remote(part, k["near_got_" + name].at[r - 1], peers[r - 1][1])
            else:
                k.store(part, k["near_own_" + name])
    own_far_c.wait()
    for copy in far_c_copies:
        copy.wait_recv()
    landing = []
    for c in range(per_block):
        rows = slice(c * Q_ROWS, (c + 1) * Q_ROWS)
        far_first[c].wait_recv()
        passed = [
            k.remote(far_n.at[0, rows_of(c)], far_n.at[r, rows_of(c)], peer) for r, peer in peers
        ]
        rows_step("far_", 0, c)
        copies = []
        for r, peer in peers:
            passed[r - 1].wait_recv()
            rows_step("far_", r, c)
            copies.append(
                k.remote(
                    k["far_grad"].at[r, rows_of(c)], k["far_got_grad"].at[r - 1, rows_of(c)], peer
                )
            )
        total = k["far_grad"][0, rows, :].astype(F32)
        for r, copy in enumerate(copies):
            copy.wait_recv()
            total = total + k["far_got_grad"][r, rows, :].astype(F32)
        k["far_grad"][0, rows, :] = total.astype(BF16)
        landing.append(k.remote(k["far_grad"].at[0, rows_of(c)], k["landed"].at[rows_of(c)], over))
    k.store(k["far_out"].at[0], k["far_own_out"])
    for r, peer in peers:
        k.remote(k["far_out"].at[r], k["far_got_out"].at[r - 1], peer)
    half = nb * rows_each
    for which in (2, 0, 1):
        name = "c" if which == 2 else "n"
        right = k[("d_gate", "d_up", "hidden")[which]]

        def col_step(i, carry):
            cols = pl.ds(pl.multiple_of(i * G_COLS, G_COLS), G_COLS)
            total = None
            for s, side in enumerate(("near_", "far_")):
                for r in range(nb):
                    start = s * half + r * rows_each
                    term = dot_tn(k[side + name][r, :, cols], right[start : start + rows_each, :])
                    total = term if total is None else total + term
            w[which, cols, :] = total.astype(BF16)
            return carry

        lax.fori_loop(0, width // G_COLS, col_step, 0)
        k.store(w.at[which], k["grads"].at[which])


def feed_forward(normed_two, cotangent, c_far, w, nb, collective_id):
    rows_each, width = normed_two.shape
    units = w.shape[2]
    sds = jax.ShapeDtypeStruct
    block = pltpu.VMEM((nb, rows_each, width), BF16)
    kept = pltpu.VMEM((2 * nb * rows_each, units), BF16)
    own = (sds((rows_each, width), BF16), "any")
    got = (sds((nb - 1, rows_each, width), BF16), "any")
    return frame_call(
        functools.partial(feed_forward_body, nb, rows_each),
        "feed_forward",
        {
            "own_n": (normed_two, "any"),
            "own_c": (cotangent, "any"),
            "own_far_c": (c_far, "any"),
            "w": (w, "load"),
        },
        {
            "grads": (sds(w.shape, BF16), "any"),
            "near_own_grad": own,
            "near_got_grad": got,
            "landed": own,
            "near_own_out": own,
            "near_got_out": got,
            "far_own_out": own,
            "far_got_out": got,
        },
        {
            "near_n": block,
            "far_n": block,
            "near_c": block,
            "far_c": block,
            "hidden": kept,
            "d_gate": kept,
            "d_up": kept,
            "near_grad": block,
            "far_grad": block,
            "near_out": block,
            "far_out": block,
            "far_got_grad": pltpu.VMEM((nb - 1, rows_each, width), BF16),
        },
        36 * nb * rows_each * width * units,
        collective_id,
    )


def attention_backward_rows(k, tag, i, length, kv):
    qkvp, dproj, datt, lse = k[tag + "qkvp"], k[tag + "dproj"], k["datt"], k[tag + "lse"]
    n = (i + 1) * Q_ROWS
    rows = slice(i * Q_ROWS, n)
    lane = lax.broadcasted_iota(jnp.int32, (Q_ROWS, PAD), 1)

    def one_head(h, carry):
        group = h // GROUP
        q_col = pl.ds(pl.multiple_of((4 * group + h % GROUP) * PAD, PAD), PAD)
        k_col = pl.ds(pl.multiple_of((4 * group + 2) * PAD, PAD), PAD)
        v_col = pl.ds(pl.multiple_of((4 * group + 3) * PAD, PAD), PAD)
        a_col = pl.ds(pl.multiple_of(h * PAD, PAD), PAD)
        q = qkvp[rows, q_col]
        keys = qkvp[0:n, k_col]
        do = datt[rows, a_col]
        row_lse = jnp.sum(jnp.where(lane == h, lse[rows, :], 0.0), axis=-1, keepdims=True)
        s = dot_nt(q, keys)
        row_ids = lax.broadcasted_iota(jnp.int32, (Q_ROWS, 1), 0) + i * Q_ROWS + 1
        limit = jnp.minimum(row_ids, length)
        col_ids = lax.broadcasted_iota(jnp.int32, (Q_ROWS, n), 1)
        s = jnp.where(col_ids < limit, s, NEGATIVE)
        p = jnp.exp2(s * (SCALE * LOG2E) - row_lse)
        dp = dot_nt(do, qkvp[0:n, v_col])
        inner = jnp.sum(p * dp, axis=-1, keepdims=True)
        ds = (p * (dp - inner)).astype(BF16)
        k["dv"][group, 0:n, :] += dot_tn(p.astype(BF16), do)
        k["dk"][group, 0:n, :] += dot_tn(ds, q)
        dq = dot_nn(ds, keys) * SCALE
        dproj[rows, q_col] = unrotate(k, dq, rows).astype(BF16)
        return carry

    lax.fori_loop(0, kv * GROUP, one_head, 0)


def unrotate(k, grad, rows):
    return grad * k["cos_t"][rows, :] - swap_halves(grad) * k["sin_t"][rows, :]


def attention_backward_body(nb, rows_each, kv, n_z, blk, k):
    d = lax.axis_index("dp")
    z, x = d // 2, lax.rem(d, 2)
    local = lax.rem(lax.axis_index("tensor"), nb)
    seq_len = nb * rows_each
    per_block = rows_each // Q_ROWS
    over = permuted("tensor", nb)
    other_x = permuted("dp", 1)
    peers = half_peers(nb)
    own_a = k.local(k["own_a"], k["near_a"].at[0])
    k.load("w_out", "near_qkvp", "near_lse", "cos_t", "sin_t", "w_qkv", "far_qkvp", "far_lse")
    k.load("spread", "near_att", "far_att", "near_normed", "far_normed")
    k.meet([over, other_x] + [peer for _, peer in peers])
    far_first = [
        k.remote(k["own_a"].at[rows_of(c)], k["far_a"].at[0, rows_of(c)], over)
        for c in range(per_block)
    ]
    near_copies = [k.remote(k["own_a"], k["near_a"].at[r], peer) for r, peer in peers]
    own_a.wait()
    for copy in near_copies:
        copy.wait_recv()
    for tag, length in (("near_", k["lengths"][0]), ("far_", k["lengths"][1])):
        blocks, parts, dproj = k[tag + "a"], k[tag + "parts"], k[tag + "dproj"]
        k["dk"][...] = jnp.zeros_like(k["dk"])
        k["dv"][...] = jnp.zeros_like(k["dv"])
        k.ready("w_out", "cos_t", "sin_t", tag + "qkvp", tag + "lse")
        for c in range(per_block):
            rows = slice(c * Q_ROWS, (c + 1) * Q_ROWS)
            if tag == "far_":
                far_first[c].wait_recv()
                passed = [
                    k.remote(blocks.at[0, rows_of(c)], blocks.at[r, rows_of(c)], peer)
                    for r, peer in peers
                ]
                for copy in passed:
                    copy.wait_recv()
            for b in range(nb):
                i = b * per_block + c
                k["datt"][i * Q_ROWS : (i + 1) * Q_ROWS, :] = dot_nn(
                    blocks[local ^ b, rows, :], k["w_out"][...]
                ).astype(BF16)
                attention_backward_rows(k, tag, i, length, kv)
        for j in range(kv):
            k_col = slice((4 * j + 2) * PAD, (4 * j + 3) * PAD)
            v_col = slice((4 * j + 3) * PAD, (4 * j + 4) * PAD)
            for i in range(seq_len // Q_ROWS):
                rows = slice(i * Q_ROWS, (i + 1) * Q_ROWS)
                dproj[rows, k_col] = unrotate(k, k["dk"][j, rows, :] * SCALE, rows).astype(BF16)
                dproj[rows, v_col] = k["dv"][j, rows, :].astype(BF16)
        k.ready("w_qkv")
        for c in range(per_block):
            rows = slice(c * Q_ROWS, (c + 1) * Q_ROWS)
            for b in range(nb):
                i = b * per_block + c
                part = dot_nt(dproj[i * Q_ROWS : (i + 1) * Q_ROWS, :], k["w_qkv"][...])
                parts[local ^ b, rows, :] = part.astype(BF16)
            if tag == "near_":
                for r, peer in peers:
                    k.remote(parts.at[r, rows_of(c)], k["near_got"].at[r - 1, rows_of(c)], peer)
            else:
                copies = [
                    k.remote(parts.at[r, rows_of(c)], k["far_got"].at[r - 1, rows_of(c)], peer)
                    for r, peer in peers
                ]
                total = parts[0, rows, :].astype(F32)
                for r, copy in enumerate(copies):
                    copy.wait_recv()
                    total = total + k["far_got"][r, rows, :].astype(F32)
                parts[0, rows, :] = total.astype(BF16)
                k.remote(parts.at[0, rows_of(c)], k["landed"].at[rows_of(c)], over)
        if tag == "near_":
            k.store(parts.at[0], k["near_own"])
    k.ready("spread", "near_att", "far_att", "near_normed", "far_normed")
    width = k["w_qkv"].shape[0]
    for which in range(kv + 1):

        def chunk(c, carry):
            cols = pl.ds(pl.multiple_of(c * G_COLS, G_COLS), G_COLS)
            total = None
            if which == 0:
                wide = k["near_att"].shape[1]
                for tag in ("near_", "far_"):
                    for r in range(nb):
                        start = pl.multiple_of((local ^ r) * rows_each, rows_each)
                        term = dot_tn(
                            k[tag + "a"][r, :, cols], k[tag + "att"][pl.ds(start, rows_each), :]
                        )
                        total = term if total is None else total + term
                compact = dot_nt(total.astype(BF16), k["spread"][:, :wide])
            else:
                part = slice((which - 1) * G_PAD, which * G_PAD)
                total = dot_tn(k["near_normed"][:, cols], k["near_dproj"][:, part])
                total += dot_tn(k["far_normed"][:, cols], k["far_dproj"][:, part])
                compact = dot_nt(total.astype(BF16), k["spread"][...])
            compact = compact.astype(BF16)
            for b in range(G_COLS // blk):
                owner = c * (G_COLS // blk) + b
                shift = lax.rem(owner // 2 + n_z - z, n_z)
                value = compact[b * blk : (b + 1) * blk, :]

                @pl.when(x == lax.rem(owner, 2))
                def _():
                    k["same"][which, shift, :, :] = value

                @pl.when(x != lax.rem(owner, 2))
                def _():
                    k["other"][which, shift, :, :] = value

            return carry

        lax.fori_loop(0, width // G_COLS, chunk, 0)
        k.remote(k["other"].at[which], k["arrived"].at[which], other_x)
    k.flush("same")


def attention_backward(attention_grad, lengths, fwd, w_qkv, w_out, tables, spread, nb, n_z, blk, collective_id):
    rows_each, width = attention_grad.shape
    seq_len = nb * rows_each
    kv = w_qkv.shape[1] // G_PAD
    heads = kv * GROUP
    sds = jax.ShapeDtypeStruct
    inputs = {
        "lengths": (lengths, "smem"),
        "own_a": (attention_grad, "any"),
        "w_qkv": (w_qkv, "load"),
        "w_out": (w_out, "load"),
        "cos_t": (tables[0], "load"),
        "sin_t": (tables[1], "load"),
        "spread": (spread, "load"),
    }
    for tag in ("near_", "far_"):
        for key in ("qkvp", "lse", "att", "normed"):
            inputs[tag + key] = (fwd[tag + key], "load")
    block = pltpu.VMEM((nb, rows_each, width), BF16)
    sums = sds((kv + 1, n_z, blk, G_COLS), BF16)
    own = (sds((rows_each, width), BF16), "any")
    return frame_call(
        functools.partial(attention_backward_body, nb, rows_each, kv, n_z, blk),
        "attention_backward",
        inputs,
        {
            "near_own": own,
            "near_got": (sds((nb - 1, rows_each, width), BF16), "any"),
            "landed": own,
            "same": (sums, "flush"),
            "arrived": (sums, "any"),
        },
        {
            "near_a": block,
            "far_a": block,
            "near_parts": block,
            "far_parts": block,
            "far_got": pltpu.VMEM((nb - 1, rows_each, width), BF16),
            "near_dproj": pltpu.VMEM((seq_len, kv * G_PAD), BF16),
            "far_dproj": pltpu.VMEM((seq_len, kv * G_PAD), BF16),
            "datt": pltpu.VMEM((seq_len, heads * PAD), BF16),
            "dk": pltpu.VMEM((kv, seq_len, PAD), F32),
            "dv": pltpu.VMEM((kv, seq_len, PAD), F32),
            "other": pltpu.VMEM(sums.shape, BF16),
        },
        8 * seq_len * width * (kv * G_PAD + heads * PAD) + heads * seq_len * seq_len * 20 * 256,
        collective_id,
    )


def all_peers(n_dp, n_t):
    d, t = lax.axis_index("dp"), lax.axis_index("tensor")
    return (
        [{"tensor": lax.rem(t + i, n_t)} for i in range(1, n_t)],
        [{"dp": lax.rem(d + i, n_dp)} for i in range(1, n_dp)],
    )


def share(k, buffer, me, peers):
    return [k.remote(buffer.at[me], buffer.at[me], peer) for peer in peers]


def sum_slots(buffer, copies):
    for copy in copies:
        copy.wait_recv()
    total = buffer[0, :, :]
    for i in range(1, len(copies) + 1):
        total = total + buffer[i, :, :]
    return total


def closing_sums_body(n_z, n_dp, n_t, nb, k):
    d, t = lax.axis_index("dp"), lax.axis_index("tensor")
    tensor_peers, dp_peers = all_peers(n_dp, n_t)
    at_z = [{"dp": lax.rem(d + 2 * i, n_dp)} for i in range(1, n_z)]
    same, other, narrow, arrived = k["same"], k["other"], k["narrow"], k["arrived"]
    k.load("same", "other")
    k["first"][t, :, :] = k["gains"][...]
    k.meet(tensor_peers + dp_peers)
    gain_copies = share(k, k["first"], t, tensor_peers)
    k.remote(k["far_out"], k["landed"], permuted("tensor", nb))
    k.ready("same", "other")
    n_which = same.shape[0]
    copies = {}
    for which in range(n_which):
        for i in range(1, n_z):
            held = same[which, i, :, :].astype(F32) + other[which, i, :, :].astype(F32)
            narrow[which, i, :, :] = held.astype(BF16)
            copies[which, i] = k.remote(
                narrow.at[which, i], arrived.at[which, i], at_z[i - 1]
            )
        if which == 0:
            k["second"][d, :, :] = sum_slots(k["first"], gain_copies)
            gain_copies = share(k, k["second"], d, dp_peers)
    for which in range(n_which):
        total = same[which, 0, :, :].astype(F32) + other[which, 0, :, :].astype(F32)
        for i in range(1, n_z):
            copies[which, i].wait_recv()
            total = total + arrived[which, i, :, :].astype(F32)
        k["sums"][which, :, :] = total
    k["gain_sums"][...] = sum_slots(k["second"], gain_copies)


def closing_sums(same, other, far_out, gains, n_z, n_dp, n_t, collective_id):
    n_which, _, blk, cols = same.shape
    sds = jax.ShapeDtypeStruct
    block = pltpu.VMEM(same.shape, BF16)
    return frame_call(
        functools.partial(closing_sums_body, n_z, n_dp, n_t, n_t // 2),
        "sum_attention_gradients",
        {
            "same": (same, "load"),
            "other": (other, "load"),
            "far_out": (far_out, "any"),
            "gains": (gains, "vmem"),
        },
        {
            "sums": (sds((n_which, blk, cols), F32), "vmem"),
            "landed": (sds(far_out.shape, BF16), "any"),
            "gain_sums": (sds(gains.shape, F32), "vmem"),
        },
        {
            "narrow": block,
            "arrived": block,
            "first": pltpu.VMEM((n_t,) + gains.shape, F32),
            "second": pltpu.VMEM((n_dp,) + gains.shape, F32),
        },
        0,
        collective_id,
        n_sems=n_which * n_z + n_dp + n_t + 4,
    )


def moments_kernel(names, kv, *refs):
    keys = [key + suffix for suffix in ("", "_first", "_second") for key in names] + ["gradient"]
    keys += ["gain_sum"] if "gains" in names else []
    keys += ["next_" + key + suffix for suffix in ("_first", "_second") for key in names]
    keys += ["update_" + key for key in names] + ["squares"]
    k = dict(zip(keys, refs))
    correct_one = 1.0 / (1.0 - BETA_ONE**STEP)
    correct_two = 1.0 / (1.0 - BETA_TWO**STEP)
    row = lax.broadcasted_iota(jnp.int32, (8, PAD), 0)
    lane = lax.broadcasted_iota(jnp.int32, (8, PAD), 1)
    squares = jnp.zeros((8, PAD), F32)
    gradient = k["gradient"]

    def step(name, index, gradient_of, rows, cols, number):
        tile = rows if rows % 32 else 32

        def one(i, carry):
            at = index + (pl.ds(pl.multiple_of(i * tile, tile) if rows > tile else 0, tile), slice(None))
            g = gradient_of(at)
            w = k[name][at]
            moment = BETA_ONE * k[name + "_first"][at] + (1.0 - BETA_ONE) * g
            square = BETA_TWO * k[name + "_second"][at] + (1.0 - BETA_TWO) * g * g
            k["next_" + name + "_first"][at] = moment
            k["next_" + name + "_second"][at] = square
            update = (moment * correct_one) / (
                jnp.sqrt(square * correct_two) + ADAM_EPSILON
            ) + WEIGHT_DECAY * w
            k["update_" + name][at] = update
            return (
                carry[0] + jnp.sum(w * w, axis=0, keepdims=True),
                carry[1] + jnp.sum(update * update, axis=0, keepdims=True),
            )

        zero = jnp.zeros((1, cols), F32)
        w_sum, u_sum = lax.fori_loop(0, rows // tile, one, (zero, zero))
        w_sum = jnp.sum(w_sum, axis=1, keepdims=True)
        u_sum = jnp.sum(u_sum, axis=1, keepdims=True)
        mark = lane == number
        return jnp.where(mark & (row == 0), w_sum, 0.0) + jnp.where(mark & (row == 1), u_sum, 0.0)

    def qkv_gradient(at):
        return jnp.concatenate([gradient[(1 + j,) + at] for j in range(kv)], axis=1)

    if "qkv" in names:
        squares += step("qkv", (), qkv_gradient, *k["qkv"].shape, 0)
    if "out" in names:
        rows, cols = k["out"].shape
        squares += step("out", (), lambda at: gradient[0, at[0], :cols], rows, cols, 1)
    if "gate_up" in names:
        for which in range(2):
            squares += step(
                "gate_up", (which,), lambda at: gradient[at].astype(F32), *k["gate_up"].shape[1:], 2 + which
            )
    if "down" in names:
        squares += step(
            "down", (), lambda at: gradient[(2,) + at].astype(F32), *k["down"].shape, 4
        )
    if "gains" in names:
        for which in range(2):
            squares += step(
                "gains", (which,), lambda at: k["gain_sum"][at], *k["gains"].shape[1:], 5 + which
            )
    k["squares"][...] = squares


def moments(weights, firsts, seconds, gradient, gain_sum, kv):
    names = list(weights)
    arrays = [table[key] for table in (weights, firsts, seconds) for key in names] + [gradient]
    arrays += [] if gain_sum is None else [gain_sum]
    sds = jax.ShapeDtypeStruct
    shapes = [sds(weights[key].shape, F32) for key in names]
    results = pl.pallas_call(
        functools.partial(moments_kernel, names, kv),
        out_shape=shapes * 3 + [sds((8, PAD), F32)],
        in_specs=[VM] * len(arrays),
        out_specs=[VM] * (3 * len(names) + 1),
        compiler_params=pltpu.CompilerParams(vmem_limit_bytes=VMEM_LIMIT),
        cost_estimate=cost(0, 14 << 20),
        name="moments",
    )(*arrays)
    n = len(names)
    return (
        dict(zip(names, results[:n])),
        dict(zip(names, results[n : 2 * n])),
        dict(zip(names, results[2 * n : 3 * n])),
        results[-1],
    )


def sum_squares_body(n_dp, n_t, k):
    d, t = lax.axis_index("dp"), lax.axis_index("tensor")
    tensor_peers, dp_peers = all_peers(n_dp, n_t)
    k["first"][t, :, :] = k["squares_one"][...] + k["squares_two"][...]
    k.meet(tensor_peers + dp_peers)
    copies = share(k, k["first"], t, tensor_peers)
    k["second"][d, :, :] = sum_slots(k["first"], copies)
    copies = share(k, k["second"], d, dp_peers)
    k["norms"][...] = jnp.sqrt(sum_slots(k["second"], copies))


def sum_squares(one, two, n_dp, n_t, collective_id):
    return frame_call(
        functools.partial(sum_squares_body, n_dp, n_t),
        "sum_squares",
        {"squares_one": (one, "vmem"), "squares_two": (two, "vmem")},
        {"norms": (jax.ShapeDtypeStruct(one.shape, F32), "vmem")},
        {
            "first": pltpu.VMEM((n_t,) + one.shape, F32),
            "second": pltpu.VMEM((n_dp,) + one.shape, F32),
        },
        0,
        collective_id,
        n_sems=n_dp + n_t,
    )["norms"]


def rms_norm(values, gain_row):
    return (
        values
        * lax.rsqrt(jnp.mean(values * values, axis=-1, keepdims=True) + NORM_EPSILON)
        * gain_row
    )


def rotary_tables():
    half = HEAD // 2
    frequency = ROPE_THETA ** (-(jnp.arange(half, dtype=F32) * (2.0 / HEAD)))
    angles = jnp.arange(SEQ_LEN, dtype=F32)[:, None] * frequency[None, :]
    cosine, sine = jnp.cos(angles), jnp.sin(angles)
    empty = jnp.zeros((SEQ_LEN, PAD - HEAD), F32)
    return (
        jnp.concatenate([cosine, cosine, empty], axis=1),
        jnp.concatenate([-sine, sine, empty], axis=1),
    )


def shards(
    tokens,
    cotangent,
    lengths,
    qkv_weight,
    out_weight,
    gate_up_weight,
    down_weight,
    norm_gains,
    qkv_first,
    out_first,
    gate_up_first,
    down_first,
    gains_first,
    qkv_second,
    out_second,
    gate_up_second,
    down_second,
    gains_second,
):
    rows_each, width = tokens.shape
    n_t = lax.axis_size("tensor")
    n_dp = lax.axis_size("dp")
    n_z = n_dp // 2
    nb = n_t // 2
    t = lax.axis_index("tensor")
    d = lax.axis_index("dp")
    mine = t // nb
    lengths = jnp.stack([lengths[mine], lengths[1 - mine]])
    spread = spread_matrix().astype(BF16)
    blk = qkv_weight.shape[0]
    kv = qkv_weight.shape[1] // G_COLS

    gain_cols = norm_gains.shape[1]
    gain_start = (d * n_t + t) * gain_cols
    gain_rows = lax.dynamic_update_slice(
        jnp.zeros((2, width), F32),
        norm_gains.astype(BF16).astype(F32),
        (0, gain_start),
    )
    out_half = out_weight.astype(BF16).T
    xs, c_far, wq, wo, gain_work = prologue(
        tokens, cotangent, qkv_weight.astype(BF16), out_half, gain_rows, n_z, n_t, n_dp
    )
    attention_gain, feedforward_gain = gain_work[0:1], gain_work[1:2]
    w_out_cols = out_half.shape[1]
    if w_out_cols % G_COLS:
        wo = jnp.pad(wo, ((0, 0), (0, -w_out_cols % G_COLS)))
    w_qkv, w_out = pad_weights(wq, wo, spread)
    w_out = w_out[:, : kv * GROUP * PAD]
    ffn_half = jnp.concatenate(
        [gate_up_weight.astype(BF16), down_weight.astype(BF16).T[None]], axis=0
    )
    w_ffn = lax.all_gather(ffn_half, "dp", axis=1, tiled=True)

    inputs = tokens.astype(F32)
    tables = rotary_tables()
    fwd = attention_forward(xs, lengths, gain_work, w_qkv, w_out, *tables, 1)
    residual = fwd["residual"]

    ff = feed_forward(fwd["normed_two"], cotangent, c_far, w_ffn, nb, 2)
    ffn_sum = lax.psum_scatter(ff["grads"], "dp", scatter_dimension=1, tiled=True)

    def total(*names):
        result = 0.0
        for name in names:
            array = ff[name].astype(F32)
            result = result + (array if array.ndim == 2 else jnp.sum(array, axis=0))
        return result

    normed_two_grad = total("near_own_grad", "near_got_grad", "landed")
    _, norm_pull = jax.vjp(rms_norm, residual, feedforward_gain)
    residual_part, ffn_gain_grad = norm_pull(normed_two_grad)
    residual_grad = cotangent.astype(F32) + residual_part
    bwd = attention_backward(
        residual_grad.astype(BF16), lengths, fwd, w_qkv, w_out, tables, spread, nb, n_z, blk, 3
    )
    near_grads = jnp.sum(bwd["near_got"].astype(F32), axis=0) + bwd["near_own"].astype(F32)
    normed_grad = near_grads + bwd["landed"].astype(F32)
    _, first_pull = jax.vjp(rms_norm, inputs, attention_gain)
    input_part, attention_gain_grad = first_pull(normed_grad)
    grad_tokens = residual_grad + input_part
    gain_grads = jnp.concatenate([attention_gain_grad, ffn_gain_grad], axis=0)
    far_out = total("far_own_out", "far_got_out").astype(BF16)
    closing = closing_sums(
        bwd["same"], bwd["arrived"], far_out, gain_grads.reshape(-1, PAD), n_z, n_dp, n_t, 4
    )
    layer_out = (
        residual + (total("near_own_out", "near_got_out") + closing["landed"].astype(F32))
    ).astype(BF16)
    gain_sum = lax.dynamic_slice(
        closing["gain_sums"].reshape(2, width), (0, gain_start), (2, gain_cols)
    )

    def lift(gains):
        return gains[:, None, :]

    gate_down = moments(
        {"gate_up": gate_up_weight, "down": down_weight.T},
        {"gate_up": gate_up_first, "down": down_first.T},
        {"gate_up": gate_up_second, "down": down_second.T},
        ffn_sum,
        None,
        kv,
    )
    attention = moments(
        {"qkv": qkv_weight, "out": out_weight.T, "gains": lift(norm_gains)},
        {"qkv": qkv_first, "out": out_first.T, "gains": lift(gains_first)},
        {"qkv": qkv_second, "out": out_second.T, "gains": lift(gains_second)},
        closing["sums"],
        lift(gain_sum),
        kv,
    )
    norms = sum_squares(gate_down[3], attention[3], n_dp, n_t, 5)
    scale = LEARN_RATE * (norms[0, :7] / norms[1, :7])
    first, second, update = ({**gate_down[i], **attention[i]} for i in range(3))
    for table in (first, second, update):
        table["gains"] = table["gains"][:, 0, :]
        table["out"] = table["out"].T
        table["down"] = table["down"].T
    new = (
        qkv_weight - scale[0] * update["qkv"],
        out_weight - scale[1] * update["out"],
        gate_up_weight - scale[2:4, None, None] * update["gate_up"],
        down_weight - scale[4] * update["down"],
        norm_gains - scale[5:7, None] * update["gains"],
    )
    names = ("qkv", "out", "gate_up", "down", "gains")
    return (
        layer_out,
        grad_tokens,
        *new,
        *[first[key] for key in names],
        *[second[key] for key in names],
        norms[0, :7],
        norms[1, :5],
        norms[1, 5:7],
    )


def solution(mesh):
    rows = P(("dp", "tensor"), None)
    gains = P(None, ("dp", "tensor"))
    weights = (P("dp", "tensor"), P("tensor", "dp"), P(None, "dp", "tensor"), P("tensor", "dp"), gains)
    in_specs = (rows, rows, P("dp")) + weights * 3
    out_specs = (rows, rows) + weights * 3 + (P(), P(), P())
    return jax.shard_map(shards, mesh=mesh, in_specs=in_specs, out_specs=out_specs, check_vma=False)
```

```python
import functools

import jax
import jax.numpy as jnp
import numpy as np
from jax import lax
from jax.experimental import pallas as pl
from jax.experimental.pallas import tpu as pltpu
from jax.sharding import PartitionSpec as P

HEAD = 96
PAD = 128
SEQ_LEN = 1024
SEQS_DEV = 2
STEP = 10
GROUP = 2

NORM_EPSILON = 1e-05
ROPE_THETA = 100000.0
BETA_ONE = 0.9
BETA_TWO = 0.999
ADAM_EPSILON = 1e-06
WEIGHT_DECAY = 0.01
LEARN_RATE = 0.3
NEGATIVE = -1e30
LOG2E = 1.4426950408889634
SCALE = HEAD ** (-0.5)
Q_ROWS = 256
G_COLS = 4 * HEAD
G_PAD = 4 * PAD
VMEM_LIMIT = 56 << 20

F32 = jnp.float32
BF16 = jnp.bfloat16
VM = pl.BlockSpec(memory_space=pltpu.VMEM)
SM = pl.BlockSpec(memory_space=pltpu.SMEM)
ANY = pl.BlockSpec(memory_space=pl.ANY)
MESH = pl.DeviceIdType.MESH
IN_VMEM, IN_SMEM, IN_HBM, LOAD, FLUSH = range(5)
NEAR, FAR = "near_", "far_"
WINDOW, SLOTS = 4, 4
HBM = "any_"


def dot_nn(a, b):
    return lax.dot_general(a, b, (((1,), (0,)), ((), ())), preferred_element_type=F32)


def dot_nt(a, b):
    return lax.dot_general(a, b, (((1,), (1,)), ((), ())), preferred_element_type=F32)


def dot_tn(a, b):
    return lax.dot_general(a, b, (((0,), (0,)), ((), ())), preferred_element_type=F32)


def cost(flops, moved):
    return pl.CostEstimate(flops=int(flops), bytes_accessed=int(moved), transcendentals=0)


def spread_matrix():
    source = lax.broadcasted_iota(jnp.int32, (G_COLS, G_PAD), 0)
    target = lax.broadcasted_iota(jnp.int32, (G_COLS, G_PAD), 1)
    return ((target // PAD) * HEAD + target % PAD == source) & (target % PAD < HEAD)


def swap_halves(values):
    lane = lax.broadcasted_iota(jnp.int32, values.shape, 1)
    return jnp.where(
        lane < HEAD // 2,
        pltpu.roll(values, PAD - HEAD // 2, 1),
        pltpu.roll(values, HEAD // 2, 1),
    )


def permuted(axis, bit):
    return {axis: lax.axis_index(axis) ^ bit}


class Remote:
    def __init__(self, copy):
        self.copy = copy
        self.landed = self.left = False

    def wait_recv(self):
        if not self.landed:
            self.copy.wait_recv()
        self.landed = True

    def wait_send(self):
        if not self.left:
            self.copy.wait_send()
        self.left = True


class Side:
    def __init__(self, refs, side):
        self.refs, self.side = refs, side

    def __getattr__(self, name):
        return self.refs[self.side + name]

    def of(self, side):
        return Side(self.refs, self.side + side)


class Frame:
    def __init__(self, names, refs):
        self.refs = dict(zip(names, refs))
        self.loading, self.remotes, self.storing = [], [], []
        self.next_local = 0
        self.hbm = Side(self.refs, HBM)

    def __getattr__(self, name):
        return self.refs[name]

    def of(self, side):
        return Side(self.refs, side)

    def meet(self, peers):
        barrier = pltpu.get_barrier_semaphore()
        for peer in peers:
            pl.semaphore_signal(barrier, inc=1, device_id=peer, device_id_type=MESH)
        pl.semaphore_wait(barrier, len(peers))

    def local(self, source, target):
        copy = pltpu.make_async_copy(source, target, self.local_sem.at[self.next_local])
        self.next_local += 1
        copy.start()
        return copy

    def load_refs(self, source, target):
        self.loading.append(self.local(source, target))

    def ready(self):
        for copy in self.loading:
            copy.wait()
        self.loading = []

    def store(self, source, target):
        pending = [self.local(source, target)]

        def wait():
            if pending:
                pending.pop().wait()

        self.storing.append(wait)
        return wait

    def flush(self, source, target):
        self.store(source, target)

    def remote(self, source, target, peer):
        n = len(self.remotes)
        copy = pltpu.make_async_remote_copy(
            src_ref=source,
            dst_ref=target,
            send_sem=self.send_sem.at[n],
            recv_sem=self.recv_sem.at[n],
            device_id=peer,
            device_id_type=MESH,
        )
        copy.start()
        self.remotes.append(Remote(copy))
        return self.remotes[-1]

    def finish(self):
        for remote in self.remotes:
            remote.wait_send()
            remote.wait_recv()
        for wait in self.storing:
            wait()


def frame_call(body, name, inputs, outputs, scratch, flops, collective_id, n_sems=40):
    names, specs, arrays = [], [], []
    spec_of = {IN_VMEM: VM, IN_SMEM: SM, IN_HBM: ANY, LOAD: ANY, FLUSH: ANY}
    for key, (array, kind) in inputs.items():
        names.append(HBM + key if kind == LOAD else key)
        specs.append(spec_of[kind])
        arrays.append(array)
    out_specs, out_shapes = [], []
    for key, (shape, kind) in outputs.items():
        names.append(HBM + key if kind == FLUSH else key)
        out_specs.append(spec_of[kind])
        out_shapes.append(shape)
    shapes = []
    for table, kind_of in ((inputs, LOAD), (outputs, FLUSH)):
        for key, (array, kind) in table.items():
            if kind == kind_of:
                names.append(key)
                shapes.append(pltpu.VMEM(array.shape, array.dtype))
    for key, shape in scratch.items():
        names.append(key)
        shapes.append(shape)
    for key in ("local_sem", "send_sem", "recv_sem"):
        names.append(key)
        shapes.append(pltpu.SemaphoreType.DMA((n_sems,)))

    def kernel(*refs):
        frame = Frame(names, refs)
        body(frame)
        frame.finish()

    moved = sum(a.size * a.dtype.itemsize for a in arrays)
    results = pl.pallas_call(
        kernel,
        out_shape=out_shapes,
        in_specs=specs,
        out_specs=out_specs,
        scratch_shapes=shapes,
        compiler_params=pltpu.CompilerParams(
            vmem_limit_bytes=VMEM_LIMIT, collective_id=collective_id, has_side_effects=True
        ),
        cost_estimate=cost(flops, moved),
        name=name,
    )(*arrays)
    return dict(zip(outputs, results))


def half_peers(nb):
    return [(r, permuted("tensor", r)) for r in range(1, nb)]


def rows_of(c):
    return pl.ds(c * Q_ROWS, Q_ROWS)


def bits_down(size):
    bits = []
    bit = size // 2
    while bit:
        bits.append(bit)
        bit //= 2
    return bits


def attention_rows(k, tag, i, length, kv):
    qkvp, att, lse = k.of(tag).qkvp, k.of(tag).att, k.of(tag).lse
    n = (i + 1) * Q_ROWS
    rows = slice(i * Q_ROWS, n)
    lane = lax.broadcasted_iota(jnp.int32, (Q_ROWS, PAD), 1)

    def one_head(h, log_totals):
        group = h // GROUP
        q_col = pl.ds(pl.multiple_of((4 * group + h % GROUP) * PAD, PAD), PAD)
        k_col = pl.ds(pl.multiple_of((4 * group + 2) * PAD, PAD), PAD)
        v_col = pl.ds(pl.multiple_of((4 * group + 3) * PAD, PAD), PAD)
        a_col = pl.ds(pl.multiple_of(h * PAD, PAD), PAD)
        s = dot_nt(qkvp[rows, q_col], qkvp[0:n, k_col])
        row_ids = lax.broadcasted_iota(jnp.int32, (Q_ROWS, 1), 0) + i * Q_ROWS + 1
        limit = jnp.minimum(row_ids, length)
        col_ids = lax.broadcasted_iota(jnp.int32, (Q_ROWS, n), 1)
        s = jnp.where(col_ids < limit, s, NEGATIVE)
        top = jnp.max(s, axis=-1, keepdims=True)
        e = jnp.exp2((s - top) * (SCALE * LOG2E))
        total = jnp.sum(e, axis=-1, keepdims=True)
        p = (e * (1.0 / total)).astype(BF16)
        att[rows, a_col] = dot_nn(p, qkvp[0:n, v_col]).astype(BF16)
        log_total = top * (SCALE * LOG2E) + jnp.log2(total)
        return jnp.where(lane == h, log_total, log_totals)

    lse[rows, :] = lax.fori_loop(0, kv * GROUP, one_head, jnp.zeros((Q_ROWS, PAD), F32))


def z_order(n_z):
    return sorted(range(1, n_z), key=lambda i: min(i, n_z - i))


def z_peers(n_z):
    d = lax.axis_index("dp")
    return {i: {"dp": lax.rem(d + 2 * i, 2 * n_z)} for i in range(1, n_z)}


class Gather:
    def __init__(self, k, streams, n_z, blk):
        d = lax.axis_index("dp")
        self.k, self.streams = k, streams
        self.peers, self.other_x = z_peers(n_z), permuted("dp", 1)
        self.order = [(s, i) for s in range(len(streams)) for i in z_order(n_z)]
        self.rows = {
            i: pl.ds(pl.multiple_of(lax.rem(d + 2 * (n_z - i), 2 * n_z) * blk, 16), blk)
            for i in range(n_z)
        }
        self.sent, self.along_x = {}, {}
        self.next_send = self.next_arrival = 0

    def send(self):
        if self.next_send < len(self.order):
            s, i = self.order[self.next_send]
            source, target, at = self.streams[s]
            self.sent[s, i] = self.k.remote(source, target.at[at + (self.rows[0],)], self.peers[i])
            self.next_send += 1

    def own_along_x(self, s):
        source, target, at = self.streams[s]
        self.along_x[s, 0] = self.k.remote(source, target.at[at + (self.rows[0],)], self.other_x)

    def pump(self):
        if self.next_arrival < len(self.order):
            s, i = self.order[self.next_arrival]
            self.next_arrival += 1
            self.sent[s, i].wait_recv()
            self.send()
            if (s, 0) not in self.along_x:
                self.own_along_x(s)
            _, target, at = self.streams[s]
            block = target.at[at + (self.rows[i],)]
            self.along_x[s, i] = self.k.remote(block, block, self.other_x)

    def complete(self, s):
        for (stream, _), copy in self.along_x.items():
            if stream == s:
                copy.wait_recv()


def opening_body(nb, rows_each, kv, n_z, blk, k):
    t = lax.axis_index("tensor")
    local = lax.rem(t, nb)
    seq_len = nb * rows_each
    per_block = rows_each // Q_ROWS
    chunk = 32
    over, other_x = permuted("tensor", nb), permuted("dp", 1)
    peers, along_z = half_peers(nb), z_peers(n_z)
    near_x, far_x = k.near_x, k.far_x
    streams = [(k.qkv_half, k.wq, ()), (k.out_half, k.wo, ())]
    streams += [(k.ffn_half.at[i], k.w_ffn, (i,)) for i in (2, 0, 1)]
    gather = Gather(k, streams, n_z, blk)
    own_tokens = k.local(k.tokens, near_x.at[0])
    own_blocks = [
        k.local(source, target.at[at + (gather.rows[0],)]) for source, target, at in streams
    ]
    k.load_refs(k.hbm.cos_t, k.cos_t)
    k.load_refs(k.hbm.sin_t, k.sin_t)
    k.load_refs(k.hbm.spread, k.spread)
    k.held[0, :, :] = k.gains[...]
    k.meet(list(along_z.values()) + [other_x, over] + [peer for _, peer in peers])

    stages = [permuted("tensor", bit) for bit in bits_down(2 * nb)] + [other_x]
    gain_copy = k.remote(k.held.at[0], k.got.at[0], stages[0])
    far_copy = k.remote(k.tokens, far_x.at[0], over)
    near_copies = [k.remote(k.tokens, near_x.at[r], peer) for r, peer in peers]
    for _ in range(WINDOW):
        gather.send()
    for stage in range(len(stages)):
        gain_copy.wait_recv()
        k.held[stage + 1, :, :] = k.held[stage, :, :] + k.got[stage, :, :]
        if stage + 1 < len(stages):
            gain_copy = k.remote(k.held.at[stage + 1], k.got.at[stage + 1], stages[stage + 1])
    last = len(stages)
    gain_copies = [
        k.remote(k.held.at[last], k.got.at[last + i - 1], along_z[i]) for i in range(1, n_z)
    ]
    gather.own_along_x(0)
    gather.own_along_x(1)
    for _ in range(2 * (n_z - 1)):
        gather.pump()
    for s in range(2, len(streams)):
        gather.own_along_x(s)
    total = k.held[last, :, :]
    for i, copy in enumerate(gain_copies):
        copy.wait_recv()
        total = total + k.got[last + i, :, :]
    k.gain_sum[...] = total
    gain_one, gain_two = k.gain_sum.at[0:1], k.gain_sum.at[1:2]
    far_copy.wait_recv()
    far_copies = [k.remote(far_x.at[0], far_x.at[r], peer) for r, peer in peers]
    own_tokens.wait()
    for copy in near_copies + far_copies:
        copy.wait_recv()

    def normalise(tag):
        for r in range(nb):
            base = (local ^ r) * rows_each

            def norm_rows(i, carry):
                rows = pl.ds(pl.multiple_of(i * chunk, chunk), chunk)
                v = k.of(tag).x[r, rows, :].astype(F32)
                inv = lax.rsqrt(jnp.mean(v * v, axis=-1, keepdims=True) + NORM_EPSILON)
                k.of(tag).normed[pl.ds(pl.multiple_of(base + i * chunk, chunk), chunk), :] = (
                    v * inv * gain_one[...]
                ).astype(BF16)
                return carry

            lax.fori_loop(0, rows_each // chunk, norm_rows, 0)
        k.flush(k.of(tag).normed, k.hbm.of(tag).normed)

    normalise(FAR)
    normalise(NEAR)
    for copy in own_blocks:
        copy.wait()
    k.ready()
    for s, (source, target) in enumerate(((k.wq, k.w_qkv), (k.wo, k.w_out))):
        gather.complete(s)
        for g in range(-(-target.shape[1] // G_PAD)):
            wide = min(G_PAD, target.shape[1] - g * G_PAD)
            part = source[:, g * G_COLS : (g + 1) * G_COLS]
            target[:, g * G_PAD : g * G_PAD + wide] = dot_nn(
                part, k.spread[0 : part.shape[1], 0:wide]
            ).astype(BF16)
        k.flush(target, k.hbm.w_out if s else k.hbm.w_qkv)

    landing, waiting = [], []
    for tag, length in ((FAR, k.lengths[1]), (NEAR, k.lengths[0])):
        normed, qkvp = k.of(tag).normed, k.of(tag).qkvp
        parts, got = k.of(tag).parts, k.of(tag).got
        for i in range(seq_len // Q_ROWS):
            rows = slice(i * Q_ROWS, (i + 1) * Q_ROWS)
            for j in range(kv):
                proj = dot_nn(normed[rows, :], k.w_qkv[:, j * G_PAD : (j + 1) * G_PAD])
                for h in range(4):
                    part = proj[:, h * PAD : (h + 1) * PAD]
                    if h < 3:
                        part = part * k.cos_t[rows, :] + swap_halves(part) * k.sin_t[rows, :]
                    qkvp[rows, (4 * j + h) * PAD : (4 * j + h + 1) * PAD] = part.astype(BF16)
        k.flush(qkvp, k.hbm.of(tag).qkvp)
        gather.pump()
        for c in range(per_block):
            rows = slice(c * Q_ROWS, (c + 1) * Q_ROWS)
            for b in range(nb):
                i = b * per_block + c
                attention_rows(k, tag, i, length, kv)
                part = dot_nt(k.of(tag).att[i * Q_ROWS : (i + 1) * Q_ROWS, :], k.w_out[...])
                parts[local ^ b, rows, :] = part.astype(BF16)
                if waiting:
                    waiting.pop()()
                gather.pump()
            copies = [
                k.remote(parts.at[r, rows_of(c)], got.at[r - 1, rows_of(c)], peer)
                for r, peer in peers
            ]

            def complete(rows=rows, c=c, copies=copies, parts=parts, got=got, tag=tag):
                total = parts[0, rows, :].astype(F32)
                for r, copy in enumerate(copies):
                    copy.wait_recv()
                    total = total + got[r, rows, :].astype(F32)
                if tag == FAR:
                    parts[0, rows, :] = total.astype(BF16)
                    landing.append(
                        k.remote(parts.at[0, rows_of(c)], k.landed.at[rows_of(c)], over)
                    )
                    if c == per_block - 1:
                        k.remote(k.cotangent, k.c_far, over)
                else:
                    k.residual[rows, :] = near_x[0, rows, :].astype(F32) + total

            waiting.append(complete)
        k.flush(k.of(tag).att, k.hbm.of(tag).att)
        k.flush(k.of(tag).lse, k.hbm.of(tag).lse)
    waiting.pop()()
    for c in range(per_block):
        landing[c].wait_recv()

        def residual_rows(i, carry):
            rows = pl.ds(pl.multiple_of(c * Q_ROWS + i * chunk, chunk), chunk)
            v = k.residual[rows, :] + k.landed[rows, :].astype(F32)
            k.residual[rows, :] = v
            inv = lax.rsqrt(jnp.mean(v * v, axis=-1, keepdims=True) + NORM_EPSILON)
            k.normed_two[rows, :] = (v * inv * gain_two[...]).astype(BF16)
            return carry

        lax.fori_loop(0, Q_ROWS // chunk, residual_rows, 0)
    k.flush(k.residual, k.hbm.residual)
    k.flush(k.normed_two, k.hbm.normed_two)
    for _ in range(3 * (n_z - 1)):
        gather.pump()


def opening(tokens, cotangent, lengths, gains, halves, tables, spread, n_t, n_z, collective_id):
    rows_each, width = tokens.shape
    qkv_half, out_half, ffn_half = halves
    blk = qkv_half.shape[0]
    n_dp = 2 * n_z
    nb = n_t // 2
    seq_len = nb * rows_each
    kv = qkv_half.shape[1] // G_COLS
    heads = kv * GROUP
    sds = jax.ShapeDtypeStruct
    normed = (sds((seq_len, width), BF16), FLUSH)
    qkvp = (sds((seq_len, kv * G_PAD), BF16), FLUSH)
    att = (sds((seq_len, heads * PAD), BF16), FLUSH)
    lse = (sds((seq_len, PAD), F32), FLUSH)
    block = pltpu.VMEM((nb, rows_each, width), BF16)
    others = pltpu.VMEM((nb - 1, rows_each, width), BF16)
    n_gain = len(bits_down(n_t)) + 1 + n_z - 1
    return frame_call(
        functools.partial(opening_body, nb, rows_each, kv, n_z, blk),
        "attention_forward",
        dict(
            tokens=(tokens, IN_HBM),
            cotangent=(cotangent, IN_HBM),
            lengths=(lengths, IN_SMEM),
            gains=(gains, IN_VMEM),
            qkv_half=(qkv_half, IN_HBM),
            out_half=(out_half, IN_HBM),
            ffn_half=(ffn_half, IN_HBM),
            cos_t=(tables[0], LOAD),
            sin_t=(tables[1], LOAD),
            spread=(spread, LOAD),
        ),
        dict(
            near_normed=normed,
            far_normed=normed,
            near_qkvp=qkvp,
            far_qkvp=qkvp,
            near_att=att,
            far_att=att,
            near_lse=lse,
            far_lse=lse,
            residual=(sds((rows_each, width), F32), FLUSH),
            normed_two=(sds((rows_each, width), BF16), FLUSH),
            w_qkv=(sds((blk * n_dp, kv * G_PAD), BF16), FLUSH),
            w_out=(sds((blk * n_dp, heads * PAD), BF16), FLUSH),
            w_ffn=(sds((3, blk * n_dp, ffn_half.shape[2]), BF16), IN_HBM),
            c_far=(sds(cotangent.shape, BF16), IN_HBM),
            gain_sum=(sds(gains.shape, F32), IN_VMEM),
        ),
        dict(
            near_x=block,
            far_x=block,
            far_parts=block,
            near_parts=block,
            far_got=others,
            near_got=others,
            landed=pltpu.VMEM((rows_each, width), BF16),
            wq=pltpu.VMEM((blk * n_dp, qkv_half.shape[1]), BF16),
            wo=pltpu.VMEM((blk * n_dp, out_half.shape[1]), BF16),
            held=pltpu.VMEM((n_gain + 1,) + gains.shape, F32),
            got=pltpu.VMEM((n_gain,) + gains.shape, F32),
        ),
        4 * seq_len * width * (kv * G_PAD + heads * PAD) + heads * seq_len * seq_len * 8 * 256,
        collective_id,
        n_sems=12 * n_z + 48,
    )


def feed_forward_body(nb, rows_each, k):
    over = permuted("tensor", nb)
    peers = half_peers(nb)
    per_block = rows_each // Q_ROWS
    w = k.w
    width = w.shape[1]
    near_n, near_c, far_n, far_c = k.near_n, k.near_c, k.far_n, k.far_c
    own_n = k.local(k.own_n, near_n.at[0])
    own_c = k.local(k.own_c, near_c.at[0])
    k.load_refs(k.hbm.w, k.w)
    own_far_c = k.local(k.own_far_c, far_c.at[0])
    k.meet([over] + [peer for _, peer in peers])
    far_first = [
        k.remote(k.own_n.at[rows_of(c)], far_n.at[0, rows_of(c)], over) for c in range(per_block)
    ]
    n_copies = [k.remote(k.own_n, near_n.at[r], peer) for r, peer in peers]
    c_copies = [k.remote(k.own_c, near_c.at[r], peer) for r, peer in peers]
    far_c_copies = [k.remote(k.own_far_c, far_c.at[r], peer) for r, peer in peers]
    own_n.wait()
    own_c.wait()
    k.ready()

    def rows_step(side, r, c):
        rows = slice(c * Q_ROWS, (c + 1) * Q_ROWS)
        start = (0 if side == NEAR else nb * rows_each) + r * rows_each + c * Q_ROWS
        kept = slice(start, start + Q_ROWS)
        n = k.of(side).n[r, rows, :]
        gate = dot_nn(n, w[0])
        up = dot_nn(n, w[1])
        sig = 1.0 / (1.0 + jnp.exp(-gate))
        silu = gate * sig
        hid = (silu * up).astype(BF16)
        k.hidden[kept, :] = hid
        dh = dot_nn(k.of(side).c[r, rows, :], w[2])
        dg = (dh * up * sig * (1.0 + gate * (1.0 - sig))).astype(BF16)
        du = (dh * silu).astype(BF16)
        k.d_gate[kept, :] = dg
        k.d_up[kept, :] = du
        k.of(side).grad[r, rows, :] = (dot_nt(dg, w[0]) + dot_nt(du, w[1])).astype(BF16)
        k.of(side).out[r, rows, :] = dot_nt(hid, w[2]).astype(BF16)

    for r in range(nb):
        if r:
            n_copies[r - 1].wait_recv()
            c_copies[r - 1].wait_recv()
        for c in range(per_block):
            rows_step(NEAR, r, c)
        for part, own, got in (
            (k.near_grad.at[r], k.near_own_grad, k.near_got_grad),
            (k.near_out.at[r], k.near_own_out, k.near_got_out),
        ):
            if r:
                k.remote(part, got.at[r - 1], peers[r - 1][1])
            else:
                k.store(part, own)
    own_far_c.wait()
    for copy in far_c_copies:
        copy.wait_recv()
    landing = []
    for c in range(per_block):
        rows = slice(c * Q_ROWS, (c + 1) * Q_ROWS)
        far_first[c].wait_recv()
        passed = [
            k.remote(far_n.at[0, rows_of(c)], far_n.at[r, rows_of(c)], peer) for r, peer in peers
        ]
        rows_step(FAR, 0, c)
        copies = []
        for r, peer in peers:
            passed[r - 1].wait_recv()
            rows_step(FAR, r, c)
            copies.append(
                k.remote(
                    k.far_grad.at[r, rows_of(c)], k.far_got_grad.at[r - 1, rows_of(c)], peer
                )
            )
        total = k.far_grad[0, rows, :].astype(F32)
        for r, copy in enumerate(copies):
            copy.wait_recv()
            total = total + k.far_got_grad[r, rows, :].astype(F32)
        k.far_grad[0, rows, :] = total.astype(BF16)
        landing.append(k.remote(k.far_grad.at[0, rows_of(c)], k.landed.at[rows_of(c)], over))
    k.store(k.far_out.at[0], k.far_own_out)
    for r, peer in peers:
        k.remote(k.far_out.at[r], k.far_got_out.at[r - 1], peer)
    half = nb * rows_each
    for which in (2, 0, 1):
        right = (k.d_gate, k.d_up, k.hidden)[which]
        lefts = {side: k.of(side).c if which == 2 else k.of(side).n for side in (NEAR, FAR)}

        def col_step(i, carry):
            cols = pl.ds(pl.multiple_of(i * G_COLS, G_COLS), G_COLS)
            total = None
            for s, side in enumerate((NEAR, FAR)):
                for r in range(nb):
                    start = s * half + r * rows_each
                    term = dot_tn(lefts[side][r, :, cols], right[start : start + rows_each, :])
                    total = term if total is None else total + term
            w[which, cols, :] = total.astype(BF16)
            return carry

        lax.fori_loop(0, width // G_COLS, col_step, 0)
        k.store(w.at[which], k.grads.at[which])


def feed_forward(normed_two, cotangent, c_far, w, nb, collective_id):
    rows_each, width = normed_two.shape
    units = w.shape[2]
    sds = jax.ShapeDtypeStruct
    block = pltpu.VMEM((nb, rows_each, width), BF16)
    kept = pltpu.VMEM((2 * nb * rows_each, units), BF16)
    own = (sds((rows_each, width), BF16), IN_HBM)
    got = (sds((nb - 1, rows_each, width), BF16), IN_HBM)
    return frame_call(
        functools.partial(feed_forward_body, nb, rows_each),
        "feed_forward",
        dict(
            own_n=(normed_two, IN_HBM),
            own_c=(cotangent, IN_HBM),
            own_far_c=(c_far, IN_HBM),
            w=(w, LOAD),
        ),
        dict(
            grads=(sds(w.shape, BF16), IN_HBM),
            near_own_grad=own,
            near_got_grad=got,
            landed=own,
            near_own_out=own,
            near_got_out=got,
            far_own_out=own,
            far_got_out=got,
        ),
        dict(
            near_n=block,
            far_n=block,
            near_c=block,
            far_c=block,
            hidden=kept,
            d_gate=kept,
            d_up=kept,
            near_grad=block,
            far_grad=block,
            near_out=block,
            far_out=block,
            far_got_grad=pltpu.VMEM((nb - 1, rows_each, width), BF16),
        ),
        36 * nb * rows_each * width * units,
        collective_id,
    )


def attention_backward_rows(k, tag, i, length, kv):
    qkvp, dproj, datt, lse = k.of(tag).qkvp, k.of(tag).dproj, k.datt, k.of(tag).lse
    n = (i + 1) * Q_ROWS
    rows = slice(i * Q_ROWS, n)
    lane = lax.broadcasted_iota(jnp.int32, (Q_ROWS, PAD), 1)

    def one_head(h, carry):
        group = h // GROUP
        q_col = pl.ds(pl.multiple_of((4 * group + h % GROUP) * PAD, PAD), PAD)
        k_col = pl.ds(pl.multiple_of((4 * group + 2) * PAD, PAD), PAD)
        v_col = pl.ds(pl.multiple_of((4 * group + 3) * PAD, PAD), PAD)
        a_col = pl.ds(pl.multiple_of(h * PAD, PAD), PAD)
        q = qkvp[rows, q_col]
        keys = qkvp[0:n, k_col]
        do = datt[rows, a_col]
        row_lse = jnp.sum(jnp.where(lane == h, lse[rows, :], 0.0), axis=-1, keepdims=True)
        s = dot_nt(q, keys)
        row_ids = lax.broadcasted_iota(jnp.int32, (Q_ROWS, 1), 0) + i * Q_ROWS + 1
        limit = jnp.minimum(row_ids, length)
        col_ids = lax.broadcasted_iota(jnp.int32, (Q_ROWS, n), 1)
        s = jnp.where(col_ids < limit, s, NEGATIVE)
        p = jnp.exp2(s * (SCALE * LOG2E) - row_lse)
        dp = dot_nt(do, qkvp[0:n, v_col])
        inner = jnp.sum(p * dp, axis=-1, keepdims=True)
        ds = (p * (dp - inner)).astype(BF16)
        k.dv[group, 0:n, :] += dot_tn(p.astype(BF16), do)
        k.dk[group, 0:n, :] += dot_tn(ds, q)
        dq = dot_nn(ds, keys) * SCALE
        dproj[rows, q_col] = unrotate(k, dq, rows).astype(BF16)
        return carry

    lax.fori_loop(0, kv * GROUP, one_head, 0)


def unrotate(k, grad, rows):
    return grad * k.cos_t[rows, :] - swap_halves(grad) * k.sin_t[rows, :]


class Scatter:
    def __init__(self, k, n_z, blk):
        d = lax.axis_index("dp")
        self.k, self.peers, self.other_x = k, z_peers(n_z), permuted("dp", 1)
        self.order = [(which, i) for which in (2, 0, 1) for i in z_order(n_z) + [0]]

        def rows(owner):
            return pl.ds(pl.multiple_of(owner * blk, 16), blk)

        owners = {i: lax.rem(d + 2 * i, 2 * n_z) for i in range(n_z)}
        self.rows = {i: rows(owner) for i, owner in owners.items()}
        self.rows_other = {i: rows(owner ^ 1) for i, owner in owners.items()}
        self.sent, self.slots = [], [None] * SLOTS
        self.next_arrival = 0

    def send(self):
        if len(self.sent) < len(self.order):
            which, i = self.order[len(self.sent)]
            self.sent.append(
                self.k.remote(
                    self.k.grads.at[which, self.rows_other[i]],
                    self.k.x_got.at[which, i],
                    self.other_x,
                )
            )

    def pump(self):
        if self.next_arrival == len(self.order):
            return False
        k, n = self.k, self.next_arrival
        which, i = self.order[n]
        self.next_arrival += 1
        own = k.local(k.grads.at[which, self.rows[i]], k.staged.at[0])
        self.sent[n].wait_recv()
        self.send()
        other = k.local(k.x_got.at[which, i], k.staged.at[1])
        slot = n % SLOTS
        if self.slots[slot] is not None:
            self.slots[slot]()
        own.wait()
        other.wait()
        k.narrow[slot, :, :] = (
            k.staged[0, :, :].astype(F32) + k.staged[1, :, :].astype(F32)
        ).astype(BF16)
        if i:
            remote = k.remote(k.narrow.at[slot], k.ffn_sums.at[which, i], self.peers[i])
            self.slots[slot] = remote.wait_send
        else:
            self.slots[slot] = k.store(k.narrow.at[slot], k.ffn_sums.at[which, 0])
        return True


def attention_backward_body(nb, rows_each, kv, n_z, blk, k):
    d = lax.axis_index("dp")
    z, x = d // 2, lax.rem(d, 2)
    local = lax.rem(lax.axis_index("tensor"), nb)
    seq_len = nb * rows_each
    per_block = rows_each // Q_ROWS
    over = permuted("tensor", nb)
    other_x = permuted("dp", 1)
    peers = half_peers(nb)
    own_a = k.local(k.own_a, k.near_a.at[0])
    k.load_refs(k.hbm.w_out, k.w_out)
    k.load_refs(k.hbm.cos_t, k.cos_t)
    k.load_refs(k.hbm.sin_t, k.sin_t)
    for tag in (NEAR, FAR):
        k.load_refs(k.hbm.of(tag).qkvp, k.of(tag).qkvp)
        k.load_refs(k.hbm.of(tag).lse, k.of(tag).lse)
    late = [k.local(k.hbm.w_qkv, k.w_qkv), k.local(k.hbm.spread, k.spread)]
    for tag in (NEAR, FAR):
        late.append(k.local(k.hbm.of(tag).att, k.of(tag).att))
        late.append(k.local(k.hbm.of(tag).normed, k.of(tag).normed))
    k.meet([over, other_x] + [peer for _, peer in peers] + list(z_peers(n_z).values()))
    far_first = [
        k.remote(k.own_a.at[rows_of(c)], k.far_a.at[0, rows_of(c)], over)
        for c in range(per_block)
    ]
    near_copies = [k.remote(k.own_a, k.near_a.at[r], peer) for r, peer in peers]
    scatter = Scatter(k, n_z, blk)
    for _ in range(WINDOW):
        scatter.send()
    own_a.wait()
    k.ready()
    for copy in near_copies:
        copy.wait_recv()
    for tag, length in ((NEAR, k.lengths[0]), (FAR, k.lengths[1])):
        blocks, parts, dproj = k.of(tag).a, k.of(tag).parts, k.of(tag).dproj
        k.dk[...] = jnp.zeros_like(k.dk)
        k.dv[...] = jnp.zeros_like(k.dv)
        for c in range(per_block):
            rows = slice(c * Q_ROWS, (c + 1) * Q_ROWS)
            if tag == FAR:
                far_first[c].wait_recv()
                passed = [
                    k.remote(blocks.at[0, rows_of(c)], blocks.at[r, rows_of(c)], peer)
                    for r, peer in peers
                ]
                for copy in passed:
                    copy.wait_recv()
            for b in range(nb):
                i = b * per_block + c
                k.datt[i * Q_ROWS : (i + 1) * Q_ROWS, :] = dot_nn(
                    blocks[local ^ b, rows, :], k.w_out[...]
                ).astype(BF16)
                attention_backward_rows(k, tag, i, length, kv)
                scatter.pump()
        for j in range(kv):
            k_col = slice((4 * j + 2) * PAD, (4 * j + 3) * PAD)
            v_col = slice((4 * j + 3) * PAD, (4 * j + 4) * PAD)
            for i in range(seq_len // Q_ROWS):
                rows = slice(i * Q_ROWS, (i + 1) * Q_ROWS)
                dproj[rows, k_col] = unrotate(k, k.dk[j, rows, :] * SCALE, rows).astype(BF16)
                dproj[rows, v_col] = k.dv[j, rows, :].astype(BF16)
        for copy in late:
            copy.wait()
        late = []
        for c in range(per_block):
            rows = slice(c * Q_ROWS, (c + 1) * Q_ROWS)
            for b in range(nb):
                i = b * per_block + c
                part = dot_nt(dproj[i * Q_ROWS : (i + 1) * Q_ROWS, :], k.w_qkv[...])
                parts[local ^ b, rows, :] = part.astype(BF16)
            if tag == NEAR:
                for r, peer in peers:
                    k.remote(parts.at[r, rows_of(c)], k.near_got.at[r - 1, rows_of(c)], peer)
            else:
                copies = [
                    k.remote(parts.at[r, rows_of(c)], k.far_got.at[r - 1, rows_of(c)], peer)
                    for r, peer in peers
                ]
                total = parts[0, rows, :].astype(F32)
                for r, copy in enumerate(copies):
                    copy.wait_recv()
                    total = total + k.far_got[r, rows, :].astype(F32)
                parts[0, rows, :] = total.astype(BF16)
                k.remote(parts.at[0, rows_of(c)], k.landed.at[rows_of(c)], over)
        if tag == NEAR:
            k.store(parts.at[0], k.near_own)
        else:
            k.remote(k.far_out, k.out_landed, over)
        scatter.pump()
    width = k.w_qkv.shape[0]
    arriving = []
    for which in range(kv + 1):

        def chunk(c, carry):
            cols = pl.ds(pl.multiple_of(c * G_COLS, G_COLS), G_COLS)
            total = None
            if which == 0:
                wide = k.near_att.shape[1]
                for tag in (NEAR, FAR):
                    for r in range(nb):
                        start = pl.multiple_of((local ^ r) * rows_each, rows_each)
                        term = dot_tn(
                            k.of(tag).a[r, :, cols], k.of(tag).att[pl.ds(start, rows_each), :]
                        )
                        total = term if total is None else total + term
                compact = dot_nt(total.astype(BF16), k.spread[:, :wide])
            else:
                part = slice((which - 1) * G_PAD, which * G_PAD)
                total = dot_tn(k.near_normed[:, cols], k.near_dproj[:, part])
                total += dot_tn(k.far_normed[:, cols], k.far_dproj[:, part])
                compact = dot_nt(total.astype(BF16), k.spread[...])
            compact = compact.astype(BF16)
            for b in range(G_COLS // blk):
                owner = c * (G_COLS // blk) + b
                shift = lax.rem(owner // 2 + n_z - z, n_z)
                value = compact[b * blk : (b + 1) * blk, :]

                @pl.when(x == lax.rem(owner, 2))
                def _():
                    k.same[which, shift, :, :] = value

                @pl.when(x != lax.rem(owner, 2))
                def _():
                    k.other[which, shift, :, :] = value

            return carry

        lax.fori_loop(0, width // G_COLS, chunk, 0)
        arriving.append(k.remote(k.other.at[which], k.arrived.at[which], other_x))
        scatter.pump()
    while scatter.pump():
        pass
    for which in range(kv + 1):
        arriving[which].wait_recv()
        for i in z_order(n_z) + [0]:
            held = k.same[which, i, :, :].astype(F32) + k.arrived[which, i, :, :].astype(F32)
            k.same[which, i, :, :] = held.astype(BF16)
            if i:
                k.remote(k.same.at[which, i], k.sums.at[which, i], scatter.peers[i])
            else:
                k.store(k.same.at[which, 0], k.sums.at[which, 0])


def attention_backward(attention_grad, lengths, fwd, grads, far_out, tables, spread, nb, n_z, collective_id):
    rows_each, width = attention_grad.shape
    seq_len = nb * rows_each
    w_qkv, w_out = fwd["w_qkv"], fwd["w_out"]
    kv = w_qkv.shape[1] // G_PAD
    heads = kv * GROUP
    blk = width // (2 * n_z)
    units = grads.shape[2]
    sds = jax.ShapeDtypeStruct
    inputs = dict(
        lengths=(lengths, IN_SMEM),
        own_a=(attention_grad, IN_HBM),
        w_qkv=(w_qkv, LOAD),
        w_out=(w_out, LOAD),
        cos_t=(tables[0], LOAD),
        sin_t=(tables[1], LOAD),
        spread=(spread, LOAD),
        grads=(grads, IN_HBM),
        far_out=(far_out, IN_HBM),
    )
    for tag in (NEAR, FAR):
        for key in ("qkvp", "lse", "att", "normed"):
            inputs[tag + key] = (fwd[tag + key], LOAD)
    block = pltpu.VMEM((nb, rows_each, width), BF16)
    sums = sds((kv + 1, n_z, blk, G_COLS), BF16)
    own = (sds((rows_each, width), BF16), IN_HBM)
    return frame_call(
        functools.partial(attention_backward_body, nb, rows_each, kv, n_z, blk),
        "attention_backward",
        inputs,
        dict(
            near_own=own,
            near_got=(sds((nb - 1, rows_each, width), BF16), IN_HBM),
            landed=own,
            out_landed=own,
            sums=(sums, IN_HBM),
            x_got=(sds((3, n_z, blk, units), BF16), IN_HBM),
            ffn_sums=(sds((3, n_z, blk, units), BF16), IN_HBM),
        ),
        dict(
            near_a=block,
            far_a=block,
            near_parts=block,
            far_parts=block,
            far_got=pltpu.VMEM((nb - 1, rows_each, width), BF16),
            near_dproj=pltpu.VMEM((seq_len, kv * G_PAD), BF16),
            far_dproj=pltpu.VMEM((seq_len, kv * G_PAD), BF16),
            datt=pltpu.VMEM((seq_len, heads * PAD), BF16),
            dk=pltpu.VMEM((kv, seq_len, PAD), F32),
            dv=pltpu.VMEM((kv, seq_len, PAD), F32),
            same=pltpu.VMEM(sums.shape, BF16),
            other=pltpu.VMEM(sums.shape, BF16),
            arrived=pltpu.VMEM(sums.shape, BF16),
            staged=pltpu.VMEM((2, blk, units), BF16),
            narrow=pltpu.VMEM((SLOTS, blk, units), BF16),
        ),
        8 * seq_len * width * (kv * G_PAD + heads * PAD) + heads * seq_len * seq_len * 20 * 256,
        collective_id,
        n_sems=12 * n_z + 48,
    )


def all_peers(n_dp, n_t):
    d, t = lax.axis_index("dp"), lax.axis_index("tensor")
    return (
        [{"tensor": lax.rem(t + i, n_t)} for i in range(1, n_t)],
        [{"dp": lax.rem(d + i, n_dp)} for i in range(1, n_dp)],
    )


def share(k, buffer, me, peers):
    return [k.remote(buffer.at[me], buffer.at[me], peer) for peer in peers]


def sum_slots(buffer, copies):
    for copy in copies:
        copy.wait_recv()
    total = buffer[0, :, :]
    for i in range(1, len(copies) + 1):
        total = total + buffer[i, :, :]
    return total


def moments_kernel(names, kv, *refs):
    keys = [key + suffix for suffix in ("", "_first", "_second") for key in names] + ["gradient"]
    keys += ["gain_sum"] if "gains" in names else []
    keys += ["next_" + key + suffix for suffix in ("_first", "_second") for key in names]
    keys += ["update_" + key for key in names] + ["squares"]
    k = dict(zip(keys, refs))
    correct_one = 1.0 / (1.0 - BETA_ONE**STEP)
    correct_two = 1.0 / (1.0 - BETA_TWO**STEP)
    row = lax.broadcasted_iota(jnp.int32, (8, PAD), 0)
    lane = lax.broadcasted_iota(jnp.int32, (8, PAD), 1)
    squares = jnp.zeros((8, PAD), F32)
    gradient = k["gradient"]

    def step(name, index, gradient_of, rows, cols, number):
        tile = rows if rows % 32 else 32

        def one(i, carry):
            at = index + (pl.ds(pl.multiple_of(i * tile, tile) if rows > tile else 0, tile), slice(None))
            g = gradient_of(at)
            w = k[name][at]
            moment = BETA_ONE * k[name + "_first"][at] + (1.0 - BETA_ONE) * g
            square = BETA_TWO * k[name + "_second"][at] + (1.0 - BETA_TWO) * g * g
            k["next_" + name + "_first"][at] = moment
            k["next_" + name + "_second"][at] = square
            update = (moment * correct_one) / (
                jnp.sqrt(square * correct_two) + ADAM_EPSILON
            ) + WEIGHT_DECAY * w
            k["update_" + name][at] = update
            return (
                carry[0] + jnp.sum(w * w, axis=0, keepdims=True),
                carry[1] + jnp.sum(update * update, axis=0, keepdims=True),
            )

        zero = jnp.zeros((1, cols), F32)
        w_sum, u_sum = lax.fori_loop(0, rows // tile, one, (zero, zero))
        w_sum = jnp.sum(w_sum, axis=1, keepdims=True)
        u_sum = jnp.sum(u_sum, axis=1, keepdims=True)
        mark = lane == number
        return jnp.where(mark & (row == 0), w_sum, 0.0) + jnp.where(mark & (row == 1), u_sum, 0.0)

    def z_sum(which, rows, cols=slice(None)):
        total = gradient[which, 0, rows, cols].astype(F32)
        for i in range(1, gradient.shape[1]):
            total = total + gradient[which, i, rows, cols].astype(F32)
        return total

    def qkv_gradient(at):
        return jnp.concatenate([z_sum(1 + j, at[0]) for j in range(kv)], axis=1)

    if "qkv" in names:
        squares += step("qkv", (), qkv_gradient, *k["qkv"].shape, 0)
    if "out" in names:
        rows, cols = k["out"].shape
        squares += step("out", (), lambda at: z_sum(0, at[0], slice(0, cols)), rows, cols, 1)
    if "gate_up" in names:
        for which in range(2):
            squares += step(
                "gate_up", (which,), lambda at: z_sum(at[0], at[1]), *k["gate_up"].shape[1:], 2 + which
            )
    if "down" in names:
        squares += step(
            "down", (), lambda at: z_sum(2, at[0]), *k["down"].shape, 4
        )
    if "gains" in names:
        for which in range(2):
            squares += step(
                "gains", (which,), lambda at: k["gain_sum"][at], *k["gains"].shape[1:], 5 + which
            )
    k["squares"][...] = squares


def moments(weights, firsts, seconds, gradient, gain_sum, kv):
    names = list(weights)
    arrays = [table[key] for table in (weights, firsts, seconds) for key in names] + [gradient]
    arrays += [] if gain_sum is None else [gain_sum]
    sds = jax.ShapeDtypeStruct
    shapes = [sds(weights[key].shape, F32) for key in names]
    results = pl.pallas_call(
        functools.partial(moments_kernel, names, kv),
        out_shape=shapes * 3 + [sds((8, PAD), F32)],
        in_specs=[VM] * len(arrays),
        out_specs=[VM] * (3 * len(names) + 1),
        compiler_params=pltpu.CompilerParams(vmem_limit_bytes=VMEM_LIMIT),
        cost_estimate=cost(0, 14 << 20),
        name="moments",
    )(*arrays)
    n = len(names)
    return (
        dict(zip(names, results[:n])),
        dict(zip(names, results[n : 2 * n])),
        dict(zip(names, results[2 * n : 3 * n])),
        results[-1],
    )


def sum_all_body(n_dp, n_t, k):
    d, t = lax.axis_index("dp"), lax.axis_index("tensor")
    tensor_peers, dp_peers = all_peers(n_dp, n_t)
    k.first[t, :, :] = k.value[...]
    k.meet(tensor_peers + dp_peers)
    copies = share(k, k.first, t, tensor_peers)
    k.second[d, :, :] = sum_slots(k.first, copies)
    copies = share(k, k.second, d, dp_peers)
    k.total[...] = sum_slots(k.second, copies)


def sum_all(value, n_dp, n_t, collective_id):
    return frame_call(
        functools.partial(sum_all_body, n_dp, n_t),
        "sum_everywhere",
        dict(value=(value, IN_VMEM)),
        dict(total=(jax.ShapeDtypeStruct(value.shape, F32), IN_VMEM)),
        dict(
            first=pltpu.VMEM((n_t,) + value.shape, F32),
            second=pltpu.VMEM((n_dp,) + value.shape, F32),
        ),
        0,
        collective_id,
        n_sems=n_dp + n_t,
    )["total"]


def rms_norm(values, gain_row):
    return (
        values
        * lax.rsqrt(jnp.mean(values * values, axis=-1, keepdims=True) + NORM_EPSILON)
        * gain_row
    )


def rotary_tables():
    half = HEAD // 2
    frequency = ROPE_THETA ** (-(jnp.arange(half, dtype=F32) * (2.0 / HEAD)))
    angles = jnp.arange(SEQ_LEN, dtype=F32)[:, None] * frequency[None, :]
    cosine, sine = jnp.cos(angles), jnp.sin(angles)
    empty = jnp.zeros((SEQ_LEN, PAD - HEAD), F32)
    return (
        jnp.concatenate([cosine, cosine, empty], axis=1),
        jnp.concatenate([-sine, sine, empty], axis=1),
    )


def shards(
    tokens,
    cotangent,
    lengths,
    qkv_weight,
    out_weight,
    gate_up_weight,
    down_weight,
    norm_gains,
    qkv_first,
    out_first,
    gate_up_first,
    down_first,
    gains_first,
    qkv_second,
    out_second,
    gate_up_second,
    down_second,
    gains_second,
):
    rows_each, width = tokens.shape
    n_t = lax.axis_size("tensor")
    n_dp = lax.axis_size("dp")
    n_z = n_dp // 2
    nb = n_t // 2
    t = lax.axis_index("tensor")
    d = lax.axis_index("dp")
    mine = t // nb
    lengths = jnp.stack([lengths[mine], lengths[1 - mine]])
    spread = spread_matrix().astype(BF16)
    blk = qkv_weight.shape[0]
    kv = qkv_weight.shape[1] // G_COLS

    gain_cols = norm_gains.shape[1]
    gain_start = (d * n_t + t) * gain_cols
    gain_rows = lax.dynamic_update_slice(
        jnp.zeros((2, width), F32),
        norm_gains.astype(BF16).astype(F32),
        (0, gain_start),
    )
    out_half = out_weight.astype(BF16).T
    ffn_half = jnp.concatenate(
        [gate_up_weight.astype(BF16), down_weight.astype(BF16).T[None]], axis=0
    )
    halves = (qkv_weight.astype(BF16), out_half, ffn_half)
    tables = rotary_tables()
    fwd = opening(
        tokens, cotangent, lengths, gain_rows, halves, tables, spread, n_t, n_z, 0
    )
    inputs = tokens.astype(F32)
    attention_gain, feedforward_gain = fwd["gain_sum"][0:1], fwd["gain_sum"][1:2]
    residual = fwd["residual"]

    ff = feed_forward(fwd["normed_two"], cotangent, fwd["c_far"], fwd["w_ffn"], nb, 2)

    def total(*arrays):
        result = 0.0
        for array in arrays:
            array = array.astype(F32)
            result = result + (array if array.ndim == 2 else jnp.sum(array, axis=0))
        return result

    normed_two_grad = total(ff["near_own_grad"], ff["near_got_grad"], ff["landed"])
    _, norm_pull = jax.vjp(rms_norm, residual, feedforward_gain)
    residual_part, ffn_gain_grad = norm_pull(normed_two_grad)
    residual_grad = cotangent.astype(F32) + residual_part
    far_out = total(ff["far_own_out"], ff["far_got_out"]).astype(BF16)
    bwd = attention_backward(
        residual_grad.astype(BF16), lengths, fwd, ff["grads"], far_out, tables, spread, nb, n_z, 3
    )
    normed_grad = total(bwd["near_own"], bwd["near_got"], bwd["landed"])
    _, first_pull = jax.vjp(rms_norm, inputs, attention_gain)
    input_part, attention_gain_grad = first_pull(normed_grad)
    grad_tokens = residual_grad + input_part
    gain_grads = jnp.concatenate([attention_gain_grad, ffn_gain_grad], axis=0)
    gain_all = sum_all(gain_grads.reshape(-1, PAD), n_dp, n_t, 4).reshape(2, width)
    layer_out = (residual + total(ff["near_own_out"], ff["near_got_out"], bwd["out_landed"])).astype(
        BF16
    )
    gain_sum = lax.dynamic_slice(gain_all, (0, gain_start), (2, gain_cols))

    def lift(gains):
        return gains[:, None, :]

    gate_down = moments(
        dict(gate_up=gate_up_weight, down=down_weight.T),
        dict(gate_up=gate_up_first, down=down_first.T),
        dict(gate_up=gate_up_second, down=down_second.T),
        bwd["ffn_sums"],
        None,
        kv,
    )
    attention = moments(
        dict(qkv=qkv_weight, out=out_weight.T, gains=lift(norm_gains)),
        dict(qkv=qkv_first, out=out_first.T, gains=lift(gains_first)),
        dict(qkv=qkv_second, out=out_second.T, gains=lift(gains_second)),
        bwd["sums"],
        lift(gain_sum),
        kv,
    )
    norms = jnp.sqrt(sum_all(gate_down[3] + attention[3], n_dp, n_t, 5))
    scale = LEARN_RATE * (norms[0, :7] / norms[1, :7])
    first, second, update = ({**gate_down[i], **attention[i]} for i in range(3))
    for table in (first, second, update):
        table["gains"] = table["gains"][:, 0, :]
        table["out"] = table["out"].T
        table["down"] = table["down"].T
    new = (
        qkv_weight - scale[0] * update["qkv"],
        out_weight - scale[1] * update["out"],
        gate_up_weight - scale[2:4, None, None] * update["gate_up"],
        down_weight - scale[4] * update["down"],
        norm_gains - scale[5:7, None] * update["gains"],
    )
    names = ("qkv", "out", "gate_up", "down", "gains")
    return (
        layer_out,
        grad_tokens,
        *new,
        *[first[key] for key in names],
        *[second[key] for key in names],
        norms[0, :7],
        norms[1, :5],
        norms[1, 5:7],
    )


def solution(mesh):
    rows = P(("dp", "tensor"), None)
    gains = P(None, ("dp", "tensor"))
    weights = (P("dp", "tensor"), P("tensor", "dp"), P(None, "dp", "tensor"), P("tensor", "dp"), gains)
    in_specs = (rows, rows, P("dp")) + weights * 3
    out_specs = (rows, rows) + weights * 3 + (P(), P(), P())
    return jax.shard_map(shards, mesh=mesh, in_specs=in_specs, out_specs=out_specs, check_vma=False)
```

```python
import functools

import jax
import jax.numpy as jnp
import numpy as np
from jax import lax
from jax.experimental import pallas as pl
from jax.experimental.pallas import tpu as pltpu
from jax.sharding import PartitionSpec as P

HEAD = 96
PAD = 128
SEQ_LEN = 1024
SEQS_DEV = 2
STEP = 10
GROUP = 2

NORM_EPSILON = 1e-05
ROPE_THETA = 100000.0
BETA_ONE = 0.9
BETA_TWO = 0.999
ADAM_EPSILON = 1e-06
WEIGHT_DECAY = 0.01
LEARN_RATE = 0.3
NEGATIVE = -1e30
LOG2E = 1.4426950408889634
SCALE = HEAD ** (-0.5)
Q_ROWS = 256
G_COLS = 4 * HEAD
G_PAD = 4 * PAD
VMEM_LIMIT = 56 << 20

F32 = jnp.float32
BF16 = jnp.bfloat16
VM = pl.BlockSpec(memory_space=pltpu.VMEM)
SM = pl.BlockSpec(memory_space=pltpu.SMEM)
ANY = pl.BlockSpec(memory_space=pl.ANY)
MESH = pl.DeviceIdType.MESH
IN_VMEM, IN_SMEM, IN_HBM, LOAD, FLUSH = range(5)
NEAR, FAR = "near_", "far_"
WINDOW, SLOTS = 4, 4
HBM = "any_"


def dot_nn(a, b):
    return lax.dot_general(a, b, (((1,), (0,)), ((), ())), preferred_element_type=F32)


def dot_nt(a, b):
    return lax.dot_general(a, b, (((1,), (1,)), ((), ())), preferred_element_type=F32)


def dot_tn(a, b):
    return lax.dot_general(a, b, (((0,), (0,)), ((), ())), preferred_element_type=F32)


def cost(flops, moved):
    return pl.CostEstimate(flops=int(flops), bytes_accessed=int(moved), transcendentals=0)


def spread_matrix():
    source = lax.broadcasted_iota(jnp.int32, (G_COLS, G_PAD), 0)
    target = lax.broadcasted_iota(jnp.int32, (G_COLS, G_PAD), 1)
    return ((target // PAD) * HEAD + target % PAD == source) & (target % PAD < HEAD)


def swap_halves(values):
    lane = lax.broadcasted_iota(jnp.int32, values.shape, 1)
    return jnp.where(
        lane < HEAD // 2,
        pltpu.roll(values, PAD - HEAD // 2, 1),
        pltpu.roll(values, HEAD // 2, 1),
    )


def permuted(axis, bit):
    return {axis: lax.axis_index(axis) ^ bit}


class Remote:
    def __init__(self, copy, sends=None, receives=None):
        self.copy, self.sends, self.receives = copy, sends, receives
        self.landed = self.left = False

    @staticmethod
    def only(condition, action):
        if condition is None:
            action()
        else:
            pl.when(condition)(action)

    def start(self):
        self.only(self.sends, self.copy.start)

    def wait_recv(self):
        if not self.landed:
            self.only(self.receives, self.copy.wait_recv)
        self.landed = True

    def wait_send(self):
        if not self.left:
            self.only(self.sends, self.copy.wait_send)
        self.left = True


class Side:
    def __init__(self, refs, side):
        self.refs, self.side = refs, side

    def __getattr__(self, name):
        return self.refs[self.side + name]

    def of(self, side):
        return Side(self.refs, self.side + side)


class Frame:
    def __init__(self, names, refs):
        self.refs = dict(zip(names, refs))
        self.loading, self.remotes, self.storing = [], [], []
        self.next_local = 0
        self.hbm = Side(self.refs, HBM)

    def __getattr__(self, name):
        return self.refs[name]

    def of(self, side):
        return Side(self.refs, side)

    def meet(self, peers):
        barrier = pltpu.get_barrier_semaphore()
        for peer in peers:
            pl.semaphore_signal(barrier, inc=1, device_id=peer, device_id_type=MESH)
        pl.semaphore_wait(barrier, len(peers))

    def local(self, source, target):
        copy = pltpu.make_async_copy(source, target, self.local_sem.at[self.next_local])
        self.next_local += 1
        copy.start()
        return copy

    def load_refs(self, source, target):
        self.loading.append(self.local(source, target))

    def ready(self):
        for copy in self.loading:
            copy.wait()
        self.loading = []

    def store(self, source, target):
        pending = [self.local(source, target)]

        def wait():
            if pending:
                pending.pop().wait()

        self.storing.append(wait)
        return wait

    def flush(self, source, target):
        self.store(source, target)

    def remote(self, source, target, peer, sends=None, receives=None):
        n = len(self.remotes)
        copy = pltpu.make_async_remote_copy(
            src_ref=source,
            dst_ref=target,
            send_sem=self.send_sem.at[n],
            recv_sem=self.recv_sem.at[n],
            device_id=peer,
            device_id_type=MESH,
        )
        self.remotes.append(Remote(copy, sends, receives))
        self.remotes[-1].start()
        return self.remotes[-1]

    def finish(self):
        for remote in self.remotes:
            remote.wait_send()
            remote.wait_recv()
        for wait in self.storing:
            wait()


def frame_call(body, name, inputs, outputs, scratch, flops, collective_id, n_sems=40):
    names, specs, arrays = [], [], []
    spec_of = {IN_VMEM: VM, IN_SMEM: SM, IN_HBM: ANY, LOAD: ANY, FLUSH: ANY}
    for key, (array, kind) in inputs.items():
        names.append(HBM + key if kind == LOAD else key)
        specs.append(spec_of[kind])
        arrays.append(array)
    out_specs, out_shapes = [], []
    for key, (shape, kind) in outputs.items():
        names.append(HBM + key if kind == FLUSH else key)
        out_specs.append(spec_of[kind])
        out_shapes.append(shape)
    shapes = []
    for table, kind_of in ((inputs, LOAD), (outputs, FLUSH)):
        for key, (array, kind) in table.items():
            if kind == kind_of:
                names.append(key)
                shapes.append(pltpu.VMEM(array.shape, array.dtype))
    for key, shape in scratch.items():
        names.append(key)
        shapes.append(shape)
    for key in ("local_sem", "send_sem", "recv_sem"):
        names.append(key)
        shapes.append(pltpu.SemaphoreType.DMA((n_sems,)))

    def kernel(*refs):
        frame = Frame(names, refs)
        body(frame)
        frame.finish()

    moved = sum(a.size * a.dtype.itemsize for a in arrays)
    results = pl.pallas_call(
        kernel,
        out_shape=out_shapes,
        in_specs=specs,
        out_specs=out_specs,
        scratch_shapes=shapes,
        compiler_params=pltpu.CompilerParams(
            vmem_limit_bytes=VMEM_LIMIT, collective_id=collective_id, has_side_effects=True
        ),
        cost_estimate=cost(flops, moved),
        name=name,
    )(*arrays)
    return dict(zip(outputs, results))


def half_peers(nb):
    return [(r, permuted("tensor", r)) for r in range(1, nb)]


def rows_of(c):
    return pl.ds(c * Q_ROWS, Q_ROWS)


def bits_down(size):
    bits = []
    bit = size // 2
    while bit:
        bits.append(bit)
        bit //= 2
    return bits


def attention_rows(k, tag, i, length, kv):
    qkvp, att, lse = k.of(tag).qkvp, k.of(tag).att, k.of(tag).lse
    n = (i + 1) * Q_ROWS
    rows = slice(i * Q_ROWS, n)
    lane = lax.broadcasted_iota(jnp.int32, (Q_ROWS, PAD), 1)

    def one_head(h, log_totals):
        group = h // GROUP
        q_col = pl.ds(pl.multiple_of((4 * group + h % GROUP) * PAD, PAD), PAD)
        k_col = pl.ds(pl.multiple_of((4 * group + 2) * PAD, PAD), PAD)
        v_col = pl.ds(pl.multiple_of((4 * group + 3) * PAD, PAD), PAD)
        a_col = pl.ds(pl.multiple_of(h * PAD, PAD), PAD)
        s = dot_nt(qkvp[rows, q_col], qkvp[0:n, k_col])
        row_ids = lax.broadcasted_iota(jnp.int32, (Q_ROWS, 1), 0) + i * Q_ROWS + 1
        limit = jnp.minimum(row_ids, length)
        col_ids = lax.broadcasted_iota(jnp.int32, (Q_ROWS, n), 1)
        s = jnp.where(col_ids < limit, s, NEGATIVE)
        top = jnp.max(s, axis=-1, keepdims=True)
        e = jnp.exp2((s - top) * (SCALE * LOG2E))
        total = jnp.sum(e, axis=-1, keepdims=True)
        p = (e * (1.0 / total)).astype(BF16)
        att[rows, a_col] = dot_nn(p, qkvp[0:n, v_col]).astype(BF16)
        log_total = top * (SCALE * LOG2E) + jnp.log2(total)
        return jnp.where(lane == h, log_total, log_totals)

    lse[rows, :] = lax.fori_loop(0, kv * GROUP, one_head, jnp.zeros((Q_ROWS, PAD), F32))


def z_order(n_z):
    return sorted(range(1, n_z), key=lambda i: min(i, n_z - i))


def z_peers(n_z):
    d = lax.axis_index("dp")
    return {i: {"dp": lax.rem(d + 2 * i, 2 * n_z)} for i in range(1, n_z)}


class Gather:
    def __init__(self, k, streams, n_z, blk):
        d = lax.axis_index("dp")
        self.k, self.streams, self.n_z = k, streams, n_z
        self.z = d // 2
        self.right = {"dp": lax.rem(d + 2, 2 * n_z)}
        self.left = {"dp": lax.rem(d + 2 * n_z - 2, 2 * n_z)}
        self.other_x = permuted("dp", 1)
        self.order = [(s, hop) for s in range(len(streams)) for hop in range(1, n_z)]
        self.rows = {
            i: pl.ds(pl.multiple_of(lax.rem(d + 2 * (n_z - i), 2 * n_z) * blk, 16), blk)
            for i in range(n_z)
        }
        self.sent, self.along_x = {}, {}
        self.next_arrival = 0

    def send(self, s, hop):
        if s >= len(self.streams) or (s, hop) in self.sent:
            return
        source, target, at = self.streams[s]
        z, n_z, far = self.z, self.n_z, hop - 1
        pair = []
        for shift, peer, sends, receives in (
            (far, self.right, (z >= far) & (z < n_z - 1), z >= hop),
            ((n_z - far) % n_z, self.left, (z < n_z - far) & (z > 0), z < n_z - hop),
        ):
            block = target.at[at + (self.rows[shift],)]
            pair.append(self.k.remote(block if far else source, block, peer, sends, receives))
        self.sent[s, hop] = pair

    def own_along_x(self, s):
        source, target, at = self.streams[s]
        block = target.at[at + (self.rows[0],)]
        self.along_x.setdefault(s, []).append(self.k.remote(source, block, self.other_x))

    def pump(self):
        if self.next_arrival == len(self.order):
            return
        s, hop = self.order[self.next_arrival]
        self.next_arrival += 1
        for copy in self.sent[s, hop]:
            copy.wait_recv()
        if hop + 1 < self.n_z:
            self.send(s, hop + 1)
        if hop == min(2, self.n_z - 1):
            self.send(s + 1, 1)
        _, target, at = self.streams[s]
        for shift, copy in zip((hop, self.n_z - hop), self.sent[s, hop]):
            block = target.at[at + (self.rows[shift],)]
            self.along_x[s].append(
                self.k.remote(block, block, self.other_x, copy.receives, copy.receives)
            )

    def complete(self, s):
        for copy in self.along_x[s]:
            copy.wait_recv()


def opening_body(nb, rows_each, kv, n_z, blk, k):
    t = lax.axis_index("tensor")
    local = lax.rem(t, nb)
    seq_len = nb * rows_each
    per_block = rows_each // Q_ROWS
    chunk = 32
    over, other_x = permuted("tensor", nb), permuted("dp", 1)
    peers, along_z = half_peers(nb), z_peers(n_z)
    near_x, far_x = k.near_x, k.far_x
    streams = [(k.qkv_half, k.wq, ()), (k.out_half, k.wo, ())]
    streams += [(k.ffn_half.at[i], k.w_ffn, (i,)) for i in (2, 0, 1)]
    gather = Gather(k, streams, n_z, blk)
    own_tokens = k.local(k.tokens, near_x.at[0])
    own_blocks = [
        k.local(source, target.at[at + (gather.rows[0],)]) for source, target, at in streams
    ]
    k.load_refs(k.hbm.cos_t, k.cos_t)
    k.load_refs(k.hbm.sin_t, k.sin_t)
    k.load_refs(k.hbm.spread, k.spread)
    k.held[0, :, :] = k.gains[...]
    k.meet(list(along_z.values()) + [other_x, over] + [peer for _, peer in peers])

    stages = [permuted("tensor", bit) for bit in bits_down(2 * nb)] + [other_x]
    gain_copy = k.remote(k.held.at[0], k.got.at[0], stages[0])
    far_copy = k.remote(k.tokens, far_x.at[0], over)
    near_copies = [k.remote(k.tokens, near_x.at[r], peer) for r, peer in peers]
    gather.send(0, 1)
    gather.send(1, 1)
    for stage in range(len(stages)):
        gain_copy.wait_recv()
        k.held[stage + 1, :, :] = k.held[stage, :, :] + k.got[stage, :, :]
        if stage + 1 < len(stages):
            gain_copy = k.remote(k.held.at[stage + 1], k.got.at[stage + 1], stages[stage + 1])
    last = len(stages)
    gain_copies = [
        k.remote(k.held.at[last], k.got.at[last + i - 1], along_z[i]) for i in range(1, n_z)
    ]
    gather.own_along_x(0)
    gather.own_along_x(1)
    for _ in range(2 * (n_z - 1)):
        gather.pump()
    for s in range(2, len(streams)):
        gather.own_along_x(s)
    total = k.held[last, :, :]
    for i, copy in enumerate(gain_copies):
        copy.wait_recv()
        total = total + k.got[last + i, :, :]
    k.gain_sum[...] = total
    gain_one, gain_two = k.gain_sum.at[0:1], k.gain_sum.at[1:2]
    far_copy.wait_recv()
    far_copies = [k.remote(far_x.at[0], far_x.at[r], peer) for r, peer in peers]
    own_tokens.wait()
    for copy in near_copies + far_copies:
        copy.wait_recv()

    def normalise(tag):
        for r in range(nb):
            base = (local ^ r) * rows_each

            def norm_rows(i, carry):
                rows = pl.ds(pl.multiple_of(i * chunk, chunk), chunk)
                v = k.of(tag).x[r, rows, :].astype(F32)
                inv = lax.rsqrt(jnp.mean(v * v, axis=-1, keepdims=True) + NORM_EPSILON)
                k.of(tag).normed[pl.ds(pl.multiple_of(base + i * chunk, chunk), chunk), :] = (
                    v * inv * gain_one[...]
                ).astype(BF16)
                return carry

            lax.fori_loop(0, rows_each // chunk, norm_rows, 0)
        k.flush(k.of(tag).normed, k.hbm.of(tag).normed)

    normalise(FAR)
    normalise(NEAR)
    for copy in own_blocks:
        copy.wait()
    k.ready()
    for s, (source, target) in enumerate(((k.wq, k.w_qkv), (k.wo, k.w_out))):
        gather.complete(s)
        for g in range(-(-target.shape[1] // G_PAD)):
            wide = min(G_PAD, target.shape[1] - g * G_PAD)
            part = source[:, g * G_COLS : (g + 1) * G_COLS]
            target[:, g * G_PAD : g * G_PAD + wide] = dot_nn(
                part, k.spread[0 : part.shape[1], 0:wide]
            ).astype(BF16)
        k.flush(target, k.hbm.w_out if s else k.hbm.w_qkv)

    landing, waiting = [], []
    for tag, length in ((FAR, k.lengths[1]), (NEAR, k.lengths[0])):
        normed, qkvp = k.of(tag).normed, k.of(tag).qkvp
        parts, got = k.of(tag).parts, k.of(tag).got
        for i in range(seq_len // Q_ROWS):
            rows = slice(i * Q_ROWS, (i + 1) * Q_ROWS)
            for j in range(kv):
                proj = dot_nn(normed[rows, :], k.w_qkv[:, j * G_PAD : (j + 1) * G_PAD])
                for h in range(4):
                    part = proj[:, h * PAD : (h + 1) * PAD]
                    if h < 3:
                        part = part * k.cos_t[rows, :] + swap_halves(part) * k.sin_t[rows, :]
                    qkvp[rows, (4 * j + h) * PAD : (4 * j + h + 1) * PAD] = part.astype(BF16)
        k.flush(qkvp, k.hbm.of(tag).qkvp)
        gather.pump()
        for c in range(per_block):
            rows = slice(c * Q_ROWS, (c + 1) * Q_ROWS)
            for b in range(nb):
                i = b * per_block + c
                attention_rows(k, tag, i, length, kv)
                part = dot_nt(k.of(tag).att[i * Q_ROWS : (i + 1) * Q_ROWS, :], k.w_out[...])
                parts[local ^ b, rows, :] = part.astype(BF16)
                if waiting:
                    waiting.pop()()
                gather.pump()
            copies = [
                k.remote(parts.at[r, rows_of(c)], got.at[r - 1, rows_of(c)], peer)
                for r, peer in peers
            ]

            def complete(rows=rows, c=c, copies=copies, parts=parts, got=got, tag=tag):
                total = parts[0, rows, :].astype(F32)
                for r, copy in enumerate(copies):
                    copy.wait_recv()
                    total = total + got[r, rows, :].astype(F32)
                if tag == FAR:
                    parts[0, rows, :] = total.astype(BF16)
                    landing.append(
                        k.remote(parts.at[0, rows_of(c)], k.landed.at[rows_of(c)], over)
                    )
                    if c == per_block - 1:
                        k.remote(k.cotangent, k.c_far, over)
                else:
                    k.residual[rows, :] = near_x[0, rows, :].astype(F32) + total

            waiting.append(complete)
        k.flush(k.of(tag).att, k.hbm.of(tag).att)
        k.flush(k.of(tag).lse, k.hbm.of(tag).lse)
    waiting.pop()()
    for c in range(per_block):
        landing[c].wait_recv()

        def residual_rows(i, carry):
            rows = pl.ds(pl.multiple_of(c * Q_ROWS + i * chunk, chunk), chunk)
            v = k.residual[rows, :] + k.landed[rows, :].astype(F32)
            k.residual[rows, :] = v
            inv = lax.rsqrt(jnp.mean(v * v, axis=-1, keepdims=True) + NORM_EPSILON)
            k.normed_two[rows, :] = (v * inv * gain_two[...]).astype(BF16)
            return carry

        lax.fori_loop(0, Q_ROWS // chunk, residual_rows, 0)
    k.flush(k.residual, k.hbm.residual)
    k.flush(k.normed_two, k.hbm.normed_two)
    for _ in range(3 * (n_z - 1)):
        gather.pump()


def opening(tokens, cotangent, lengths, gains, halves, tables, spread, n_t, n_z, collective_id):
    rows_each, width = tokens.shape
    qkv_half, out_half, ffn_half = halves
    blk = qkv_half.shape[0]
    n_dp = 2 * n_z
    nb = n_t // 2
    seq_len = nb * rows_each
    kv = qkv_half.shape[1] // G_COLS
    heads = kv * GROUP
    sds = jax.ShapeDtypeStruct
    normed = (sds((seq_len, width), BF16), FLUSH)
    qkvp = (sds((seq_len, kv * G_PAD), BF16), FLUSH)
    att = (sds((seq_len, heads * PAD), BF16), FLUSH)
    lse = (sds((seq_len, PAD), F32), FLUSH)
    block = pltpu.VMEM((nb, rows_each, width), BF16)
    others = pltpu.VMEM((nb - 1, rows_each, width), BF16)
    n_gain = len(bits_down(n_t)) + 1 + n_z - 1
    return frame_call(
        functools.partial(opening_body, nb, rows_each, kv, n_z, blk),
        "attention_forward",
        dict(
            tokens=(tokens, IN_HBM),
            cotangent=(cotangent, IN_HBM),
            lengths=(lengths, IN_SMEM),
            gains=(gains, IN_VMEM),
            qkv_half=(qkv_half, IN_HBM),
            out_half=(out_half, IN_HBM),
            ffn_half=(ffn_half, IN_HBM),
            cos_t=(tables[0], LOAD),
            sin_t=(tables[1], LOAD),
            spread=(spread, LOAD),
        ),
        dict(
            near_normed=normed,
            far_normed=normed,
            near_qkvp=qkvp,
            far_qkvp=qkvp,
            near_att=att,
            far_att=att,
            near_lse=lse,
            far_lse=lse,
            residual=(sds((rows_each, width), F32), FLUSH),
            normed_two=(sds((rows_each, width), BF16), FLUSH),
            w_qkv=(sds((blk * n_dp, kv * G_PAD), BF16), FLUSH),
            w_out=(sds((blk * n_dp, heads * PAD), BF16), FLUSH),
            w_ffn=(sds((3, blk * n_dp, ffn_half.shape[2]), BF16), IN_HBM),
            c_far=(sds(cotangent.shape, BF16), IN_HBM),
            gain_sum=(sds(gains.shape, F32), IN_VMEM),
        ),
        dict(
            near_x=block,
            far_x=block,
            far_parts=block,
            near_parts=block,
            far_got=others,
            near_got=others,
            landed=pltpu.VMEM((rows_each, width), BF16),
            wq=pltpu.VMEM((blk * n_dp, qkv_half.shape[1]), BF16),
            wo=pltpu.VMEM((blk * n_dp, out_half.shape[1]), BF16),
            held=pltpu.VMEM((n_gain + 1,) + gains.shape, F32),
            got=pltpu.VMEM((n_gain,) + gains.shape, F32),
        ),
        4 * seq_len * width * (kv * G_PAD + heads * PAD) + heads * seq_len * seq_len * 8 * 256,
        collective_id,
        n_sems=12 * n_z + 48,
    )


def feed_forward_body(nb, rows_each, k):
    over = permuted("tensor", nb)
    peers = half_peers(nb)
    per_block = rows_each // Q_ROWS
    w = k.w
    width = w.shape[1]
    near_n, near_c, far_n, far_c = k.near_n, k.near_c, k.far_n, k.far_c
    own_n = k.local(k.own_n, near_n.at[0])
    own_c = k.local(k.own_c, near_c.at[0])
    k.load_refs(k.hbm.w, k.w)
    own_far_c = k.local(k.own_far_c, far_c.at[0])
    k.meet([over] + [peer for _, peer in peers])
    far_first = [
        k.remote(k.own_n.at[rows_of(c)], far_n.at[0, rows_of(c)], over) for c in range(per_block)
    ]
    n_copies = [k.remote(k.own_n, near_n.at[r], peer) for r, peer in peers]
    c_copies = [k.remote(k.own_c, near_c.at[r], peer) for r, peer in peers]
    far_c_copies = [k.remote(k.own_far_c, far_c.at[r], peer) for r, peer in peers]
    own_n.wait()
    own_c.wait()
    k.ready()

    def rows_step(side, r, c):
        rows = slice(c * Q_ROWS, (c + 1) * Q_ROWS)
        start = (0 if side == NEAR else nb * rows_each) + r * rows_each + c * Q_ROWS
        kept = slice(start, start + Q_ROWS)
        n = k.of(side).n[r, rows, :]
        gate = dot_nn(n, w[0])
        up = dot_nn(n, w[1])
        sig = 1.0 / (1.0 + jnp.exp(-gate))
        silu = gate * sig
        hid = (silu * up).astype(BF16)
        k.hidden[kept, :] = hid
        dh = dot_nn(k.of(side).c[r, rows, :], w[2])
        dg = (dh * up * sig * (1.0 + gate * (1.0 - sig))).astype(BF16)
        du = (dh * silu).astype(BF16)
        k.d_gate[kept, :] = dg
        k.d_up[kept, :] = du
        k.of(side).grad[r, rows, :] = (dot_nt(dg, w[0]) + dot_nt(du, w[1])).astype(BF16)
        k.of(side).out[r, rows, :] = dot_nt(hid, w[2]).astype(BF16)

    for r in range(nb):
        if r:
            n_copies[r - 1].wait_recv()
            c_copies[r - 1].wait_recv()
        for c in range(per_block):
            rows_step(NEAR, r, c)
        for part, own, got in (
            (k.near_grad.at[r], k.near_own_grad, k.near_got_grad),
            (k.near_out.at[r], k.near_own_out, k.near_got_out),
        ):
            if r:
                k.remote(part, got.at[r - 1], peers[r - 1][1])
            else:
                k.store(part, own)
    own_far_c.wait()
    for copy in far_c_copies:
        copy.wait_recv()
    landing = []
    for c in range(per_block):
        rows = slice(c * Q_ROWS, (c + 1) * Q_ROWS)
        far_first[c].wait_recv()
        passed = [
            k.remote(far_n.at[0, rows_of(c)], far_n.at[r, rows_of(c)], peer) for r, peer in peers
        ]
        rows_step(FAR, 0, c)
        copies = []
        for r, peer in peers:
            passed[r - 1].wait_recv()
            rows_step(FAR, r, c)
            copies.append(
                k.remote(
                    k.far_grad.at[r, rows_of(c)], k.far_got_grad.at[r - 1, rows_of(c)], peer
                )
            )
        total = k.far_grad[0, rows, :].astype(F32)
        for r, copy in enumerate(copies):
            copy.wait_recv()
            total = total + k.far_got_grad[r, rows, :].astype(F32)
        k.far_grad[0, rows, :] = total.astype(BF16)
        landing.append(k.remote(k.far_grad.at[0, rows_of(c)], k.landed.at[rows_of(c)], over))
    k.store(k.far_out.at[0], k.far_own_out)
    for r, peer in peers:
        k.remote(k.far_out.at[r], k.far_got_out.at[r - 1], peer)
    half = nb * rows_each
    for which in (2, 0, 1):
        right = (k.d_gate, k.d_up, k.hidden)[which]
        lefts = {side: k.of(side).c if which == 2 else k.of(side).n for side in (NEAR, FAR)}

        def col_step(i, carry):
            cols = pl.ds(pl.multiple_of(i * G_COLS, G_COLS), G_COLS)
            total = None
            for s, side in enumerate((NEAR, FAR)):
                for r in range(nb):
                    start = s * half + r * rows_each
                    term = dot_tn(lefts[side][r, :, cols], right[start : start + rows_each, :])
                    total = term if total is None else total + term
            w[which, cols, :] = total.astype(BF16)
            return carry

        lax.fori_loop(0, width // G_COLS, col_step, 0)
        k.store(w.at[which], k.grads.at[which])


def feed_forward(normed_two, cotangent, c_far, w, nb, collective_id):
    rows_each, width = normed_two.shape
    units = w.shape[2]
    sds = jax.ShapeDtypeStruct
    block = pltpu.VMEM((nb, rows_each, width), BF16)
    kept = pltpu.VMEM((2 * nb * rows_each, units), BF16)
    own = (sds((rows_each, width), BF16), IN_HBM)
    got = (sds((nb - 1, rows_each, width), BF16), IN_HBM)
    return frame_call(
        functools.partial(feed_forward_body, nb, rows_each),
        "feed_forward",
        dict(
            own_n=(normed_two, IN_HBM),
            own_c=(cotangent, IN_HBM),
            own_far_c=(c_far, IN_HBM),
            w=(w, LOAD),
        ),
        dict(
            grads=(sds(w.shape, BF16), IN_HBM),
            near_own_grad=own,
            near_got_grad=got,
            landed=own,
            near_own_out=own,
            near_got_out=got,
            far_own_out=own,
            far_got_out=got,
        ),
        dict(
            near_n=block,
            far_n=block,
            near_c=block,
            far_c=block,
            hidden=kept,
            d_gate=kept,
            d_up=kept,
            near_grad=block,
            far_grad=block,
            near_out=block,
            far_out=block,
            far_got_grad=pltpu.VMEM((nb - 1, rows_each, width), BF16),
        ),
        36 * nb * rows_each * width * units,
        collective_id,
    )


def attention_backward_rows(k, tag, i, length, kv):
    qkvp, dproj, datt, lse = k.of(tag).qkvp, k.of(tag).dproj, k.datt, k.of(tag).lse
    n = (i + 1) * Q_ROWS
    rows = slice(i * Q_ROWS, n)
    lane = lax.broadcasted_iota(jnp.int32, (Q_ROWS, PAD), 1)

    def one_head(h, carry):
        group = h // GROUP
        q_col = pl.ds(pl.multiple_of((4 * group + h % GROUP) * PAD, PAD), PAD)
        k_col = pl.ds(pl.multiple_of((4 * group + 2) * PAD, PAD), PAD)
        v_col = pl.ds(pl.multiple_of((4 * group + 3) * PAD, PAD), PAD)
        a_col = pl.ds(pl.multiple_of(h * PAD, PAD), PAD)
        q = qkvp[rows, q_col]
        keys = qkvp[0:n, k_col]
        do = datt[rows, a_col]
        row_lse = jnp.sum(jnp.where(lane == h, lse[rows, :], 0.0), axis=-1, keepdims=True)
        s = dot_nt(q, keys)
        row_ids = lax.broadcasted_iota(jnp.int32, (Q_ROWS, 1), 0) + i * Q_ROWS + 1
        limit = jnp.minimum(row_ids, length)
        col_ids = lax.broadcasted_iota(jnp.int32, (Q_ROWS, n), 1)
        s = jnp.where(col_ids < limit, s, NEGATIVE)
        p = jnp.exp2(s * (SCALE * LOG2E) - row_lse)
        dp = dot_nt(do, qkvp[0:n, v_col])
        inner = jnp.sum(p * dp, axis=-1, keepdims=True)
        ds = (p * (dp - inner)).astype(BF16)
        k.dv[group, 0:n, :] += dot_tn(p.astype(BF16), do)
        k.dk[group, 0:n, :] += dot_tn(ds, q)
        dq = dot_nn(ds, keys) * SCALE
        dproj[rows, q_col] = unrotate(k, dq, rows).astype(BF16)
        return carry

    lax.fori_loop(0, kv * GROUP, one_head, 0)


def unrotate(k, grad, rows):
    return grad * k.cos_t[rows, :] - swap_halves(grad) * k.sin_t[rows, :]


class Scatter:
    def __init__(self, k, n_z, blk):
        d = lax.axis_index("dp")
        self.k, self.peers, self.other_x = k, z_peers(n_z), permuted("dp", 1)
        self.order = [(which, i) for which in (2, 0, 1) for i in z_order(n_z) + [0]]

        def rows(owner):
            return pl.ds(pl.multiple_of(owner * blk, 16), blk)

        owners = {i: lax.rem(d + 2 * i, 2 * n_z) for i in range(n_z)}
        self.rows = {i: rows(owner) for i, owner in owners.items()}
        self.rows_other = {i: rows(owner ^ 1) for i, owner in owners.items()}
        self.sent, self.slots = [], [None] * SLOTS
        self.next_arrival = 0

    def send(self):
        if len(self.sent) < len(self.order):
            which, i = self.order[len(self.sent)]
            self.sent.append(
                self.k.remote(
                    self.k.grads.at[which, self.rows_other[i]],
                    self.k.x_got.at[which, i],
                    self.other_x,
                )
            )

    def pump(self):
        if self.next_arrival == len(self.order):
            return False
        k, n = self.k, self.next_arrival
        which, i = self.order[n]
        self.next_arrival += 1
        own = k.local(k.grads.at[which, self.rows[i]], k.staged.at[0])
        self.sent[n].wait_recv()
        self.send()
        other = k.local(k.x_got.at[which, i], k.staged.at[1])
        slot = n % SLOTS
        if self.slots[slot] is not None:
            self.slots[slot]()
        own.wait()
        other.wait()
        k.narrow[slot, :, :] = (
            k.staged[0, :, :].astype(F32) + k.staged[1, :, :].astype(F32)
        ).astype(BF16)
        if i:
            remote = k.remote(k.narrow.at[slot], k.ffn_sums.at[which, i], self.peers[i])
            self.slots[slot] = remote.wait_send
        else:
            self.slots[slot] = k.store(k.narrow.at[slot], k.ffn_sums.at[which, 0])
        return True


def attention_backward_body(nb, rows_each, kv, n_z, blk, k):
    d = lax.axis_index("dp")
    z, x = d // 2, lax.rem(d, 2)
    local = lax.rem(lax.axis_index("tensor"), nb)
    seq_len = nb * rows_each
    per_block = rows_each // Q_ROWS
    over = permuted("tensor", nb)
    other_x = permuted("dp", 1)
    peers = half_peers(nb)
    own_a = k.local(k.own_a, k.near_a.at[0])
    k.load_refs(k.hbm.w_out, k.w_out)
    k.load_refs(k.hbm.cos_t, k.cos_t)
    k.load_refs(k.hbm.sin_t, k.sin_t)
    for tag in (NEAR, FAR):
        k.load_refs(k.hbm.of(tag).qkvp, k.of(tag).qkvp)
        k.load_refs(k.hbm.of(tag).lse, k.of(tag).lse)
    late = [k.local(k.hbm.w_qkv, k.w_qkv), k.local(k.hbm.spread, k.spread)]
    for tag in (NEAR, FAR):
        late.append(k.local(k.hbm.of(tag).att, k.of(tag).att))
        late.append(k.local(k.hbm.of(tag).normed, k.of(tag).normed))
    tensor_peers, dp_peers = all_peers(2 * n_z, 2 * nb)
    k.meet(tensor_peers + dp_peers)
    far_first = [
        k.remote(k.own_a.at[rows_of(c)], k.far_a.at[0, rows_of(c)], over)
        for c in range(per_block)
    ]
    near_copies = [k.remote(k.own_a, k.near_a.at[r], peer) for r, peer in peers]
    landing, near_landing = [], []
    scatter = Scatter(k, n_z, blk)
    for _ in range(WINDOW):
        scatter.send()
    own_a.wait()
    k.ready()
    for copy in near_copies:
        copy.wait_recv()
    for tag, length in ((NEAR, k.lengths[0]), (FAR, k.lengths[1])):
        blocks, parts, dproj = k.of(tag).a, k.of(tag).parts, k.of(tag).dproj
        k.dk[...] = jnp.zeros_like(k.dk)
        k.dv[...] = jnp.zeros_like(k.dv)
        for c in range(per_block):
            rows = slice(c * Q_ROWS, (c + 1) * Q_ROWS)
            if tag == FAR:
                far_first[c].wait_recv()
                passed = [
                    k.remote(blocks.at[0, rows_of(c)], blocks.at[r, rows_of(c)], peer)
                    for r, peer in peers
                ]
                for copy in passed:
                    copy.wait_recv()
            for b in range(nb):
                i = b * per_block + c
                k.datt[i * Q_ROWS : (i + 1) * Q_ROWS, :] = dot_nn(
                    blocks[local ^ b, rows, :], k.w_out[...]
                ).astype(BF16)
                attention_backward_rows(k, tag, i, length, kv)
                scatter.pump()
        for j in range(kv):
            k_col = slice((4 * j + 2) * PAD, (4 * j + 3) * PAD)
            v_col = slice((4 * j + 3) * PAD, (4 * j + 4) * PAD)
            for i in range(seq_len // Q_ROWS):
                rows = slice(i * Q_ROWS, (i + 1) * Q_ROWS)
                dproj[rows, k_col] = unrotate(k, k.dk[j, rows, :] * SCALE, rows).astype(BF16)
                dproj[rows, v_col] = k.dv[j, rows, :].astype(BF16)
        for copy in late:
            copy.wait()
        late = []
        for c in range(per_block):
            rows = slice(c * Q_ROWS, (c + 1) * Q_ROWS)
            for b in range(nb):
                i = b * per_block + c
                part = dot_nt(dproj[i * Q_ROWS : (i + 1) * Q_ROWS, :], k.w_qkv[...])
                parts[local ^ b, rows, :] = part.astype(BF16)
            if tag == NEAR:
                for r, peer in peers:
                    near_landing.append(
                        k.remote(parts.at[r, rows_of(c)], k.near_got.at[r - 1, rows_of(c)], peer)
                    )
            else:
                copies = [
                    k.remote(parts.at[r, rows_of(c)], k.far_got.at[r - 1, rows_of(c)], peer)
                    for r, peer in peers
                ]
                total = parts[0, rows, :].astype(F32)
                for r, copy in enumerate(copies):
                    copy.wait_recv()
                    total = total + k.far_got[r, rows, :].astype(F32)
                parts[0, rows, :] = total.astype(BF16)
                landing.append(k.remote(parts.at[0, rows_of(c)], k.landed.at[rows_of(c)], over))
        if tag == NEAR:
            k.store(parts.at[0], k.near_own)
        scatter.pump()
    width = k.w_qkv.shape[0]
    arriving = []
    for which in range(kv + 1):

        def chunk(c, carry):
            cols = pl.ds(pl.multiple_of(c * G_COLS, G_COLS), G_COLS)
            total = None
            if which == 0:
                wide = k.near_att.shape[1]
                for tag in (NEAR, FAR):
                    for r in range(nb):
                        start = pl.multiple_of((local ^ r) * rows_each, rows_each)
                        term = dot_tn(
                            k.of(tag).a[r, :, cols], k.of(tag).att[pl.ds(start, rows_each), :]
                        )
                        total = term if total is None else total + term
                compact = dot_nt(total.astype(BF16), k.spread[:, :wide])
            else:
                part = slice((which - 1) * G_PAD, which * G_PAD)
                total = dot_tn(k.near_normed[:, cols], k.near_dproj[:, part])
                total += dot_tn(k.far_normed[:, cols], k.far_dproj[:, part])
                compact = dot_nt(total.astype(BF16), k.spread[...])
            compact = compact.astype(BF16)
            for b in range(G_COLS // blk):
                owner = c * (G_COLS // blk) + b
                shift = lax.rem(owner // 2 + n_z - z, n_z)
                value = compact[b * blk : (b + 1) * blk, :]

                @pl.when(x == lax.rem(owner, 2))
                def _():
                    k.same[which, shift, :, :] = value

                @pl.when(x != lax.rem(owner, 2))
                def _():
                    k.other[which, shift, :, :] = value

            return carry

        lax.fori_loop(0, width // G_COLS, chunk, 0)
        arriving.append(k.remote(k.other.at[which], k.arrived.at[which], other_x))
        if which == 0:
            k.remote(k.far_out, k.out_landed, over)
        scatter.pump()
    while scatter.pump():
        pass
    for which in range(kv + 1):
        arriving[which].wait_recv()
        for i in z_order(n_z) + [0]:
            held = k.same[which, i, :, :].astype(F32) + k.arrived[which, i, :, :].astype(F32)
            k.same[which, i, :, :] = held.astype(BF16)
            if i:
                k.remote(k.same.at[which, i], k.sums.at[which, i], scatter.peers[i])
            else:
                k.store(k.same.at[which, 0], k.sums.at[which, 0])
    for copy in landing + near_landing:
        copy.wait_recv()
    k.flush(k.near_got, k.hbm.near_got)
    loads = [k.local(k.landed, k.near_a.at[0]), k.local(k.tokens, k.near_a.at[1])]
    for copy in loads:
        copy.wait()

    def gain_rows(i, carry):
        rows = pl.ds(pl.multiple_of(i * 32, 32), 32)
        dn = k.near_parts[0, rows, :].astype(F32) + k.near_a[0, rows, :].astype(F32)
        for r in range(nb - 1):
            dn = dn + k.near_got[r, rows, :].astype(F32)
        v = k.near_a[1, rows, :].astype(F32)
        inv = lax.rsqrt(jnp.mean(v * v, axis=-1, keepdims=True) + NORM_EPSILON)
        return carry + jnp.sum(dn * v * inv, axis=0, keepdims=True)

    t = lax.axis_index("tensor")
    k.first[t, 0:1, :] = lax.fori_loop(0, rows_each // 32, gain_rows, jnp.zeros((1, width), F32))
    k.first[t, 1:2, :] = k.gain_part[...]
    gain_copies = share(k, k.first, t, tensor_peers)
    k.second[d, :, :] = sum_slots(k.first, gain_copies)
    gain_copies = share(k, k.second, d, dp_peers)
    k.gain_sums[...] = sum_slots(k.second, gain_copies)


def attention_backward(
    attention_grad, tokens, gain_part, lengths, fwd, grads, far_out, tables, spread, nb, n_z, collective_id
):
    rows_each, width = attention_grad.shape
    seq_len = nb * rows_each
    w_qkv, w_out = fwd["w_qkv"], fwd["w_out"]
    kv = w_qkv.shape[1] // G_PAD
    heads = kv * GROUP
    blk = width // (2 * n_z)
    units = grads.shape[2]
    sds = jax.ShapeDtypeStruct
    inputs = dict(
        lengths=(lengths, IN_SMEM),
        own_a=(attention_grad, IN_HBM),
        w_qkv=(w_qkv, LOAD),
        w_out=(w_out, LOAD),
        cos_t=(tables[0], LOAD),
        sin_t=(tables[1], LOAD),
        spread=(spread, LOAD),
        grads=(grads, IN_HBM),
        far_out=(far_out, IN_HBM),
        tokens=(tokens, IN_HBM),
        gain_part=(gain_part, IN_VMEM),
    )
    for tag in (NEAR, FAR):
        for key in ("qkvp", "lse", "att", "normed"):
            inputs[tag + key] = (fwd[tag + key], LOAD)
    block = pltpu.VMEM((nb, rows_each, width), BF16)
    sums = sds((kv + 1, n_z, blk, G_COLS), BF16)
    own = (sds((rows_each, width), BF16), IN_HBM)
    return frame_call(
        functools.partial(attention_backward_body, nb, rows_each, kv, n_z, blk),
        "attention_backward",
        inputs,
        dict(
            near_own=own,
            near_got=(sds((nb - 1, rows_each, width), BF16), FLUSH),
            landed=own,
            out_landed=own,
            gain_sums=(sds((2, width), F32), IN_VMEM),
            sums=(sums, IN_HBM),
            x_got=(sds((3, n_z, blk, units), BF16), IN_HBM),
            ffn_sums=(sds((3, n_z, blk, units), BF16), IN_HBM),
        ),
        dict(
            near_a=block,
            far_a=block,
            near_parts=block,
            far_parts=block,
            far_got=pltpu.VMEM((nb - 1, rows_each, width), BF16),
            near_dproj=pltpu.VMEM((seq_len, kv * G_PAD), BF16),
            far_dproj=pltpu.VMEM((seq_len, kv * G_PAD), BF16),
            datt=pltpu.VMEM((seq_len, heads * PAD), BF16),
            dk=pltpu.VMEM((kv, seq_len, PAD), F32),
            dv=pltpu.VMEM((kv, seq_len, PAD), F32),
            same=pltpu.VMEM(sums.shape, BF16),
            other=pltpu.VMEM(sums.shape, BF16),
            arrived=pltpu.VMEM(sums.shape, BF16),
            staged=pltpu.VMEM((2, blk, units), BF16),
            first=pltpu.VMEM((2 * nb, 2, width), F32),
            second=pltpu.VMEM((2 * n_z, 2, width), F32),
            narrow=pltpu.VMEM((SLOTS, blk, units), BF16),
        ),
        8 * seq_len * width * (kv * G_PAD + heads * PAD) + heads * seq_len * seq_len * 20 * 256,
        collective_id,
        n_sems=12 * n_z + 48,
    )


def all_peers(n_dp, n_t):
    d, t = lax.axis_index("dp"), lax.axis_index("tensor")
    return (
        [{"tensor": lax.rem(t + i, n_t)} for i in range(1, n_t)],
        [{"dp": lax.rem(d + i, n_dp)} for i in range(1, n_dp)],
    )


def share(k, buffer, me, peers):
    return [k.remote(buffer.at[me], buffer.at[me], peer) for peer in peers]


def sum_slots(buffer, copies):
    for copy in copies:
        copy.wait_recv()
    total = buffer[0, :, :]
    for i in range(1, len(copies) + 1):
        total = total + buffer[i, :, :]
    return total


def moments_kernel(names, kv, *refs):
    keys = [key + suffix for suffix in ("", "_first", "_second") for key in names] + ["gradient"]
    keys += ["gain_sum"] if "gains" in names else []
    keys += ["next_" + key + suffix for suffix in ("_first", "_second") for key in names]
    keys += ["update_" + key for key in names] + ["squares"]
    k = dict(zip(keys, refs))
    correct_one = 1.0 / (1.0 - BETA_ONE**STEP)
    correct_two = 1.0 / (1.0 - BETA_TWO**STEP)
    row = lax.broadcasted_iota(jnp.int32, (8, PAD), 0)
    lane = lax.broadcasted_iota(jnp.int32, (8, PAD), 1)
    squares = jnp.zeros((8, PAD), F32)
    gradient = k["gradient"]

    def step(name, index, gradient_of, rows, cols, number):
        tile = rows if rows % 32 else 32

        def one(i, carry):
            at = index + (pl.ds(pl.multiple_of(i * tile, tile) if rows > tile else 0, tile), slice(None))
            g = gradient_of(at)
            w = k[name][at]
            moment = BETA_ONE * k[name + "_first"][at] + (1.0 - BETA_ONE) * g
            square = BETA_TWO * k[name + "_second"][at] + (1.0 - BETA_TWO) * g * g
            k["next_" + name + "_first"][at] = moment
            k["next_" + name + "_second"][at] = square
            update = (moment * correct_one) / (
                jnp.sqrt(square * correct_two) + ADAM_EPSILON
            ) + WEIGHT_DECAY * w
            k["update_" + name][at] = update
            return (
                carry[0] + jnp.sum(w * w, axis=0, keepdims=True),
                carry[1] + jnp.sum(update * update, axis=0, keepdims=True),
            )

        zero = jnp.zeros((1, cols), F32)
        w_sum, u_sum = lax.fori_loop(0, rows // tile, one, (zero, zero))
        w_sum = jnp.sum(w_sum, axis=1, keepdims=True)
        u_sum = jnp.sum(u_sum, axis=1, keepdims=True)
        mark = lane == number
        return jnp.where(mark & (row == 0), w_sum, 0.0) + jnp.where(mark & (row == 1), u_sum, 0.0)

    def z_sum(which, rows, cols=slice(None)):
        total = gradient[which, 0, rows, cols].astype(F32)
        for i in range(1, gradient.shape[1]):
            total = total + gradient[which, i, rows, cols].astype(F32)
        return total

    def qkv_gradient(at):
        return jnp.concatenate([z_sum(1 + j, at[0]) for j in range(kv)], axis=1)

    if "qkv" in names:
        squares += step("qkv", (), qkv_gradient, *k["qkv"].shape, 0)
    if "out" in names:
        rows, cols = k["out"].shape
        squares += step("out", (), lambda at: z_sum(0, at[0], slice(0, cols)), rows, cols, 1)
    if "gate_up" in names:
        for which in range(2):
            squares += step(
                "gate_up", (which,), lambda at: z_sum(at[0], at[1]), *k["gate_up"].shape[1:], 2 + which
            )
    if "down" in names:
        squares += step(
            "down", (), lambda at: z_sum(2, at[0]), *k["down"].shape, 4
        )
    if "gains" in names:
        for which in range(2):
            squares += step(
                "gains", (which,), lambda at: k["gain_sum"][at], *k["gains"].shape[1:], 5 + which
            )
    k["squares"][...] = squares


def moments(weights, firsts, seconds, gradient, gain_sum, kv):
    names = list(weights)
    arrays = [table[key] for table in (weights, firsts, seconds) for key in names] + [gradient]
    arrays += [] if gain_sum is None else [gain_sum]
    sds = jax.ShapeDtypeStruct
    shapes = [sds(weights[key].shape, F32) for key in names]
    results = pl.pallas_call(
        functools.partial(moments_kernel, names, kv),
        out_shape=shapes * 3 + [sds((8, PAD), F32)],
        in_specs=[VM] * len(arrays),
        out_specs=[VM] * (3 * len(names) + 1),
        compiler_params=pltpu.CompilerParams(vmem_limit_bytes=VMEM_LIMIT),
        cost_estimate=cost(0, 14 << 20),
        name="moments",
    )(*arrays)
    n = len(names)
    return (
        dict(zip(names, results[:n])),
        dict(zip(names, results[n : 2 * n])),
        dict(zip(names, results[2 * n : 3 * n])),
        results[-1],
    )


def sum_all_body(n_dp, n_t, k):
    d, t = lax.axis_index("dp"), lax.axis_index("tensor")
    tensor_peers, dp_peers = all_peers(n_dp, n_t)
    k.first[t, :, :] = k.value[...]
    k.meet(tensor_peers + dp_peers)
    copies = share(k, k.first, t, tensor_peers)
    k.second[d, :, :] = sum_slots(k.first, copies)
    copies = share(k, k.second, d, dp_peers)
    k.total[...] = sum_slots(k.second, copies)


def sum_all(value, n_dp, n_t, collective_id):
    return frame_call(
        functools.partial(sum_all_body, n_dp, n_t),
        "sum_everywhere",
        dict(value=(value, IN_VMEM)),
        dict(total=(jax.ShapeDtypeStruct(value.shape, F32), IN_VMEM)),
        dict(
            first=pltpu.VMEM((n_t,) + value.shape, F32),
            second=pltpu.VMEM((n_dp,) + value.shape, F32),
        ),
        0,
        collective_id,
        n_sems=n_dp + n_t,
    )["total"]


def rms_norm(values, gain_row):
    return (
        values
        * lax.rsqrt(jnp.mean(values * values, axis=-1, keepdims=True) + NORM_EPSILON)
        * gain_row
    )


def rotary_tables():
    half = HEAD // 2
    frequency = ROPE_THETA ** (-(jnp.arange(half, dtype=F32) * (2.0 / HEAD)))
    angles = jnp.arange(SEQ_LEN, dtype=F32)[:, None] * frequency[None, :]
    cosine, sine = jnp.cos(angles), jnp.sin(angles)
    empty = jnp.zeros((SEQ_LEN, PAD - HEAD), F32)
    return (
        jnp.concatenate([cosine, cosine, empty], axis=1),
        jnp.concatenate([-sine, sine, empty], axis=1),
    )


def shards(
    tokens,
    cotangent,
    lengths,
    qkv_weight,
    out_weight,
    gate_up_weight,
    down_weight,
    norm_gains,
    qkv_first,
    out_first,
    gate_up_first,
    down_first,
    gains_first,
    qkv_second,
    out_second,
    gate_up_second,
    down_second,
    gains_second,
):
    rows_each, width = tokens.shape
    n_t = lax.axis_size("tensor")
    n_dp = lax.axis_size("dp")
    n_z = n_dp // 2
    nb = n_t // 2
    t = lax.axis_index("tensor")
    d = lax.axis_index("dp")
    mine = t // nb
    lengths = jnp.stack([lengths[mine], lengths[1 - mine]])
    spread = spread_matrix().astype(BF16)
    blk = qkv_weight.shape[0]
    kv = qkv_weight.shape[1] // G_COLS

    gain_cols = norm_gains.shape[1]
    gain_start = (d * n_t + t) * gain_cols
    gain_rows = lax.dynamic_update_slice(
        jnp.zeros((2, width), F32),
        norm_gains.astype(BF16).astype(F32),
        (0, gain_start),
    )
    out_half = out_weight.astype(BF16).T
    ffn_half = jnp.concatenate(
        [gate_up_weight.astype(BF16), down_weight.astype(BF16).T[None]], axis=0
    )
    halves = (qkv_weight.astype(BF16), out_half, ffn_half)
    tables = rotary_tables()
    fwd = opening(
        tokens, cotangent, lengths, gain_rows, halves, tables, spread, n_t, n_z, 0
    )
    inputs = tokens.astype(F32)
    attention_gain, feedforward_gain = fwd["gain_sum"][0:1], fwd["gain_sum"][1:2]
    residual = fwd["residual"]

    ff = feed_forward(fwd["normed_two"], cotangent, fwd["c_far"], fwd["w_ffn"], nb, 2)

    def total(*arrays):
        result = 0.0
        for array in arrays:
            array = array.astype(F32)
            result = result + (array if array.ndim == 2 else jnp.sum(array, axis=0))
        return result

    normed_two_grad = total(ff["near_own_grad"], ff["near_got_grad"], ff["landed"])
    _, norm_pull = jax.vjp(rms_norm, residual, feedforward_gain)
    residual_part, ffn_gain_grad = norm_pull(normed_two_grad)
    residual_grad = cotangent.astype(F32) + residual_part
    far_out = total(ff["far_own_out"], ff["far_got_out"]).astype(BF16)
    bwd = attention_backward(
        residual_grad.astype(BF16),
        tokens,
        ffn_gain_grad,
        lengths,
        fwd,
        ff["grads"],
        far_out,
        tables,
        spread,
        nb,
        n_z,
        3,
    )
    normed_grad = total(bwd["near_own"], bwd["near_got"], bwd["landed"])
    _, first_pull = jax.vjp(rms_norm, inputs, attention_gain)
    input_part, _ = first_pull(normed_grad)
    grad_tokens = residual_grad + input_part
    layer_out = (residual + total(ff["near_own_out"], ff["near_got_out"], bwd["out_landed"])).astype(
        BF16
    )
    gain_sum = lax.dynamic_slice(bwd["gain_sums"], (0, gain_start), (2, gain_cols))

    def lift(gains):
        return gains[:, None, :]

    gate_down = moments(
        dict(gate_up=gate_up_weight, down=down_weight.T),
        dict(gate_up=gate_up_first, down=down_first.T),
        dict(gate_up=gate_up_second, down=down_second.T),
        bwd["ffn_sums"],
        None,
        kv,
    )
    attention = moments(
        dict(qkv=qkv_weight, out=out_weight.T, gains=lift(norm_gains)),
        dict(qkv=qkv_first, out=out_first.T, gains=lift(gains_first)),
        dict(qkv=qkv_second, out=out_second.T, gains=lift(gains_second)),
        bwd["sums"],
        lift(gain_sum),
        kv,
    )
    norms = jnp.sqrt(sum_all(gate_down[3] + attention[3], n_dp, n_t, 5))
    scale = LEARN_RATE * (norms[0, :7] / norms[1, :7])
    first, second, update = ({**gate_down[i], **attention[i]} for i in range(3))
    for table in (first, second, update):
        table["gains"] = table["gains"][:, 0, :]
        table["out"] = table["out"].T
        table["down"] = table["down"].T
    new = (
        qkv_weight - scale[0] * update["qkv"],
        out_weight - scale[1] * update["out"],
        gate_up_weight - scale[2:4, None, None] * update["gate_up"],
        down_weight - scale[4] * update["down"],
        norm_gains - scale[5:7, None] * update["gains"],
    )
    names = ("qkv", "out", "gate_up", "down", "gains")
    return (
        layer_out,
        grad_tokens,
        *new,
        *[first[key] for key in names],
        *[second[key] for key in names],
        norms[0, :7],
        norms[1, :5],
        norms[1, 5:7],
    )


def solution(mesh):
    rows = P(("dp", "tensor"), None)
    gains = P(None, ("dp", "tensor"))
    weights = (P("dp", "tensor"), P("tensor", "dp"), P(None, "dp", "tensor"), P("tensor", "dp"), gains)
    in_specs = (rows, rows, P("dp")) + weights * 3
    out_specs = (rows, rows) + weights * 3 + (P(), P(), P())
    return jax.shard_map(shards, mesh=mesh, in_specs=in_specs, out_specs=out_specs, check_vma=False)
```

```python
import functools

import jax
import jax.numpy as jnp
import numpy as np
from jax import lax
from jax.experimental import pallas as pl
from jax.experimental.pallas import tpu as pltpu
from jax.sharding import PartitionSpec as P

HEAD = 96
PAD = 128
SEQ_LEN = 1024
SEQS_DEV = 2
STEP = 10
GROUP = 2

NORM_EPSILON = 1e-05
ROPE_THETA = 100000.0
BETA_ONE = 0.9
BETA_TWO = 0.999
ADAM_EPSILON = 1e-06
WEIGHT_DECAY = 0.01
LEARN_RATE = 0.3
NEGATIVE = -1e30
LOG2E = 1.4426950408889634
SCALE = HEAD ** (-0.5)
Q_ROWS = 256
G_COLS = 4 * HEAD
G_PAD = 4 * PAD
VMEM_LIMIT = 56 << 20

F32 = jnp.float32
BF16 = jnp.bfloat16
VM = pl.BlockSpec(memory_space=pltpu.VMEM)
SM = pl.BlockSpec(memory_space=pltpu.SMEM)
ANY = pl.BlockSpec(memory_space=pl.ANY)
MESH = pl.DeviceIdType.MESH
IN_VMEM, IN_SMEM, IN_HBM, LOAD, FLUSH = range(5)
NEAR, FAR = "near_", "far_"
GATE_UP, DOWN, QKV_, OUT, GAINS = "gate_up_", "down_", "qkv_", "out_", "gains_"
WINDOW, SLOTS, EARLY = 3, 4, 2
HBM = "any_"


def dot_nn(a, b):
    return lax.dot_general(a, b, (((1,), (0,)), ((), ())), preferred_element_type=F32)


def dot_nt(a, b):
    return lax.dot_general(a, b, (((1,), (1,)), ((), ())), preferred_element_type=F32)


def dot_tn(a, b):
    return lax.dot_general(a, b, (((0,), (0,)), ((), ())), preferred_element_type=F32)


def cost(flops, moved):
    return pl.CostEstimate(flops=int(flops), bytes_accessed=int(moved), transcendentals=0)


def spread_matrix():
    source = lax.broadcasted_iota(jnp.int32, (G_COLS, G_PAD), 0)
    target = lax.broadcasted_iota(jnp.int32, (G_COLS, G_PAD), 1)
    return ((target // PAD) * HEAD + target % PAD == source) & (target % PAD < HEAD)


def swap_halves(values):
    lane = lax.broadcasted_iota(jnp.int32, values.shape, 1)
    return jnp.where(
        lane < HEAD // 2,
        pltpu.roll(values, PAD - HEAD // 2, 1),
        pltpu.roll(values, HEAD // 2, 1),
    )


def permuted(axis, bit):
    return {axis: lax.axis_index(axis) ^ bit}


class Remote:
    def __init__(self, copy, sends=None, receives=None):
        self.copy, self.sends, self.receives = copy, sends, receives
        self.landed = self.left = False

    @staticmethod
    def only(condition, action):
        if condition is None:
            action()
        else:
            pl.when(condition)(action)

    def start(self):
        self.only(self.sends, self.copy.start)

    def wait_recv(self):
        if not self.landed:
            self.only(self.receives, self.copy.wait_recv)
        self.landed = True

    def wait_send(self):
        if not self.left:
            self.only(self.sends, self.copy.wait_send)
        self.left = True


class Side:
    def __init__(self, refs, side):
        self.refs, self.side = refs, side

    def __getattr__(self, name):
        return self.refs[self.side + name]

    def of(self, side):
        return Side(self.refs, self.side + side)


class Frame:
    def __init__(self, names, refs):
        self.refs = dict(zip(names, refs))
        self.loading, self.remotes, self.storing = [], [], []
        self.next_local = 0
        self.hbm = Side(self.refs, HBM)

    def __getattr__(self, name):
        return self.refs[name]

    def of(self, side):
        return Side(self.refs, side)

    def meet(self, peers):
        barrier = pltpu.get_barrier_semaphore()
        for peer in peers:
            pl.semaphore_signal(barrier, inc=1, device_id=peer, device_id_type=MESH)
        pl.semaphore_wait(barrier, len(peers))

    def local(self, source, target):
        copy = pltpu.make_async_copy(source, target, self.local_sem.at[self.next_local])
        self.next_local += 1
        copy.start()
        return copy

    def load_refs(self, source, target):
        self.loading.append(self.local(source, target))

    def ready(self):
        for copy in self.loading:
            copy.wait()
        self.loading = []

    def store(self, source, target):
        pending = [self.local(source, target)]

        def wait():
            if pending:
                pending.pop().wait()

        self.storing.append(wait)
        return wait

    def flush(self, source, target):
        self.store(source, target)

    def remote(self, source, target, peer, sends=None, receives=None):
        n = len(self.remotes)
        copy = pltpu.make_async_remote_copy(
            src_ref=source,
            dst_ref=target,
            send_sem=self.send_sem.at[n],
            recv_sem=self.recv_sem.at[n],
            device_id=peer,
            device_id_type=MESH,
        )
        self.remotes.append(Remote(copy, sends, receives))
        self.remotes[-1].start()
        return self.remotes[-1]

    def finish(self):
        for remote in self.remotes:
            remote.wait_send()
            remote.wait_recv()
        for wait in self.storing:
            wait()


def frame_call(body, name, inputs, outputs, scratch, flops, collective_id, n_sems=40):
    names, specs, arrays = [], [], []
    spec_of = {IN_VMEM: VM, IN_SMEM: SM, IN_HBM: ANY, LOAD: ANY, FLUSH: ANY}
    for key, (array, kind) in inputs.items():
        names.append(HBM + key if kind == LOAD else key)
        specs.append(spec_of[kind])
        arrays.append(array)
    out_specs, out_shapes = [], []
    for key, (shape, kind) in outputs.items():
        names.append(HBM + key if kind == FLUSH else key)
        out_specs.append(spec_of[kind])
        out_shapes.append(shape)
    shapes = []
    for table, kind_of in ((inputs, LOAD), (outputs, FLUSH)):
        for key, (array, kind) in table.items():
            if kind == kind_of:
                names.append(key)
                shapes.append(pltpu.VMEM(array.shape, array.dtype))
    for key, shape in scratch.items():
        names.append(key)
        shapes.append(shape)
    extra = {}
    for key in ("local_sem", "send_sem", "recv_sem"):
        if key == "local_sem" or collective_id is not None:
            names.append(key)
            shapes.append(pltpu.SemaphoreType.DMA((n_sems,)))
    if collective_id is not None:
        extra = dict(collective_id=collective_id, has_side_effects=True)

    def kernel(*refs):
        frame = Frame(names, refs)
        body(frame)
        frame.finish()

    moved = sum(a.size * a.dtype.itemsize for a in arrays)
    results = pl.pallas_call(
        kernel,
        out_shape=out_shapes,
        in_specs=specs,
        out_specs=out_specs,
        scratch_shapes=shapes,
        compiler_params=pltpu.CompilerParams(vmem_limit_bytes=VMEM_LIMIT, **extra),
        cost_estimate=cost(flops, moved),
        name=name,
    )(*arrays)
    return dict(zip(outputs, results))


def half_peers(nb):
    return [(r, permuted("tensor", r)) for r in range(1, nb)]


def rows_of(c):
    return pl.ds(c * Q_ROWS, Q_ROWS)


def bits_down(size):
    bits = []
    bit = size // 2
    while bit:
        bits.append(bit)
        bit //= 2
    return bits


def attention_rows(k, tag, i, length, kv):
    qkvp, att, lse = k.of(tag).qkvp, k.of(tag).att, k.of(tag).lse
    n = (i + 1) * Q_ROWS
    rows = slice(i * Q_ROWS, n)
    lane = lax.broadcasted_iota(jnp.int32, (Q_ROWS, PAD), 1)

    def one_head(h, log_totals):
        group = h // GROUP
        q_col = pl.ds(pl.multiple_of((4 * group + h % GROUP) * PAD, PAD), PAD)
        k_col = pl.ds(pl.multiple_of((4 * group + 2) * PAD, PAD), PAD)
        v_col = pl.ds(pl.multiple_of((4 * group + 3) * PAD, PAD), PAD)
        a_col = pl.ds(pl.multiple_of(h * PAD, PAD), PAD)
        s = dot_nt(qkvp[rows, q_col], qkvp[0:n, k_col])
        row_ids = lax.broadcasted_iota(jnp.int32, (Q_ROWS, 1), 0) + i * Q_ROWS + 1
        limit = jnp.minimum(row_ids, length)
        col_ids = lax.broadcasted_iota(jnp.int32, (Q_ROWS, n), 1)
        s = jnp.where(col_ids < limit, s, NEGATIVE)
        top = jnp.max(s, axis=-1, keepdims=True)
        e = jnp.exp2((s - top) * (SCALE * LOG2E))
        total = jnp.sum(e, axis=-1, keepdims=True)
        p = (e * (1.0 / total)).astype(BF16)
        att[rows, a_col] = dot_nn(p, qkvp[0:n, v_col]).astype(BF16)
        log_total = top * (SCALE * LOG2E) + jnp.log2(total)
        return jnp.where(lane == h, log_total, log_totals)

    lse[rows, :] = lax.fori_loop(0, kv * GROUP, one_head, jnp.zeros((Q_ROWS, PAD), F32))


def z_order(n_z):
    return sorted(range(1, n_z), key=lambda i: min(i, n_z - i))


def z_peers(n_z):
    d = lax.axis_index("dp")
    return {i: {"dp": lax.rem(d + 2 * i, 2 * n_z)} for i in range(1, n_z)}


class Stream:
    def __init__(self, k, source, place, paired=False):
        self.source, self.place, self.paired = source, place, paired
        d = lax.axis_index("dp")
        n_dp = lax.axis_size("dp")
        blk = source.shape[0]
        own = place(pl.ds(pl.multiple_of(d * blk, 16), blk))
        self.own, self.local = own, k.local(source, own)
        self.shifted = {}
        for i in range(n_dp // 2):
            if paired:
                start, size = lax.rem(d // 2 + n_dp // 2 - i, n_dp // 2) * (2 * blk), 2 * blk
            else:
                start, size = lax.rem(d + n_dp - 2 * i, n_dp) * blk, blk
            self.shifted[i] = place(pl.ds(pl.multiple_of(start, 16), size))
        self.along_x, self.sent = [], {}


class Gather:
    def __init__(self, k, streams, n_z):
        d = lax.axis_index("dp")
        self.k, self.streams, self.n_z = k, streams, n_z
        self.z = d // 2
        self.right = {"dp": lax.rem(d + 2, 2 * n_z)}
        self.left = {"dp": lax.rem(d + 2 * n_z - 2, 2 * n_z)}
        self.other_x = permuted("dp", 1)
        self.order = [(s, hop) for s in range(len(streams)) for hop in range(1, n_z)]
        self.next_arrival = 0

    def send(self, s, hop):
        if s >= len(self.streams) or hop in self.streams[s].sent:
            return
        stream = self.streams[s]
        z, n_z, far = self.z, self.n_z, hop - 1
        if stream.paired and not far:
            stream.local.wait()
            self.complete(s)
        pair = []
        for shift, peer, sends, receives in (
            (far, self.right, (z >= far) & (z < n_z - 1), z >= hop),
            ((n_z - far) % n_z, self.left, (z < n_z - far) & (z > 0), z < n_z - hop),
        ):
            block = stream.shifted[shift]
            source = block if far or stream.paired else stream.source
            pair.append(self.k.remote(source, block, peer, sends, receives))
        stream.sent[hop] = pair

    def own_along_x(self, s):
        stream = self.streams[s]
        stream.along_x.append(self.k.remote(stream.source, stream.own, self.other_x))

    def pump(self):
        if self.next_arrival == len(self.order):
            return
        s, hop = self.order[self.next_arrival]
        self.next_arrival += 1
        stream = self.streams[s]
        for copy in stream.sent[hop]:
            copy.wait_recv()
        if hop + 1 < self.n_z:
            self.send(s, hop + 1)
        if hop == min(2, self.n_z - 1):
            self.send(s + 1, 1)
        if not stream.paired:
            for shift, copy in zip((hop, self.n_z - hop), stream.sent[hop]):
                block = stream.shifted[shift]
                stream.along_x.append(
                    self.k.remote(block, block, self.other_x, copy.receives, copy.receives)
                )

    def complete(self, s):
        for copy in self.streams[s].along_x:
            copy.wait_recv()


def opening_body(nb, rows_each, kv, n_z, blk, k):
    t = lax.axis_index("tensor")
    local = lax.rem(t, nb)
    seq_len = nb * rows_each
    per_block = rows_each // Q_ROWS
    chunk = 32
    over, other_x = permuted("tensor", nb), permuted("dp", 1)
    peers, along_z = half_peers(nb), z_peers(n_z)
    near_x, far_x = k.near_x, k.far_x
    early = k.ffn_half.shape[2] // 4
    up_early, up_late = pl.ds(0, early), pl.ds(early, 3 * early)
    own_tokens = k.local(k.tokens, near_x.at[0])
    streams = [
        Stream(k, k.qkv_half, lambda rows: k.wq.at[rows]),
        Stream(k, k.out_half, lambda rows: k.wo.at[rows], True),
        Stream(k, k.ffn_half.at[1, :, up_early], lambda rows: k.w_ffn.at[1, rows, up_early], True),
        Stream(k, k.ffn_half.at[2], lambda rows: k.w_ffn.at[2, rows]),
        Stream(k, k.ffn_half.at[0], lambda rows: k.w_ffn.at[0, rows]),
        Stream(k, k.ffn_half.at[1, :, up_late], lambda rows: k.w_ffn.at[1, rows, up_late]),
    ]
    gather = Gather(k, streams, n_z)
    k.load_refs(k.hbm.cos_t, k.cos_t)
    k.load_refs(k.hbm.sin_t, k.sin_t)
    k.load_refs(k.hbm.spread, k.spread)
    k.held[0, :, :] = k.gains[...]
    k.meet(list(along_z.values()) + [other_x, over] + [peer for _, peer in peers])

    stages = [permuted("tensor", bit) for bit in bits_down(2 * nb)] + [other_x]
    gain_copy = k.remote(k.held.at[0], k.got.at[0], stages[0])
    far_copy = k.remote(k.tokens, far_x.at[0], over)
    near_copies = [k.remote(k.tokens, near_x.at[r], peer) for r, peer in peers]
    gather.own_along_x(1)
    gather.own_along_x(0)
    gather.own_along_x(2)
    gather.send(0, 1)
    for stage in range(len(stages)):
        gain_copy.wait_recv()
        k.held[stage + 1, :, :] = k.held[stage, :, :] + k.got[stage, :, :]
        if stage + 1 < len(stages):
            gain_copy = k.remote(k.held.at[stage + 1], k.got.at[stage + 1], stages[stage + 1])
    last = len(stages)
    gain_copies = [
        k.remote(k.held.at[last], k.got.at[last + i - 1], along_z[i]) for i in range(1, n_z)
    ]
    for _ in range(2 * (n_z - 1)):
        gather.pump()
    for s in range(3, len(streams)):
        gather.own_along_x(s)
    total = k.held[last, :, :]
    for i, copy in enumerate(gain_copies):
        copy.wait_recv()
        total = total + k.got[last + i, :, :]
    k.gain_sum[...] = total
    gain_one, gain_two = k.gain_sum.at[0:1], k.gain_sum.at[1:2]
    far_copy.wait_recv()
    far_copies = [k.remote(far_x.at[0], far_x.at[r], peer) for r, peer in peers]
    own_tokens.wait()
    for copy in near_copies + far_copies:
        copy.wait_recv()

    def normalise(tag):
        for r in range(nb):
            base = (local ^ r) * rows_each

            def norm_rows(i, carry):
                rows = pl.ds(pl.multiple_of(i * chunk, chunk), chunk)
                v = k.of(tag).x[r, rows, :].astype(F32)
                inv = lax.rsqrt(jnp.mean(v * v, axis=-1, keepdims=True) + NORM_EPSILON)
                k.of(tag).normed[pl.ds(pl.multiple_of(base + i * chunk, chunk), chunk), :] = (
                    v * inv * gain_one[...]
                ).astype(BF16)
                return carry

            lax.fori_loop(0, rows_each // chunk, norm_rows, 0)
        k.flush(k.of(tag).normed, k.hbm.of(tag).normed)

    normalise(FAR)
    normalise(NEAR)
    for stream in streams:
        if not stream.paired:
            stream.local.wait()
    k.ready()
    for s, (source, target) in enumerate(((k.wq, k.w_qkv), (k.wo, k.w_out))):
        gather.complete(s)
        for g in range(-(-target.shape[1] // G_PAD)):
            wide = min(G_PAD, target.shape[1] - g * G_PAD)
            part = source[:, g * G_COLS : (g + 1) * G_COLS]
            target[:, g * G_PAD : g * G_PAD + wide] = dot_nn(
                part, k.spread[0 : part.shape[1], 0:wide]
            ).astype(BF16)
        k.flush(target, k.hbm.w_out if s else k.hbm.w_qkv)

    landing, waiting = [], []
    for tag, length in ((FAR, k.lengths[1]), (NEAR, k.lengths[0])):
        normed, qkvp = k.of(tag).normed, k.of(tag).qkvp
        parts, got = k.of(tag).parts, k.of(tag).got
        for i in range(seq_len // Q_ROWS):
            rows = slice(i * Q_ROWS, (i + 1) * Q_ROWS)
            for j in range(kv):
                proj = dot_nn(normed[rows, :], k.w_qkv[:, j * G_PAD : (j + 1) * G_PAD])
                for h in range(4):
                    part = proj[:, h * PAD : (h + 1) * PAD]
                    if h < 3:
                        part = part * k.cos_t[rows, :] + swap_halves(part) * k.sin_t[rows, :]
                    qkvp[rows, (4 * j + h) * PAD : (4 * j + h + 1) * PAD] = part.astype(BF16)
        k.flush(qkvp, k.hbm.of(tag).qkvp)
        gather.pump()
        for c in range(per_block):
            rows = slice(c * Q_ROWS, (c + 1) * Q_ROWS)
            for b in range(nb):
                i = b * per_block + c
                attention_rows(k, tag, i, length, kv)
                part = dot_nt(k.of(tag).att[i * Q_ROWS : (i + 1) * Q_ROWS, :], k.w_out[...])
                parts[local ^ b, rows, :] = part.astype(BF16)
                if waiting:
                    waiting.pop()()
                gather.pump()
            copies = [
                k.remote(parts.at[r, rows_of(c)], got.at[r - 1, rows_of(c)], peer)
                for r, peer in peers
            ]

            def complete(rows=rows, c=c, copies=copies, parts=parts, got=got, tag=tag):
                total = parts[0, rows, :].astype(F32)
                for r, copy in enumerate(copies):
                    copy.wait_recv()
                    total = total + got[r, rows, :].astype(F32)
                if tag == FAR:
                    parts[0, rows, :] = total.astype(BF16)
                    landing.append(
                        k.remote(parts.at[0, rows_of(c)], k.landed.at[rows_of(c)], over)
                    )
                    if c == per_block - 1:
                        k.remote(k.cotangent, k.c_far, over)
                else:
                    k.residual[rows, :] = near_x[0, rows, :].astype(F32) + total

            waiting.append(complete)
        k.flush(k.of(tag).att, k.hbm.of(tag).att)
        k.flush(k.of(tag).lse, k.hbm.of(tag).lse)
    waiting.pop()()
    for c in range(per_block):
        landing[c].wait_recv()

        def residual_rows(i, carry):
            rows = pl.ds(pl.multiple_of(c * Q_ROWS + i * chunk, chunk), chunk)
            v = k.residual[rows, :] + k.landed[rows, :].astype(F32)
            k.residual[rows, :] = v
            inv = lax.rsqrt(jnp.mean(v * v, axis=-1, keepdims=True) + NORM_EPSILON)
            k.normed_two[rows, :] = (v * inv * gain_two[...]).astype(BF16)
            return carry

        lax.fori_loop(0, Q_ROWS // chunk, residual_rows, 0)
    k.flush(k.residual, k.hbm.residual)
    k.flush(k.normed_two, k.hbm.normed_two)
    for _ in range(4 * (n_z - 1)):
        gather.pump()


def opening(tokens, cotangent, lengths, gains, halves, tables, spread, n_t, n_z, collective_id):
    rows_each, width = tokens.shape
    qkv_half, out_half, ffn_half = halves
    blk = qkv_half.shape[0]
    n_dp = 2 * n_z
    nb = n_t // 2
    seq_len = nb * rows_each
    kv = qkv_half.shape[1] // G_COLS
    heads = kv * GROUP
    sds = jax.ShapeDtypeStruct
    normed = (sds((seq_len, width), BF16), FLUSH)
    qkvp = (sds((seq_len, kv * G_PAD), BF16), FLUSH)
    att = (sds((seq_len, heads * PAD), BF16), FLUSH)
    lse = (sds((seq_len, PAD), F32), FLUSH)
    block = pltpu.VMEM((nb, rows_each, width), BF16)
    others = pltpu.VMEM((nb - 1, rows_each, width), BF16)
    n_gain = len(bits_down(n_t)) + 1 + n_z - 1
    return frame_call(
        functools.partial(opening_body, nb, rows_each, kv, n_z, blk),
        "attention_forward",
        dict(
            tokens=(tokens, IN_HBM),
            cotangent=(cotangent, IN_HBM),
            lengths=(lengths, IN_SMEM),
            gains=(gains, IN_VMEM),
            qkv_half=(qkv_half, IN_HBM),
            out_half=(out_half, IN_HBM),
            ffn_half=(ffn_half, IN_HBM),
            cos_t=(tables[0], LOAD),
            sin_t=(tables[1], LOAD),
            spread=(spread, LOAD),
        ),
        dict(
            near_normed=normed,
            far_normed=normed,
            near_qkvp=qkvp,
            far_qkvp=qkvp,
            near_att=att,
            far_att=att,
            near_lse=lse,
            far_lse=lse,
            residual=(sds((rows_each, width), F32), FLUSH),
            normed_two=(sds((rows_each, width), BF16), FLUSH),
            w_qkv=(sds((blk * n_dp, kv * G_PAD), BF16), FLUSH),
            w_out=(sds((blk * n_dp, heads * PAD), BF16), FLUSH),
            w_ffn=(sds((3, blk * n_dp, ffn_half.shape[2]), BF16), IN_HBM),
            c_far=(sds(cotangent.shape, BF16), IN_HBM),
            gain_sum=(sds(gains.shape, F32), IN_VMEM),
        ),
        dict(
            near_x=block,
            far_x=block,
            far_parts=block,
            near_parts=block,
            far_got=others,
            near_got=others,
            landed=pltpu.VMEM((rows_each, width), BF16),
            wq=pltpu.VMEM((blk * n_dp, qkv_half.shape[1]), BF16),
            wo=pltpu.VMEM((blk * n_dp, out_half.shape[1]), BF16),
            held=pltpu.VMEM((n_gain + 1,) + gains.shape, F32),
            got=pltpu.VMEM((n_gain,) + gains.shape, F32),
        ),
        4 * seq_len * width * (kv * G_PAD + heads * PAD) + heads * seq_len * seq_len * 8 * 256,
        collective_id,
        n_sems=12 * n_z + 48,
    )


def feed_forward_body(nb, rows_each, n_z, k):
    over = permuted("tensor", nb)
    peers = half_peers(nb)
    per_block = rows_each // Q_ROWS
    w = k.w
    width = w.shape[1]
    blk = width // (2 * n_z)
    other_x = permuted("dp", 1)
    near_n, near_c, far_n, far_c = k.near_n, k.near_c, k.far_n, k.far_c
    own_n = k.local(k.own_n, near_n.at[0])
    own_c = k.local(k.own_c, near_c.at[0])
    k.load_refs(k.hbm.w, k.w)
    own_far_c = k.local(k.own_far_c, far_c.at[0])
    k.meet([over, other_x] + [peer for _, peer in peers])
    far_first = [
        k.remote(k.own_n.at[rows_of(c)], far_n.at[0, rows_of(c)], over) for c in range(per_block)
    ]
    n_copies = [k.remote(k.own_n, near_n.at[r], peer) for r, peer in peers]
    c_copies = [k.remote(k.own_c, near_c.at[r], peer) for r, peer in peers]
    far_c_copies = [k.remote(k.own_far_c, far_c.at[r], peer) for r, peer in peers]
    own_n.wait()
    own_c.wait()
    k.ready()

    def rows_step(side, r, c):
        rows = slice(c * Q_ROWS, (c + 1) * Q_ROWS)
        start = (0 if side == NEAR else nb * rows_each) + r * rows_each + c * Q_ROWS
        kept = slice(start, start + Q_ROWS)
        n = k.of(side).n[r, rows, :]
        gate = dot_nn(n, w[0])
        up = dot_nn(n, w[1])
        sig = 1.0 / (1.0 + jnp.exp(-gate))
        silu = gate * sig
        hid = (silu * up).astype(BF16)
        k.hidden[kept, :] = hid
        dh = dot_nn(k.of(side).c[r, rows, :], w[2])
        dg = (dh * up * sig * (1.0 + gate * (1.0 - sig))).astype(BF16)
        du = (dh * silu).astype(BF16)
        k.d_gate[kept, :] = dg
        k.d_up[kept, :] = du
        k.of(side).grad[r, rows, :] = (dot_nt(dg, w[0]) + dot_nt(du, w[1])).astype(BF16)
        k.of(side).out[r, rows, :] = dot_nt(hid, w[2]).astype(BF16)

    for r in range(nb):
        if r:
            n_copies[r - 1].wait_recv()
            c_copies[r - 1].wait_recv()
        for c in range(per_block):
            rows_step(NEAR, r, c)
        for part, own, got in (
            (k.near_grad.at[r], k.near_own_grad, k.near_got_grad),
            (k.near_out.at[r], k.near_own_out, k.near_got_out),
        ):
            if r:
                k.remote(part, got.at[r - 1], peers[r - 1][1])
            else:
                k.store(part, own)
    own_far_c.wait()
    for copy in far_c_copies:
        copy.wait_recv()
    landing = []
    for c in range(per_block):
        rows = slice(c * Q_ROWS, (c + 1) * Q_ROWS)
        far_first[c].wait_recv()
        passed = [
            k.remote(far_n.at[0, rows_of(c)], far_n.at[r, rows_of(c)], peer) for r, peer in peers
        ]
        rows_step(FAR, 0, c)
        copies = []
        for r, peer in peers:
            passed[r - 1].wait_recv()
            rows_step(FAR, r, c)
            copies.append(
                k.remote(
                    k.far_grad.at[r, rows_of(c)], k.far_got_grad.at[r - 1, rows_of(c)], peer
                )
            )
        total = k.far_grad[0, rows, :].astype(F32)
        for r, copy in enumerate(copies):
            copy.wait_recv()
            total = total + k.far_got_grad[r, rows, :].astype(F32)
        k.far_grad[0, rows, :] = total.astype(BF16)
        landing.append(k.remote(k.far_grad.at[0, rows_of(c)], k.landed.at[rows_of(c)], over))
    k.store(k.far_out.at[0], k.far_own_out)
    for r, peer in peers:
        k.remote(k.far_out.at[r], k.far_got_out.at[r - 1], peer)
    half = nb * rows_each
    for which in (2, 0, 1):
        right = (k.d_gate, k.d_up, k.hidden)[which]
        lefts = {side: k.of(side).c if which == 2 else k.of(side).n for side in (NEAR, FAR)}

        def col_step(i, carry):
            cols = pl.ds(pl.multiple_of(i * G_COLS, G_COLS), G_COLS)
            total = None
            for s, side in enumerate((NEAR, FAR)):
                for r in range(nb):
                    start = s * half + r * rows_each
                    term = dot_tn(lefts[side][r, :, cols], right[start : start + rows_each, :])
                    total = term if total is None else total + term
            w[which, cols, :] = total.astype(BF16)
            return carry

        lax.fori_loop(0, width // G_COLS, col_step, 0)
        k.store(w.at[which], k.grads.at[which])
        if which == 2:
            d = lax.axis_index("dp")
            for n, i in enumerate((z_order(n_z) + [0])[:EARLY]):
                start = (lax.rem(d + 2 * i, 2 * n_z) ^ 1) * blk
                rows = pl.ds(pl.multiple_of(start, 16), blk)
                k.remote(w.at[which, rows], k.early.at[n], other_x)


def feed_forward(normed_two, cotangent, c_far, w, nb, n_z, collective_id):
    rows_each, width = normed_two.shape
    units = w.shape[2]
    sds = jax.ShapeDtypeStruct
    block = pltpu.VMEM((nb, rows_each, width), BF16)
    kept = pltpu.VMEM((2 * nb * rows_each, units), BF16)
    own = (sds((rows_each, width), BF16), IN_HBM)
    got = (sds((nb - 1, rows_each, width), BF16), IN_HBM)
    return frame_call(
        functools.partial(feed_forward_body, nb, rows_each, n_z),
        "feed_forward",
        dict(
            own_n=(normed_two, IN_HBM),
            own_c=(cotangent, IN_HBM),
            own_far_c=(c_far, IN_HBM),
            w=(w, LOAD),
        ),
        dict(
            grads=(sds(w.shape, BF16), IN_HBM),
            early=(sds((EARLY, width // (2 * n_z), units), BF16), IN_HBM),
            near_own_grad=own,
            near_got_grad=got,
            landed=own,
            near_own_out=own,
            near_got_out=got,
            far_own_out=own,
            far_got_out=got,
        ),
        dict(
            near_n=block,
            far_n=block,
            near_c=block,
            far_c=block,
            hidden=kept,
            d_gate=kept,
            d_up=kept,
            near_grad=block,
            far_grad=block,
            near_out=block,
            far_out=block,
            far_got_grad=pltpu.VMEM((nb - 1, rows_each, width), BF16),
        ),
        36 * nb * rows_each * width * units,
        collective_id,
    )


def attention_backward_rows(k, tag, i, length, kv):
    qkvp, dproj, datt, lse = k.of(tag).qkvp, k.of(tag).dproj, k.datt, k.of(tag).lse
    n = (i + 1) * Q_ROWS
    rows = slice(i * Q_ROWS, n)
    lane = lax.broadcasted_iota(jnp.int32, (Q_ROWS, PAD), 1)

    def one_head(h, carry):
        group = h // GROUP
        q_col = pl.ds(pl.multiple_of((4 * group + h % GROUP) * PAD, PAD), PAD)
        k_col = pl.ds(pl.multiple_of((4 * group + 2) * PAD, PAD), PAD)
        v_col = pl.ds(pl.multiple_of((4 * group + 3) * PAD, PAD), PAD)
        a_col = pl.ds(pl.multiple_of(h * PAD, PAD), PAD)
        q = qkvp[rows, q_col]
        keys = qkvp[0:n, k_col]
        do = datt[rows, a_col]
        row_lse = jnp.sum(jnp.where(lane == h, lse[rows, :], 0.0), axis=-1, keepdims=True)
        s = dot_nt(q, keys)
        row_ids = lax.broadcasted_iota(jnp.int32, (Q_ROWS, 1), 0) + i * Q_ROWS + 1
        limit = jnp.minimum(row_ids, length)
        col_ids = lax.broadcasted_iota(jnp.int32, (Q_ROWS, n), 1)
        s = jnp.where(col_ids < limit, s, NEGATIVE)
        p = jnp.exp2(s * (SCALE * LOG2E) - row_lse)
        dp = dot_nt(do, qkvp[0:n, v_col])
        inner = jnp.sum(p * dp, axis=-1, keepdims=True)
        ds = (p * (dp - inner)).astype(BF16)
        k.dv[group, 0:n, :] += dot_tn(p.astype(BF16), do)
        k.dk[group, 0:n, :] += dot_tn(ds, q)
        dq = dot_nn(ds, keys) * SCALE
        dproj[rows, q_col] = unrotate(k, dq, rows).astype(BF16)
        return carry

    lax.fori_loop(0, kv * GROUP, one_head, 0)


def unrotate(k, grad, rows):
    return grad * k.cos_t[rows, :] - swap_halves(grad) * k.sin_t[rows, :]


class Scatter:
    def __init__(self, k, n_z, blk):
        d = lax.axis_index("dp")
        self.k, self.peers, self.other_x = k, z_peers(n_z), permuted("dp", 1)
        self.order = [(which, i) for which in (2, 0, 1) for i in z_order(n_z) + [0]]

        def rows(owner):
            return pl.ds(pl.multiple_of(owner * blk, 16), blk)

        owners = {i: lax.rem(d + 2 * i, 2 * n_z) for i in range(n_z)}
        self.rows = {i: rows(owner) for i, owner in owners.items()}
        self.rows_other = {i: rows(owner ^ 1) for i, owner in owners.items()}
        self.z, self.extra, self.blank = d // 2, {}, []
        self.joined = n_z == 4
        if self.joined:
            k.zeros[...] = jnp.zeros_like(k.zeros)
            for end, i in ((self.z == 0, 1), (self.z == 3, 3)):
                for which in range(3):
                    sem = k.local_sem.at[k.next_local]
                    k.next_local += 1
                    copy = pltpu.make_async_copy(k.zeros, k.ffn_sums.at[which, i], sem)
                    pl.when(end)(copy.start)
                    self.blank.append((end, copy))
        self.sent, self.slots = [None] * EARLY, [None] * SLOTS
        self.next_arrival = 0

    def send(self):
        if len(self.sent) < len(self.order):
            which, i = self.order[len(self.sent)]
            self.sent.append(
                self.k.remote(
                    self.k.grads.at[which, self.rows_other[i]],
                    self.k.x_got.at[which, i],
                    self.other_x,
                )
            )

    def pump(self):
        if self.next_arrival == len(self.order):
            return False
        k, n = self.k, self.next_arrival
        which, i = self.order[n]
        self.next_arrival += 1
        own = k.local(k.grads.at[which, self.rows[i]], k.staged.at[0])
        if n < EARLY:
            other = k.local(k.early.at[n], k.staged.at[1])
        else:
            self.sent[n].wait_recv()
            self.send()
            other = k.local(k.x_got.at[which, i], k.staged.at[1])
        slot = n % SLOTS
        if self.slots[slot] is not None:
            self.slots[slot]()
        own.wait()
        other.wait()
        held = k.staged[0, :, :].astype(F32) + k.staged[1, :, :].astype(F32)
        k.narrow[slot, :, :] = held.astype(BF16)
        z = self.z
        if i and self.joined:
            sends = receives = None
            if i == 2:
                for extra in self.extra[which]:
                    extra.wait_recv()

                @pl.when((z == 1) | (z == 2))
                def _():
                    copy = pltpu.make_async_copy(
                        k.extra.at[which], k.staged.at[0], k.local_sem.at[k.next_local]
                    )
                    copy.start()
                    copy.wait()
                    k.narrow[slot, :, :] = (held + k.staged[0, :, :].astype(F32)).astype(BF16)

                k.next_local += 1
            elif i == 1:
                sends, receives = z < 3, z > 0
                past, gets, neighbour = z == 3, z == 2, self.peers[3]
            else:
                sends, receives = z > 0, z < 3
                past, gets, neighbour = z == 0, z == 1, self.peers[1]
            copies = [
                k.remote(k.narrow.at[slot], k.ffn_sums.at[which, i], self.peers[i], sends, receives)
            ]
            if i != 2:
                copies.append(
                    k.remote(k.narrow.at[slot], k.extra.at[which], neighbour, past, gets)
                )
                self.extra.setdefault(which, []).append(copies[1])

            def wait(copies=copies):
                for copy in copies:
                    copy.wait_send()

            self.slots[slot] = wait
        elif i:
            remote = k.remote(k.narrow.at[slot], k.ffn_sums.at[which, i], self.peers[i])
            self.slots[slot] = remote.wait_send
        else:
            self.slots[slot] = k.store(k.narrow.at[slot], k.ffn_sums.at[which, 0])
        return True


def attention_backward_body(nb, rows_each, kv, n_z, blk, k):
    d = lax.axis_index("dp")
    z, x = d // 2, lax.rem(d, 2)
    local = lax.rem(lax.axis_index("tensor"), nb)
    seq_len = nb * rows_each
    per_block = rows_each // Q_ROWS
    over = permuted("tensor", nb)
    other_x = permuted("dp", 1)
    peers = half_peers(nb)
    own_a = k.local(k.own_a, k.near_a.at[0])
    k.load_refs(k.hbm.w_out, k.w_out)
    k.load_refs(k.hbm.cos_t, k.cos_t)
    k.load_refs(k.hbm.sin_t, k.sin_t)
    for tag in (NEAR, FAR):
        k.load_refs(k.hbm.of(tag).qkvp, k.of(tag).qkvp)
        k.load_refs(k.hbm.of(tag).lse, k.of(tag).lse)
    late = [k.local(k.hbm.w_qkv, k.w_qkv), k.local(k.hbm.spread, k.spread)]
    for tag in (NEAR, FAR):
        late.append(k.local(k.hbm.of(tag).att, k.of(tag).att))
        late.append(k.local(k.hbm.of(tag).normed, k.of(tag).normed))
    tensor_peers, dp_peers = all_peers(2 * n_z, 2 * nb)
    k.meet(tensor_peers + dp_peers)
    far_first = [
        k.remote(k.own_a.at[rows_of(c)], k.far_a.at[0, rows_of(c)], over)
        for c in range(per_block)
    ]
    near_copies = [k.remote(k.own_a, k.near_a.at[r], peer) for r, peer in peers]
    landing, near_landing = [], []
    scatter = Scatter(k, n_z, blk)
    for _ in range(WINDOW):
        scatter.send()
    own_a.wait()
    k.ready()
    for copy in near_copies:
        copy.wait_recv()
    for tag, length in ((NEAR, k.lengths[0]), (FAR, k.lengths[1])):
        blocks, parts, dproj = k.of(tag).a, k.of(tag).parts, k.of(tag).dproj
        k.dk[...] = jnp.zeros_like(k.dk)
        k.dv[...] = jnp.zeros_like(k.dv)
        for c in range(per_block):
            rows = slice(c * Q_ROWS, (c + 1) * Q_ROWS)
            if tag == FAR:
                far_first[c].wait_recv()
                passed = [
                    k.remote(blocks.at[0, rows_of(c)], blocks.at[r, rows_of(c)], peer)
                    for r, peer in peers
                ]
                for copy in passed:
                    copy.wait_recv()
            for b in range(nb):
                i = b * per_block + c
                k.datt[i * Q_ROWS : (i + 1) * Q_ROWS, :] = dot_nn(
                    blocks[local ^ b, rows, :], k.w_out[...]
                ).astype(BF16)
                attention_backward_rows(k, tag, i, length, kv)
                scatter.pump()
        for j in range(kv):
            k_col = slice((4 * j + 2) * PAD, (4 * j + 3) * PAD)
            v_col = slice((4 * j + 3) * PAD, (4 * j + 4) * PAD)
            for i in range(seq_len // Q_ROWS):
                rows = slice(i * Q_ROWS, (i + 1) * Q_ROWS)
                dproj[rows, k_col] = unrotate(k, k.dk[j, rows, :] * SCALE, rows).astype(BF16)
                dproj[rows, v_col] = k.dv[j, rows, :].astype(BF16)
        for copy in late:
            copy.wait()
        late = []
        for c in range(per_block):
            rows = slice(c * Q_ROWS, (c + 1) * Q_ROWS)
            for b in range(nb):
                i = b * per_block + c
                part = dot_nt(dproj[i * Q_ROWS : (i + 1) * Q_ROWS, :], k.w_qkv[...])
                parts[local ^ b, rows, :] = part.astype(BF16)
            if tag == NEAR:
                for r, peer in peers:
                    near_landing.append(
                        k.remote(parts.at[r, rows_of(c)], k.near_got.at[r - 1, rows_of(c)], peer)
                    )
            else:
                copies = [
                    k.remote(parts.at[r, rows_of(c)], k.far_got.at[r - 1, rows_of(c)], peer)
                    for r, peer in peers
                ]
                total = parts[0, rows, :].astype(F32)
                for r, copy in enumerate(copies):
                    copy.wait_recv()
                    total = total + k.far_got[r, rows, :].astype(F32)
                parts[0, rows, :] = total.astype(BF16)
                landing.append(k.remote(parts.at[0, rows_of(c)], k.landed.at[rows_of(c)], over))
        if tag == NEAR:
            k.store(parts.at[0], k.near_own)
        scatter.pump()
    width = k.w_qkv.shape[0]
    arriving = []
    for which in range(kv + 1):

        def chunk(c, carry):
            cols = pl.ds(pl.multiple_of(c * G_COLS, G_COLS), G_COLS)
            total = None
            if which == 0:
                wide = k.near_att.shape[1]
                for tag in (NEAR, FAR):
                    for r in range(nb):
                        start = pl.multiple_of((local ^ r) * rows_each, rows_each)
                        term = dot_tn(
                            k.of(tag).a[r, :, cols], k.of(tag).att[pl.ds(start, rows_each), :]
                        )
                        total = term if total is None else total + term
                compact = dot_nt(total.astype(BF16), k.spread[:, :wide])
            else:
                part = slice((which - 1) * G_PAD, which * G_PAD)
                total = dot_tn(k.near_normed[:, cols], k.near_dproj[:, part])
                total += dot_tn(k.far_normed[:, cols], k.far_dproj[:, part])
                compact = dot_nt(total.astype(BF16), k.spread[...])
            compact = compact.astype(BF16)
            for b in range(G_COLS // blk):
                owner = c * (G_COLS // blk) + b
                shift = lax.rem(owner // 2 + n_z - z, n_z)
                value = compact[b * blk : (b + 1) * blk, :]

                @pl.when(x == lax.rem(owner, 2))
                def _():
                    k.same[which, shift, :, :] = value

                @pl.when(x != lax.rem(owner, 2))
                def _():
                    k.other[which, shift, :, :] = value

            return carry

        lax.fori_loop(0, width // G_COLS, chunk, 0)
        arriving.append(k.remote(k.other.at[which], k.arrived.at[which], other_x))
        if which == 0:
            k.remote(k.far_out, k.out_landed, over)
        scatter.pump()
    while scatter.pump():
        pass
    for end, copy in scatter.blank:
        pl.when(end)(copy.wait)
    for which in range(kv + 1):
        arriving[which].wait_recv()
        for i in z_order(n_z) + [0]:
            held = k.same[which, i, :, :].astype(F32) + k.arrived[which, i, :, :].astype(F32)
            k.same[which, i, :, :] = held.astype(BF16)
            if i:
                k.remote(k.same.at[which, i], k.sums.at[which, i], scatter.peers[i])
            else:
                k.store(k.same.at[which, 0], k.sums.at[which, 0])
    for copy in landing + near_landing:
        copy.wait_recv()
    k.flush(k.near_got, k.hbm.near_got)
    loads = [k.local(k.landed, k.near_a.at[0]), k.local(k.tokens, k.near_a.at[1])]
    for copy in loads:
        copy.wait()

    def gain_rows(i, carry):
        rows = pl.ds(pl.multiple_of(i * 32, 32), 32)
        dn = k.near_parts[0, rows, :].astype(F32) + k.near_a[0, rows, :].astype(F32)
        for r in range(nb - 1):
            dn = dn + k.near_got[r, rows, :].astype(F32)
        v = k.near_a[1, rows, :].astype(F32)
        inv = lax.rsqrt(jnp.mean(v * v, axis=-1, keepdims=True) + NORM_EPSILON)
        return carry + jnp.sum(dn * v * inv, axis=0, keepdims=True)

    t = lax.axis_index("tensor")
    k.first[t, 0:1, :] = lax.fori_loop(0, rows_each // 32, gain_rows, jnp.zeros((1, width), F32))
    k.first[t, 1:2, :] = k.gain_part[...]
    gain_copies = share(k, k.first, t, tensor_peers)
    k.second[d, :, :] = sum_slots(k.first, gain_copies)
    gain_copies = share(k, k.second, d, dp_peers)
    k.gain_sums[...] = sum_slots(k.second, gain_copies)


def attention_backward(
    attention_grad, tokens, gain_part, lengths, fwd, grads, early, far_out, tables, spread, nb, n_z, collective_id
):
    rows_each, width = attention_grad.shape
    seq_len = nb * rows_each
    w_qkv, w_out = fwd["w_qkv"], fwd["w_out"]
    kv = w_qkv.shape[1] // G_PAD
    heads = kv * GROUP
    blk = width // (2 * n_z)
    units = grads.shape[2]
    sds = jax.ShapeDtypeStruct
    inputs = dict(
        lengths=(lengths, IN_SMEM),
        own_a=(attention_grad, IN_HBM),
        w_qkv=(w_qkv, LOAD),
        w_out=(w_out, LOAD),
        cos_t=(tables[0], LOAD),
        sin_t=(tables[1], LOAD),
        spread=(spread, LOAD),
        grads=(grads, IN_HBM),
        early=(early, IN_HBM),
        far_out=(far_out, IN_HBM),
        tokens=(tokens, IN_HBM),
        gain_part=(gain_part, IN_VMEM),
    )
    for tag in (NEAR, FAR):
        for key in ("qkvp", "lse", "att", "normed"):
            inputs[tag + key] = (fwd[tag + key], LOAD)
    block = pltpu.VMEM((nb, rows_each, width), BF16)
    sums = sds((kv + 1, n_z, blk, G_COLS), BF16)
    own = (sds((rows_each, width), BF16), IN_HBM)
    return frame_call(
        functools.partial(attention_backward_body, nb, rows_each, kv, n_z, blk),
        "attention_backward",
        inputs,
        dict(
            near_own=own,
            near_got=(sds((nb - 1, rows_each, width), BF16), FLUSH),
            landed=own,
            out_landed=own,
            gain_sums=(sds((2, width), F32), IN_VMEM),
            sums=(sums, IN_HBM),
            x_got=(sds((3, n_z, blk, units), BF16), IN_HBM),
            ffn_sums=(sds((3, n_z, blk, units), BF16), IN_HBM),
            extra=(sds((3, blk, units), BF16), IN_HBM),
        ),
        dict(
            near_a=block,
            far_a=block,
            near_parts=block,
            far_parts=block,
            far_got=pltpu.VMEM((nb - 1, rows_each, width), BF16),
            near_dproj=pltpu.VMEM((seq_len, kv * G_PAD), BF16),
            far_dproj=pltpu.VMEM((seq_len, kv * G_PAD), BF16),
            datt=pltpu.VMEM((seq_len, heads * PAD), BF16),
            dk=pltpu.VMEM((kv, seq_len, PAD), F32),
            dv=pltpu.VMEM((kv, seq_len, PAD), F32),
            same=pltpu.VMEM(sums.shape, BF16),
            other=pltpu.VMEM(sums.shape, BF16),
            arrived=pltpu.VMEM(sums.shape, BF16),
            staged=pltpu.VMEM((2, blk, units), BF16),
            zeros=pltpu.VMEM((blk, units), BF16),
            first=pltpu.VMEM((2 * nb, 2, width), F32),
            second=pltpu.VMEM((2 * n_z, 2, width), F32),
            narrow=pltpu.VMEM((SLOTS, blk, units), BF16),
        ),
        8 * seq_len * width * (kv * G_PAD + heads * PAD) + heads * seq_len * seq_len * 20 * 256,
        collective_id,
        n_sems=12 * n_z + 48,
    )


def all_peers(n_dp, n_t):
    d, t = lax.axis_index("dp"), lax.axis_index("tensor")
    return (
        [{"tensor": lax.rem(t + i, n_t)} for i in range(1, n_t)],
        [{"dp": lax.rem(d + i, n_dp)} for i in range(1, n_dp)],
    )


def share(k, buffer, me, peers):
    return [k.remote(buffer.at[me], buffer.at[me], peer) for peer in peers]


def sum_slots(buffer, copies):
    for copy in copies:
        copy.wait_recv()
    total = buffer[0, :, :]
    for i in range(1, len(copies) + 1):
        total = total + buffer[i, :, :]
    return total


class Master:
    def __init__(self, refs, at, rows, cols, number, gradient, gradient_refs):
        self.refs, self.at, self.rows, self.cols = refs, at, rows, cols
        self.number, self.gradient, self.gradient_refs = number, gradient, gradient_refs


def moments_body(kv, n_z, k):
    correct_one = 1.0 / (1.0 - BETA_ONE**STEP)
    correct_two = 1.0 / (1.0 - BETA_TWO**STEP)
    row = lax.broadcasted_iota(jnp.int32, (8, PAD), 0)
    lane = lax.broadcasted_iota(jnp.int32, (8, PAD), 1)

    def z_sum(ref, which, rows, cols=slice(None)):
        total = ref[which, 0, rows, cols].astype(F32)
        for i in range(1, n_z):
            total = total + ref[which, i, rows, cols].astype(F32)
        return total

    def parts(h, m):
        return [
            (h.weight, m.weight),
            (h.first, m.first),
            (h.second, m.second),
            (h.next_first, m.next_first),
            (h.next_second, m.next_second),
            (h.update, m.update),
        ]

    gate_up = parts(k.hbm.of(GATE_UP), k.of(GATE_UP))
    down = parts(k.hbm.of(DOWN), k.of(DOWN))
    qkv = parts(k.hbm.of(QKV_), k.of(QKV_))
    out = parts(k.hbm.of(OUT), k.of(OUT))
    gains = parts(k.hbm.of(GAINS), k.of(GAINS))
    cols_out = k.of(OUT).weight.shape[1]
    units = []
    for which in range(2):
        rows, cols = k.of(GATE_UP).weight.shape[1:]
        units.append(
            Master(
                gate_up,
                (which,),
                rows,
                cols,
                2 + which,
                lambda at, which=which: z_sum(k.ffn_sums, which, at),
                [(k.hbm.ffn_sums.at[which], k.ffn_sums.at[which])],
            )
        )
    units.append(
        Master(
            down,
            (),
            *k.of(DOWN).weight.shape,
            4,
            lambda at: z_sum(k.ffn_sums, 2, at),
            [(k.hbm.ffn_sums.at[2], k.ffn_sums.at[2])],
        )
    )
    units.append(
        Master(
            qkv,
            (),
            *k.of(QKV_).weight.shape,
            0,
            lambda at: jnp.concatenate([z_sum(k.sums, 1 + j, at) for j in range(kv)], axis=1),
            [(k.hbm.sums, k.sums)],
        )
    )
    units.append(
        Master(
            out,
            (),
            *k.of(OUT).weight.shape,
            1,
            lambda at: z_sum(k.sums, 0, at, slice(0, cols_out)),
            [],
        )
    )
    for which in range(2):
        units.append(
            Master(
                gains,
                (which,),
                1,
                k.of(GAINS).weight.shape[2],
                5 + which,
                lambda at, which=which: k.gain_sum[which, at, :],
                [],
            )
        )
    loads = []
    for unit in units:
        pairs = list(unit.gradient_refs)
        for source, target in unit.refs[:3]:
            pairs.append((source.at[unit.at], target.at[unit.at]) if unit.at else (source, target))
        loads.append([k.local(source, target) for source, target in pairs])
    squares = jnp.zeros((8, PAD), F32)
    for unit, copies in zip(units, loads):
        for copy in copies:
            copy.wait()
        weight, first, second, next_first, next_second, direction = [ref for _, ref in unit.refs]
        tile = unit.rows if unit.rows % 32 else 32

        def one(i, carry):
            rows = pl.ds(pl.multiple_of(i * tile, tile) if unit.rows > tile else 0, tile)
            at = unit.at + (rows, slice(None))
            g = unit.gradient(rows)
            w = weight[at]
            moment = BETA_ONE * first[at] + (1.0 - BETA_ONE) * g
            square = BETA_TWO * second[at] + (1.0 - BETA_TWO) * g * g
            next_first[at] = moment
            next_second[at] = square
            update = (moment * correct_one) / (
                jnp.sqrt(square * correct_two) + ADAM_EPSILON
            ) + WEIGHT_DECAY * w
            direction[at] = update
            return (
                carry[0] + jnp.sum(w * w, axis=0, keepdims=True),
                carry[1] + jnp.sum(update * update, axis=0, keepdims=True),
            )

        zero = jnp.zeros((1, unit.cols), F32)
        w_sum, u_sum = lax.fori_loop(0, unit.rows // tile, one, (zero, zero))
        w_sum = jnp.sum(w_sum, axis=1, keepdims=True)
        u_sum = jnp.sum(u_sum, axis=1, keepdims=True)
        mark = lane == unit.number
        squares += jnp.where(mark & (row == 0), w_sum, 0.0)
        squares += jnp.where(mark & (row == 1), u_sum, 0.0)
        for target, source in unit.refs[3:]:
            if unit.at:
                k.store(source.at[unit.at], target.at[unit.at])
            else:
                k.store(source, target)
    k.squares[...] = squares


def moments(weights, firsts, seconds, ffn_sums, sums, gain_sum, kv, n_z):
    inputs, outputs = {}, {}
    sds = jax.ShapeDtypeStruct
    names = (GATE_UP, DOWN, QKV_, OUT, GAINS)
    for key, weight, first, second in zip(names, weights, firsts, seconds):
        shape = (sds(weight.shape, F32), FLUSH)
        for table, prefix in (
            (dict(weight=(weight, LOAD), first=(first, LOAD), second=(second, LOAD)), inputs),
            (dict(next_first=shape, next_second=shape, update=shape), outputs),
        ):
            prefix.update({key + part: entry for part, entry in table.items()})
    inputs.update(
        ffn_sums=(ffn_sums, LOAD), sums=(sums, LOAD), gain_sum=(gain_sum, IN_VMEM)
    )
    outputs.update(squares=(sds((8, PAD), F32), IN_VMEM))
    return frame_call(
        functools.partial(moments_body, kv, n_z),
        "moments",
        inputs,
        outputs,
        {},
        0,
        None,
        n_sems=64,
    )


def sum_all_body(n_dp, n_t, k):
    d, t = lax.axis_index("dp"), lax.axis_index("tensor")
    tensor_peers, dp_peers = all_peers(n_dp, n_t)
    k.first[t, :, :] = k.value[...]
    k.meet(tensor_peers + dp_peers)
    copies = share(k, k.first, t, tensor_peers)
    k.second[d, :, :] = sum_slots(k.first, copies)
    copies = share(k, k.second, d, dp_peers)
    k.total[...] = sum_slots(k.second, copies)


def sum_all(value, n_dp, n_t, collective_id):
    return frame_call(
        functools.partial(sum_all_body, n_dp, n_t),
        "sum_everywhere",
        dict(value=(value, IN_VMEM)),
        dict(total=(jax.ShapeDtypeStruct(value.shape, F32), IN_VMEM)),
        dict(
            first=pltpu.VMEM((n_t,) + value.shape, F32),
            second=pltpu.VMEM((n_dp,) + value.shape, F32),
        ),
        0,
        collective_id,
        n_sems=n_dp + n_t,
    )["total"]


def rms_norm(values, gain_row):
    return (
        values
        * lax.rsqrt(jnp.mean(values * values, axis=-1, keepdims=True) + NORM_EPSILON)
        * gain_row
    )


def rotary_tables():
    half = HEAD // 2
    frequency = ROPE_THETA ** (-(jnp.arange(half, dtype=F32) * (2.0 / HEAD)))
    angles = jnp.arange(SEQ_LEN, dtype=F32)[:, None] * frequency[None, :]
    cosine, sine = jnp.cos(angles), jnp.sin(angles)
    empty = jnp.zeros((SEQ_LEN, PAD - HEAD), F32)
    return (
        jnp.concatenate([cosine, cosine, empty], axis=1),
        jnp.concatenate([-sine, sine, empty], axis=1),
    )


def shards(
    tokens,
    cotangent,
    lengths,
    qkv_weight,
    out_weight,
    gate_up_weight,
    down_weight,
    norm_gains,
    qkv_first,
    out_first,
    gate_up_first,
    down_first,
    gains_first,
    qkv_second,
    out_second,
    gate_up_second,
    down_second,
    gains_second,
):
    rows_each, width = tokens.shape
    n_t = lax.axis_size("tensor")
    n_dp = lax.axis_size("dp")
    n_z = n_dp // 2
    nb = n_t // 2
    t = lax.axis_index("tensor")
    d = lax.axis_index("dp")
    mine = t // nb
    lengths = jnp.stack([lengths[mine], lengths[1 - mine]])
    spread = spread_matrix().astype(BF16)
    blk = qkv_weight.shape[0]
    kv = qkv_weight.shape[1] // G_COLS

    gain_cols = norm_gains.shape[1]
    gain_start = (d * n_t + t) * gain_cols
    gain_rows = lax.dynamic_update_slice(
        jnp.zeros((2, width), F32),
        norm_gains.astype(BF16).astype(F32),
        (0, gain_start),
    )
    out_half = out_weight.astype(BF16).T
    ffn_half = jnp.concatenate(
        [gate_up_weight.astype(BF16), down_weight.astype(BF16).T[None]], axis=0
    )
    halves = (qkv_weight.astype(BF16), out_half, ffn_half)
    tables = rotary_tables()
    fwd = opening(
        tokens, cotangent, lengths, gain_rows, halves, tables, spread, n_t, n_z, 0
    )
    inputs = tokens.astype(F32)
    attention_gain, feedforward_gain = fwd["gain_sum"][0:1], fwd["gain_sum"][1:2]
    residual = fwd["residual"]

    ff = feed_forward(fwd["normed_two"], cotangent, fwd["c_far"], fwd["w_ffn"], nb, n_z, 2)

    def total(*arrays):
        result = 0.0
        for array in arrays:
            array = array.astype(F32)
            result = result + (array if array.ndim == 2 else jnp.sum(array, axis=0))
        return result

    normed_two_grad = total(ff["near_own_grad"], ff["near_got_grad"], ff["landed"])
    _, norm_pull = jax.vjp(rms_norm, residual, feedforward_gain)
    residual_part, ffn_gain_grad = norm_pull(normed_two_grad)
    residual_grad = cotangent.astype(F32) + residual_part
    far_out = total(ff["far_own_out"], ff["far_got_out"]).astype(BF16)
    bwd = attention_backward(
        residual_grad.astype(BF16),
        tokens,
        ffn_gain_grad,
        lengths,
        fwd,
        ff["grads"],
        ff["early"],
        far_out,
        tables,
        spread,
        nb,
        n_z,
        3,
    )
    normed_grad = total(bwd["near_own"], bwd["near_got"], bwd["landed"])
    _, first_pull = jax.vjp(rms_norm, inputs, attention_gain)
    input_part, _ = first_pull(normed_grad)
    grad_tokens = residual_grad + input_part
    layer_out = (residual + total(ff["near_own_out"], ff["near_got_out"], bwd["out_landed"])).astype(
        BF16
    )
    gain_sum = lax.dynamic_slice(bwd["gain_sums"], (0, gain_start), (2, gain_cols))

    def lift(gains):
        return gains[:, None, :]

    done = moments(
        (gate_up_weight, down_weight.T, qkv_weight, out_weight.T, lift(norm_gains)),
        (gate_up_first, down_first.T, qkv_first, out_first.T, lift(gains_first)),
        (gate_up_second, down_second.T, qkv_second, out_second.T, lift(gains_second)),
        bwd["ffn_sums"],
        bwd["sums"],
        lift(gain_sum),
        kv,
        n_z,
    )
    norms = jnp.sqrt(sum_all(done["squares"], n_dp, n_t, 5))
    scale = LEARN_RATE * (norms[0, :7] / norms[1, :7])
    first, second, update = (
        dict(
            gate_up=done[GATE_UP + part],
            down=done[DOWN + part].T,
            qkv=done[QKV_ + part],
            out=done[OUT + part].T,
            gains=done[GAINS + part][:, 0, :],
        )
        for part in ("next_first", "next_second", "update")
    )
    new = (
        qkv_weight - scale[0] * update["qkv"],
        out_weight - scale[1] * update["out"],
        gate_up_weight - scale[2:4, None, None] * update["gate_up"],
        down_weight - scale[4] * update["down"],
        norm_gains - scale[5:7, None] * update["gains"],
    )
    names = ("qkv", "out", "gate_up", "down", "gains")
    return (
        layer_out,
        grad_tokens,
        *new,
        *[first[key] for key in names],
        *[second[key] for key in names],
        norms[0, :7],
        norms[1, :5],
        norms[1, 5:7],
    )


def solution(mesh):
    rows = P(("dp", "tensor"), None)
    gains = P(None, ("dp", "tensor"))
    weights = (P("dp", "tensor"), P("tensor", "dp"), P(None, "dp", "tensor"), P("tensor", "dp"), gains)
    in_specs = (rows, rows, P("dp")) + weights * 3
    out_specs = (rows, rows) + weights * 3 + (P(), P(), P())
    return jax.shard_map(shards, mesh=mesh, in_specs=in_specs, out_specs=out_specs, check_vma=False)
```

```python
import functools

import jax
import jax.numpy as jnp
import numpy as np
from jax import lax
from jax.experimental import pallas as pl
from jax.experimental.pallas import tpu as pltpu
from jax.sharding import PartitionSpec as P

HEAD = 96
PAD = 128
SEQ_LEN = 1024
SEQS_DEV = 2
STEP = 10
GROUP = 2

NORM_EPSILON = 1e-05
ROPE_THETA = 100000.0
BETA_ONE = 0.9
BETA_TWO = 0.999
ADAM_EPSILON = 1e-06
WEIGHT_DECAY = 0.01
LEARN_RATE = 0.3
NEGATIVE = -1e30
LOG2E = 1.4426950408889634
SCALE = HEAD ** (-0.5)
Q_ROWS = 256
G_COLS = 4 * HEAD
G_PAD = 4 * PAD
VMEM_LIMIT = 56 << 20

F32 = jnp.float32
BF16 = jnp.bfloat16
VM = pl.BlockSpec(memory_space=pltpu.VMEM)
SM = pl.BlockSpec(memory_space=pltpu.SMEM)
ANY = pl.BlockSpec(memory_space=pl.ANY)
MESH = pl.DeviceIdType.MESH
IN_VMEM, IN_SMEM, IN_HBM, LOAD, FLUSH = range(5)
NEAR, FAR = "near_", "far_"
GATE_UP, DOWN, QKV_, OUT, GAINS = "gate_up_", "down_", "qkv_", "out_", "gains_"
WINDOW, SLOTS, EARLY = 3, 4, 2
HBM = "any_"


def dot_nn(a, b):
    return lax.dot_general(a, b, (((1,), (0,)), ((), ())), preferred_element_type=F32)


def dot_nt(a, b):
    return lax.dot_general(a, b, (((1,), (1,)), ((), ())), preferred_element_type=F32)


def dot_tn(a, b):
    return lax.dot_general(a, b, (((0,), (0,)), ((), ())), preferred_element_type=F32)


def cost(flops, moved):
    return pl.CostEstimate(flops=int(flops), bytes_accessed=int(moved), transcendentals=0)


def spread_matrix():
    source = lax.broadcasted_iota(jnp.int32, (G_COLS, G_PAD), 0)
    target = lax.broadcasted_iota(jnp.int32, (G_COLS, G_PAD), 1)
    return ((target // PAD) * HEAD + target % PAD == source) & (target % PAD < HEAD)


def swap_halves(values):
    lane = lax.broadcasted_iota(jnp.int32, values.shape, 1)
    return jnp.where(
        lane < HEAD // 2,
        pltpu.roll(values, PAD - HEAD // 2, 1),
        pltpu.roll(values, HEAD // 2, 1),
    )


def permuted(axis, bit):
    return {axis: lax.axis_index(axis) ^ bit}


class Remote:
    def __init__(self, copy, sends=None, receives=None):
        self.copy, self.sends, self.receives = copy, sends, receives
        self.landed = self.left = False

    @staticmethod
    def only(condition, action):
        if condition is None:
            action()
        else:
            pl.when(condition)(action)

    def start(self):
        self.only(self.sends, self.copy.start)

    def wait_recv(self):
        if not self.landed:
            self.only(self.receives, self.copy.wait_recv)
        self.landed = True

    def wait_send(self):
        if not self.left:
            self.only(self.sends, self.copy.wait_send)
        self.left = True


class Side:
    def __init__(self, refs, side):
        self.refs, self.side = refs, side

    def __getattr__(self, name):
        return self.refs[self.side + name]

    def of(self, side):
        return Side(self.refs, self.side + side)


class Frame:
    def __init__(self, names, refs):
        self.refs = dict(zip(names, refs))
        self.loading, self.remotes, self.storing = [], [], []
        self.next_local = 0
        self.hbm = Side(self.refs, HBM)

    def __getattr__(self, name):
        return self.refs[name]

    def of(self, side):
        return Side(self.refs, side)

    def meet(self, peers):
        barrier = pltpu.get_barrier_semaphore()
        for peer in peers:
            pl.semaphore_signal(barrier, inc=1, device_id=peer, device_id_type=MESH)
        pl.semaphore_wait(barrier, len(peers))

    def local(self, source, target):
        copy = pltpu.make_async_copy(source, target, self.local_sem.at[self.next_local])
        self.next_local += 1
        copy.start()
        return copy

    def load_refs(self, source, target):
        self.loading.append(self.local(source, target))

    def ready(self):
        for copy in self.loading:
            copy.wait()
        self.loading = []

    def store(self, source, target):
        pending = [self.local(source, target)]

        def wait():
            if pending:
                pending.pop().wait()

        self.storing.append(wait)
        return wait

    def flush(self, source, target):
        self.store(source, target)

    def remote(self, source, target, peer, sends=None, receives=None):
        n = len(self.remotes)
        copy = pltpu.make_async_remote_copy(
            src_ref=source,
            dst_ref=target,
            send_sem=self.send_sem.at[n],
            recv_sem=self.recv_sem.at[n],
            device_id=peer,
            device_id_type=MESH,
        )
        self.remotes.append(Remote(copy, sends, receives))
        self.remotes[-1].start()
        return self.remotes[-1]

    def finish(self):
        for remote in self.remotes:
            remote.wait_send()
            remote.wait_recv()
        for wait in self.storing:
            wait()


def frame_call(body, name, inputs, outputs, scratch, flops, collective_id, n_sems=40):
    names, specs, arrays = [], [], []
    spec_of = {IN_VMEM: VM, IN_SMEM: SM, IN_HBM: ANY, LOAD: ANY, FLUSH: ANY}
    for key, (array, kind) in inputs.items():
        names.append(HBM + key if kind == LOAD else key)
        specs.append(spec_of[kind])
        arrays.append(array)
    out_specs, out_shapes = [], []
    for key, (shape, kind) in outputs.items():
        names.append(HBM + key if kind == FLUSH else key)
        out_specs.append(spec_of[kind])
        out_shapes.append(shape)
    shapes = []
    for table, kind_of in ((inputs, LOAD), (outputs, FLUSH)):
        for key, (array, kind) in table.items():
            if kind == kind_of:
                names.append(key)
                shapes.append(pltpu.VMEM(array.shape, array.dtype))
    for key, shape in scratch.items():
        names.append(key)
        shapes.append(shape)
    extra = {}
    for key in ("local_sem", "send_sem", "recv_sem"):
        if key == "local_sem" or collective_id is not None:
            names.append(key)
            shapes.append(pltpu.SemaphoreType.DMA((n_sems,)))
    if collective_id is not None:
        extra = dict(collective_id=collective_id, has_side_effects=True)

    def kernel(*refs):
        frame = Frame(names, refs)
        body(frame)
        frame.finish()

    moved = sum(a.size * a.dtype.itemsize for a in arrays)
    results = pl.pallas_call(
        kernel,
        out_shape=out_shapes,
        in_specs=specs,
        out_specs=out_specs,
        scratch_shapes=shapes,
        compiler_params=pltpu.CompilerParams(vmem_limit_bytes=VMEM_LIMIT, **extra),
        cost_estimate=cost(flops, moved),
        name=name,
    )(*arrays)
    return dict(zip(outputs, results))


def half_peers(nb):
    return [(r, permuted("tensor", r)) for r in range(1, nb)]


def rows_of(c):
    return pl.ds(c * Q_ROWS, Q_ROWS)


def bits_down(size):
    bits = []
    bit = size // 2
    while bit:
        bits.append(bit)
        bit //= 2
    return bits


def attention_rows(k, tag, i, length, kv):
    qkvp, att, lse = k.of(tag).qkvp, k.of(tag).att, k.of(tag).lse
    n = (i + 1) * Q_ROWS
    rows = slice(i * Q_ROWS, n)
    lane = lax.broadcasted_iota(jnp.int32, (Q_ROWS, PAD), 1)

    def one_head(h, log_totals):
        group = h // GROUP
        q_col = pl.ds(pl.multiple_of((4 * group + h % GROUP) * PAD, PAD), PAD)
        k_col = pl.ds(pl.multiple_of((4 * group + 2) * PAD, PAD), PAD)
        v_col = pl.ds(pl.multiple_of((4 * group + 3) * PAD, PAD), PAD)
        a_col = pl.ds(pl.multiple_of(h * PAD, PAD), PAD)
        s = dot_nt(qkvp[rows, q_col], qkvp[0:n, k_col])
        row_ids = lax.broadcasted_iota(jnp.int32, (Q_ROWS, 1), 0) + i * Q_ROWS + 1
        limit = jnp.minimum(row_ids, length)
        col_ids = lax.broadcasted_iota(jnp.int32, (Q_ROWS, n), 1)
        s = jnp.where(col_ids < limit, s, NEGATIVE)
        top = jnp.max(s, axis=-1, keepdims=True)
        e = jnp.exp2((s - top) * (SCALE * LOG2E))
        total = jnp.sum(e, axis=-1, keepdims=True)
        p = (e * (1.0 / total)).astype(BF16)
        att[rows, a_col] = dot_nn(p, qkvp[0:n, v_col]).astype(BF16)
        log_total = top * (SCALE * LOG2E) + jnp.log2(total)
        return jnp.where(lane == h, log_total, log_totals)

    lse[rows, :] = lax.fori_loop(0, kv * GROUP, one_head, jnp.zeros((Q_ROWS, PAD), F32))


def z_order(n_z):
    return sorted(range(1, n_z), key=lambda i: min(i, n_z - i))


def z_peers(n_z):
    d = lax.axis_index("dp")
    return {i: {"dp": lax.rem(d + 2 * i, 2 * n_z)} for i in range(1, n_z)}


class Stream:
    def __init__(self, k, source, place, paired=False):
        self.source, self.place, self.paired = source, place, paired
        d = lax.axis_index("dp")
        n_dp = lax.axis_size("dp")
        blk = source.shape[0]
        own = place(pl.ds(pl.multiple_of(d * blk, 16), blk))
        self.own, self.local = own, k.local(source, own)
        self.shifted = {}
        for i in range(n_dp // 2):
            if paired:
                start, size = lax.rem(d // 2 + n_dp // 2 - i, n_dp // 2) * (2 * blk), 2 * blk
            else:
                start, size = lax.rem(d + n_dp - 2 * i, n_dp) * blk, blk
            self.shifted[i] = place(pl.ds(pl.multiple_of(start, 16), size))
        self.along_x, self.sent = [], {}


class Gather:
    def __init__(self, k, streams, n_z):
        d = lax.axis_index("dp")
        self.k, self.streams, self.n_z = k, streams, n_z
        self.z = d // 2
        self.right = {"dp": lax.rem(d + 2, 2 * n_z)}
        self.left = {"dp": lax.rem(d + 2 * n_z - 2, 2 * n_z)}
        self.other_x = permuted("dp", 1)
        self.order = [(s, hop) for s in range(len(streams)) for hop in range(1, n_z)]
        self.next_arrival = 0

    def send(self, s, hop):
        if s >= len(self.streams) or hop in self.streams[s].sent:
            return
        stream = self.streams[s]
        z, n_z, far = self.z, self.n_z, hop - 1
        if stream.paired and not far:
            stream.local.wait()
            self.complete(s)
        pair = []
        for shift, peer, sends, receives in (
            (far, self.right, (z >= far) & (z < n_z - 1), z >= hop),
            ((n_z - far) % n_z, self.left, (z < n_z - far) & (z > 0), z < n_z - hop),
        ):
            block = stream.shifted[shift]
            source = block if far or stream.paired else stream.source
            pair.append(self.k.remote(source, block, peer, sends, receives))
        stream.sent[hop] = pair

    def own_along_x(self, s):
        stream = self.streams[s]
        stream.along_x.append(self.k.remote(stream.source, stream.own, self.other_x))

    def pump(self):
        if self.next_arrival == len(self.order):
            return
        s, hop = self.order[self.next_arrival]
        self.next_arrival += 1
        stream = self.streams[s]
        for copy in stream.sent[hop]:
            copy.wait_recv()
        if hop + 1 < self.n_z:
            self.send(s, hop + 1)
        if hop == min(2, self.n_z - 1):
            self.send(s + 1, 1)
        if not stream.paired:
            for shift, copy in zip((hop, self.n_z - hop), stream.sent[hop]):
                block = stream.shifted[shift]
                stream.along_x.append(
                    self.k.remote(block, block, self.other_x, copy.receives, copy.receives)
                )

    def complete(self, s):
        for copy in self.streams[s].along_x:
            copy.wait_recv()


def opening_body(nb, rows_each, kv, n_z, blk, k):
    t = lax.axis_index("tensor")
    local = lax.rem(t, nb)
    seq_len = nb * rows_each
    per_block = rows_each // Q_ROWS
    chunk = 32
    over, other_x = permuted("tensor", nb), permuted("dp", 1)
    peers, along_z = half_peers(nb), z_peers(n_z)
    near_x, far_x = k.near_x, k.far_x
    early = k.ffn_half.shape[2] // 4
    up_early, up_late = pl.ds(0, early), pl.ds(early, 3 * early)
    own_tokens = k.local(k.tokens, near_x.at[0])
    k.load_refs(k.hbm.qkv_w, k.qkv_w)
    k.load_refs(k.hbm.out_w, k.out_w)
    k.load_refs(k.hbm.gate_up_w, k.gate_up_w)
    k.load_refs(k.hbm.down_w, k.down_w)
    k.held[0, :, :] = k.gains[...]
    k.meet(list(along_z.values()) + [other_x, over] + [peer for _, peer in peers])

    stages = [permuted("tensor", bit) for bit in bits_down(2 * nb)] + [other_x]
    gain_copy = k.remote(k.held.at[0], k.got.at[0], stages[0])
    far_copy = k.remote(k.tokens, far_x.at[0], over)
    near_copies = [k.remote(k.tokens, near_x.at[r], peer) for r, peer in peers]
    k.ready()
    k.qkv_half[...] = k.qkv_w[...].astype(BF16)
    k.out_half[...] = k.out_w[...].astype(BF16)
    for i in range(2):
        k.ffn_half[i, :, :] = k.gate_up_w[i, :, :].astype(BF16)
    k.ffn_half[2, :, :] = k.down_w[...].astype(BF16)
    streams = [
        Stream(k, k.qkv_half, lambda rows: k.wq.at[rows]),
        Stream(k, k.out_half, lambda rows: k.wo.at[rows], True),
        Stream(k, k.ffn_half.at[1, :, up_early], lambda rows: k.w_ffn.at[1, rows, up_early], True),
        Stream(k, k.ffn_half.at[2], lambda rows: k.w_ffn.at[2, rows]),
        Stream(k, k.ffn_half.at[0], lambda rows: k.w_ffn.at[0, rows]),
        Stream(k, k.ffn_half.at[1, :, up_late], lambda rows: k.w_ffn.at[1, rows, up_late]),
    ]
    gather = Gather(k, streams, n_z)
    k.load_refs(k.hbm.cos_t, k.cos_t)
    k.load_refs(k.hbm.sin_t, k.sin_t)
    k.load_refs(k.hbm.spread, k.spread)
    gather.own_along_x(1)
    gather.own_along_x(0)
    gather.own_along_x(2)
    gather.send(0, 1)
    for stage in range(len(stages)):
        gain_copy.wait_recv()
        k.held[stage + 1, :, :] = k.held[stage, :, :] + k.got[stage, :, :]
        if stage + 1 < len(stages):
            gain_copy = k.remote(k.held.at[stage + 1], k.got.at[stage + 1], stages[stage + 1])
    last = len(stages)
    gain_copies = [
        k.remote(k.held.at[last], k.got.at[last + i - 1], along_z[i]) for i in range(1, n_z)
    ]
    for _ in range(2 * (n_z - 1)):
        gather.pump()
    for s in range(3, len(streams)):
        gather.own_along_x(s)
    total = k.held[last, :, :]
    for i, copy in enumerate(gain_copies):
        copy.wait_recv()
        total = total + k.got[last + i, :, :]
    k.gain_sum[...] = total
    gain_one, gain_two = k.gain_sum.at[0:1], k.gain_sum.at[1:2]
    far_copy.wait_recv()
    far_copies = [k.remote(far_x.at[0], far_x.at[r], peer) for r, peer in peers]
    own_tokens.wait()
    for copy in near_copies + far_copies:
        copy.wait_recv()

    def normalise(tag):
        for r in range(nb):
            base = (local ^ r) * rows_each

            def norm_rows(i, carry):
                rows = pl.ds(pl.multiple_of(i * chunk, chunk), chunk)
                v = k.of(tag).x[r, rows, :].astype(F32)
                inv = lax.rsqrt(jnp.mean(v * v, axis=-1, keepdims=True) + NORM_EPSILON)
                k.of(tag).normed[pl.ds(pl.multiple_of(base + i * chunk, chunk), chunk), :] = (
                    v * inv * gain_one[...]
                ).astype(BF16)
                return carry

            lax.fori_loop(0, rows_each // chunk, norm_rows, 0)
        k.flush(k.of(tag).normed, k.hbm.of(tag).normed)

    normalise(FAR)
    normalise(NEAR)
    for stream in streams:
        if not stream.paired:
            stream.local.wait()
    k.ready()
    for s, (source, target) in enumerate(((k.wq, k.w_qkv), (k.wo, k.w_out))):
        gather.complete(s)
        for g in range(-(-target.shape[1] // G_PAD)):
            wide = min(G_PAD, target.shape[1] - g * G_PAD)
            part = source[:, g * G_COLS : (g + 1) * G_COLS]
            target[:, g * G_PAD : g * G_PAD + wide] = dot_nn(
                part, k.spread[0 : part.shape[1], 0:wide]
            ).astype(BF16)
        k.flush(target, k.hbm.w_out if s else k.hbm.w_qkv)

    landing, waiting = [], []
    for tag, length in ((FAR, k.lengths[1]), (NEAR, k.lengths[0])):
        normed, qkvp = k.of(tag).normed, k.of(tag).qkvp
        parts, got = k.of(tag).parts, k.of(tag).got
        for i in range(seq_len // Q_ROWS):
            rows = slice(i * Q_ROWS, (i + 1) * Q_ROWS)
            for j in range(kv):
                proj = dot_nn(normed[rows, :], k.w_qkv[:, j * G_PAD : (j + 1) * G_PAD])
                for h in range(4):
                    part = proj[:, h * PAD : (h + 1) * PAD]
                    if h < 3:
                        part = part * k.cos_t[rows, :] + swap_halves(part) * k.sin_t[rows, :]
                    qkvp[rows, (4 * j + h) * PAD : (4 * j + h + 1) * PAD] = part.astype(BF16)
        k.flush(qkvp, k.hbm.of(tag).qkvp)
        gather.pump()
        for c in range(per_block):
            rows = slice(c * Q_ROWS, (c + 1) * Q_ROWS)
            for b in range(nb):
                i = b * per_block + c
                attention_rows(k, tag, i, length, kv)
                part = dot_nt(k.of(tag).att[i * Q_ROWS : (i + 1) * Q_ROWS, :], k.w_out[...])
                parts[local ^ b, rows, :] = part.astype(BF16)
                if waiting:
                    waiting.pop()()
                gather.pump()
            copies = [
                k.remote(parts.at[r, rows_of(c)], got.at[r - 1, rows_of(c)], peer)
                for r, peer in peers
            ]

            def complete(rows=rows, c=c, copies=copies, parts=parts, got=got, tag=tag):
                total = parts[0, rows, :].astype(F32)
                for r, copy in enumerate(copies):
                    copy.wait_recv()
                    total = total + got[r, rows, :].astype(F32)
                if tag == FAR:
                    parts[0, rows, :] = total.astype(BF16)
                    landing.append(
                        k.remote(parts.at[0, rows_of(c)], k.landed.at[rows_of(c)], over)
                    )
                    if c == per_block - 1:
                        k.remote(k.cotangent, k.c_far, over)
                else:
                    k.residual[rows, :] = near_x[0, rows, :].astype(F32) + total

            waiting.append(complete)
        k.flush(k.of(tag).att, k.hbm.of(tag).att)
        k.flush(k.of(tag).lse, k.hbm.of(tag).lse)
    waiting.pop()()
    for c in range(per_block):
        landing[c].wait_recv()

        def residual_rows(i, carry):
            rows = pl.ds(pl.multiple_of(c * Q_ROWS + i * chunk, chunk), chunk)
            v = k.residual[rows, :] + k.landed[rows, :].astype(F32)
            k.residual[rows, :] = v
            inv = lax.rsqrt(jnp.mean(v * v, axis=-1, keepdims=True) + NORM_EPSILON)
            k.normed_two[rows, :] = (v * inv * gain_two[...]).astype(BF16)
            return carry

        lax.fori_loop(0, Q_ROWS // chunk, residual_rows, 0)
    k.flush(k.residual, k.hbm.residual)
    k.flush(k.normed_two, k.hbm.normed_two)
    for _ in range(4 * (n_z - 1)):
        gather.pump()


def opening(tokens, cotangent, lengths, gains, weights, tables, spread, n_t, n_z, collective_id):
    rows_each, width = tokens.shape
    qkv_w, out_w, gate_up_w, down_w = weights
    blk = qkv_w.shape[0]
    n_dp = 2 * n_z
    nb = n_t // 2
    seq_len = nb * rows_each
    kv = qkv_w.shape[1] // G_COLS
    heads = kv * GROUP
    sds = jax.ShapeDtypeStruct
    normed = (sds((seq_len, width), BF16), FLUSH)
    qkvp = (sds((seq_len, kv * G_PAD), BF16), FLUSH)
    att = (sds((seq_len, heads * PAD), BF16), FLUSH)
    lse = (sds((seq_len, PAD), F32), FLUSH)
    block = pltpu.VMEM((nb, rows_each, width), BF16)
    others = pltpu.VMEM((nb - 1, rows_each, width), BF16)
    n_gain = len(bits_down(n_t)) + 1 + n_z - 1
    return frame_call(
        functools.partial(opening_body, nb, rows_each, kv, n_z, blk),
        "attention_forward",
        dict(
            tokens=(tokens, IN_HBM),
            cotangent=(cotangent, IN_HBM),
            lengths=(lengths, IN_SMEM),
            gains=(gains, IN_VMEM),
            qkv_w=(qkv_w, LOAD),
            out_w=(out_w, LOAD),
            gate_up_w=(gate_up_w, LOAD),
            down_w=(down_w, LOAD),
            cos_t=(tables[0], LOAD),
            sin_t=(tables[1], LOAD),
            spread=(spread, LOAD),
        ),
        dict(
            near_normed=normed,
            far_normed=normed,
            near_qkvp=qkvp,
            far_qkvp=qkvp,
            near_att=att,
            far_att=att,
            near_lse=lse,
            far_lse=lse,
            residual=(sds((rows_each, width), F32), FLUSH),
            normed_two=(sds((rows_each, width), BF16), FLUSH),
            w_qkv=(sds((blk * n_dp, kv * G_PAD), BF16), FLUSH),
            w_out=(sds((blk * n_dp, heads * PAD), BF16), FLUSH),
            w_ffn=(sds((3, blk * n_dp, gate_up_w.shape[2]), BF16), IN_HBM),
            c_far=(sds(cotangent.shape, BF16), IN_HBM),
            gain_sum=(sds(gains.shape, F32), IN_VMEM),
        ),
        dict(
            near_x=block,
            far_x=block,
            far_parts=block,
            near_parts=block,
            far_got=others,
            near_got=others,
            landed=pltpu.VMEM((rows_each, width), BF16),
            qkv_half=pltpu.VMEM(qkv_w.shape, BF16),
            out_half=pltpu.VMEM(out_w.shape, BF16),
            ffn_half=pltpu.VMEM((3,) + down_w.shape, BF16),
            wq=pltpu.VMEM((blk * n_dp, qkv_w.shape[1]), BF16),
            wo=pltpu.VMEM((blk * n_dp, out_w.shape[1]), BF16),
            held=pltpu.VMEM((n_gain + 1,) + gains.shape, F32),
            got=pltpu.VMEM((n_gain,) + gains.shape, F32),
        ),
        4 * seq_len * width * (kv * G_PAD + heads * PAD) + heads * seq_len * seq_len * 8 * 256,
        collective_id,
        n_sems=12 * n_z + 48,
    )


def feed_forward_body(nb, rows_each, n_z, k):
    over = permuted("tensor", nb)
    peers = half_peers(nb)
    per_block = rows_each // Q_ROWS
    w = k.w
    width = w.shape[1]
    blk = width // (2 * n_z)
    other_x = permuted("dp", 1)
    near_n, near_c, far_n, far_c = k.near_n, k.near_c, k.far_n, k.far_c
    own_n = k.local(k.own_n, near_n.at[0])
    own_c = k.local(k.own_c, near_c.at[0])
    k.load_refs(k.hbm.w, k.w)
    own_far_c = k.local(k.own_far_c, far_c.at[0])
    k.meet([over, other_x] + [peer for _, peer in peers])
    far_first = [
        k.remote(k.own_n.at[rows_of(c)], far_n.at[0, rows_of(c)], over) for c in range(per_block)
    ]
    n_copies = [k.remote(k.own_n, near_n.at[r], peer) for r, peer in peers]
    c_copies = [k.remote(k.own_c, near_c.at[r], peer) for r, peer in peers]
    far_c_copies = [k.remote(k.own_far_c, far_c.at[r], peer) for r, peer in peers]
    own_n.wait()
    own_c.wait()
    k.ready()

    def rows_step(side, r, c):
        rows = slice(c * Q_ROWS, (c + 1) * Q_ROWS)
        start = (0 if side == NEAR else nb * rows_each) + r * rows_each + c * Q_ROWS
        kept = slice(start, start + Q_ROWS)
        n = k.of(side).n[r, rows, :]
        gate = dot_nn(n, w[0])
        up = dot_nn(n, w[1])
        sig = 1.0 / (1.0 + jnp.exp(-gate))
        silu = gate * sig
        hid = (silu * up).astype(BF16)
        k.hidden[kept, :] = hid
        dh = dot_nn(k.of(side).c[r, rows, :], w[2])
        dg = (dh * up * sig * (1.0 + gate * (1.0 - sig))).astype(BF16)
        du = (dh * silu).astype(BF16)
        k.d_gate[kept, :] = dg
        k.d_up[kept, :] = du
        k.of(side).grad[r, rows, :] = (dot_nt(dg, w[0]) + dot_nt(du, w[1])).astype(BF16)
        k.of(side).out[r, rows, :] = dot_nt(hid, w[2]).astype(BF16)

    for r in range(nb):
        if r:
            n_copies[r - 1].wait_recv()
            c_copies[r - 1].wait_recv()
        for c in range(per_block):
            rows_step(NEAR, r, c)
        for part, own, got in (
            (k.near_grad.at[r], k.near_own_grad, k.near_got_grad),
            (k.near_out.at[r], k.near_own_out, k.near_got_out),
        ):
            if r:
                k.remote(part, got.at[r - 1], peers[r - 1][1])
            else:
                k.store(part, own)
    own_far_c.wait()
    for copy in far_c_copies:
        copy.wait_recv()
    landing = []
    for c in range(per_block):
        rows = slice(c * Q_ROWS, (c + 1) * Q_ROWS)
        far_first[c].wait_recv()
        passed = [
            k.remote(far_n.at[0, rows_of(c)], far_n.at[r, rows_of(c)], peer) for r, peer in peers
        ]
        rows_step(FAR, 0, c)
        copies = []
        for r, peer in peers:
            passed[r - 1].wait_recv()
            rows_step(FAR, r, c)
            copies.append(
                k.remote(
                    k.far_grad.at[r, rows_of(c)], k.far_got_grad.at[r - 1, rows_of(c)], peer
                )
            )
        total = k.far_grad[0, rows, :].astype(F32)
        for r, copy in enumerate(copies):
            copy.wait_recv()
            total = total + k.far_got_grad[r, rows, :].astype(F32)
        k.far_grad[0, rows, :] = total.astype(BF16)
        landing.append(k.remote(k.far_grad.at[0, rows_of(c)], k.landed.at[rows_of(c)], over))
    k.store(k.far_out.at[0], k.far_own_out)
    for r, peer in peers:
        k.remote(k.far_out.at[r], k.far_got_out.at[r - 1], peer)
    half = nb * rows_each
    for which in (2, 0, 1):
        right = (k.d_gate, k.d_up, k.hidden)[which]
        lefts = {side: k.of(side).c if which == 2 else k.of(side).n for side in (NEAR, FAR)}

        def col_step(i, carry):
            cols = pl.ds(pl.multiple_of(i * G_COLS, G_COLS), G_COLS)
            total = None
            for s, side in enumerate((NEAR, FAR)):
                for r in range(nb):
                    start = s * half + r * rows_each
                    term = dot_tn(lefts[side][r, :, cols], right[start : start + rows_each, :])
                    total = term if total is None else total + term
            w[which, cols, :] = total.astype(BF16)
            return carry

        lax.fori_loop(0, width // G_COLS, col_step, 0)
        k.store(w.at[which], k.grads.at[which])
        if which == 2:
            d = lax.axis_index("dp")
            for n, i in enumerate((z_order(n_z) + [0])[:EARLY]):
                start = (lax.rem(d + 2 * i, 2 * n_z) ^ 1) * blk
                rows = pl.ds(pl.multiple_of(start, 16), blk)
                k.remote(w.at[which, rows], k.early.at[n], other_x)


def feed_forward(normed_two, cotangent, c_far, w, nb, n_z, collective_id):
    rows_each, width = normed_two.shape
    units = w.shape[2]
    sds = jax.ShapeDtypeStruct
    block = pltpu.VMEM((nb, rows_each, width), BF16)
    kept = pltpu.VMEM((2 * nb * rows_each, units), BF16)
    own = (sds((rows_each, width), BF16), IN_HBM)
    got = (sds((nb - 1, rows_each, width), BF16), IN_HBM)
    return frame_call(
        functools.partial(feed_forward_body, nb, rows_each, n_z),
        "feed_forward",
        dict(
            own_n=(normed_two, IN_HBM),
            own_c=(cotangent, IN_HBM),
            own_far_c=(c_far, IN_HBM),
            w=(w, LOAD),
        ),
        dict(
            grads=(sds(w.shape, BF16), IN_HBM),
            early=(sds((EARLY, width // (2 * n_z), units), BF16), IN_HBM),
            near_own_grad=own,
            near_got_grad=got,
            landed=own,
            near_own_out=own,
            near_got_out=got,
            far_own_out=own,
            far_got_out=got,
        ),
        dict(
            near_n=block,
            far_n=block,
            near_c=block,
            far_c=block,
            hidden=kept,
            d_gate=kept,
            d_up=kept,
            near_grad=block,
            far_grad=block,
            near_out=block,
            far_out=block,
            far_got_grad=pltpu.VMEM((nb - 1, rows_each, width), BF16),
        ),
        36 * nb * rows_each * width * units,
        collective_id,
    )


def attention_backward_rows(k, tag, i, length, kv):
    qkvp, dproj, datt, lse = k.of(tag).qkvp, k.of(tag).dproj, k.datt, k.of(tag).lse
    n = (i + 1) * Q_ROWS
    rows = slice(i * Q_ROWS, n)
    lane = lax.broadcasted_iota(jnp.int32, (Q_ROWS, PAD), 1)

    def one_head(h, carry):
        group = h // GROUP
        q_col = pl.ds(pl.multiple_of((4 * group + h % GROUP) * PAD, PAD), PAD)
        k_col = pl.ds(pl.multiple_of((4 * group + 2) * PAD, PAD), PAD)
        v_col = pl.ds(pl.multiple_of((4 * group + 3) * PAD, PAD), PAD)
        a_col = pl.ds(pl.multiple_of(h * PAD, PAD), PAD)
        q = qkvp[rows, q_col]
        keys = qkvp[0:n, k_col]
        do = datt[rows, a_col]
        row_lse = jnp.sum(jnp.where(lane == h, lse[rows, :], 0.0), axis=-1, keepdims=True)
        s = dot_nt(q, keys)
        row_ids = lax.broadcasted_iota(jnp.int32, (Q_ROWS, 1), 0) + i * Q_ROWS + 1
        limit = jnp.minimum(row_ids, length)
        col_ids = lax.broadcasted_iota(jnp.int32, (Q_ROWS, n), 1)
        s = jnp.where(col_ids < limit, s, NEGATIVE)
        p = jnp.exp2(s * (SCALE * LOG2E) - row_lse)
        dp = dot_nt(do, qkvp[0:n, v_col])
        inner = jnp.sum(p * dp, axis=-1, keepdims=True)
        ds = (p * (dp - inner)).astype(BF16)
        k.dv[group, 0:n, :] += dot_tn(p.astype(BF16), do)
        k.dk[group, 0:n, :] += dot_tn(ds, q)
        dq = dot_nn(ds, keys) * SCALE
        dproj[rows, q_col] = unrotate(k, dq, rows).astype(BF16)
        return carry

    lax.fori_loop(0, kv * GROUP, one_head, 0)


def unrotate(k, grad, rows):
    return grad * k.cos_t[rows, :] - swap_halves(grad) * k.sin_t[rows, :]


class Scatter:
    def __init__(self, k, n_z, blk):
        d = lax.axis_index("dp")
        self.k, self.peers, self.other_x = k, z_peers(n_z), permuted("dp", 1)
        self.order = [(which, i) for which in (2, 0, 1) for i in z_order(n_z) + [0]]

        def rows(owner):
            return pl.ds(pl.multiple_of(owner * blk, 16), blk)

        owners = {i: lax.rem(d + 2 * i, 2 * n_z) for i in range(n_z)}
        self.rows = {i: rows(owner) for i, owner in owners.items()}
        self.rows_other = {i: rows(owner ^ 1) for i, owner in owners.items()}
        self.z, self.extra, self.blank = d // 2, {}, []
        self.joined = n_z == 4
        if self.joined:
            k.zeros[...] = jnp.zeros_like(k.zeros)
            for end, i in ((self.z == 0, 1), (self.z == 3, 3)):
                for which in range(3):
                    sem = k.local_sem.at[k.next_local]
                    k.next_local += 1
                    copy = pltpu.make_async_copy(k.zeros, k.ffn_sums.at[which, i], sem)
                    pl.when(end)(copy.start)
                    self.blank.append((end, copy))
        self.sent, self.slots = [None] * EARLY, [None] * SLOTS
        self.next_arrival = 0

    def send(self):
        if len(self.sent) < len(self.order):
            which, i = self.order[len(self.sent)]
            self.sent.append(
                self.k.remote(
                    self.k.grads.at[which, self.rows_other[i]],
                    self.k.x_got.at[which, i],
                    self.other_x,
                )
            )

    def pump(self):
        if self.next_arrival == len(self.order):
            return False
        k, n = self.k, self.next_arrival
        which, i = self.order[n]
        self.next_arrival += 1
        own = k.local(k.grads.at[which, self.rows[i]], k.staged.at[0])
        if n < EARLY:
            other = k.local(k.early.at[n], k.staged.at[1])
        else:
            self.sent[n].wait_recv()
            self.send()
            other = k.local(k.x_got.at[which, i], k.staged.at[1])
        slot = n % SLOTS
        if self.slots[slot] is not None:
            self.slots[slot]()
        own.wait()
        other.wait()
        held = k.staged[0, :, :].astype(F32) + k.staged[1, :, :].astype(F32)
        k.narrow[slot, :, :] = held.astype(BF16)
        z = self.z
        if i and self.joined:
            sends = receives = None
            if i == 2:
                for extra in self.extra[which]:
                    extra.wait_recv()

                @pl.when((z == 1) | (z == 2))
                def _():
                    copy = pltpu.make_async_copy(
                        k.extra.at[which], k.staged.at[0], k.local_sem.at[k.next_local]
                    )
                    copy.start()
                    copy.wait()
                    k.narrow[slot, :, :] = (held + k.staged[0, :, :].astype(F32)).astype(BF16)

                k.next_local += 1
            elif i == 1:
                sends, receives = z < 3, z > 0
                past, gets, neighbour = z == 3, z == 2, self.peers[3]
            else:
                sends, receives = z > 0, z < 3
                past, gets, neighbour = z == 0, z == 1, self.peers[1]
            copies = [
                k.remote(k.narrow.at[slot], k.ffn_sums.at[which, i], self.peers[i], sends, receives)
            ]
            if i != 2:
                copies.append(
                    k.remote(k.narrow.at[slot], k.extra.at[which], neighbour, past, gets)
                )
                self.extra.setdefault(which, []).append(copies[1])

            def wait(copies=copies):
                for copy in copies:
                    copy.wait_send()

            self.slots[slot] = wait
        elif i:
            remote = k.remote(k.narrow.at[slot], k.ffn_sums.at[which, i], self.peers[i])
            self.slots[slot] = remote.wait_send
        else:
            self.slots[slot] = k.store(k.narrow.at[slot], k.ffn_sums.at[which, 0])
        return True


def attention_backward_body(nb, rows_each, kv, n_z, blk, k):
    d = lax.axis_index("dp")
    z, x = d // 2, lax.rem(d, 2)
    local = lax.rem(lax.axis_index("tensor"), nb)
    seq_len = nb * rows_each
    per_block = rows_each // Q_ROWS
    over = permuted("tensor", nb)
    other_x = permuted("dp", 1)
    peers = half_peers(nb)
    own_a = k.local(k.own_a, k.near_a.at[0])
    k.load_refs(k.hbm.w_out, k.w_out)
    k.load_refs(k.hbm.cos_t, k.cos_t)
    k.load_refs(k.hbm.sin_t, k.sin_t)
    for tag in (NEAR, FAR):
        k.load_refs(k.hbm.of(tag).qkvp, k.of(tag).qkvp)
        k.load_refs(k.hbm.of(tag).lse, k.of(tag).lse)
    late = [k.local(k.hbm.w_qkv, k.w_qkv), k.local(k.hbm.spread, k.spread)]
    for tag in (NEAR, FAR):
        late.append(k.local(k.hbm.of(tag).att, k.of(tag).att))
        late.append(k.local(k.hbm.of(tag).normed, k.of(tag).normed))
    tensor_peers, dp_peers = all_peers(2 * n_z, 2 * nb)
    k.meet(tensor_peers + dp_peers)
    far_first = [
        k.remote(k.own_a.at[rows_of(c)], k.far_a.at[0, rows_of(c)], over)
        for c in range(per_block)
    ]
    near_copies = [k.remote(k.own_a, k.near_a.at[r], peer) for r, peer in peers]
    landing, near_landing = [], []
    scatter = Scatter(k, n_z, blk)
    for _ in range(WINDOW):
        scatter.send()
    own_a.wait()
    k.ready()
    for copy in near_copies:
        copy.wait_recv()
    for tag, length in ((NEAR, k.lengths[0]), (FAR, k.lengths[1])):
        blocks, parts, dproj = k.of(tag).a, k.of(tag).parts, k.of(tag).dproj
        k.dk[...] = jnp.zeros_like(k.dk)
        k.dv[...] = jnp.zeros_like(k.dv)
        for c in range(per_block):
            rows = slice(c * Q_ROWS, (c + 1) * Q_ROWS)
            if tag == FAR:
                far_first[c].wait_recv()
                passed = [
                    k.remote(blocks.at[0, rows_of(c)], blocks.at[r, rows_of(c)], peer)
                    for r, peer in peers
                ]
                for copy in passed:
                    copy.wait_recv()
            for b in range(nb):
                i = b * per_block + c
                k.datt[i * Q_ROWS : (i + 1) * Q_ROWS, :] = dot_nn(
                    blocks[local ^ b, rows, :], k.w_out[...]
                ).astype(BF16)
                attention_backward_rows(k, tag, i, length, kv)
                scatter.pump()
        for j in range(kv):
            k_col = slice((4 * j + 2) * PAD, (4 * j + 3) * PAD)
            v_col = slice((4 * j + 3) * PAD, (4 * j + 4) * PAD)
            for i in range(seq_len // Q_ROWS):
                rows = slice(i * Q_ROWS, (i + 1) * Q_ROWS)
                dproj[rows, k_col] = unrotate(k, k.dk[j, rows, :] * SCALE, rows).astype(BF16)
                dproj[rows, v_col] = k.dv[j, rows, :].astype(BF16)
        for copy in late:
            copy.wait()
        late = []
        for c in range(per_block):
            rows = slice(c * Q_ROWS, (c + 1) * Q_ROWS)
            for b in range(nb):
                i = b * per_block + c
                part = dot_nt(dproj[i * Q_ROWS : (i + 1) * Q_ROWS, :], k.w_qkv[...])
                parts[local ^ b, rows, :] = part.astype(BF16)
            if tag == NEAR:
                for r, peer in peers:
                    near_landing.append(
                        k.remote(parts.at[r, rows_of(c)], k.near_got.at[r - 1, rows_of(c)], peer)
                    )
            else:
                copies = [
                    k.remote(parts.at[r, rows_of(c)], k.far_got.at[r - 1, rows_of(c)], peer)
                    for r, peer in peers
                ]
                total = parts[0, rows, :].astype(F32)
                for r, copy in enumerate(copies):
                    copy.wait_recv()
                    total = total + k.far_got[r, rows, :].astype(F32)
                parts[0, rows, :] = total.astype(BF16)
                landing.append(k.remote(parts.at[0, rows_of(c)], k.landed.at[rows_of(c)], over))
        if tag == NEAR:
            k.store(parts.at[0], k.near_own)
        scatter.pump()
    width = k.w_qkv.shape[0]
    arriving = []
    for which in range(kv + 1):

        def chunk(c, carry):
            cols = pl.ds(pl.multiple_of(c * G_COLS, G_COLS), G_COLS)
            total = None
            if which == 0:
                wide = k.near_att.shape[1]
                for tag in (NEAR, FAR):
                    for r in range(nb):
                        start = pl.multiple_of((local ^ r) * rows_each, rows_each)
                        term = dot_tn(
                            k.of(tag).a[r, :, cols], k.of(tag).att[pl.ds(start, rows_each), :]
                        )
                        total = term if total is None else total + term
                compact = dot_nt(total.astype(BF16), k.spread[:, :wide])
            else:
                part = slice((which - 1) * G_PAD, which * G_PAD)
                total = dot_tn(k.near_normed[:, cols], k.near_dproj[:, part])
                total += dot_tn(k.far_normed[:, cols], k.far_dproj[:, part])
                compact = dot_nt(total.astype(BF16), k.spread[...])
            compact = compact.astype(BF16)
            for b in range(G_COLS // blk):
                owner = c * (G_COLS // blk) + b
                shift = lax.rem(owner // 2 + n_z - z, n_z)
                value = compact[b * blk : (b + 1) * blk, :]

                @pl.when(x == lax.rem(owner, 2))
                def _():
                    k.same[which, shift, :, :] = value

                @pl.when(x != lax.rem(owner, 2))
                def _():
                    k.other[which, shift, :, :] = value

            return carry

        lax.fori_loop(0, width // G_COLS, chunk, 0)
        arriving.append(k.remote(k.other.at[which], k.arrived.at[which], other_x))
        if which == 0:
            k.remote(k.far_out, k.out_landed, over)
        scatter.pump()
    while scatter.pump():
        pass
    for end, copy in scatter.blank:
        pl.when(end)(copy.wait)
    for which in range(kv + 1):
        arriving[which].wait_recv()
        for i in z_order(n_z) + [0]:
            held = k.same[which, i, :, :].astype(F32) + k.arrived[which, i, :, :].astype(F32)
            k.same[which, i, :, :] = held.astype(BF16)
            if i:
                k.remote(k.same.at[which, i], k.sums.at[which, i], scatter.peers[i])
            else:
                k.store(k.same.at[which, 0], k.sums.at[which, 0])
    for copy in landing + near_landing:
        copy.wait_recv()
    k.flush(k.near_got, k.hbm.near_got)
    loads = [k.local(k.landed, k.near_a.at[0]), k.local(k.tokens, k.near_a.at[1])]
    for copy in loads:
        copy.wait()

    def gain_rows(i, carry):
        rows = pl.ds(pl.multiple_of(i * 32, 32), 32)
        dn = k.near_parts[0, rows, :].astype(F32) + k.near_a[0, rows, :].astype(F32)
        for r in range(nb - 1):
            dn = dn + k.near_got[r, rows, :].astype(F32)
        v = k.near_a[1, rows, :].astype(F32)
        inv = lax.rsqrt(jnp.mean(v * v, axis=-1, keepdims=True) + NORM_EPSILON)
        return carry + jnp.sum(dn * v * inv, axis=0, keepdims=True)

    t = lax.axis_index("tensor")
    k.first[t, 0:1, :] = lax.fori_loop(0, rows_each // 32, gain_rows, jnp.zeros((1, width), F32))
    k.first[t, 1:2, :] = k.gain_part[...]
    gain_copies = share(k, k.first, t, tensor_peers)
    k.second[d, :, :] = sum_slots(k.first, gain_copies)
    gain_copies = share(k, k.second, d, dp_peers)
    k.gain_sums[...] = sum_slots(k.second, gain_copies)


def attention_backward(
    attention_grad, tokens, gain_part, lengths, fwd, grads, early, far_out, tables, spread, nb, n_z, collective_id
):
    rows_each, width = attention_grad.shape
    seq_len = nb * rows_each
    w_qkv, w_out = fwd["w_qkv"], fwd["w_out"]
    kv = w_qkv.shape[1] // G_PAD
    heads = kv * GROUP
    blk = width // (2 * n_z)
    units = grads.shape[2]
    sds = jax.ShapeDtypeStruct
    inputs = dict(
        lengths=(lengths, IN_SMEM),
        own_a=(attention_grad, IN_HBM),
        w_qkv=(w_qkv, LOAD),
        w_out=(w_out, LOAD),
        cos_t=(tables[0], LOAD),
        sin_t=(tables[1], LOAD),
        spread=(spread, LOAD),
        grads=(grads, IN_HBM),
        early=(early, IN_HBM),
        far_out=(far_out, IN_HBM),
        tokens=(tokens, IN_HBM),
        gain_part=(gain_part, IN_VMEM),
    )
    for tag in (NEAR, FAR):
        for key in ("qkvp", "lse", "att", "normed"):
            inputs[tag + key] = (fwd[tag + key], LOAD)
    block = pltpu.VMEM((nb, rows_each, width), BF16)
    sums = sds((kv + 1, n_z, blk, G_COLS), BF16)
    own = (sds((rows_each, width), BF16), IN_HBM)
    return frame_call(
        functools.partial(attention_backward_body, nb, rows_each, kv, n_z, blk),
        "attention_backward",
        inputs,
        dict(
            near_own=own,
            near_got=(sds((nb - 1, rows_each, width), BF16), FLUSH),
            landed=own,
            out_landed=own,
            gain_sums=(sds((2, width), F32), IN_VMEM),
            sums=(sums, IN_HBM),
            x_got=(sds((3, n_z, blk, units), BF16), IN_HBM),
            ffn_sums=(sds((3, n_z, blk, units), BF16), IN_HBM),
            extra=(sds((3, blk, units), BF16), IN_HBM),
        ),
        dict(
            near_a=block,
            far_a=block,
            near_parts=block,
            far_parts=block,
            far_got=pltpu.VMEM((nb - 1, rows_each, width), BF16),
            near_dproj=pltpu.VMEM((seq_len, kv * G_PAD), BF16),
            far_dproj=pltpu.VMEM((seq_len, kv * G_PAD), BF16),
            datt=pltpu.VMEM((seq_len, heads * PAD), BF16),
            dk=pltpu.VMEM((kv, seq_len, PAD), F32),
            dv=pltpu.VMEM((kv, seq_len, PAD), F32),
            same=pltpu.VMEM(sums.shape, BF16),
            other=pltpu.VMEM(sums.shape, BF16),
            arrived=pltpu.VMEM(sums.shape, BF16),
            staged=pltpu.VMEM((2, blk, units), BF16),
            zeros=pltpu.VMEM((blk, units), BF16),
            first=pltpu.VMEM((2 * nb, 2, width), F32),
            second=pltpu.VMEM((2 * n_z, 2, width), F32),
            narrow=pltpu.VMEM((SLOTS, blk, units), BF16),
        ),
        8 * seq_len * width * (kv * G_PAD + heads * PAD) + heads * seq_len * seq_len * 20 * 256,
        collective_id,
        n_sems=12 * n_z + 48,
    )


def all_peers(n_dp, n_t):
    d, t = lax.axis_index("dp"), lax.axis_index("tensor")
    return (
        [{"tensor": lax.rem(t + i, n_t)} for i in range(1, n_t)],
        [{"dp": lax.rem(d + i, n_dp)} for i in range(1, n_dp)],
    )


def share(k, buffer, me, peers):
    return [k.remote(buffer.at[me], buffer.at[me], peer) for peer in peers]


def sum_slots(buffer, copies):
    for copy in copies:
        copy.wait_recv()
    total = buffer[0, :, :]
    for i in range(1, len(copies) + 1):
        total = total + buffer[i, :, :]
    return total


class Master:
    def __init__(self, refs, at, rows, cols, number, gradient, gradient_refs):
        self.refs, self.at, self.rows, self.cols = refs, at, rows, cols
        self.number, self.gradient, self.gradient_refs = number, gradient, gradient_refs


def moments_body(kv, n_z, k):
    correct_one = 1.0 / (1.0 - BETA_ONE**STEP)
    correct_two = 1.0 / (1.0 - BETA_TWO**STEP)
    row = lax.broadcasted_iota(jnp.int32, (8, PAD), 0)
    lane = lax.broadcasted_iota(jnp.int32, (8, PAD), 1)

    def z_sum(ref, which, rows, cols=slice(None)):
        total = ref[which, 0, rows, cols].astype(F32)
        for i in range(1, n_z):
            total = total + ref[which, i, rows, cols].astype(F32)
        return total

    def parts(h, m):
        return [
            (h.weight, m.weight),
            (h.first, m.first),
            (h.second, m.second),
            (h.next_first, m.next_first),
            (h.next_second, m.next_second),
            (h.update, m.update),
        ]

    gate_up = parts(k.hbm.of(GATE_UP), k.of(GATE_UP))
    down = parts(k.hbm.of(DOWN), k.of(DOWN))
    qkv = parts(k.hbm.of(QKV_), k.of(QKV_))
    out = parts(k.hbm.of(OUT), k.of(OUT))
    gains = parts(k.hbm.of(GAINS), k.of(GAINS))
    cols_out = k.of(OUT).weight.shape[1]
    units = []
    for which in range(2):
        rows, cols = k.of(GATE_UP).weight.shape[1:]
        units.append(
            Master(
                gate_up,
                (which,),
                rows,
                cols,
                2 + which,
                lambda at, which=which: z_sum(k.ffn_sums, which, at),
                [(k.hbm.ffn_sums.at[which], k.ffn_sums.at[which])],
            )
        )
    units.append(
        Master(
            down,
            (),
            *k.of(DOWN).weight.shape,
            4,
            lambda at: z_sum(k.ffn_sums, 2, at),
            [(k.hbm.ffn_sums.at[2], k.ffn_sums.at[2])],
        )
    )
    units.append(
        Master(
            qkv,
            (),
            *k.of(QKV_).weight.shape,
            0,
            lambda at: jnp.concatenate([z_sum(k.sums, 1 + j, at) for j in range(kv)], axis=1),
            [(k.hbm.sums, k.sums)],
        )
    )
    units.append(
        Master(
            out,
            (),
            *k.of(OUT).weight.shape,
            1,
            lambda at: z_sum(k.sums, 0, at, slice(0, cols_out)),
            [],
        )
    )
    for which in range(2):
        units.append(
            Master(
                gains,
                (which,),
                1,
                k.of(GAINS).weight.shape[2],
                5 + which,
                lambda at, which=which: k.gain_sum[which, at, :],
                [],
            )
        )
    loads = []
    for unit in units:
        pairs = list(unit.gradient_refs)
        for source, target in unit.refs[:3]:
            pairs.append((source.at[unit.at], target.at[unit.at]) if unit.at else (source, target))
        loads.append([k.local(source, target) for source, target in pairs])
    squares = jnp.zeros((8, PAD), F32)
    for unit, copies in zip(units, loads):
        for copy in copies:
            copy.wait()
        weight, first, second, next_first, next_second, direction = [ref for _, ref in unit.refs]
        tile = unit.rows if unit.rows % 32 else 32

        def one(i, carry):
            rows = pl.ds(pl.multiple_of(i * tile, tile) if unit.rows > tile else 0, tile)
            at = unit.at + (rows, slice(None))
            g = unit.gradient(rows)
            w = weight[at]
            moment = BETA_ONE * first[at] + (1.0 - BETA_ONE) * g
            square = BETA_TWO * second[at] + (1.0 - BETA_TWO) * g * g
            next_first[at] = moment
            next_second[at] = square
            update = (moment * correct_one) / (
                jnp.sqrt(square * correct_two) + ADAM_EPSILON
            ) + WEIGHT_DECAY * w
            direction[at] = update
            return (
                carry[0] + jnp.sum(w * w, axis=0, keepdims=True),
                carry[1] + jnp.sum(update * update, axis=0, keepdims=True),
            )

        zero = jnp.zeros((1, unit.cols), F32)
        w_sum, u_sum = lax.fori_loop(0, unit.rows // tile, one, (zero, zero))
        w_sum = jnp.sum(w_sum, axis=1, keepdims=True)
        u_sum = jnp.sum(u_sum, axis=1, keepdims=True)
        mark = lane == unit.number
        squares += jnp.where(mark & (row == 0), w_sum, 0.0)
        squares += jnp.where(mark & (row == 1), u_sum, 0.0)
        for target, source in unit.refs[3:]:
            if unit.at:
                k.store(source.at[unit.at], target.at[unit.at])
            else:
                k.store(source, target)
    k.squares[...] = squares


def moments(weights, firsts, seconds, ffn_sums, sums, gain_sum, kv, n_z):
    inputs, outputs = {}, {}
    sds = jax.ShapeDtypeStruct
    names = (GATE_UP, DOWN, QKV_, OUT, GAINS)
    for key, weight, first, second in zip(names, weights, firsts, seconds):
        shape = (sds(weight.shape, F32), FLUSH)
        for table, prefix in (
            (dict(weight=(weight, LOAD), first=(first, LOAD), second=(second, LOAD)), inputs),
            (dict(next_first=shape, next_second=shape, update=shape), outputs),
        ):
            prefix.update({key + part: entry for part, entry in table.items()})
    inputs.update(
        ffn_sums=(ffn_sums, LOAD), sums=(sums, LOAD), gain_sum=(gain_sum, IN_VMEM)
    )
    outputs.update(squares=(sds((8, PAD), F32), IN_VMEM))
    return frame_call(
        functools.partial(moments_body, kv, n_z),
        "moments",
        inputs,
        outputs,
        {},
        0,
        None,
        n_sems=64,
    )


def sum_all_body(n_dp, n_t, k):
    d, t = lax.axis_index("dp"), lax.axis_index("tensor")
    tensor_peers, dp_peers = all_peers(n_dp, n_t)
    k.first[t, :, :] = k.value[...]
    k.meet(tensor_peers + dp_peers)
    copies = share(k, k.first, t, tensor_peers)
    k.second[d, :, :] = sum_slots(k.first, copies)
    copies = share(k, k.second, d, dp_peers)
    k.total[...] = sum_slots(k.second, copies)


def sum_all(value, n_dp, n_t, collective_id):
    return frame_call(
        functools.partial(sum_all_body, n_dp, n_t),
        "sum_everywhere",
        dict(value=(value, IN_VMEM)),
        dict(total=(jax.ShapeDtypeStruct(value.shape, F32), IN_VMEM)),
        dict(
            first=pltpu.VMEM((n_t,) + value.shape, F32),
            second=pltpu.VMEM((n_dp,) + value.shape, F32),
        ),
        0,
        collective_id,
        n_sems=n_dp + n_t,
    )["total"]


def apply_body(numbers, k):
    scale = LEARN_RATE * (jnp.sqrt(k.squares[0:1, :]) / jnp.sqrt(k.squares[1:2, :]))
    names = (GATE_UP, DOWN, QKV_, OUT, GAINS)
    loads = [
        [
            k.local(k.hbm.of(name).weight, k.of(name).weight),
            k.local(k.hbm.of(name).update, k.of(name).update),
        ]
        for name in names
    ]
    for name, number, copies in zip(names, numbers, loads):
        for copy in copies:
            copy.wait()
        weight, update, new = k.of(name).weight, k.of(name).update, k.of(name).new
        for which in range(weight.shape[0]):
            factor = scale[:, number + which : number + which + 1]
            rows = weight.shape[1]
            tile = rows if rows % 32 else 32

            def one(i, carry):
                at = pl.ds(pl.multiple_of(i * tile, tile) if rows > tile else 0, tile)
                new[which, at, :] = weight[which, at, :] - factor * update[which, at, :]
                return carry

            lax.fori_loop(0, rows // tile, one, 0)
        k.flush(new, k.hbm.of(name).new)


def apply_updates(weights, updates, squares):
    names = (GATE_UP, DOWN, QKV_, OUT, GAINS)
    inputs, outputs = dict(squares=(squares, IN_VMEM)), {}
    for key, weight, update in zip(names, weights, updates):
        for part, array in dict(weight=weight, update=update).items():
            inputs[key + part] = (array, LOAD)
        for part in dict(new=0):
            outputs[key + part] = (jax.ShapeDtypeStruct(weight.shape, F32), FLUSH)
    done = frame_call(
        functools.partial(apply_body, (2, 4, 0, 1, 5)), "new_masters", inputs, outputs, {}, 0, None
    )
    return [done[key + part] for key in names for part in dict(new=0)]


def rms_norm(values, gain_row):
    return (
        values
        * lax.rsqrt(jnp.mean(values * values, axis=-1, keepdims=True) + NORM_EPSILON)
        * gain_row
    )


def rotary_tables():
    half = HEAD // 2
    frequency = ROPE_THETA ** (-(jnp.arange(half, dtype=F32) * (2.0 / HEAD)))
    angles = jnp.arange(SEQ_LEN, dtype=F32)[:, None] * frequency[None, :]
    cosine, sine = jnp.cos(angles), jnp.sin(angles)
    empty = jnp.zeros((SEQ_LEN, PAD - HEAD), F32)
    return (
        jnp.concatenate([cosine, cosine, empty], axis=1),
        jnp.concatenate([-sine, sine, empty], axis=1),
    )


def shards(
    tokens,
    cotangent,
    lengths,
    qkv_weight,
    out_weight,
    gate_up_weight,
    down_weight,
    norm_gains,
    qkv_first,
    out_first,
    gate_up_first,
    down_first,
    gains_first,
    qkv_second,
    out_second,
    gate_up_second,
    down_second,
    gains_second,
):
    rows_each, width = tokens.shape
    n_t = lax.axis_size("tensor")
    n_dp = lax.axis_size("dp")
    n_z = n_dp // 2
    nb = n_t // 2
    t = lax.axis_index("tensor")
    d = lax.axis_index("dp")
    mine = t // nb
    lengths = jnp.stack([lengths[mine], lengths[1 - mine]])
    spread = spread_matrix().astype(BF16)
    blk = qkv_weight.shape[0]
    kv = qkv_weight.shape[1] // G_COLS

    gain_cols = norm_gains.shape[1]
    gain_start = (d * n_t + t) * gain_cols
    gain_rows = lax.dynamic_update_slice(
        jnp.zeros((2, width), F32),
        norm_gains.astype(BF16).astype(F32),
        (0, gain_start),
    )
    halves = (qkv_weight, out_weight.T, gate_up_weight, down_weight.T)
    tables = rotary_tables()
    fwd = opening(
        tokens, cotangent, lengths, gain_rows, halves, tables, spread, n_t, n_z, 0
    )
    inputs = tokens.astype(F32)
    attention_gain, feedforward_gain = fwd["gain_sum"][0:1], fwd["gain_sum"][1:2]
    residual = fwd["residual"]

    ff = feed_forward(fwd["normed_two"], cotangent, fwd["c_far"], fwd["w_ffn"], nb, n_z, 2)

    def total(*arrays):
        result = 0.0
        for array in arrays:
            array = array.astype(F32)
            result = result + (array if array.ndim == 2 else jnp.sum(array, axis=0))
        return result

    normed_two_grad = total(ff["near_own_grad"], ff["near_got_grad"], ff["landed"])
    _, norm_pull = jax.vjp(rms_norm, residual, feedforward_gain)
    residual_part, ffn_gain_grad = norm_pull(normed_two_grad)
    residual_grad = cotangent.astype(F32) + residual_part
    far_out = total(ff["far_own_out"], ff["far_got_out"]).astype(BF16)
    bwd = attention_backward(
        residual_grad.astype(BF16),
        tokens,
        ffn_gain_grad,
        lengths,
        fwd,
        ff["grads"],
        ff["early"],
        far_out,
        tables,
        spread,
        nb,
        n_z,
        3,
    )
    normed_grad = total(bwd["near_own"], bwd["near_got"], bwd["landed"])
    _, first_pull = jax.vjp(rms_norm, inputs, attention_gain)
    input_part, _ = first_pull(normed_grad)
    grad_tokens = residual_grad + input_part
    layer_out = (residual + total(ff["near_own_out"], ff["near_got_out"], bwd["out_landed"])).astype(
        BF16
    )
    gain_sum = lax.dynamic_slice(bwd["gain_sums"], (0, gain_start), (2, gain_cols))

    def lift(gains):
        return gains[:, None, :]

    done = moments(
        (gate_up_weight, down_weight.T, qkv_weight, out_weight.T, lift(norm_gains)),
        (gate_up_first, down_first.T, qkv_first, out_first.T, lift(gains_first)),
        (gate_up_second, down_second.T, qkv_second, out_second.T, lift(gains_second)),
        bwd["ffn_sums"],
        bwd["sums"],
        lift(gain_sum),
        kv,
        n_z,
    )
    all_squares = sum_all(done["squares"], n_dp, n_t, 5)
    norms = jnp.sqrt(all_squares)

    def flat(array):
        return array if array.ndim == 3 else array[None]

    new_gate_up, new_down, new_qkv, new_out, new_gains = apply_updates(
        [flat(a) for a in (gate_up_weight, down_weight.T, qkv_weight, out_weight.T, lift(norm_gains))],
        [flat(done[key + part]) for key in (GATE_UP, DOWN, QKV_, OUT, GAINS) for part in dict(update=0)],
        all_squares,
    )
    first, second = (
        dict(
            gate_up=done[GATE_UP + part],
            down=done[DOWN + part].T,
            qkv=done[QKV_ + part],
            out=done[OUT + part].T,
            gains=done[GAINS + part][:, 0, :],
        )
        for part in ("next_first", "next_second")
    )
    new = (new_qkv[0], new_out[0].T, new_gate_up, new_down[0].T, new_gains[:, 0, :])
    names = ("qkv", "out", "gate_up", "down", "gains")
    return (
        layer_out,
        grad_tokens,
        *new,
        *[first[key] for key in names],
        *[second[key] for key in names],
        norms[0, :7],
        norms[1, :5],
        norms[1, 5:7],
    )


def solution(mesh):
    rows = P(("dp", "tensor"), None)
    gains = P(None, ("dp", "tensor"))
    weights = (P("dp", "tensor"), P("tensor", "dp"), P(None, "dp", "tensor"), P("tensor", "dp"), gains)
    in_specs = (rows, rows, P("dp")) + weights * 3
    out_specs = (rows, rows) + weights * 3 + (P(), P(), P())
    return jax.shard_map(shards, mesh=mesh, in_specs=in_specs, out_specs=out_specs, check_vma=False)
```

```python
import functools

import jax
import jax.numpy as jnp
import numpy as np
from jax import lax
from jax.experimental import pallas as pl
from jax.experimental.pallas import tpu as pltpu
from jax.sharding import PartitionSpec as P

HEAD = 96
PAD = 128
SEQ_LEN = 1024
SEQS_DEV = 2
STEP = 10
GROUP = 2

NORM_EPSILON = 1e-05
ROPE_THETA = 100000.0
BETA_ONE = 0.9
BETA_TWO = 0.999
ADAM_EPSILON = 1e-06
WEIGHT_DECAY = 0.01
LEARN_RATE = 0.3
NEGATIVE = -1e30
LOG2E = 1.4426950408889634
SCALE = HEAD ** (-0.5)
Q_ROWS = 256
G_COLS = 4 * HEAD
G_PAD = 4 * PAD
VMEM_LIMIT = 56 << 20

F32 = jnp.float32
BF16 = jnp.bfloat16
VM = pl.BlockSpec(memory_space=pltpu.VMEM)
SM = pl.BlockSpec(memory_space=pltpu.SMEM)
ANY = pl.BlockSpec(memory_space=pl.ANY)
MESH = pl.DeviceIdType.MESH
IN_VMEM, IN_SMEM, IN_HBM, LOAD, FLUSH = range(5)
NEAR, FAR = "near_", "far_"
GATE_UP, DOWN, QKV_, OUT, GAINS = "gate_up_", "down_", "qkv_", "out_", "gains_"
WINDOW, SLOTS, EARLY = 3, 4, 2
HBM = "any_"


def dot_nn(a, b):
    return lax.dot_general(a, b, (((1,), (0,)), ((), ())), preferred_element_type=F32)


def dot_nt(a, b):
    return lax.dot_general(a, b, (((1,), (1,)), ((), ())), preferred_element_type=F32)


def dot_tn(a, b):
    return lax.dot_general(a, b, (((0,), (0,)), ((), ())), preferred_element_type=F32)


def cost(flops, moved):
    return pl.CostEstimate(flops=int(flops), bytes_accessed=int(moved), transcendentals=0)


def spread_matrix():
    source = lax.broadcasted_iota(jnp.int32, (G_COLS, G_PAD), 0)
    target = lax.broadcasted_iota(jnp.int32, (G_COLS, G_PAD), 1)
    return ((target // PAD) * HEAD + target % PAD == source) & (target % PAD < HEAD)


def swap_halves(values):
    lane = lax.broadcasted_iota(jnp.int32, values.shape, 1)
    return jnp.where(
        lane < HEAD // 2,
        pltpu.roll(values, PAD - HEAD // 2, 1),
        pltpu.roll(values, HEAD // 2, 1),
    )


def permuted(axis, bit):
    return {axis: lax.axis_index(axis) ^ bit}


class Remote:
    def __init__(self, copy, sends=None, receives=None):
        self.copy, self.sends, self.receives = copy, sends, receives
        self.landed = self.left = False

    @staticmethod
    def only(condition, action):
        if condition is None:
            action()
        else:
            pl.when(condition)(action)

    def start(self):
        self.only(self.sends, self.copy.start)

    def wait_recv(self):
        if not self.landed:
            self.only(self.receives, self.copy.wait_recv)
        self.landed = True

    def wait_send(self):
        if not self.left:
            self.only(self.sends, self.copy.wait_send)
        self.left = True


class Side:
    def __init__(self, refs, side):
        self.refs, self.side = refs, side

    def __getattr__(self, name):
        return self.refs[self.side + name]

    def of(self, side):
        return Side(self.refs, self.side + side)


class Frame:
    def __init__(self, names, refs):
        self.refs = dict(zip(names, refs))
        self.loading, self.remotes, self.storing = [], [], []
        self.next_local = 0
        self.hbm = Side(self.refs, HBM)

    def __getattr__(self, name):
        return self.refs[name]

    def of(self, side):
        return Side(self.refs, side)

    def meet(self, peers):
        barrier = pltpu.get_barrier_semaphore()
        for peer in peers:
            pl.semaphore_signal(barrier, inc=1, device_id=peer, device_id_type=MESH)
        pl.semaphore_wait(barrier, len(peers))

    def local(self, source, target):
        copy = pltpu.make_async_copy(source, target, self.local_sem.at[self.next_local])
        self.next_local += 1
        copy.start()
        return copy

    def load_refs(self, source, target):
        self.loading.append(self.local(source, target))

    def ready(self):
        for copy in self.loading:
            copy.wait()
        self.loading = []

    def store(self, source, target):
        pending = [self.local(source, target)]

        def wait():
            if pending:
                pending.pop().wait()

        self.storing.append(wait)
        return wait

    def flush(self, source, target):
        self.store(source, target)

    def remote(self, source, target, peer, sends=None, receives=None):
        n = len(self.remotes)
        copy = pltpu.make_async_remote_copy(
            src_ref=source,
            dst_ref=target,
            send_sem=self.send_sem.at[n],
            recv_sem=self.recv_sem.at[n],
            device_id=peer,
            device_id_type=MESH,
        )
        self.remotes.append(Remote(copy, sends, receives))
        self.remotes[-1].start()
        return self.remotes[-1]

    def finish(self):
        for remote in self.remotes:
            remote.wait_send()
            remote.wait_recv()
        for wait in self.storing:
            wait()


def frame_call(body, name, inputs, outputs, scratch, flops, collective_id, n_sems=40):
    names, specs, arrays = [], [], []
    spec_of = {IN_VMEM: VM, IN_SMEM: SM, IN_HBM: ANY, LOAD: ANY, FLUSH: ANY}
    for key, (array, kind) in inputs.items():
        names.append(HBM + key if kind == LOAD else key)
        specs.append(spec_of[kind])
        arrays.append(array)
    out_specs, out_shapes = [], []
    for key, (shape, kind) in outputs.items():
        names.append(HBM + key if kind == FLUSH else key)
        out_specs.append(spec_of[kind])
        out_shapes.append(shape)
    shapes = []
    for table, kind_of in ((inputs, LOAD), (outputs, FLUSH)):
        for key, (array, kind) in table.items():
            if kind == kind_of:
                names.append(key)
                shapes.append(pltpu.VMEM(array.shape, array.dtype))
    for key, shape in scratch.items():
        names.append(key)
        shapes.append(shape)
    extra = {}
    for key in ("local_sem", "send_sem", "recv_sem"):
        if key == "local_sem" or collective_id is not None:
            names.append(key)
            shapes.append(pltpu.SemaphoreType.DMA((n_sems,)))
    if collective_id is not None:
        extra = dict(collective_id=collective_id, has_side_effects=True)

    def kernel(*refs):
        frame = Frame(names, refs)
        body(frame)
        frame.finish()

    moved = sum(a.size * a.dtype.itemsize for a in arrays)
    results = pl.pallas_call(
        kernel,
        out_shape=out_shapes,
        in_specs=specs,
        out_specs=out_specs,
        scratch_shapes=shapes,
        compiler_params=pltpu.CompilerParams(vmem_limit_bytes=VMEM_LIMIT, **extra),
        cost_estimate=cost(flops, moved),
        name=name,
    )(*arrays)
    return dict(zip(outputs, results))


def half_peers(nb):
    return [(r, permuted("tensor", r)) for r in range(1, nb)]


def rows_of(c):
    return pl.ds(c * Q_ROWS, Q_ROWS)


def bits_down(size):
    bits = []
    bit = size // 2
    while bit:
        bits.append(bit)
        bit //= 2
    return bits


def attention_rows(k, tag, i, length, kv):
    qkvp, att, lse = k.of(tag).qkvp, k.of(tag).att, k.of(tag).lse
    n = (i + 1) * Q_ROWS
    rows = slice(i * Q_ROWS, n)
    lane = lax.broadcasted_iota(jnp.int32, (Q_ROWS, PAD), 1)

    def one_head(h, log_totals):
        group = h // GROUP
        q_col = pl.ds(pl.multiple_of((4 * group + h % GROUP) * PAD, PAD), PAD)
        k_col = pl.ds(pl.multiple_of((4 * group + 2) * PAD, PAD), PAD)
        v_col = pl.ds(pl.multiple_of((4 * group + 3) * PAD, PAD), PAD)
        a_col = pl.ds(pl.multiple_of(h * PAD, PAD), PAD)
        s = dot_nt(qkvp[rows, q_col], qkvp[0:n, k_col])
        row_ids = lax.broadcasted_iota(jnp.int32, (Q_ROWS, 1), 0) + i * Q_ROWS + 1
        limit = jnp.minimum(row_ids, length)
        col_ids = lax.broadcasted_iota(jnp.int32, (Q_ROWS, n), 1)
        s = jnp.where(col_ids < limit, s, NEGATIVE)
        top = jnp.max(s, axis=-1, keepdims=True)
        e = jnp.exp2((s - top) * (SCALE * LOG2E))
        total = jnp.sum(e, axis=-1, keepdims=True)
        p = (e * (1.0 / total)).astype(BF16)
        att[rows, a_col] = dot_nn(p, qkvp[0:n, v_col]).astype(BF16)
        log_total = top * (SCALE * LOG2E) + jnp.log2(total)
        return jnp.where(lane == h, log_total, log_totals)

    lse[rows, :] = lax.fori_loop(0, kv * GROUP, one_head, jnp.zeros((Q_ROWS, PAD), F32))


def z_order(n_z):
    return sorted(range(1, n_z), key=lambda i: min(i, n_z - i))


def z_peers(n_z):
    d = lax.axis_index("dp")
    return {i: {"dp": lax.rem(d + 2 * i, 2 * n_z)} for i in range(1, n_z)}


class Stream:
    def __init__(self, k, source, place, paired=False):
        self.source, self.place, self.paired = source, place, paired
        d = lax.axis_index("dp")
        n_dp = lax.axis_size("dp")
        blk = source.shape[0]
        own = place(pl.ds(pl.multiple_of(d * blk, 16), blk))
        self.own, self.local = own, k.local(source, own)
        self.shifted = {}
        for i in range(n_dp // 2):
            if paired:
                start, size = lax.rem(d // 2 + n_dp // 2 - i, n_dp // 2) * (2 * blk), 2 * blk
            else:
                start, size = lax.rem(d + n_dp - 2 * i, n_dp) * blk, blk
            self.shifted[i] = place(pl.ds(pl.multiple_of(start, 16), size))
        self.along_x, self.sent = [], {}


class Gather:
    def __init__(self, k, streams, n_z):
        d = lax.axis_index("dp")
        self.k, self.streams, self.n_z = k, streams, n_z
        self.z = d // 2
        self.right = {"dp": lax.rem(d + 2, 2 * n_z)}
        self.left = {"dp": lax.rem(d + 2 * n_z - 2, 2 * n_z)}
        self.other_x = permuted("dp", 1)
        self.order = [(s, hop) for s in range(len(streams)) for hop in range(1, n_z)]
        self.next_arrival = 0

    def send(self, s, hop):
        if s >= len(self.streams) or hop in self.streams[s].sent:
            return
        stream = self.streams[s]
        z, n_z, far = self.z, self.n_z, hop - 1
        if stream.paired and not far:
            stream.local.wait()
            self.complete(s)
        pair = []
        for shift, peer, sends, receives in (
            (far, self.right, (z >= far) & (z < n_z - 1), z >= hop),
            ((n_z - far) % n_z, self.left, (z < n_z - far) & (z > 0), z < n_z - hop),
        ):
            block = stream.shifted[shift]
            source = block if far or stream.paired else stream.source
            pair.append(self.k.remote(source, block, peer, sends, receives))
        stream.sent[hop] = pair

    def own_along_x(self, s):
        stream = self.streams[s]
        stream.along_x.append(self.k.remote(stream.source, stream.own, self.other_x))

    def pump(self):
        if self.next_arrival == len(self.order):
            return
        s, hop = self.order[self.next_arrival]
        self.next_arrival += 1
        stream = self.streams[s]
        for copy in stream.sent[hop]:
            copy.wait_recv()
        if hop + 1 < self.n_z:
            self.send(s, hop + 1)
        if hop == min(2, self.n_z - 1):
            self.send(s + 1, 1)
        if not stream.paired:
            for shift, copy in zip((hop, self.n_z - hop), stream.sent[hop]):
                block = stream.shifted[shift]
                stream.along_x.append(
                    self.k.remote(block, block, self.other_x, copy.receives, copy.receives)
                )

    def complete(self, s):
        for copy in self.streams[s].along_x:
            copy.wait_recv()


def opening_body(nb, rows_each, kv, n_z, blk, k):
    t = lax.axis_index("tensor")
    local = lax.rem(t, nb)
    seq_len = nb * rows_each
    per_block = rows_each // Q_ROWS
    chunk = 32
    over, other_x = permuted("tensor", nb), permuted("dp", 1)
    peers, along_z = half_peers(nb), z_peers(n_z)
    near_x, far_x = k.near_x, k.far_x
    early = k.ffn_half.shape[2] // 4
    up_early, up_late = pl.ds(0, early), pl.ds(early, 3 * early)
    own_tokens = k.local(k.tokens, near_x.at[0])
    k.load_refs(k.hbm.qkv_w, k.qkv_w)
    k.load_refs(k.hbm.out_w, k.out_w)
    k.load_refs(k.hbm.gate_up_w, k.gate_up_w)
    k.load_refs(k.hbm.down_w, k.down_w)
    k.held[0, :, :] = k.gains[...]
    k.meet(list(along_z.values()) + [other_x, over] + [peer for _, peer in peers])

    stages = [permuted("tensor", bit) for bit in bits_down(2 * nb)] + [other_x]
    gain_copy = k.remote(k.held.at[0], k.got.at[0], stages[0])
    far_copy = k.remote(k.tokens, far_x.at[0], over)
    near_copies = [k.remote(k.tokens, near_x.at[r], peer) for r, peer in peers]
    k.ready()
    k.qkv_half[...] = k.qkv_w[...].astype(BF16)
    k.out_half[...] = k.out_w[...].astype(BF16)
    for i in range(2):
        k.ffn_half[i, :, :] = k.gate_up_w[i, :, :].astype(BF16)
    k.ffn_half[2, :, :] = k.down_w[...].astype(BF16)
    streams = [
        Stream(k, k.qkv_half, lambda rows: k.wq.at[rows]),
        Stream(k, k.out_half, lambda rows: k.wo.at[rows], True),
        Stream(k, k.ffn_half.at[1, :, up_early], lambda rows: k.w_ffn.at[1, rows, up_early], True),
        Stream(k, k.ffn_half.at[2], lambda rows: k.w_ffn.at[2, rows]),
        Stream(k, k.ffn_half.at[0], lambda rows: k.w_ffn.at[0, rows]),
        Stream(k, k.ffn_half.at[1, :, up_late], lambda rows: k.w_ffn.at[1, rows, up_late]),
    ]
    gather = Gather(k, streams, n_z)
    k.load_refs(k.hbm.cos_t, k.cos_t)
    k.load_refs(k.hbm.sin_t, k.sin_t)
    k.load_refs(k.hbm.spread, k.spread)
    gather.own_along_x(1)
    gather.own_along_x(0)
    gather.own_along_x(2)
    gather.send(0, 1)
    for stage in range(len(stages)):
        gain_copy.wait_recv()
        k.held[stage + 1, :, :] = k.held[stage, :, :] + k.got[stage, :, :]
        if stage + 1 < len(stages):
            gain_copy = k.remote(k.held.at[stage + 1], k.got.at[stage + 1], stages[stage + 1])
    last = len(stages)
    gain_copies = [
        k.remote(k.held.at[last], k.got.at[last + i - 1], along_z[i]) for i in range(1, n_z)
    ]
    for _ in range(2 * (n_z - 1)):
        gather.pump()
    total = k.held[last, :, :]
    for i, copy in enumerate(gain_copies):
        copy.wait_recv()
        total = total + k.got[last + i, :, :]
    k.gain_sum[...] = total
    gain_one, gain_two = k.gain_sum.at[0:1], k.gain_sum.at[1:2]
    far_copy.wait_recv()
    far_copies = [k.remote(far_x.at[0], far_x.at[r], peer) for r, peer in peers]
    own_tokens.wait()
    for copy in near_copies + far_copies:
        copy.wait_recv()

    def normalise(tag):
        for r in range(nb):
            base = (local ^ r) * rows_each

            def norm_rows(i, carry):
                rows = pl.ds(pl.multiple_of(i * chunk, chunk), chunk)
                v = k.of(tag).x[r, rows, :].astype(F32)
                inv = lax.rsqrt(jnp.mean(v * v, axis=-1, keepdims=True) + NORM_EPSILON)
                k.of(tag).normed[pl.ds(pl.multiple_of(base + i * chunk, chunk), chunk), :] = (
                    v * inv * gain_one[...]
                ).astype(BF16)
                return carry

            lax.fori_loop(0, rows_each // chunk, norm_rows, 0)
        k.flush(k.of(tag).normed, k.hbm.of(tag).normed)

    normalise(FAR)
    normalise(NEAR)
    for stream in streams:
        if not stream.paired:
            stream.local.wait()
    k.ready()
    gather.complete(0)
    for s in range(3, len(streams)):
        gather.own_along_x(s)
    for s, (source, target) in enumerate(((k.wq, k.w_qkv), (k.wo, k.w_out))):
        gather.complete(s)
        for g in range(-(-target.shape[1] // G_PAD)):
            wide = min(G_PAD, target.shape[1] - g * G_PAD)
            part = source[:, g * G_COLS : (g + 1) * G_COLS]
            target[:, g * G_PAD : g * G_PAD + wide] = dot_nn(
                part, k.spread[0 : part.shape[1], 0:wide]
            ).astype(BF16)
        k.flush(target, k.hbm.w_out if s else k.hbm.w_qkv)

    landing, waiting = [], []
    for tag, length in ((FAR, k.lengths[1]), (NEAR, k.lengths[0])):
        normed, qkvp = k.of(tag).normed, k.of(tag).qkvp
        parts, got = k.of(tag).parts, k.of(tag).got
        for i in range(seq_len // Q_ROWS):
            rows = slice(i * Q_ROWS, (i + 1) * Q_ROWS)
            for j in range(kv):
                proj = dot_nn(normed[rows, :], k.w_qkv[:, j * G_PAD : (j + 1) * G_PAD])
                for h in range(4):
                    part = proj[:, h * PAD : (h + 1) * PAD]
                    if h < 3:
                        part = part * k.cos_t[rows, :] + swap_halves(part) * k.sin_t[rows, :]
                    qkvp[rows, (4 * j + h) * PAD : (4 * j + h + 1) * PAD] = part.astype(BF16)
        k.flush(qkvp, k.hbm.of(tag).qkvp)
        gather.pump()
        for c in range(per_block):
            rows = slice(c * Q_ROWS, (c + 1) * Q_ROWS)
            for b in range(nb):
                i = b * per_block + c
                attention_rows(k, tag, i, length, kv)
                part = dot_nt(k.of(tag).att[i * Q_ROWS : (i + 1) * Q_ROWS, :], k.w_out[...])
                parts[local ^ b, rows, :] = part.astype(BF16)
                if waiting:
                    waiting.pop()()
                gather.pump()
            copies = [
                k.remote(parts.at[r, rows_of(c)], got.at[r - 1, rows_of(c)], peer)
                for r, peer in peers
            ]

            def complete(rows=rows, c=c, copies=copies, parts=parts, got=got, tag=tag):
                total = parts[0, rows, :].astype(F32)
                for r, copy in enumerate(copies):
                    copy.wait_recv()
                    total = total + got[r, rows, :].astype(F32)
                if tag == FAR:
                    parts[0, rows, :] = total.astype(BF16)
                    landing.append(
                        k.remote(parts.at[0, rows_of(c)], k.landed.at[rows_of(c)], over)
                    )
                    if c == per_block - 1:
                        k.remote(k.cotangent, k.c_far, over)
                else:
                    k.residual[rows, :] = near_x[0, rows, :].astype(F32) + total

            waiting.append(complete)
        k.flush(k.of(tag).att, k.hbm.of(tag).att)
        k.flush(k.of(tag).lse, k.hbm.of(tag).lse)
    waiting.pop()()
    for c in range(per_block):
        landing[c].wait_recv()

        def residual_rows(i, carry):
            rows = pl.ds(pl.multiple_of(c * Q_ROWS + i * chunk, chunk), chunk)
            v = k.residual[rows, :] + k.landed[rows, :].astype(F32)
            k.residual[rows, :] = v
            inv = lax.rsqrt(jnp.mean(v * v, axis=-1, keepdims=True) + NORM_EPSILON)
            k.normed_two[rows, :] = (v * inv * gain_two[...]).astype(BF16)
            return carry

        lax.fori_loop(0, Q_ROWS // chunk, residual_rows, 0)
    k.flush(k.residual, k.hbm.residual)
    k.flush(k.normed_two, k.hbm.normed_two)
    for _ in range(4 * (n_z - 1)):
        gather.pump()


def opening(tokens, cotangent, lengths, gains, weights, tables, spread, n_t, n_z, collective_id):
    rows_each, width = tokens.shape
    qkv_w, out_w, gate_up_w, down_w = weights
    blk = qkv_w.shape[0]
    n_dp = 2 * n_z
    nb = n_t // 2
    seq_len = nb * rows_each
    kv = qkv_w.shape[1] // G_COLS
    heads = kv * GROUP
    sds = jax.ShapeDtypeStruct
    normed = (sds((seq_len, width), BF16), FLUSH)
    qkvp = (sds((seq_len, kv * G_PAD), BF16), FLUSH)
    att = (sds((seq_len, heads * PAD), BF16), FLUSH)
    lse = (sds((seq_len, PAD), F32), FLUSH)
    block = pltpu.VMEM((nb, rows_each, width), BF16)
    others = pltpu.VMEM((nb - 1, rows_each, width), BF16)
    n_gain = len(bits_down(n_t)) + 1 + n_z - 1
    return frame_call(
        functools.partial(opening_body, nb, rows_each, kv, n_z, blk),
        "attention_forward",
        dict(
            tokens=(tokens, IN_HBM),
            cotangent=(cotangent, IN_HBM),
            lengths=(lengths, IN_SMEM),
            gains=(gains, IN_VMEM),
            qkv_w=(qkv_w, LOAD),
            out_w=(out_w, LOAD),
            gate_up_w=(gate_up_w, LOAD),
            down_w=(down_w, LOAD),
            cos_t=(tables[0], LOAD),
            sin_t=(tables[1], LOAD),
            spread=(spread, LOAD),
        ),
        dict(
            near_normed=normed,
            far_normed=normed,
            near_qkvp=qkvp,
            far_qkvp=qkvp,
            near_att=att,
            far_att=att,
            near_lse=lse,
            far_lse=lse,
            residual=(sds((rows_each, width), F32), FLUSH),
            normed_two=(sds((rows_each, width), BF16), FLUSH),
            w_qkv=(sds((blk * n_dp, kv * G_PAD), BF16), FLUSH),
            w_out=(sds((blk * n_dp, heads * PAD), BF16), FLUSH),
            w_ffn=(sds((3, blk * n_dp, gate_up_w.shape[2]), BF16), IN_HBM),
            c_far=(sds(cotangent.shape, BF16), IN_HBM),
            gain_sum=(sds(gains.shape, F32), IN_VMEM),
        ),
        dict(
            near_x=block,
            far_x=block,
            far_parts=block,
            near_parts=block,
            far_got=others,
            near_got=others,
            landed=pltpu.VMEM((rows_each, width), BF16),
            qkv_half=pltpu.VMEM(qkv_w.shape, BF16),
            out_half=pltpu.VMEM(out_w.shape, BF16),
            ffn_half=pltpu.VMEM((3,) + down_w.shape, BF16),
            wq=pltpu.VMEM((blk * n_dp, qkv_w.shape[1]), BF16),
            wo=pltpu.VMEM((blk * n_dp, out_w.shape[1]), BF16),
            held=pltpu.VMEM((n_gain + 1,) + gains.shape, F32),
            got=pltpu.VMEM((n_gain,) + gains.shape, F32),
        ),
        4 * seq_len * width * (kv * G_PAD + heads * PAD) + heads * seq_len * seq_len * 8 * 256,
        collective_id,
        n_sems=12 * n_z + 48,
    )


def feed_forward_body(nb, rows_each, n_z, k):
    over = permuted("tensor", nb)
    peers = half_peers(nb)
    per_block = rows_each // Q_ROWS
    w = k.w
    width = w.shape[1]
    blk = width // (2 * n_z)
    other_x = permuted("dp", 1)
    near_n, near_c, far_n, far_c = k.near_n, k.near_c, k.far_n, k.far_c
    own_n = k.local(k.own_n, near_n.at[0])
    own_c = k.local(k.own_c, near_c.at[0])
    k.load_refs(k.hbm.w, k.w)
    own_far_c = k.local(k.own_far_c, far_c.at[0])
    k.meet([over, other_x] + [peer for _, peer in peers])
    far_first = [
        k.remote(k.own_n.at[rows_of(c)], far_n.at[0, rows_of(c)], over) for c in range(per_block)
    ]
    n_copies = [k.remote(k.own_n, near_n.at[r], peer) for r, peer in peers]
    c_copies = [k.remote(k.own_c, near_c.at[r], peer) for r, peer in peers]
    far_c_copies = [k.remote(k.own_far_c, far_c.at[r], peer) for r, peer in peers]
    own_n.wait()
    own_c.wait()
    k.ready()

    def rows_step(side, r, c):
        rows = slice(c * Q_ROWS, (c + 1) * Q_ROWS)
        start = (0 if side == NEAR else nb * rows_each) + r * rows_each + c * Q_ROWS
        kept = slice(start, start + Q_ROWS)
        n = k.of(side).n[r, rows, :]
        gate = dot_nn(n, w[0])
        up = dot_nn(n, w[1])
        sig = 1.0 / (1.0 + jnp.exp(-gate))
        silu = gate * sig
        hid = (silu * up).astype(BF16)
        k.hidden[kept, :] = hid
        dh = dot_nn(k.of(side).c[r, rows, :], w[2])
        dg = (dh * up * sig * (1.0 + gate * (1.0 - sig))).astype(BF16)
        du = (dh * silu).astype(BF16)
        k.d_gate[kept, :] = dg
        k.d_up[kept, :] = du
        k.of(side).grad[r, rows, :] = (dot_nt(dg, w[0]) + dot_nt(du, w[1])).astype(BF16)
        k.of(side).out[r, rows, :] = dot_nt(hid, w[2]).astype(BF16)

    for r in range(nb):
        if r:
            n_copies[r - 1].wait_recv()
            c_copies[r - 1].wait_recv()
        for c in range(per_block):
            rows_step(NEAR, r, c)
        for part, own, got in (
            (k.near_grad.at[r], k.near_own_grad, k.near_got_grad),
            (k.near_out.at[r], k.near_own_out, k.near_got_out),
        ):
            if r:
                k.remote(part, got.at[r - 1], peers[r - 1][1])
            else:
                k.store(part, own)
    own_far_c.wait()
    for copy in far_c_copies:
        copy.wait_recv()
    landing = []
    for c in range(per_block):
        rows = slice(c * Q_ROWS, (c + 1) * Q_ROWS)
        far_first[c].wait_recv()
        passed = [
            k.remote(far_n.at[0, rows_of(c)], far_n.at[r, rows_of(c)], peer) for r, peer in peers
        ]
        rows_step(FAR, 0, c)
        copies = []
        for r, peer in peers:
            passed[r - 1].wait_recv()
            rows_step(FAR, r, c)
            copies.append(
                k.remote(
                    k.far_grad.at[r, rows_of(c)], k.far_got_grad.at[r - 1, rows_of(c)], peer
                )
            )
        total = k.far_grad[0, rows, :].astype(F32)
        for r, copy in enumerate(copies):
            copy.wait_recv()
            total = total + k.far_got_grad[r, rows, :].astype(F32)
        k.far_grad[0, rows, :] = total.astype(BF16)
        landing.append(k.remote(k.far_grad.at[0, rows_of(c)], k.landed.at[rows_of(c)], over))
    k.store(k.far_out.at[0], k.far_own_out)
    for r, peer in peers:
        k.remote(k.far_out.at[r], k.far_got_out.at[r - 1], peer)
    half = nb * rows_each
    for which in (2, 0, 1):
        right = (k.d_gate, k.d_up, k.hidden)[which]
        lefts = {side: k.of(side).c if which == 2 else k.of(side).n for side in (NEAR, FAR)}

        def col_step(i, carry):
            cols = pl.ds(pl.multiple_of(i * G_COLS, G_COLS), G_COLS)
            total = None
            for s, side in enumerate((NEAR, FAR)):
                for r in range(nb):
                    start = s * half + r * rows_each
                    term = dot_tn(lefts[side][r, :, cols], right[start : start + rows_each, :])
                    total = term if total is None else total + term
            w[which, cols, :] = total.astype(BF16)
            return carry

        lax.fori_loop(0, width // G_COLS, col_step, 0)
        k.store(w.at[which], k.grads.at[which])
        if which == 2:
            d = lax.axis_index("dp")
            for n, i in enumerate((z_order(n_z) + [0])[:EARLY]):
                start = (lax.rem(d + 2 * i, 2 * n_z) ^ 1) * blk
                rows = pl.ds(pl.multiple_of(start, 16), blk)
                k.remote(w.at[which, rows], k.early.at[n], other_x)


def feed_forward(normed_two, cotangent, c_far, w, nb, n_z, collective_id):
    rows_each, width = normed_two.shape
    units = w.shape[2]
    sds = jax.ShapeDtypeStruct
    block = pltpu.VMEM((nb, rows_each, width), BF16)
    kept = pltpu.VMEM((2 * nb * rows_each, units), BF16)
    own = (sds((rows_each, width), BF16), IN_HBM)
    got = (sds((nb - 1, rows_each, width), BF16), IN_HBM)
    return frame_call(
        functools.partial(feed_forward_body, nb, rows_each, n_z),
        "feed_forward",
        dict(
            own_n=(normed_two, IN_HBM),
            own_c=(cotangent, IN_HBM),
            own_far_c=(c_far, IN_HBM),
            w=(w, LOAD),
        ),
        dict(
            grads=(sds(w.shape, BF16), IN_HBM),
            early=(sds((EARLY, width // (2 * n_z), units), BF16), IN_HBM),
            near_own_grad=own,
            near_got_grad=got,
            landed=own,
            near_own_out=own,
            near_got_out=got,
            far_own_out=own,
            far_got_out=got,
        ),
        dict(
            near_n=block,
            far_n=block,
            near_c=block,
            far_c=block,
            hidden=kept,
            d_gate=kept,
            d_up=kept,
            near_grad=block,
            far_grad=block,
            near_out=block,
            far_out=block,
            far_got_grad=pltpu.VMEM((nb - 1, rows_each, width), BF16),
        ),
        36 * nb * rows_each * width * units,
        collective_id,
    )


def attention_backward_rows(k, tag, i, length, kv):
    qkvp, dproj, datt, lse = k.of(tag).qkvp, k.of(tag).dproj, k.datt, k.of(tag).lse
    n = (i + 1) * Q_ROWS
    rows = slice(i * Q_ROWS, n)
    lane = lax.broadcasted_iota(jnp.int32, (Q_ROWS, PAD), 1)

    def one_head(h, carry):
        group = h // GROUP
        q_col = pl.ds(pl.multiple_of((4 * group + h % GROUP) * PAD, PAD), PAD)
        k_col = pl.ds(pl.multiple_of((4 * group + 2) * PAD, PAD), PAD)
        v_col = pl.ds(pl.multiple_of((4 * group + 3) * PAD, PAD), PAD)
        a_col = pl.ds(pl.multiple_of(h * PAD, PAD), PAD)
        q = qkvp[rows, q_col]
        keys = qkvp[0:n, k_col]
        do = datt[rows, a_col]
        row_lse = jnp.sum(jnp.where(lane == h, lse[rows, :], 0.0), axis=-1, keepdims=True)
        s = dot_nt(q, keys)
        row_ids = lax.broadcasted_iota(jnp.int32, (Q_ROWS, 1), 0) + i * Q_ROWS + 1
        limit = jnp.minimum(row_ids, length)
        col_ids = lax.broadcasted_iota(jnp.int32, (Q_ROWS, n), 1)
        s = jnp.where(col_ids < limit, s, NEGATIVE)
        p = jnp.exp2(s * (SCALE * LOG2E) - row_lse)
        dp = dot_nt(do, qkvp[0:n, v_col])
        inner = jnp.sum(p * dp, axis=-1, keepdims=True)
        ds = (p * (dp - inner)).astype(BF16)
        k.dv[group, 0:n, :] += dot_tn(p.astype(BF16), do)
        k.dk[group, 0:n, :] += dot_tn(ds, q)
        dq = dot_nn(ds, keys) * SCALE
        dproj[rows, q_col] = unrotate(k, dq, rows).astype(BF16)
        return carry

    lax.fori_loop(0, kv * GROUP, one_head, 0)


def unrotate(k, grad, rows):
    return grad * k.cos_t[rows, :] - swap_halves(grad) * k.sin_t[rows, :]


class Scatter:
    def __init__(self, k, n_z, blk):
        d = lax.axis_index("dp")
        self.k, self.peers, self.other_x = k, z_peers(n_z), permuted("dp", 1)
        self.order = [(which, i) for which in (2, 0, 1) for i in z_order(n_z) + [0]]

        def rows(owner):
            return pl.ds(pl.multiple_of(owner * blk, 16), blk)

        owners = {i: lax.rem(d + 2 * i, 2 * n_z) for i in range(n_z)}
        self.rows = {i: rows(owner) for i, owner in owners.items()}
        self.rows_other = {i: rows(owner ^ 1) for i, owner in owners.items()}
        self.z, self.extra, self.blank = d // 2, {}, []
        self.joined = n_z == 4
        if self.joined:
            k.zeros[...] = jnp.zeros_like(k.zeros)
            for end, i in ((self.z == 0, 1), (self.z == 3, 3)):
                for which in range(3):
                    sem = k.local_sem.at[k.next_local]
                    k.next_local += 1
                    copy = pltpu.make_async_copy(k.zeros, k.ffn_sums.at[which, i], sem)
                    pl.when(end)(copy.start)
                    self.blank.append((end, copy))
        self.sent, self.slots = [None] * EARLY, [None] * SLOTS
        self.next_arrival = 0

    def send(self):
        if len(self.sent) < len(self.order):
            which, i = self.order[len(self.sent)]
            self.sent.append(
                self.k.remote(
                    self.k.grads.at[which, self.rows_other[i]],
                    self.k.x_got.at[which, i],
                    self.other_x,
                )
            )

    def pump(self):
        if self.next_arrival == len(self.order):
            return False
        k, n = self.k, self.next_arrival
        which, i = self.order[n]
        self.next_arrival += 1
        own = k.local(k.grads.at[which, self.rows[i]], k.staged.at[0])
        if n < EARLY:
            other = k.local(k.early.at[n], k.staged.at[1])
        else:
            self.sent[n].wait_recv()
            self.send()
            other = k.local(k.x_got.at[which, i], k.staged.at[1])
        slot = n % SLOTS
        if self.slots[slot] is not None:
            self.slots[slot]()
        own.wait()
        other.wait()
        held = k.staged[0, :, :].astype(F32) + k.staged[1, :, :].astype(F32)
        k.narrow[slot, :, :] = held.astype(BF16)
        z = self.z
        if i and self.joined:
            sends = receives = None
            if i == 2:
                for extra in self.extra[which]:
                    extra.wait_recv()

                @pl.when((z == 1) | (z == 2))
                def _():
                    copy = pltpu.make_async_copy(
                        k.extra.at[which], k.staged.at[0], k.local_sem.at[k.next_local]
                    )
                    copy.start()
                    copy.wait()
                    k.narrow[slot, :, :] = (held + k.staged[0, :, :].astype(F32)).astype(BF16)

                k.next_local += 1
            elif i == 1:
                sends, receives = z < 3, z > 0
                past, gets, neighbour = z == 3, z == 2, self.peers[3]
            else:
                sends, receives = z > 0, z < 3
                past, gets, neighbour = z == 0, z == 1, self.peers[1]
            copies = [
                k.remote(k.narrow.at[slot], k.ffn_sums.at[which, i], self.peers[i], sends, receives)
            ]
            if i != 2:
                copies.append(
                    k.remote(k.narrow.at[slot], k.extra.at[which], neighbour, past, gets)
                )
                self.extra.setdefault(which, []).append(copies[1])

            def wait(copies=copies):
                for copy in copies:
                    copy.wait_send()

            self.slots[slot] = wait
        elif i:
            remote = k.remote(k.narrow.at[slot], k.ffn_sums.at[which, i], self.peers[i])
            self.slots[slot] = remote.wait_send
        else:
            self.slots[slot] = k.store(k.narrow.at[slot], k.ffn_sums.at[which, 0])
        return True


def attention_backward_body(nb, rows_each, kv, n_z, blk, k):
    d = lax.axis_index("dp")
    z, x = d // 2, lax.rem(d, 2)
    local = lax.rem(lax.axis_index("tensor"), nb)
    seq_len = nb * rows_each
    per_block = rows_each // Q_ROWS
    over = permuted("tensor", nb)
    other_x = permuted("dp", 1)
    peers = half_peers(nb)
    own_a = k.local(k.own_a, k.near_a.at[0])
    k.load_refs(k.hbm.w_out, k.w_out)
    k.load_refs(k.hbm.cos_t, k.cos_t)
    k.load_refs(k.hbm.sin_t, k.sin_t)
    for tag in (NEAR, FAR):
        k.load_refs(k.hbm.of(tag).qkvp, k.of(tag).qkvp)
        k.load_refs(k.hbm.of(tag).lse, k.of(tag).lse)
    late = [k.local(k.hbm.w_qkv, k.w_qkv), k.local(k.hbm.spread, k.spread)]
    for tag in (NEAR, FAR):
        late.append(k.local(k.hbm.of(tag).att, k.of(tag).att))
        late.append(k.local(k.hbm.of(tag).normed, k.of(tag).normed))
    tensor_peers, dp_peers = all_peers(2 * n_z, 2 * nb)
    k.meet(tensor_peers + dp_peers)
    far_first = [
        k.remote(k.own_a.at[rows_of(c)], k.far_a.at[0, rows_of(c)], over)
        for c in range(per_block)
    ]
    near_copies = [k.remote(k.own_a, k.near_a.at[r], peer) for r, peer in peers]
    landing, near_landing = [], []
    scatter = Scatter(k, n_z, blk)
    for _ in range(WINDOW):
        scatter.send()
    own_a.wait()
    k.ready()
    for copy in near_copies:
        copy.wait_recv()
    for tag, length in ((NEAR, k.lengths[0]), (FAR, k.lengths[1])):
        blocks, parts, dproj = k.of(tag).a, k.of(tag).parts, k.of(tag).dproj
        k.dk[...] = jnp.zeros_like(k.dk)
        k.dv[...] = jnp.zeros_like(k.dv)
        for c in range(per_block):
            rows = slice(c * Q_ROWS, (c + 1) * Q_ROWS)
            if tag == FAR:
                far_first[c].wait_recv()
                passed = [
                    k.remote(blocks.at[0, rows_of(c)], blocks.at[r, rows_of(c)], peer)
                    for r, peer in peers
                ]
                for copy in passed:
                    copy.wait_recv()
            for b in range(nb):
                i = b * per_block + c
                k.datt[i * Q_ROWS : (i + 1) * Q_ROWS, :] = dot_nn(
                    blocks[local ^ b, rows, :], k.w_out[...]
                ).astype(BF16)
                attention_backward_rows(k, tag, i, length, kv)
                scatter.pump()
        for j in range(kv):
            k_col = slice((4 * j + 2) * PAD, (4 * j + 3) * PAD)
            v_col = slice((4 * j + 3) * PAD, (4 * j + 4) * PAD)
            for i in range(seq_len // Q_ROWS):
                rows = slice(i * Q_ROWS, (i + 1) * Q_ROWS)
                dproj[rows, k_col] = unrotate(k, k.dk[j, rows, :] * SCALE, rows).astype(BF16)
                dproj[rows, v_col] = k.dv[j, rows, :].astype(BF16)
        for copy in late:
            copy.wait()
        late = []
        for c in range(per_block):
            rows = slice(c * Q_ROWS, (c + 1) * Q_ROWS)
            for b in range(nb):
                i = b * per_block + c
                part = dot_nt(dproj[i * Q_ROWS : (i + 1) * Q_ROWS, :], k.w_qkv[...])
                parts[local ^ b, rows, :] = part.astype(BF16)
            if tag == NEAR:
                for r, peer in peers:
                    near_landing.append(
                        k.remote(parts.at[r, rows_of(c)], k.near_got.at[r - 1, rows_of(c)], peer)
                    )
            else:
                copies = [
                    k.remote(parts.at[r, rows_of(c)], k.far_got.at[r - 1, rows_of(c)], peer)
                    for r, peer in peers
                ]
                total = parts[0, rows, :].astype(F32)
                for r, copy in enumerate(copies):
                    copy.wait_recv()
                    total = total + k.far_got[r, rows, :].astype(F32)
                parts[0, rows, :] = total.astype(BF16)
                landing.append(k.remote(parts.at[0, rows_of(c)], k.landed.at[rows_of(c)], over))
        if tag == NEAR:
            k.store(parts.at[0], k.near_own)
        scatter.pump()
    width = k.w_qkv.shape[0]
    arriving = []
    for which in range(kv + 1):

        def chunk(c, carry):
            cols = pl.ds(pl.multiple_of(c * G_COLS, G_COLS), G_COLS)
            total = None
            if which == 0:
                wide = k.near_att.shape[1]
                for tag in (NEAR, FAR):
                    for r in range(nb):
                        start = pl.multiple_of((local ^ r) * rows_each, rows_each)
                        term = dot_tn(
                            k.of(tag).a[r, :, cols], k.of(tag).att[pl.ds(start, rows_each), :]
                        )
                        total = term if total is None else total + term
                compact = dot_nt(total.astype(BF16), k.spread[:, :wide])
            else:
                part = slice((which - 1) * G_PAD, which * G_PAD)
                total = dot_tn(k.near_normed[:, cols], k.near_dproj[:, part])
                total += dot_tn(k.far_normed[:, cols], k.far_dproj[:, part])
                compact = dot_nt(total.astype(BF16), k.spread[...])
            compact = compact.astype(BF16)
            for b in range(G_COLS // blk):
                owner = c * (G_COLS // blk) + b
                shift = lax.rem(owner // 2 + n_z - z, n_z)
                value = compact[b * blk : (b + 1) * blk, :]

                @pl.when(x == lax.rem(owner, 2))
                def _():
                    k.same[which, shift, :, :] = value

                @pl.when(x != lax.rem(owner, 2))
                def _():
                    k.other[which, shift, :, :] = value

            return carry

        lax.fori_loop(0, width // G_COLS, chunk, 0)
        arriving.append(k.remote(k.other.at[which], k.arrived.at[which], other_x))
        if which == 0:
            k.remote(k.far_out, k.out_landed, over)
        scatter.pump()
    while scatter.pump():
        pass
    for end, copy in scatter.blank:
        pl.when(end)(copy.wait)
    for which in range(kv + 1):
        arriving[which].wait_recv()
        for i in z_order(n_z) + [0]:
            held = k.same[which, i, :, :].astype(F32) + k.arrived[which, i, :, :].astype(F32)
            k.same[which, i, :, :] = held.astype(BF16)
            if i:
                k.remote(k.same.at[which, i], k.sums.at[which, i], scatter.peers[i])
            else:
                k.store(k.same.at[which, 0], k.sums.at[which, 0])
    for copy in landing + near_landing:
        copy.wait_recv()
    k.flush(k.near_got, k.hbm.near_got)
    loads = [k.local(k.landed, k.near_a.at[0]), k.local(k.tokens, k.near_a.at[1])]
    for copy in loads:
        copy.wait()

    def gain_rows(i, carry):
        rows = pl.ds(pl.multiple_of(i * 32, 32), 32)
        dn = k.near_parts[0, rows, :].astype(F32) + k.near_a[0, rows, :].astype(F32)
        for r in range(nb - 1):
            dn = dn + k.near_got[r, rows, :].astype(F32)
        v = k.near_a[1, rows, :].astype(F32)
        inv = lax.rsqrt(jnp.mean(v * v, axis=-1, keepdims=True) + NORM_EPSILON)
        return carry + jnp.sum(dn * v * inv, axis=0, keepdims=True)

    t = lax.axis_index("tensor")
    k.first[t, 0:1, :] = lax.fori_loop(0, rows_each // 32, gain_rows, jnp.zeros((1, width), F32))
    k.first[t, 1:2, :] = k.gain_part[...]
    gain_copies = share(k, k.first, t, tensor_peers)
    k.second[d, :, :] = sum_slots(k.first, gain_copies)
    gain_copies = share(k, k.second, d, dp_peers)
    k.gain_sums[...] = sum_slots(k.second, gain_copies)


def attention_backward(
    attention_grad, tokens, gain_part, lengths, fwd, grads, early, far_out, tables, spread, nb, n_z, collective_id
):
    rows_each, width = attention_grad.shape
    seq_len = nb * rows_each
    w_qkv, w_out = fwd["w_qkv"], fwd["w_out"]
    kv = w_qkv.shape[1] // G_PAD
    heads = kv * GROUP
    blk = width // (2 * n_z)
    units = grads.shape[2]
    sds = jax.ShapeDtypeStruct
    inputs = dict(
        lengths=(lengths, IN_SMEM),
        own_a=(attention_grad, IN_HBM),
        w_qkv=(w_qkv, LOAD),
        w_out=(w_out, LOAD),
        cos_t=(tables[0], LOAD),
        sin_t=(tables[1], LOAD),
        spread=(spread, LOAD),
        grads=(grads, IN_HBM),
        early=(early, IN_HBM),
        far_out=(far_out, IN_HBM),
        tokens=(tokens, IN_HBM),
        gain_part=(gain_part, IN_VMEM),
    )
    for tag in (NEAR, FAR):
        for key in ("qkvp", "lse", "att", "normed"):
            inputs[tag + key] = (fwd[tag + key], LOAD)
    block = pltpu.VMEM((nb, rows_each, width), BF16)
    sums = sds((kv + 1, n_z, blk, G_COLS), BF16)
    own = (sds((rows_each, width), BF16), IN_HBM)
    return frame_call(
        functools.partial(attention_backward_body, nb, rows_each, kv, n_z, blk),
        "attention_backward",
        inputs,
        dict(
            near_own=own,
            near_got=(sds((nb - 1, rows_each, width), BF16), FLUSH),
            landed=own,
            out_landed=own,
            gain_sums=(sds((2, width), F32), IN_VMEM),
            sums=(sums, IN_HBM),
            x_got=(sds((3, n_z, blk, units), BF16), IN_HBM),
            ffn_sums=(sds((3, n_z, blk, units), BF16), IN_HBM),
            extra=(sds((3, blk, units), BF16), IN_HBM),
        ),
        dict(
            near_a=block,
            far_a=block,
            near_parts=block,
            far_parts=block,
            far_got=pltpu.VMEM((nb - 1, rows_each, width), BF16),
            near_dproj=pltpu.VMEM((seq_len, kv * G_PAD), BF16),
            far_dproj=pltpu.VMEM((seq_len, kv * G_PAD), BF16),
            datt=pltpu.VMEM((seq_len, heads * PAD), BF16),
            dk=pltpu.VMEM((kv, seq_len, PAD), F32),
            dv=pltpu.VMEM((kv, seq_len, PAD), F32),
            same=pltpu.VMEM(sums.shape, BF16),
            other=pltpu.VMEM(sums.shape, BF16),
            arrived=pltpu.VMEM(sums.shape, BF16),
            staged=pltpu.VMEM((2, blk, units), BF16),
            zeros=pltpu.VMEM((blk, units), BF16),
            first=pltpu.VMEM((2 * nb, 2, width), F32),
            second=pltpu.VMEM((2 * n_z, 2, width), F32),
            narrow=pltpu.VMEM((SLOTS, blk, units), BF16),
        ),
        8 * seq_len * width * (kv * G_PAD + heads * PAD) + heads * seq_len * seq_len * 20 * 256,
        collective_id,
        n_sems=12 * n_z + 48,
    )


def all_peers(n_dp, n_t):
    d, t = lax.axis_index("dp"), lax.axis_index("tensor")
    return (
        [{"tensor": lax.rem(t + i, n_t)} for i in range(1, n_t)],
        [{"dp": lax.rem(d + i, n_dp)} for i in range(1, n_dp)],
    )


def share(k, buffer, me, peers):
    return [k.remote(buffer.at[me], buffer.at[me], peer) for peer in peers]


def sum_slots(buffer, copies):
    for copy in copies:
        copy.wait_recv()
    total = buffer[0, :, :]
    for i in range(1, len(copies) + 1):
        total = total + buffer[i, :, :]
    return total


class Master:
    def __init__(self, refs, at, rows, cols, number, gradient, gradient_refs):
        self.refs, self.at, self.rows, self.cols = refs, at, rows, cols
        self.number, self.gradient, self.gradient_refs = number, gradient, gradient_refs


def moments_body(kv, n_z, k):
    correct_one = 1.0 / (1.0 - BETA_ONE**STEP)
    correct_two = 1.0 / (1.0 - BETA_TWO**STEP)
    row = lax.broadcasted_iota(jnp.int32, (8, PAD), 0)
    lane = lax.broadcasted_iota(jnp.int32, (8, PAD), 1)

    def z_sum(ref, which, rows, cols=slice(None)):
        total = ref[which, 0, rows, cols].astype(F32)
        for i in range(1, n_z):
            total = total + ref[which, i, rows, cols].astype(F32)
        return total

    def parts(h, m):
        return [
            (h.weight, m.weight),
            (h.first, m.first),
            (h.second, m.second),
            (h.next_first, m.next_first),
            (h.next_second, m.next_second),
            (h.update, m.update),
        ]

    gate_up = parts(k.hbm.of(GATE_UP), k.of(GATE_UP))
    down = parts(k.hbm.of(DOWN), k.of(DOWN))
    qkv = parts(k.hbm.of(QKV_), k.of(QKV_))
    out = parts(k.hbm.of(OUT), k.of(OUT))
    gains = parts(k.hbm.of(GAINS), k.of(GAINS))
    cols_out = k.of(OUT).weight.shape[1]
    units = []
    for which in range(2):
        rows, cols = k.of(GATE_UP).weight.shape[1:]
        units.append(
            Master(
                gate_up,
                (which,),
                rows,
                cols,
                2 + which,
                lambda at, which=which: z_sum(k.ffn_sums, which, at),
                [(k.hbm.ffn_sums.at[which], k.ffn_sums.at[which])],
            )
        )
    units.append(
        Master(
            down,
            (),
            *k.of(DOWN).weight.shape,
            4,
            lambda at: z_sum(k.ffn_sums, 2, at),
            [(k.hbm.ffn_sums.at[2], k.ffn_sums.at[2])],
        )
    )
    units.append(
        Master(
            qkv,
            (),
            *k.of(QKV_).weight.shape,
            0,
            lambda at: jnp.concatenate([z_sum(k.sums, 1 + j, at) for j in range(kv)], axis=1),
            [(k.hbm.sums, k.sums)],
        )
    )
    units.append(
        Master(
            out,
            (),
            *k.of(OUT).weight.shape,
            1,
            lambda at: z_sum(k.sums, 0, at, slice(0, cols_out)),
            [],
        )
    )
    for which in range(2):
        units.append(
            Master(
                gains,
                (which,),
                1,
                k.of(GAINS).weight.shape[2],
                5 + which,
                lambda at, which=which: k.gain_sum[which, at, :],
                [],
            )
        )
    loads = []
    for unit in units:
        pairs = list(unit.gradient_refs)
        for source, target in unit.refs[:3]:
            pairs.append((source.at[unit.at], target.at[unit.at]) if unit.at else (source, target))
        loads.append([k.local(source, target) for source, target in pairs])
    squares = jnp.zeros((8, PAD), F32)
    for unit, copies in zip(units, loads):
        for copy in copies:
            copy.wait()
        weight, first, second, next_first, next_second, direction = [ref for _, ref in unit.refs]
        tile = unit.rows if unit.rows % 32 else 32

        def one(i, carry):
            rows = pl.ds(pl.multiple_of(i * tile, tile) if unit.rows > tile else 0, tile)
            at = unit.at + (rows, slice(None))
            g = unit.gradient(rows)
            w = weight[at]
            moment = BETA_ONE * first[at] + (1.0 - BETA_ONE) * g
            square = BETA_TWO * second[at] + (1.0 - BETA_TWO) * g * g
            next_first[at] = moment
            next_second[at] = square
            update = (moment * correct_one) / (
                jnp.sqrt(square * correct_two) + ADAM_EPSILON
            ) + WEIGHT_DECAY * w
            direction[at] = update
            return (
                carry[0] + jnp.sum(w * w, axis=0, keepdims=True),
                carry[1] + jnp.sum(update * update, axis=0, keepdims=True),
            )

        zero = jnp.zeros((1, unit.cols), F32)
        w_sum, u_sum = lax.fori_loop(0, unit.rows // tile, one, (zero, zero))
        w_sum = jnp.sum(w_sum, axis=1, keepdims=True)
        u_sum = jnp.sum(u_sum, axis=1, keepdims=True)
        mark = lane == unit.number
        squares += jnp.where(mark & (row == 0), w_sum, 0.0)
        squares += jnp.where(mark & (row == 1), u_sum, 0.0)
        for target, source in unit.refs[3:]:
            if unit.at:
                k.store(source.at[unit.at], target.at[unit.at])
            else:
                k.store(source, target)
    k.squares[...] = squares


def moments(weights, firsts, seconds, ffn_sums, sums, gain_sum, kv, n_z):
    inputs, outputs = {}, {}
    sds = jax.ShapeDtypeStruct
    names = (GATE_UP, DOWN, QKV_, OUT, GAINS)
    for key, weight, first, second in zip(names, weights, firsts, seconds):
        shape = (sds(weight.shape, F32), FLUSH)
        for table, prefix in (
            (dict(weight=(weight, LOAD), first=(first, LOAD), second=(second, LOAD)), inputs),
            (dict(next_first=shape, next_second=shape, update=shape), outputs),
        ):
            prefix.update({key + part: entry for part, entry in table.items()})
    inputs.update(
        ffn_sums=(ffn_sums, LOAD), sums=(sums, LOAD), gain_sum=(gain_sum, IN_VMEM)
    )
    outputs.update(squares=(sds((8, PAD), F32), IN_VMEM))
    return frame_call(
        functools.partial(moments_body, kv, n_z),
        "moments",
        inputs,
        outputs,
        {},
        0,
        None,
        n_sems=64,
    )


def sum_all_body(n_dp, n_t, k):
    d, t = lax.axis_index("dp"), lax.axis_index("tensor")
    tensor_peers, dp_peers = all_peers(n_dp, n_t)
    k.first[t, :, :] = k.value[...]
    k.meet(tensor_peers + dp_peers)
    copies = share(k, k.first, t, tensor_peers)
    k.second[d, :, :] = sum_slots(k.first, copies)
    copies = share(k, k.second, d, dp_peers)
    k.total[...] = sum_slots(k.second, copies)


def sum_all(value, n_dp, n_t, collective_id):
    return frame_call(
        functools.partial(sum_all_body, n_dp, n_t),
        "sum_everywhere",
        dict(value=(value, IN_VMEM)),
        dict(total=(jax.ShapeDtypeStruct(value.shape, F32), IN_VMEM)),
        dict(
            first=pltpu.VMEM((n_t,) + value.shape, F32),
            second=pltpu.VMEM((n_dp,) + value.shape, F32),
        ),
        0,
        collective_id,
        n_sems=n_dp + n_t,
    )["total"]


def apply_body(numbers, k):
    scale = LEARN_RATE * (jnp.sqrt(k.squares[0:1, :]) / jnp.sqrt(k.squares[1:2, :]))
    names = (GATE_UP, DOWN, QKV_, OUT, GAINS)
    loads = [
        [
            k.local(k.hbm.of(name).weight, k.of(name).weight),
            k.local(k.hbm.of(name).update, k.of(name).update),
        ]
        for name in names
    ]
    for name, number, copies in zip(names, numbers, loads):
        for copy in copies:
            copy.wait()
        weight, update, new = k.of(name).weight, k.of(name).update, k.of(name).new
        for which in range(weight.shape[0]):
            factor = scale[:, number + which : number + which + 1]
            rows = weight.shape[1]
            tile = rows if rows % 32 else 32

            def one(i, carry):
                at = pl.ds(pl.multiple_of(i * tile, tile) if rows > tile else 0, tile)
                new[which, at, :] = weight[which, at, :] - factor * update[which, at, :]
                return carry

            lax.fori_loop(0, rows // tile, one, 0)
        k.flush(new, k.hbm.of(name).new)


def apply_updates(weights, updates, squares):
    names = (GATE_UP, DOWN, QKV_, OUT, GAINS)
    inputs, outputs = dict(squares=(squares, IN_VMEM)), {}
    for key, weight, update in zip(names, weights, updates):
        for part, array in dict(weight=weight, update=update).items():
            inputs[key + part] = (array, LOAD)
        for part in dict(new=0):
            outputs[key + part] = (jax.ShapeDtypeStruct(weight.shape, F32), FLUSH)
    done = frame_call(
        functools.partial(apply_body, (2, 4, 0, 1, 5)), "new_masters", inputs, outputs, {}, 0, None
    )
    return [done[key + part] for key in names for part in dict(new=0)]


def rms_norm(values, gain_row):
    return (
        values
        * lax.rsqrt(jnp.mean(values * values, axis=-1, keepdims=True) + NORM_EPSILON)
        * gain_row
    )


def rotary_tables():
    half = HEAD // 2
    frequency = ROPE_THETA ** (-(jnp.arange(half, dtype=F32) * (2.0 / HEAD)))
    angles = jnp.arange(SEQ_LEN, dtype=F32)[:, None] * frequency[None, :]
    cosine, sine = jnp.cos(angles), jnp.sin(angles)
    empty = jnp.zeros((SEQ_LEN, PAD - HEAD), F32)
    return (
        jnp.concatenate([cosine, cosine, empty], axis=1),
        jnp.concatenate([-sine, sine, empty], axis=1),
    )


def shards(
    tokens,
    cotangent,
    lengths,
    qkv_weight,
    out_weight,
    gate_up_weight,
    down_weight,
    norm_gains,
    qkv_first,
    out_first,
    gate_up_first,
    down_first,
    gains_first,
    qkv_second,
    out_second,
    gate_up_second,
    down_second,
    gains_second,
):
    rows_each, width = tokens.shape
    n_t = lax.axis_size("tensor")
    n_dp = lax.axis_size("dp")
    n_z = n_dp // 2
    nb = n_t // 2
    t = lax.axis_index("tensor")
    d = lax.axis_index("dp")
    mine = t // nb
    lengths = jnp.stack([lengths[mine], lengths[1 - mine]])
    spread = spread_matrix().astype(BF16)
    blk = qkv_weight.shape[0]
    kv = qkv_weight.shape[1] // G_COLS

    gain_cols = norm_gains.shape[1]
    gain_start = (d * n_t + t) * gain_cols
    gain_rows = lax.dynamic_update_slice(
        jnp.zeros((2, width), F32),
        norm_gains.astype(BF16).astype(F32),
        (0, gain_start),
    )
    halves = (qkv_weight, out_weight.T, gate_up_weight, down_weight.T)
    tables = rotary_tables()
    fwd = opening(
        tokens, cotangent, lengths, gain_rows, halves, tables, spread, n_t, n_z, 0
    )
    inputs = tokens.astype(F32)
    attention_gain, feedforward_gain = fwd["gain_sum"][0:1], fwd["gain_sum"][1:2]
    residual = fwd["residual"]

    ff = feed_forward(fwd["normed_two"], cotangent, fwd["c_far"], fwd["w_ffn"], nb, n_z, 2)

    def total(*arrays):
        result = 0.0
        for array in arrays:
            array = array.astype(F32)
            result = result + (array if array.ndim == 2 else jnp.sum(array, axis=0))
        return result

    normed_two_grad = total(ff["near_own_grad"], ff["near_got_grad"], ff["landed"])
    _, norm_pull = jax.vjp(rms_norm, residual, feedforward_gain)
    residual_part, ffn_gain_grad = norm_pull(normed_two_grad)
    residual_grad = cotangent.astype(F32) + residual_part
    far_out = total(ff["far_own_out"], ff["far_got_out"]).astype(BF16)
    bwd = attention_backward(
        residual_grad.astype(BF16),
        tokens,
        ffn_gain_grad,
        lengths,
        fwd,
        ff["grads"],
        ff["early"],
        far_out,
        tables,
        spread,
        nb,
        n_z,
        3,
    )
    normed_grad = total(bwd["near_own"], bwd["near_got"], bwd["landed"])
    _, first_pull = jax.vjp(rms_norm, inputs, attention_gain)
    input_part, _ = first_pull(normed_grad)
    grad_tokens = residual_grad + input_part
    layer_out = (residual + total(ff["near_own_out"], ff["near_got_out"], bwd["out_landed"])).astype(
        BF16
    )
    gain_sum = lax.dynamic_slice(bwd["gain_sums"], (0, gain_start), (2, gain_cols))

    def lift(gains):
        return gains[:, None, :]

    done = moments(
        (gate_up_weight, down_weight.T, qkv_weight, out_weight.T, lift(norm_gains)),
        (gate_up_first, down_first.T, qkv_first, out_first.T, lift(gains_first)),
        (gate_up_second, down_second.T, qkv_second, out_second.T, lift(gains_second)),
        bwd["ffn_sums"],
        bwd["sums"],
        lift(gain_sum),
        kv,
        n_z,
    )
    all_squares = sum_all(done["squares"], n_dp, n_t, 5)
    norms = jnp.sqrt(all_squares)

    def flat(array):
        return array if array.ndim == 3 else array[None]

    new_gate_up, new_down, new_qkv, new_out, new_gains = apply_updates(
        [flat(a) for a in (gate_up_weight, down_weight.T, qkv_weight, out_weight.T, lift(norm_gains))],
        [flat(done[key + part]) for key in (GATE_UP, DOWN, QKV_, OUT, GAINS) for part in dict(update=0)],
        all_squares,
    )
    first, second = (
        dict(
            gate_up=done[GATE_UP + part],
            down=done[DOWN + part].T,
            qkv=done[QKV_ + part],
            out=done[OUT + part].T,
            gains=done[GAINS + part][:, 0, :],
        )
        for part in ("next_first", "next_second")
    )
    new = (new_qkv[0], new_out[0].T, new_gate_up, new_down[0].T, new_gains[:, 0, :])
    names = ("qkv", "out", "gate_up", "down", "gains")
    return (
        layer_out,
        grad_tokens,
        *new,
        *[first[key] for key in names],
        *[second[key] for key in names],
        norms[0, :7],
        norms[1, :5],
        norms[1, 5:7],
    )


def solution(mesh):
    rows = P(("dp", "tensor"), None)
    gains = P(None, ("dp", "tensor"))
    weights = (P("dp", "tensor"), P("tensor", "dp"), P(None, "dp", "tensor"), P("tensor", "dp"), gains)
    in_specs = (rows, rows, P("dp")) + weights * 3
    out_specs = (rows, rows) + weights * 3 + (P(), P(), P())
    return jax.shard_map(shards, mesh=mesh, in_specs=in_specs, out_specs=out_specs, check_vma=False)
```
